32 devices in a mesh: grp: 2 (over y), blk: 4 (over z), col: 2 (over x), rep: 2 (over core).
Axes of the slice: x: 2, y: 2, z: 4, core: 2. Of those that a mesh axis runs over, the one named last changes fastest.
Arguments:
- coords: float32 [3, 131072], P(None, ('grp', 'blk')), parts along dimension 1, may hold values from 0 to 1
- observations: float32 [131072], P(('grp', 'blk')), parts along dimension 0, may hold values from -6 to 6
- nugget: float32 [131072], P(('grp', 'blk')), parts along dimension 0, may hold values from 0.1 to 1
- tile_pairs: int32 [2, 8192], P(None, ('grp', 'blk', 'col', 'rep')), parts along dimension 1, may hold values from 0 to 511, as said below
- tile_live: int32 [32], P(('grp', 'blk', 'col', 'rep')), parts along dimension 0, may hold values from 64 to 256, as said below
Outputs:
- solution_field: float32 [131072], P(('grp', 'blk')), parts along dimension 0
- residual: float32 [131072], P(('grp', 'blk')), parts along dimension 0
The draws below stay inside these ranges and needn't reach their ends.
There are 2 independent parts, one for each index of `grp`. The reference program is written for one: setup_inputs(seed, part) draws one part's arguments, and reference() takes and returns one part's arrays. A program takes and returns all parts, laid end to end along the dimension named above; each array names one. Nothing has to cross between parts.
Inputs may be any that keep to these rules, and one draw needn't show every extreme that they name: `tile_pairs`: entries name point blocks. Every slot has its row block, or else its column block, among the 128 blocks of its own device's index of blk; most slots have the row block there. Call the slot's other block its column block when the row block is the device's own, else its row block. Of one device's slots, at most (259) // 4 have their other block among the blocks of any one index of blk, and on every device some index gets exactly that many. Slots at or beyond a device's live count are ignored. `tile_live`: some device has all 256 slots live.
All inputs are finite; a program needn't handle non-finite values.
Results may differ from the reference program's by a relative error of at most 0.0003.
Values sent between devices are 32-bit elements; how exact they have to be, the bound alone decides.
No kernel may reach another device: no remote copies, remote signals or barrier semaphores. Data moves between devices by JAX's collectives and lax.ppermute only.
A program may use at most 128 MiB of HBM per device.

```python
import math
import jax
import jax.numpy as jnp
from jax import lax

BS = 128
RB = 128
SLOTS = 256
ITERS = 3
NB = 512
NPTS = 65536
GROUP = 4
DEVS = 16
TILES = 4096
TPR = 8


def draw_tile_pairs(key, part):
    key = jax.random.fold_in(key, 11)
    keys = jax.random.split(key, 5)
    owners_count = NB // RB
    slot_ids = jnp.arange(TILES, dtype=jnp.int32)
    device = slot_ids // SLOTS
    within = slot_ids % SLOTS
    owner = device // GROUP
    shifts = jax.random.randint(keys[4], (DEVS,), 0, owners_count)
    partner = (within + shifts[device]) % owners_count
    home = owner * RB + jax.random.randint(keys[0], (TILES,), 0, RB)
    remote = partner * RB + jax.random.randint(keys[1], (TILES,), 0, RB)
    spilled = jax.random.randint(keys[2], (TILES,), 0, 4) == 0
    rows_ids = jnp.where(spilled, remote, home)
    cols_ids = jnp.where(spilled, home, remote)
    return jnp.stack([rows_ids, cols_ids]).astype(jnp.int32)


def draw_tile_live(key, part):
    key = jax.random.fold_in(key, 23)
    keys = jax.random.split(key, 2)
    counts = jax.random.randint(keys[0], (DEVS,), max(1, SLOTS // 4), SLOTS + 1)
    fullest = jax.random.randint(keys[1], (), 0, DEVS)
    return jnp.where(jnp.arange(DEVS) == fullest, SLOTS, counts).astype(jnp.int32)


def levels(stream_key, dims, cuts, smallest, top_value):
    def one(dim, shards_of):
        heights = jax.random.uniform(jax.random.fold_in(jax.random.fold_in(stream_key, 6), dim), (shards_of,), jnp.float32, smallest / len(cuts), top_value / len(cuts))
        return jnp.repeat(jnp.exp(heights), dims[dim] // shards_of).reshape((-1,) + (1,) * (len(dims) - dim - 1))

    level = one(*cuts[0])
    for cut in cuts[1:]:
        level = level * one(*cut)
    return level


def centred(own_key, shape, width, limit, cuts=(), kind=jnp.bfloat16):
    loudness = levels(own_key, shape, cuts, -0.22, 0.18) if cuts else 1.0
    drawn = jax.random.normal(own_key, shape, jnp.float32) * width * loudness
    return jnp.minimum(jnp.maximum(drawn, -limit), limit).astype(kind)


def setup_inputs(seed: int = 0, part: int = 0) -> dict:
    streams_of = jax.random.split(jax.random.key(seed), 6)
    part_splits = jax.random.split(jax.random.fold_in(streams_of[5], part), 6)
    return {
        "coords": jnp.clip(1.0 * jax.random.uniform(part_splits[0], (3, NPTS), jnp.float32) ** levels(part_splits[0], (3, NPTS), ((1, 4),), -0.2, 0.2), 0.0, 1.0),
        "observations": centred(part_splits[1], (NPTS,), 1.0, 6.0, ((0, 4),), jnp.float32),
        "nugget": jnp.clip(jnp.exp(math.log(1.0) - 2.3025851 * jax.random.uniform(part_splits[2], (NPTS,), jnp.float32) ** levels(part_splits[2], (NPTS,), ((0, 4),), -0.2, 0.2)), 0.1, 1.0),
        "tile_pairs": draw_tile_pairs(jax.random.fold_in(jax.random.fold_in(streams_of[5], part), 71), part),
        "tile_live": draw_tile_live(jax.random.fold_in(jax.random.fold_in(streams_of[5], part), 71), part),
    }


support = 0.3

def tile_of(row_points, col_points, amplitude):
    offset = row_points[:, :, None] - col_points[:, None, :]
    scaled = jnp.sqrt(lax.optimization_barrier(jnp.sum(offset * offset, axis=0))) / support
    remain = jnp.maximum(1.0 - scaled, 0.0)
    return amplitude * remain ** 4 * (4.0 * scaled + 1.0)

def apply_off(coords, tile_pairs, tile_live, vector_in):
    amplitude = 16.0 / (BS * TPR)
    grouped = coords.reshape(3, NB, BS)
    blocks = vector_in.reshape(NB, BS)
    slot_ids = jnp.arange(TILES, dtype=jnp.int32)
    alive_mask = (slot_ids % SLOTS < tile_live[slot_ids // SLOTS]).astype(jnp.float32)

    def accumulate(summed, entries):
        row_block, col_block, live_flag = entries
        tiles = tile_of(grouped[:, row_block], grouped[:, col_block], amplitude) * live_flag
        forward = jnp.dot(tiles, blocks[col_block], precision=lax.Precision.HIGHEST)
        backward = jnp.dot(blocks[row_block], tiles, precision=lax.Precision.HIGHEST)
        summed = summed.at[row_block].add(forward)
        summed = summed.at[col_block].add(backward)
        return (summed, None)
    summed, unused = lax.scan(accumulate, jnp.zeros((NB, BS), jnp.float32), (tile_pairs[0], tile_pairs[1], alive_mask))
    return summed.reshape(NB * BS)

def reference(coords, observations, nugget, tile_pairs, tile_live):
    diagonal = nugget + apply_off(coords, tile_pairs, tile_live, jnp.ones((NB * BS,), jnp.float32))

    def mapped_of(vector_in):
        return diagonal * vector_in + apply_off(coords, tile_pairs, tile_live, vector_in)
    solution_field = jnp.zeros_like(observations)
    residual, direction = (observations, observations)
    norm_now = jnp.sum(residual * residual)
    for sweep in range(ITERS):
        mapped = mapped_of(direction)
        step_len = norm_now / jnp.sum(direction * mapped)
        solution_field = solution_field + step_len * direction
        residual = residual - step_len * mapped
        norm_next = jnp.sum(residual * residual)
        direction = residual + norm_next / norm_now * direction
        norm_now = norm_next
    return (solution_field, residual)
```

```python
import functools

import jax
import jax.numpy as jnp
from jax import lax
from jax.experimental import pallas as pl
from jax.experimental.pallas import tpu as pltpu
from jax.sharding import PartitionSpec as P

BS = 128
ITERS = 3
SUPPORT = 0.3
DEPTH = 48
UNROLL = 4
EVERY = ("blk", "col", "rep")
PLANE = ("col", "rep")
VMEM = pl.BlockSpec(memory_space=pltpu.VMEM)
SMEM = pl.BlockSpec(memory_space=pltpu.SMEM)
PARAMS = pltpu.CompilerParams(vmem_limit_bytes=48 * 1024 * 1024)
BF16 = jnp.bfloat16
F32 = jnp.float32


class Sizes:
    def __init__(self, points, slots):
        self.blks = lax.axis_size("blk")
        self.reps = lax.axis_size("rep")
        self.plane = lax.axis_size("col") * self.reps
        self.devs = self.blks * self.plane
        self.points = points
        self.slots = slots
        self.local_blocks = points // BS
        self.blocks = self.local_blocks * self.blks
        self.own = self.local_blocks // self.plane
        self.capacity = 2 * self.plane * slots
        per_row = slots * self.devs // self.blocks
        self.scale = 16.0 / (BS * per_row) / 256.0

    def me(self):
        return (lax.axis_index("blk") * lax.axis_size("col") + lax.axis_index("col")) * self.reps + lax.axis_index(
            "rep"
        )


def swap(x, axes, count, code):
    return lax.ppermute(x, axes, [(i, i ^ code) for i in range(count)])


def spread(x, sz):
    if sz.devs <= 16:
        return [x] + [swap(x, EVERY, sz.devs, s) for s in range(1, sz.devs)], [[s] for s in range(sz.devs)]
    column = jnp.concatenate([x] + [swap(x, "blk", sz.blks, s) for s in range(1, sz.blks)], axis=0)
    arrays = [column] + [swap(column, PLANE, sz.plane, s) for s in range(1, sz.plane)]
    return arrays, [[z * sz.plane + s for z in range(sz.blks)] for s in range(sz.plane)]


def assemble(refs, codes, me, rows, target):
    for ref, parts in zip(refs, codes):
        for k, code in enumerate(parts):
            start = pl.multiple_of(jnp.bitwise_xor(me, code) * rows, 8)
            target[pl.ds(start, rows), :] = ref[k * rows : (k + 1) * rows, :]


def split3(x):
    high = x.astype(BF16).astype(F32)
    rest = x - high
    middle = rest.astype(BF16).astype(F32)
    return high, middle, rest - middle


def lhs_kernel(sz, coords_ref, out_ref):
    quarter = lax.axis_index("col") * sz.reps + lax.axis_index("rep")
    unit = jnp.ones((1, BS), F32)
    for i in range(sz.own):
        start = pl.multiple_of((quarter * sz.own + i) * BS, BS)
        x = (coords_ref[:, pl.ds(start, BS)] - 0.5) * (4.0 / SUPPORT)
        norm = jnp.sum(x * x, axis=0, keepdims=True)
        h, m, l = split3(jnp.concatenate([x, unit, norm, jnp.zeros((3, BS), F32)], axis=0))
        feats = jnp.concatenate([h, h, m, m, h, l, jnp.zeros((BS - DEPTH, BS), F32)], axis=0)
        out_ref[i * BS : (i + 1) * BS, :] = feats.T.astype(BF16)
    out_ref[sz.own * BS :, :] = jnp.zeros((BS, BS), BF16)


def list_kernel(sz, codes, *refs):
    pieces = refs[: len(codes)]
    out_ref, count_ref, target, other, place, value = refs[len(codes) :]
    me = sz.me()
    lines = sz.slots // BS
    at = 0
    for ref, parts in zip(pieces, codes):
        for k in range(len(parts)):
            base = 2 * lines * k
            rows = ref[base : base + lines, :]
            cols = ref[base + lines : base + 2 * lines, :]
            target[at : at + lines, :] = rows
            other[at : at + lines, :] = cols
            target[at + lines : at + 2 * lines, :] = cols
            other[at + lines : at + 2 * lines, :] = rows
            at += 2 * lines
    local = target[...] - me * sz.own
    mine = jnp.logical_and(local >= 0, local < sz.own)
    flags = jnp.where(mine, 1.0, 0.0)
    a = lax.broadcasted_iota(jnp.int32, (BS, BS), 0)
    b = lax.broadcasted_iota(jnp.int32, (BS, BS), 1)
    before = jnp.dot(flags.astype(BF16), jnp.where(a < b, 1.0, 0.0).astype(BF16), preferred_element_type=F32)
    totals = jnp.broadcast_to(jnp.sum(flags, axis=1, keepdims=True), (at, BS))
    a = lax.broadcasted_iota(jnp.int32, (at, at), 0)
    b = lax.broadcasted_iota(jnp.int32, (at, at), 1)
    above = jnp.dot(jnp.where(b < a, 1.0, 0.0).astype(BF16), totals.astype(BF16), preferred_element_type=F32)
    place[...] = jnp.where(mine, above + before, -1.0)
    value[...] = (local + 256 * other[...]).astype(F32)
    count = jnp.sum(flags).astype(jnp.int32)
    count_ref[0] = count
    sub = lax.broadcasted_iota(jnp.int32, (BS, BS), 0)
    lane = lax.broadcasted_iota(jnp.int32, (1, BS), 1)

    def chunk(c, unused):
        slot = (sub + c * BS).astype(F32)

        def line(r, total):
            hit = place[pl.ds(r, 1), :] == slot
            return total + jnp.where(hit, value[pl.ds(r, 1), :], 0.0)

        total = lax.fori_loop(0, at, line, jnp.zeros((BS, BS), F32), unroll=4)
        found = jnp.sum(total.T, axis=0, keepdims=True).astype(jnp.int32)
        out_ref[pl.ds(c, 1), :] = jnp.where(lane + c * BS < count, found, sz.own)
        return unused

    lax.fori_loop(0, lax.shift_right_logical(count + BS - 1, 7), chunk, 0)


def sweep(list_ref, count_ref, lhs_ref, rhs_ref, vec_ref, acc, acc_ones=None):
    acc[...] = jnp.zeros_like(acc)
    if acc_ones is not None:
        acc_ones[...] = jnp.zeros_like(acc_ones)

    def group(g, unused):
        for u in range(UNROLL):
            entry = list_ref[g * UNROLL + u]
            i = jnp.bitwise_and(entry, 255)
            j = lax.shift_right_logical(entry, 8)
            rows = pl.ds(pl.multiple_of(i * BS, BS), BS)
            squared = jnp.dot(
                lhs_ref[rows, :DEPTH],
                rhs_ref[pl.ds(pl.multiple_of(j * DEPTH, DEPTH), DEPTH), :],
                preferred_element_type=F32,
            )
            squared = jnp.maximum(squared, 1e-20)
            remain = jnp.maximum(4.0 - squared * lax.rsqrt(squared), 0.0)
            twice = remain * remain
            tile = twice * twice * (5.0 - remain)
            if acc_ones is not None:
                acc_ones[rows, :] += tile
            acc[rows, :] += tile * vec_ref[pl.ds(j, 1), :]
        return unused

    groups = lax.div(count_ref[0] + (UNROLL - 1), UNROLL)
    lax.fori_loop(0, groups, group, 0)


def finish(sz, acc, out_ref):
    unit = jnp.ones((8, BS), BF16)
    across = (((1,), (1,)), ((), ()))
    for i in range(sz.own):
        whole = acc[i * BS : (i + 1) * BS, :]
        high = whole.astype(BF16)
        low = (whole - high.astype(F32)).astype(BF16)
        y = lax.dot_general(unit, high, across, preferred_element_type=F32)
        y = y + lax.dot_general(unit, low, across, preferred_element_type=F32)
        out_ref[i : i + 1, :] = y[0:1, :] * sz.scale


def total_of(x):
    return jnp.sum(jnp.sum(x, axis=0, keepdims=True), axis=1, keepdims=True)


def first_kernel(sz, coord_codes, *refs):
    list_ref, count_ref, lhs_ref, nugget_ref = refs[:4]
    pieces = len(coord_codes)
    coord_refs = refs[4 : 4 + pieces]
    obs_refs = refs[4 + pieces : 4 + 2 * pieces]
    rhs_ref, obs_ref, diag_ref, mapped_ref, norm_ref, acc, acc_ones, total_row = refs[4 + 2 * pieces :]
    blk, rep = lax.axis_index("blk"), lax.axis_index("rep")
    unit = jnp.ones((1, BS), F32)
    for (z, r), coord_ref, piece_ref in zip(coord_codes, coord_refs, obs_refs):
        rows = piece_ref.shape[0]
        first = jnp.bitwise_xor(blk, z) * sz.local_blocks
        if r is not None:
            first = first + jnp.bitwise_xor(rep, r) * rows
        first = pl.multiple_of(first, 8)
        obs_ref[pl.ds(first, rows), :] = piece_ref[...]

        def one(k, unused, coord_ref=coord_ref, first=first):
            x = (coord_ref[:, pl.ds(pl.multiple_of(k * BS, BS), BS)] - 0.5) * (4.0 / SUPPORT)
            norm = jnp.sum(x * x, axis=0, keepdims=True)
            h, m, l = split3(jnp.concatenate([-2.0 * x, norm, unit, jnp.zeros((3, BS), F32)], axis=0))
            feats = jnp.concatenate([h, m, h, m, l, h], axis=0).astype(BF16)
            rhs_ref[pl.ds(pl.multiple_of((first + k) * DEPTH, DEPTH), DEPTH), :] = feats
            return unused

        lax.fori_loop(0, rows, one, 0, unroll=4)
    sweep(list_ref, count_ref, lhs_ref, rhs_ref, obs_ref, acc, acc_ones)
    finish(sz, acc_ones, total_row)
    finish(sz, acc, mapped_ref)
    quarter = lax.axis_index("col") * sz.reps + rep
    diag = nugget_ref[pl.ds(pl.multiple_of(quarter * sz.own, 8), sz.own), :] + total_row[...]
    diag_ref[...] = diag
    mapped_ref[...] += diag * obs_ref[pl.ds(pl.multiple_of(sz.me() * sz.own, 8), sz.own), :]
    norm_ref[...] = jnp.broadcast_to(total_of(obs_ref[...] * obs_ref[...]), (8, BS))


def step_kernel(sz, codes, last, *refs):
    list_ref, count_ref, lhs_ref, rhs_ref, diag_ref, norm_ref, field_ref, resid_ref, dirn_ref = refs[:9]
    pieces = refs[9 : 9 + len(codes)]
    rest = refs[9 + len(codes) :]
    mapped_ref, next_norm_ref, next_field_ref, next_resid_ref, next_dirn_ref = rest[:5]
    if last:
        dot_ref, mapped, dirn, acc = rest[5:]
    else:
        mapped, acc = rest[5:]
        dirn = next_dirn_ref
    me = sz.me()
    assemble(pieces, codes, me, sz.own, mapped)
    norm = norm_ref[0:1, 0:1]
    step = norm / total_of(dirn_ref[...] * mapped[...])
    resid = resid_ref[...] - step * mapped[...]
    next_norm = total_of(resid * resid)
    dirn[...] = resid + (next_norm / norm) * dirn_ref[...]
    next_norm_ref[...] = jnp.broadcast_to(next_norm, (8, BS))
    home = pl.ds(pl.multiple_of(lax.axis_index("blk") * sz.local_blocks, 8), sz.local_blocks)
    own = pl.ds(pl.multiple_of(me * sz.own, 8), sz.own)
    field = step * dirn_ref[home, :]
    if last:
        next_field_ref[...] = field_ref[...] + field
        next_resid_ref[...] = resid_ref[home, :] - step * mapped[home, :]
        next_dirn_ref[...] = dirn[home, :]
    else:
        next_field_ref[...] = field
        next_resid_ref[...] = resid
    sweep(list_ref, count_ref, lhs_ref, rhs_ref, dirn, acc)
    finish(sz, acc, mapped_ref)
    mapped_ref[...] += diag_ref[...] * dirn[own, :]
    if last:
        dot_ref[...] = jnp.broadcast_to(total_of(mapped_ref[...] * dirn[own, :]), (8, BS))


def last_kernel(sz, dots, *refs):
    norm_ref, field_ref, resid_ref, dirn_ref = refs[:4]
    pieces = refs[4 : 4 + sz.plane]
    dot_refs = refs[4 + sz.plane : 4 + sz.plane + dots]
    out_field_ref, out_resid_ref, mapped = refs[4 + sz.plane + dots :]
    quarter = lax.axis_index("col") * sz.reps + lax.axis_index("rep")
    assemble(pieces, [[s] for s in range(sz.plane)], quarter, sz.own, mapped)
    product = jnp.zeros((1, BS), F32)
    for ref in dot_refs:
        for k in range(ref.shape[0] // 8):
            product = product + ref[8 * k : 8 * k + 1, :]
    step = norm_ref[0:1, :] / product
    out_field_ref[...] = field_ref[...] + step * dirn_ref[...]
    out_resid_ref[...] = resid_ref[...] - step * mapped[...]


def call(kernel, in_specs, shapes, out_specs, scratch, flops, *args):
    return pl.pallas_call(
        kernel,
        in_specs=in_specs,
        out_shape=shapes,
        out_specs=out_specs,
        scratch_shapes=scratch,
        compiler_params=PARAMS,
        cost_estimate=pl.CostEstimate(flops=flops, bytes_accessed=1 << 20, transcendentals=0),
    )(*args)


def array(*shape, dtype=F32):
    return jax.ShapeDtypeStruct(shape, dtype)


def local(coords, observations, nugget, tile_pairs, tile_live):
    sz = Sizes(observations.shape[0], tile_pairs.shape[1])
    own, blocks, home = sz.own, sz.blocks, sz.local_blocks
    alive = jnp.arange(sz.slots, dtype=jnp.int32) < tile_live[0]
    pairs = jnp.where(alive, tile_pairs, -1).reshape(2 * sz.slots // BS, BS)
    pair_arrays, codes = spread(pairs, sz)

    rep = lax.axis_index("rep")
    obs_rows = observations.reshape(home, BS)
    half = sz.points // sz.reps
    part = lax.dynamic_slice_in_dim(coords, rep * half, half, axis=1)
    obs_part = lax.dynamic_slice_in_dim(obs_rows, rep * (home // sz.reps), home // sz.reps, axis=0)
    coord_arrays, obs_arrays, coord_codes = [coords], [obs_rows], [(0, None)]
    for z in range(1, sz.blks):
        near, near_obs = swap(part, "blk", sz.blks, z), swap(obs_part, "blk", sz.blks, z)
        for r in range(sz.reps):
            coord_arrays.append(swap(near, "rep", sz.reps, r) if r else near)
            obs_arrays.append(swap(near_obs, "rep", sz.reps, r) if r else near_obs)
            coord_codes.append((z, r))

    lhs = call(
        functools.partial(lhs_kernel, sz),
        [VMEM],
        array((own + 1) * BS, BS, dtype=BF16),
        VMEM,
        [],
        10_000_000,
        coords,
    )
    lines = 2 * sz.slots // BS * sz.devs
    table, count = call(
        functools.partial(list_kernel, sz, codes),
        [VMEM] * len(pair_arrays),
        (array(sz.capacity // BS, BS, dtype=jnp.int32), array(1, dtype=jnp.int32)),
        (VMEM, SMEM),
        [pltpu.VMEM((lines, BS), jnp.int32)] * 2 + [pltpu.VMEM((lines, BS), F32)] * 2,
        10_000_000,
        *pair_arrays,
    )
    table = table.reshape(sz.capacity)
    tall = pltpu.VMEM(((own + 1) * BS, BS), F32)
    rhs, obs, diag, mapped, norm = call(
        functools.partial(first_kernel, sz, coord_codes),
        [SMEM, SMEM] + [VMEM] * (2 + 2 * len(coord_codes)),
        (
            array(blocks * DEPTH, BS, dtype=BF16),
            array(blocks, BS),
            array(own, BS),
            array(own, BS),
            array(8, BS),
        ),
        (VMEM,) * 5,
        [tall, tall, pltpu.VMEM((own, BS), F32)],
        100_000_000,
        table,
        count,
        lhs,
        nugget.reshape(home, BS),
        *coord_arrays,
        *obs_arrays,
    )
    field, resid, dirn = norm, obs, obs
    for sweep_index in range(1, ITERS):
        last = sweep_index + 1 == ITERS
        arrays, codes = spread(mapped, sz)
        kept = home if last else blocks
        whole = pltpu.VMEM((blocks, BS), F32)
        outs = [array(own, BS), array(8, BS), array(home, BS), array(kept, BS), array(kept, BS)]
        mapped, norm, field, resid, dirn, *dot = call(
            functools.partial(step_kernel, sz, codes, last),
            [SMEM, SMEM] + [VMEM] * (7 + len(arrays)),
            outs + [array(8, BS)] * last,
            [VMEM] * (len(outs) + last),
            [whole] * (1 + last) + [tall],
            100_000_000,
            table,
            count,
            lhs,
            rhs,
            diag,
            norm,
            field,
            resid,
            dirn,
            *arrays,
        )
    dots, unused = spread(dot[0], sz)
    mapped_arrays = [mapped] + [swap(mapped, PLANE, sz.plane, s) for s in range(1, sz.plane)]
    field, resid = call(
        functools.partial(last_kernel, sz, len(dots)),
        [VMEM] * (4 + len(mapped_arrays) + len(dots)),
        (array(home, BS), array(home, BS)),
        (VMEM, VMEM),
        [pltpu.VMEM((home, BS), F32)],
        100_000,
        norm,
        field,
        resid,
        dirn,
        *mapped_arrays,
        *dots,
    )
    return field.reshape(sz.points), resid.reshape(sz.points)


def solution(mesh):
    in_specs = (
        P(None, ("grp", "blk")),
        P(("grp", "blk")),
        P(("grp", "blk")),
        P(None, ("grp", "blk", "col", "rep")),
        P(("grp", "blk", "col", "rep")),
    )
    out_specs = (P(("grp", "blk")), P(("grp", "blk")))
    return jax.shard_map(local, mesh=mesh, in_specs=in_specs, out_specs=out_specs, check_vma=False)
```

```python
import functools

import jax
import jax.numpy as jnp
from jax import lax
from jax.experimental import pallas as pl
from jax.experimental.pallas import tpu as pltpu
from jax.sharding import PartitionSpec as P

BS = 128
ITERS = 3
SUPPORT = 0.3
DEPTH = 48
UNROLL = 4
EVERY = ("blk", "col", "rep")
PLANE = ("col", "rep")
VMEM = pl.BlockSpec(memory_space=pltpu.VMEM)
SMEM = pl.BlockSpec(memory_space=pltpu.SMEM)
PARAMS = pltpu.CompilerParams(vmem_limit_bytes=48 * 1024 * 1024)
BF16 = jnp.bfloat16
F32 = jnp.float32


class Sizes:
    def __init__(self, points, slots):
        self.blks = lax.axis_size("blk")
        self.reps = lax.axis_size("rep")
        self.plane = lax.axis_size("col") * self.reps
        self.devs = self.blks * self.plane
        self.points = points
        self.slots = slots
        self.local_blocks = points // BS
        self.blocks = self.local_blocks * self.blks
        self.own = self.local_blocks // self.plane
        self.capacity = 2 * self.plane * slots
        per_row = slots * self.devs // self.blocks
        self.scale = 16.0 / (BS * per_row) / 256.0

    def me(self):
        return (lax.axis_index("blk") * lax.axis_size("col") + lax.axis_index("col")) * self.reps + lax.axis_index(
            "rep"
        )


def exchange(x, axes):
    return lax.all_to_all(x, axes, split_axis=0, concat_axis=0, tiled=True)


def copies(x, count):
    return jnp.broadcast_to(x[None], (count,) + x.shape).reshape((count * x.shape[0],) + x.shape[1:])


def split3(x):
    high = x.astype(BF16).astype(F32)
    rest = x - high
    middle = rest.astype(BF16).astype(F32)
    return high, middle, rest - middle


def lhs_kernel(sz, coords_ref, out_ref):
    quarter = lax.axis_index("col") * sz.reps + lax.axis_index("rep")
    unit = jnp.ones((1, BS), F32)
    for i in range(sz.own):
        start = pl.multiple_of((quarter * sz.own + i) * BS, BS)
        x = (coords_ref[:, pl.ds(start, BS)] - 0.5) * (4.0 / SUPPORT)
        norm = jnp.sum(x * x, axis=0, keepdims=True)
        h, m, l = split3(jnp.concatenate([x, unit, norm, jnp.zeros((3, BS), F32)], axis=0))
        feats = jnp.concatenate([h, h, m, m, h, l, jnp.zeros((BS - DEPTH, BS), F32)], axis=0)
        out_ref[i * BS : (i + 1) * BS, :] = feats.T.astype(BF16)
    out_ref[sz.own * BS :, :] = jnp.zeros((BS, BS), BF16)


def list_kernel(sz, pairs_ref, out_ref, count_ref, target, other, place, value):
    me = sz.me()
    lines = sz.slots // BS
    at = 2 * lines * sz.devs
    for base in range(0, at, 2 * lines):
        rows = pairs_ref[base : base + lines, :]
        cols = pairs_ref[base + lines : base + 2 * lines, :]
        target[base : base + lines, :] = rows
        other[base : base + lines, :] = cols
        target[base + lines : base + 2 * lines, :] = cols
        other[base + lines : base + 2 * lines, :] = rows
    local = target[...] - me * sz.own
    mine = jnp.logical_and(local >= 0, local < sz.own)
    flags = jnp.where(mine, 1.0, 0.0)
    a = lax.broadcasted_iota(jnp.int32, (BS, BS), 0)
    b = lax.broadcasted_iota(jnp.int32, (BS, BS), 1)
    before = jnp.dot(flags.astype(BF16), jnp.where(a < b, 1.0, 0.0).astype(BF16), preferred_element_type=F32)
    totals = jnp.broadcast_to(jnp.sum(flags, axis=1, keepdims=True), (at, BS))
    a = lax.broadcasted_iota(jnp.int32, (at, at), 0)
    b = lax.broadcasted_iota(jnp.int32, (at, at), 1)
    above = jnp.dot(jnp.where(b < a, 1.0, 0.0).astype(BF16), totals.astype(BF16), preferred_element_type=F32)
    place[...] = jnp.where(mine, above + before, -1.0)
    value[...] = (local + 256 * other[...]).astype(F32)
    count = jnp.sum(flags).astype(jnp.int32)
    count_ref[0] = count
    sub = lax.broadcasted_iota(jnp.int32, (BS, BS), 0)
    lane = lax.broadcasted_iota(jnp.int32, (1, BS), 1)

    def chunk(c, unused):
        slot = (sub + c * BS).astype(F32)

        def line(r, total):
            hit = place[pl.ds(r, 1), :] == slot
            return total + jnp.where(hit, value[pl.ds(r, 1), :], 0.0)

        total = lax.fori_loop(0, at, line, jnp.zeros((BS, BS), F32), unroll=4)
        found = jnp.sum(total.T, axis=0, keepdims=True).astype(jnp.int32)
        out_ref[pl.ds(c, 1), :] = jnp.where(lane + c * BS < count, found, sz.own)
        return unused

    lax.fori_loop(0, lax.shift_right_logical(count + BS - 1, 7), chunk, 0)


def sweep(list_ref, count_ref, lhs_ref, rhs_ref, vec_ref, acc, acc_ones=None):
    acc[...] = jnp.zeros_like(acc)
    if acc_ones is not None:
        acc_ones[...] = jnp.zeros_like(acc_ones)

    def group(g, unused):
        for u in range(UNROLL):
            entry = list_ref[g * UNROLL + u]
            i = jnp.bitwise_and(entry, 255)
            j = lax.shift_right_logical(entry, 8)
            rows = pl.ds(pl.multiple_of(i * BS, BS), BS)
            squared = jnp.dot(
                lhs_ref[rows, :DEPTH],
                rhs_ref[pl.ds(pl.multiple_of(j * DEPTH, DEPTH), DEPTH), :],
                preferred_element_type=F32,
            )
            squared = jnp.maximum(squared, 1e-20)
            remain = jnp.maximum(4.0 - squared * lax.rsqrt(squared), 0.0)
            twice = remain * remain
            tile = twice * twice * (5.0 - remain)
            if acc_ones is not None:
                acc_ones[rows, :] += tile
            acc[rows, :] += tile * vec_ref[pl.ds(j, 1), :]
        return unused

    groups = lax.div(count_ref[0] + (UNROLL - 1), UNROLL)
    lax.fori_loop(0, groups, group, 0)


def finish(sz, acc, out_ref):
    unit = jnp.ones((8, BS), BF16)
    across = (((1,), (1,)), ((), ()))
    for i in range(sz.own):
        whole = acc[i * BS : (i + 1) * BS, :]
        high = whole.astype(BF16)
        low = (whole - high.astype(F32)).astype(BF16)
        y = lax.dot_general(unit, high, across, preferred_element_type=F32)
        y = y + lax.dot_general(unit, low, across, preferred_element_type=F32)
        out_ref[i : i + 1, :] = y[0:1, :] * sz.scale


def fan_out(ref, rows, value):
    for k in range(ref.shape[0] // rows):
        ref[k * rows : (k + 1) * rows, :] = value


def total_of(x):
    return jnp.sum(jnp.sum(x, axis=0, keepdims=True), axis=1, keepdims=True)


def first_kernel(sz, *refs):
    list_ref, count_ref, lhs_ref, nugget_ref, obs_home_ref, near_ref, far_ref = refs[:7]
    rhs_ref, obs_ref, diag_ref, mapped_ref, norm_ref, acc, acc_ones, total_row = refs[7:]
    rep = lax.axis_index("rep")
    part = sz.local_blocks // sz.reps
    feature = lax.broadcasted_iota(jnp.int32, (8, BS), 0)
    for piece_ref, turn in ((near_ref, 0), (far_ref, 1)):
        for z in range(sz.blks):
            base = z * 4 * part
            first = pl.multiple_of(z * sz.local_blocks + jnp.bitwise_xor(rep, turn) * part, 8)
            obs_ref[pl.ds(first, part), :] = piece_ref[base + 3 * part : base + 4 * part, :]

            def one(k, unused, base=base, first=first, piece_ref=piece_ref):
                x, y, z = ((piece_ref[pl.ds(base + c * part + k, 1), :] - 0.5) * (4.0 / SUPPORT) for c in range(3))
                feats = jnp.where(feature == 4, 1.0, 0.0)
                for place, row in enumerate((-2.0 * x, -2.0 * y, -2.0 * z, x * x + y * y + z * z)):
                    feats = jnp.where(feature == place, row, feats)
                h, m, l = split3(feats)
                feats = jnp.concatenate([h, m, h, m, l, h], axis=0).astype(BF16)
                rhs_ref[pl.ds(pl.multiple_of((first + k) * DEPTH, DEPTH), DEPTH), :] = feats
                return unused

            lax.fori_loop(0, part, one, 0, unroll=4)
    sweep(list_ref, count_ref, lhs_ref, rhs_ref, obs_ref, acc, acc_ones)
    finish(sz, acc_ones, total_row)
    finish(sz, acc, mapped_ref)
    quarter = lax.axis_index("col") * sz.reps + rep
    own = pl.ds(pl.multiple_of(sz.me() * sz.own, 8), sz.own)
    diag = nugget_ref[pl.ds(pl.multiple_of(quarter * sz.own, 8), sz.own), :] + total_row[...]
    diag_ref[...] = diag
    fan_out(mapped_ref, sz.own, mapped_ref[: sz.own, :] + diag * obs_ref[own, :])
    norm_ref[...] = jnp.broadcast_to(total_of(obs_ref[...] * obs_ref[...]), (8, BS))


def step_kernel(sz, last, *refs):
    list_ref, count_ref, lhs_ref, rhs_ref, diag_ref, norm_ref, field_ref, resid_ref, dirn_ref, mapped = refs[:10]
    rest = refs[10:]
    mapped_ref, next_norm_ref, next_field_ref, next_resid_ref, next_dirn_ref = rest[:5]
    if last:
        dot_ref, dirn, acc = rest[5:]
    else:
        acc = rest[5]
        dirn = next_dirn_ref
    me = sz.me()
    norm = norm_ref[0:1, 0:1]
    step = norm / total_of(dirn_ref[...] * mapped[...])
    resid = resid_ref[...] - step * mapped[...]
    next_norm = total_of(resid * resid)
    dirn[...] = resid + (next_norm / norm) * dirn_ref[...]
    next_norm_ref[...] = jnp.broadcast_to(next_norm, (8, BS))
    home = pl.ds(pl.multiple_of(lax.axis_index("blk") * sz.local_blocks, 8), sz.local_blocks)
    own = pl.ds(pl.multiple_of(me * sz.own, 8), sz.own)
    field = step * dirn_ref[home, :]
    if last:
        next_field_ref[...] = field_ref[...] + field
        next_resid_ref[...] = resid_ref[home, :] - step * mapped[home, :]
        next_dirn_ref[...] = dirn[home, :]
    else:
        next_field_ref[...] = field
        next_resid_ref[...] = resid
    sweep(list_ref, count_ref, lhs_ref, rhs_ref, dirn, acc)
    finish(sz, acc, mapped_ref)
    ours = mapped_ref[: sz.own, :] + diag_ref[...] * dirn[own, :]
    fan_out(mapped_ref, sz.own, ours)
    if last:
        dot_ref[...] = jnp.broadcast_to(total_of(ours * dirn[own, :]), dot_ref.shape)


def last_kernel(sz, norm_ref, field_ref, resid_ref, dirn_ref, mapped_ref, dot_ref, out_field_ref, out_resid_ref):
    product = jnp.sum(dot_ref[...], axis=0, keepdims=True) * 0.125
    step = norm_ref[0:1, :] / product
    out_field_ref[...] = field_ref[...] + step * dirn_ref[...]
    out_resid_ref[...] = resid_ref[...] - step * mapped_ref[...]


def call(kernel, in_specs, shapes, out_specs, scratch, flops, *args):
    return pl.pallas_call(
        kernel,
        in_specs=in_specs,
        out_shape=shapes,
        out_specs=out_specs,
        scratch_shapes=scratch,
        compiler_params=PARAMS,
        cost_estimate=pl.CostEstimate(flops=flops, bytes_accessed=1 << 20, transcendentals=0),
    )(*args)


def array(*shape, dtype=F32):
    return jax.ShapeDtypeStruct(shape, dtype)


def local(coords, observations, nugget, tile_pairs, tile_live):
    sz = Sizes(observations.shape[0], tile_pairs.shape[1])
    own, blocks, home = sz.own, sz.blocks, sz.local_blocks
    alive = jnp.arange(sz.slots, dtype=jnp.int32) < tile_live[0]
    pairs = jnp.where(alive, tile_pairs, -1).reshape(2 * sz.slots // BS, BS)
    pairs = exchange(copies(pairs, sz.devs), EVERY)

    rep = lax.axis_index("rep")
    obs_rows = observations.reshape(home, BS)
    half = sz.points // sz.reps
    payload = jnp.concatenate([coords, observations[None]], axis=0)
    payload = lax.dynamic_slice_in_dim(payload, rep * half, half, axis=1)
    near = exchange(copies(payload.reshape(4 * home // sz.reps, BS), sz.blks), "blk")
    far = lax.ppermute(near, "rep", [(i, i ^ 1) for i in range(sz.reps)])

    lhs = call(
        functools.partial(lhs_kernel, sz),
        [VMEM],
        array((own + 1) * BS, BS, dtype=BF16),
        VMEM,
        [],
        10_000_000,
        coords,
    )
    lines = 2 * sz.slots // BS * sz.devs
    table, count = call(
        functools.partial(list_kernel, sz),
        [VMEM],
        (array(sz.capacity // BS, BS, dtype=jnp.int32), array(1, dtype=jnp.int32)),
        (VMEM, SMEM),
        [pltpu.VMEM((lines, BS), jnp.int32)] * 2 + [pltpu.VMEM((lines, BS), F32)] * 2,
        10_000_000,
        pairs,
    )
    table = table.reshape(sz.capacity)
    tall = pltpu.VMEM(((own + 1) * BS, BS), F32)
    rhs, obs, diag, mapped, norm = call(
        functools.partial(first_kernel, sz),
        [SMEM, SMEM] + [VMEM] * 5,
        (
            array(blocks * DEPTH, BS, dtype=BF16),
            array(blocks, BS),
            array(own, BS),
            array(sz.devs * own, BS),
            array(8, BS),
        ),
        (VMEM,) * 5,
        [tall, tall, pltpu.VMEM((own, BS), F32)],
        100_000_000,
        table,
        count,
        lhs,
        nugget.reshape(home, BS),
        obs_rows,
        near,
        far,
    )
    field, resid, dirn = norm, obs, obs
    for sweep_index in range(1, ITERS):
        last = sweep_index + 1 == ITERS
        kept = home if last else blocks
        peers = sz.plane if last else sz.devs
        outs = [array(peers * own, BS), array(8, BS), array(home, BS), array(kept, BS), array(kept, BS)]
        mapped, norm, field, resid, dirn, *dot = call(
            functools.partial(step_kernel, sz, last),
            [SMEM, SMEM] + [VMEM] * 8,
            outs + [array(8 * sz.devs, BS)] * last,
            [VMEM] * (len(outs) + last),
            [pltpu.VMEM((blocks, BS), F32)] * last + [tall],
            100_000_000,
            table,
            count,
            lhs,
            rhs,
            diag,
            norm,
            field,
            resid,
            dirn,
            exchange(mapped, EVERY),
        )
    field, resid = call(
        functools.partial(last_kernel, sz),
        [VMEM] * 6,
        (array(home, BS), array(home, BS)),
        (VMEM, VMEM),
        [],
        100_000,
        norm,
        field,
        resid,
        dirn,
        exchange(mapped, PLANE),
        exchange(dot[0], EVERY),
    )
    return field.reshape(sz.points), resid.reshape(sz.points)


def solution(mesh):
    in_specs = (
        P(None, ("grp", "blk")),
        P(("grp", "blk")),
        P(("grp", "blk")),
        P(None, ("grp", "blk", "col", "rep")),
        P(("grp", "blk", "col", "rep")),
    )
    out_specs = (P(("grp", "blk")), P(("grp", "blk")))
    return jax.shard_map(local, mesh=mesh, in_specs=in_specs, out_specs=out_specs, check_vma=False)
```

```python
import functools

import jax
import jax.numpy as jnp
from jax import lax
from jax.experimental import pallas as pl
from jax.experimental.pallas import tpu as pltpu
from jax.sharding import PartitionSpec as P

BS = 128
ITERS = 3
SUPPORT = 0.3
DEPTH = 48
UNROLL = 4
ARRAYS = 4
MIB = 1024 * 1024
EVERY = ("blk", "col", "rep")
PLANE = ("col", "rep")
VMEM = pl.BlockSpec(memory_space=pltpu.VMEM)
SMEM = pl.BlockSpec(memory_space=pltpu.SMEM)
ANY = pl.BlockSpec(memory_space=pl.ANY)
BF16 = jnp.bfloat16
F32 = jnp.float32


class Sizes:
    def __init__(self, points, slots):
        self.blks = lax.axis_size("blk")
        self.reps = lax.axis_size("rep")
        self.plane = lax.axis_size("col") * self.reps
        self.devs = self.blks * self.plane
        self.points = points
        self.slots = slots
        self.local_blocks = points // BS
        self.blocks = self.local_blocks * self.blks
        self.own = self.local_blocks // self.plane
        self.capacity = 2 * self.plane * slots
        per_row = slots * self.devs // self.blocks
        self.first_mib = 6 + self.blocks * DEPTH * BS * 2 // MIB
        self.kept = min(448, (48 - self.first_mib) * 16) // ARRAYS
        self.scale = 16.0 / (BS * per_row) / 256.0

    def me(self):
        return (lax.axis_index("blk") * lax.axis_size("col") + lax.axis_index("col")) * self.reps + lax.axis_index(
            "rep"
        )


def exchange(x, axes):
    return lax.all_to_all(x, axes, split_axis=0, concat_axis=0, tiled=True)


def copies(x, count):
    return jnp.broadcast_to(x[None], (count,) + x.shape).reshape((count * x.shape[0],) + x.shape[1:])


def split3(x):
    high = x.astype(BF16).astype(F32)
    rest = x - high
    middle = rest.astype(BF16).astype(F32)
    return high, middle, rest - middle


def lhs_kernel(sz, coords_ref, out_ref):
    quarter = lax.axis_index("col") * sz.reps + lax.axis_index("rep")
    unit = jnp.ones((1, BS), F32)
    for i in range(sz.own):
        start = pl.multiple_of((quarter * sz.own + i) * BS, BS)
        x = (coords_ref[:, pl.ds(start, BS)] - 0.5) * (4.0 / SUPPORT)
        norm = jnp.sum(x * x, axis=0, keepdims=True)
        h, m, l = split3(jnp.concatenate([x, unit, norm, jnp.zeros((3, BS), F32)], axis=0))
        feats = jnp.concatenate([h, h, m, m, h, l, jnp.zeros((BS - DEPTH, BS), F32)], axis=0)
        out_ref[i * BS : (i + 1) * BS, :] = feats.T.astype(BF16)
    out_ref[sz.own * BS :, :] = jnp.zeros((BS, BS), BF16)


def list_kernel(sz, pairs_ref, out_ref, count_ref, target, other, place, value, key_column, key_row, entry_row):
    me = sz.me()
    lines = sz.slots // BS
    at = 2 * lines * sz.devs
    for base in range(0, at, 2 * lines):
        rows = pairs_ref[base : base + lines, :]
        cols = pairs_ref[base + lines : base + 2 * lines, :]
        target[base : base + lines, :] = rows
        other[base : base + lines, :] = cols
        target[base + lines : base + 2 * lines, :] = cols
        other[base + lines : base + 2 * lines, :] = rows
    local = target[...] - me * sz.own
    mine = jnp.logical_and(local >= 0, local < sz.own)
    flags = jnp.where(mine, 1.0, 0.0)
    a = lax.broadcasted_iota(jnp.int32, (BS, BS), 0)
    b = lax.broadcasted_iota(jnp.int32, (BS, BS), 1)
    before = jnp.dot(flags.astype(BF16), jnp.where(a < b, 1.0, 0.0).astype(BF16), preferred_element_type=F32)
    totals = jnp.broadcast_to(jnp.sum(flags, axis=1, keepdims=True), (at, BS))
    a = lax.broadcasted_iota(jnp.int32, (at, at), 0)
    b = lax.broadcasted_iota(jnp.int32, (at, at), 1)
    above = jnp.dot(jnp.where(b < a, 1.0, 0.0).astype(BF16), totals.astype(BF16), preferred_element_type=F32)
    place[...] = jnp.where(mine, above + before, -1.0)
    value[...] = (local + 256 * other[...]).astype(F32)
    count = jnp.sum(flags).astype(jnp.int32)
    count_ref[0] = count
    sub = lax.broadcasted_iota(jnp.int32, (BS, BS), 0)
    lane = lax.broadcasted_iota(jnp.int32, (1, BS), 1)

    chunks = lax.shift_right_logical(count + BS - 1, 7)

    def key_of(found, slot):
        entry = jnp.where(slot < count, found.astype(jnp.int32), sz.own)
        return entry.astype(F32), (jnp.bitwise_and(entry, 255) * 65536 + slot).astype(F32)

    def compact(c, unused):
        slot = (sub + c * BS).astype(F32)

        def line(r, total):
            hit = place[pl.ds(r, 1), :] == slot
            return total + jnp.where(hit, value[pl.ds(r, 1), :], 0.0)

        total = lax.fori_loop(0, at, line, jnp.zeros((BS, BS), F32), unroll=4)
        entry, key = key_of(jnp.sum(total.T, axis=0, keepdims=True), lane + c * BS)
        entry_row[pl.ds(c, 1), :] = entry
        key_row[pl.ds(c, 1), :] = key
        unused_entry, key = key_of(jnp.sum(total, axis=1, keepdims=True), sub[:, 0:1] + c * BS)
        key_column[pl.ds(pl.multiple_of(c * BS, BS), BS), :] = jnp.broadcast_to(key, (BS, BS))
        return unused

    lax.fori_loop(0, chunks, compact, 0)

    def rank(c, unused):
        def below(k, total):
            lower = key_column[pl.ds(pl.multiple_of(k * BS, BS), BS), :] < key_row[pl.ds(c, 1), :]
            return total + jnp.where(lower, 1.0, 0.0)

        total = lax.fori_loop(0, chunks, below, jnp.zeros((BS, BS), F32))
        place[pl.ds(c, 1), :] = jnp.sum(total, axis=0, keepdims=True)
        return unused

    lax.fori_loop(0, chunks, rank, 0)

    def arrange(c, unused):
        slot = (sub + c * BS).astype(F32)

        def line(r, total):
            hit = place[pl.ds(r, 1), :] == slot
            return total + jnp.where(hit, entry_row[pl.ds(r, 1), :], 0.0)

        total = lax.fori_loop(0, chunks, line, jnp.zeros((BS, BS), F32))
        out_ref[pl.ds(c, 1), :] = jnp.sum(total.T, axis=0, keepdims=True).astype(jnp.int32)
        return unused

    lax.fori_loop(0, chunks, arrange, 0)


def entry_of(list_ref, k):
    entry = list_ref[k]
    return jnp.bitwise_and(entry, 255), lax.shift_right_logical(entry, 8)


def tile_of(features, other_features):
    squared = jnp.maximum(jnp.dot(features, other_features, preferred_element_type=F32), 1e-20)
    remain = jnp.maximum(4.0 - squared * lax.rsqrt(squared), 0.0)
    twice = remain * remain
    return twice * twice * (5.0 - remain)


def kept_groups(sz, count, at):
    first = at * (sz.kept // UNROLL)
    last = jnp.minimum(lax.div(count + (UNROLL - 1), UNROLL), first + sz.kept // UNROLL)
    return first, jnp.maximum(first, last)


def generate(sz, list_ref, count, lhs_ref, rhs_ref, tile_refs):
    for at, tile_ref in enumerate(tile_refs):

        def group(g, unused, at=at, tile_ref=tile_ref):
            for u in range(UNROLL):
                i, j = entry_of(list_ref, g * UNROLL + u)
                start = pl.multiple_of((g * UNROLL + u - at * sz.kept) * BS, BS)
                tile_ref[pl.ds(start, BS), :] = tile_of(
                    lhs_ref[pl.ds(pl.multiple_of(i * BS, BS), BS), :DEPTH],
                    rhs_ref[pl.ds(pl.multiple_of(j * DEPTH, DEPTH), DEPTH), :],
                )
            return unused

        lax.fori_loop(*kept_groups(sz, count, at), group, 0)


def sweep(sz, list_ref, count, tile_refs, vec_ref, acc, acc_ones, remake):
    accs = [acc] if acc_ones is None else [acc, acc_ones]
    for ref in accs:
        ref[...] = jnp.zeros_like(ref)
    carry = (jnp.int32(-1),) + tuple(jnp.zeros((BS, BS), F32) for unused in accs)
    for at, tile_ref in enumerate(tile_refs):

        def group(g, carry, at=at, tile_ref=tile_ref):
            before, *sums = carry
            for u in range(UNROLL):
                i, j = entry_of(list_ref, g * UNROLL + u)
                keep = jnp.where(i == before, 1.0, 0.0)
                start = pl.multiple_of((g * UNROLL + u - at * sz.kept) * BS, BS)
                tile = tile_ref[pl.ds(start, BS), :]
                terms = [tile * vec_ref[pl.ds(j, 1), :], tile]
                sums = [total * keep + term for total, term in zip(sums, terms)]
                for ref, total in zip(accs, sums):
                    ref[pl.ds(pl.multiple_of(i * BS, BS), BS), :] = total
                before = i
            return (before, *sums)

        carry = lax.fori_loop(*kept_groups(sz, count, at), group, carry)

    def extra(k, unused):
        i, j = entry_of(list_ref, k)
        tile = tile_of(*remake(i, j))
        rows = pl.ds(pl.multiple_of(i * BS, BS), BS)
        acc[rows, :] += tile * vec_ref[pl.ds(j, 1), :]
        if acc_ones is not None:
            acc_ones[rows, :] += tile
        return unused

    kept = sz.kept * len(tile_refs)
    lax.fori_loop(kept, jnp.maximum(count, kept), extra, 0)


def finish(sz, acc, out_ref):
    unit = jnp.ones((8, BS), BF16)
    across = (((1,), (1,)), ((), ()))
    for i in range(sz.own):
        whole = acc[i * BS : (i + 1) * BS, :]
        high = whole.astype(BF16)
        low = (whole - high.astype(F32)).astype(BF16)
        y = lax.dot_general(unit, high, across, preferred_element_type=F32)
        y = y + lax.dot_general(unit, low, across, preferred_element_type=F32)
        out_ref[i : i + 1, :] = y[0:1, :] * sz.scale


def fan_out(ref, rows, value):
    for k in range(ref.shape[0] // rows):
        ref[k * rows : (k + 1) * rows, :] = value


def total_of(x):
    return jnp.sum(jnp.sum(x, axis=0, keepdims=True), axis=1, keepdims=True)


def first_kernel(sz, *refs):
    list_ref, count_ref, lhs_ref, nugget_ref, obs_home_ref, near_ref, far_ref = refs[:7]
    tile_refs = refs[7 : 7 + ARRAYS]
    spare_ref, obs_ref, diag_ref, mapped_ref, norm_ref, rhs_ref, acc, acc_ones, total_row, done = refs[7 + ARRAYS :]
    rep = lax.axis_index("rep")
    part = sz.local_blocks // sz.reps
    feature = lax.broadcasted_iota(jnp.int32, (8, BS), 0)
    for piece_ref, turn in ((near_ref, 0), (far_ref, 1)):
        for z in range(sz.blks):
            base = z * 4 * part
            first = pl.multiple_of(z * sz.local_blocks + jnp.bitwise_xor(rep, turn) * part, 8)
            obs_ref[pl.ds(first, part), :] = piece_ref[base + 3 * part : base + 4 * part, :]

            def one(k, unused, base=base, first=first, piece_ref=piece_ref):
                x, y, z = ((piece_ref[pl.ds(base + c * part + k, 1), :] - 0.5) * (4.0 / SUPPORT) for c in range(3))
                feats = jnp.where(feature == 4, 1.0, 0.0)
                for place, row in enumerate((-2.0 * x, -2.0 * y, -2.0 * z, x * x + y * y + z * z)):
                    feats = jnp.where(feature == place, row, feats)
                h, m, l = split3(feats)
                feats = jnp.concatenate([h, m, h, m, l, h], axis=0).astype(BF16)
                rhs_ref[pl.ds(pl.multiple_of((first + k) * DEPTH, DEPTH), DEPTH), :] = feats
                return unused

            lax.fori_loop(0, part, one, 0, unroll=4)
    count = count_ref[0]
    generate(sz, list_ref, count, lhs_ref, rhs_ref, tile_refs)

    def remake(i, j):
        features = lhs_ref[pl.ds(pl.multiple_of(i * BS, BS), BS), :DEPTH]
        return features, rhs_ref[pl.ds(pl.multiple_of(j * DEPTH, DEPTH), DEPTH), :]

    sweep(sz, list_ref, count, tile_refs, obs_ref, acc, acc_ones, remake)

    @pl.when(count > sz.kept * ARRAYS)
    def save():
        copy = pltpu.make_async_copy(rhs_ref, spare_ref, done)
        copy.start()
        copy.wait()

    finish(sz, acc_ones, total_row)
    finish(sz, acc, mapped_ref)
    quarter = lax.axis_index("col") * sz.reps + rep
    own = pl.ds(pl.multiple_of(sz.me() * sz.own, 8), sz.own)
    diag = nugget_ref[pl.ds(pl.multiple_of(quarter * sz.own, 8), sz.own), :] + total_row[...]
    diag_ref[...] = diag
    fan_out(mapped_ref, sz.own, mapped_ref[: sz.own, :] + diag * obs_ref[own, :])
    norm_ref[...] = jnp.broadcast_to(total_of(obs_ref[...] * obs_ref[...]), (8, BS))


def step_kernel(sz, last, *refs):
    list_ref, count_ref, lhs_ref, spare_ref, diag_ref, norm_ref, field_ref, resid_ref, dirn_ref, mapped = refs[:10]
    tile_refs = refs[10 : 10 + ARRAYS]
    rest = refs[10 + ARRAYS :]
    mapped_ref, next_norm_ref, next_field_ref, next_resid_ref, next_dirn_ref = rest[:5]
    if last:
        dot_ref, dirn = rest[5:7]
    else:
        dirn = next_dirn_ref
    acc, features, others, done = rest[-4:]
    me = sz.me()
    norm = norm_ref[0:1, 0:1]
    step = norm / total_of(dirn_ref[...] * mapped[...])
    resid = resid_ref[...] - step * mapped[...]
    next_norm = total_of(resid * resid)
    dirn[...] = resid + (next_norm / norm) * dirn_ref[...]
    next_norm_ref[...] = jnp.broadcast_to(next_norm, (8, BS))
    home = pl.ds(pl.multiple_of(lax.axis_index("blk") * sz.local_blocks, 8), sz.local_blocks)
    own = pl.ds(pl.multiple_of(me * sz.own, 8), sz.own)
    field = step * dirn_ref[home, :]
    if last:
        next_field_ref[...] = field_ref[...] + field
        next_resid_ref[...] = resid_ref[home, :] - step * mapped[home, :]
        next_dirn_ref[...] = dirn[home, :]
    else:
        next_field_ref[...] = field
        next_resid_ref[...] = resid

    def remake(i, j):
        for source, start, size, target in ((lhs_ref, i, BS, features), (spare_ref, j, DEPTH, others)):
            copy = pltpu.make_async_copy(source.at[pl.ds(pl.multiple_of(start * size, size), size), :], target, done)
            copy.start()
            copy.wait()
        return features[:, :DEPTH], others[...]

    sweep(sz, list_ref, count_ref[0], tile_refs, dirn, acc, None, remake)
    finish(sz, acc, mapped_ref)
    ours = mapped_ref[: sz.own, :] + diag_ref[...] * dirn[own, :]
    fan_out(mapped_ref, sz.own, ours)
    if last:
        dot_ref[...] = jnp.broadcast_to(total_of(ours * dirn[own, :]), dot_ref.shape)


def last_kernel(sz, norm_ref, field_ref, resid_ref, dirn_ref, mapped_ref, dot_ref, out_field_ref, out_resid_ref):
    product = jnp.sum(dot_ref[...], axis=0, keepdims=True) * 0.125
    step = norm_ref[0:1, :] / product
    out_field_ref[...] = field_ref[...] + step * dirn_ref[...]
    out_resid_ref[...] = resid_ref[...] - step * mapped_ref[...]


def call(kernel, mib, in_specs, shapes, out_specs, scratch, flops, *args):
    return pl.pallas_call(
        kernel,
        in_specs=in_specs,
        out_shape=shapes,
        out_specs=out_specs,
        scratch_shapes=scratch,
        compiler_params=pltpu.CompilerParams(vmem_limit_bytes=mib * MIB),
        cost_estimate=pl.CostEstimate(flops=flops, bytes_accessed=1 << 20, transcendentals=0),
    )(*args)


def array(*shape, dtype=F32):
    return jax.ShapeDtypeStruct(shape, dtype)


def local(coords, observations, nugget, tile_pairs, tile_live):
    sz = Sizes(observations.shape[0], tile_pairs.shape[1])
    own, blocks, home = sz.own, sz.blocks, sz.local_blocks
    alive = jnp.arange(sz.slots, dtype=jnp.int32) < tile_live[0]
    pairs = jnp.where(alive, tile_pairs, -1).reshape(2 * sz.slots // BS, BS)
    pairs = exchange(copies(pairs, sz.devs), EVERY)

    rep = lax.axis_index("rep")
    obs_rows = observations.reshape(home, BS)
    half = sz.points // sz.reps
    payload = jnp.concatenate([coords, observations[None]], axis=0)
    payload = lax.dynamic_slice_in_dim(payload, rep * half, half, axis=1)
    near = exchange(copies(payload.reshape(4 * home // sz.reps, BS), sz.blks), "blk")
    far = lax.ppermute(near, "rep", [(i, i ^ 1) for i in range(sz.reps)])

    lhs = call(
        functools.partial(lhs_kernel, sz),
        12,
        [VMEM],
        array((own + 1) * BS, BS, dtype=BF16),
        VMEM,
        [],
        10_000_000,
        coords,
    )
    lines = 2 * sz.slots // BS * sz.devs
    table, count = call(
        functools.partial(list_kernel, sz),
        12,
        [VMEM],
        (array(sz.capacity // BS, BS, dtype=jnp.int32), array(1, dtype=jnp.int32)),
        (VMEM, SMEM),
        [pltpu.VMEM((lines, BS), jnp.int32)] * 2
        + [pltpu.VMEM((lines, BS), F32)] * 2
        + [pltpu.VMEM((sz.capacity, BS), F32)]
        + [pltpu.VMEM((sz.capacity // BS, BS), F32)] * 2,
        10_000_000,
        pairs,
    )
    table = table.reshape(sz.capacity)
    tall = pltpu.VMEM(((own + 1) * BS, BS), F32)
    kept = [pltpu.VMEM((sz.kept * BS, BS), F32)] * ARRAYS
    *tiles, spare, obs, diag, mapped, norm = call(
        functools.partial(first_kernel, sz),
        sz.first_mib,
        [SMEM, SMEM] + [VMEM] * 5,
        kept
        + [
            pltpu.HBM((blocks * DEPTH, BS), BF16),
            array(blocks, BS),
            array(own, BS),
            array(sz.devs * own, BS),
            array(8, BS),
        ],
        [VMEM] * ARRAYS + [ANY] + [VMEM] * 4,
        [
            pltpu.VMEM((blocks * DEPTH, BS), BF16),
            tall,
            tall,
            pltpu.VMEM((own, BS), F32),
            pltpu.SemaphoreType.DMA,
        ],
        100_000_000,
        table,
        count,
        lhs,
        nugget.reshape(home, BS),
        obs_rows,
        near,
        far,
    )
    tiles = [pltpu.with_memory_space_constraint(tile, pltpu.VMEM) for tile in tiles]
    spare = pltpu.with_memory_space_constraint(spare, pltpu.HBM)
    field, resid, dirn = norm, obs, obs
    for sweep_index in range(1, ITERS):
        last = sweep_index + 1 == ITERS
        span = home if last else blocks
        peers = sz.plane if last else sz.devs
        outs = [array(peers * own, BS), array(8, BS), array(home, BS), array(span, BS), array(span, BS)]
        mapped, norm, field, resid, dirn, *dot = call(
            functools.partial(step_kernel, sz, last),
            5,
            [SMEM, SMEM, ANY, ANY] + [VMEM] * (6 + ARRAYS),
            outs + [array(8 * sz.devs, BS)] * last,
            [VMEM] * (len(outs) + last),
            [pltpu.VMEM((blocks, BS), F32)] * last
            + [tall, pltpu.VMEM((BS, BS), BF16), pltpu.VMEM((DEPTH, BS), BF16), pltpu.SemaphoreType.DMA],
            100_000_000,
            table,
            count,
            lhs,
            spare,
            diag,
            norm,
            field,
            resid,
            dirn,
            exchange(mapped, EVERY),
            *tiles,
        )
    field, resid = call(
        functools.partial(last_kernel, sz),
        4,
        [VMEM] * 6,
        (array(home, BS), array(home, BS)),
        (VMEM, VMEM),
        [],
        100_000,
        norm,
        field,
        resid,
        dirn,
        exchange(mapped, PLANE),
        exchange(dot[0], EVERY),
    )
    return field.reshape(sz.points), resid.reshape(sz.points)


def solution(mesh):
    in_specs = (
        P(None, ("grp", "blk")),
        P(("grp", "blk")),
        P(("grp", "blk")),
        P(None, ("grp", "blk", "col", "rep")),
        P(("grp", "blk", "col", "rep")),
    )
    out_specs = (P(("grp", "blk")), P(("grp", "blk")))
    return jax.shard_map(local, mesh=mesh, in_specs=in_specs, out_specs=out_specs, check_vma=False)
```

```python
import functools

import jax
import jax.numpy as jnp
from jax import lax
from jax.experimental import pallas as pl
from jax.experimental.pallas import tpu as pltpu
from jax.sharding import PartitionSpec as P

BS = 128
ITERS = 3
SUPPORT = 0.3
DEPTH = 48
UNROLL = 4
ARRAYS = 4
MIB = 1024 * 1024
VMEM = pl.BlockSpec(memory_space=pltpu.VMEM)
SMEM = pl.BlockSpec(memory_space=pltpu.SMEM)
ANY = pl.BlockSpec(memory_space=pl.ANY)
BF16 = jnp.bfloat16
F32 = jnp.float32


class Sizes:
    def __init__(self, points, slots):
        self.blks = lax.axis_size("blk")
        self.reps = lax.axis_size("rep")
        self.plane = lax.axis_size("col") * self.reps
        self.devs = self.blks * self.plane
        self.points = points
        self.slots = slots
        self.local_blocks = points // BS
        self.blocks = self.local_blocks * self.blks
        self.own = self.local_blocks // self.plane
        self.capacity = 2 * self.plane * slots
        per_row = slots * self.devs // self.blocks
        self.first_mib = 6 + self.blocks * DEPTH * BS * 2 // MIB
        self.kept = min(448, (48 - self.first_mib) * 16) // ARRAYS
        self.scale = 16.0 / (BS * per_row) / 256.0

    def me(self):
        return (lax.axis_index("blk") * lax.axis_size("col") + lax.axis_index("col")) * self.reps + lax.axis_index(
            "rep"
        )


def swap(x, axis, code):
    return lax.ppermute(x, axis, [(i, i ^ code) for i in range(lax.axis_size(axis))])


def along_blk(x):
    return jnp.concatenate([x] + [swap(x, "blk", k) for k in range(1, lax.axis_size("blk"))], axis=0)


def over_plane(x):
    reps = lax.axis_size("rep")
    found = {0: x}
    for c in range(1, lax.axis_size("col")):
        found[c * reps] = swap(x, "col", c)
    for start in sorted(found):
        for r in range(1, reps):
            found[start + r] = swap(found[start], "rep", r)
    return [found[k] for k in sorted(found)]


def assemble(sz, refs, rows, target):
    me = sz.me()
    for k, ref in enumerate(refs):
        for z in range(ref.shape[0] // rows):
            start = pl.multiple_of(jnp.bitwise_xor(me, z * sz.plane + k) * rows, 8)
            target[pl.ds(start, rows), :] = ref[z * rows : (z + 1) * rows, :]


def features_of(x_row, y_row, z_row, order):
    feature = lax.broadcasted_iota(jnp.int32, (8, BS), 0)
    x, y, z = ((row - 0.5) * (4.0 / SUPPORT) for row in (x_row, y_row, z_row))
    factor, unit, norm = order
    feats = jnp.where(feature == unit, 1.0, 0.0)
    for place, row in ((0, factor * x), (1, factor * y), (2, factor * z), (norm, x * x + y * y + z * z)):
        feats = jnp.where(feature == place, row, feats)
    return split3(feats)


def split3(x):
    high = x.astype(BF16).astype(F32)
    rest = x - high
    middle = rest.astype(BF16).astype(F32)
    return high, middle, rest - middle


def lhs_kernel(sz, home_ref, out_ref):
    quarter = lax.axis_index("col") * sz.reps + lax.axis_index("rep")
    for i in range(sz.own):
        rows = (home_ref[pl.ds(c * sz.local_blocks + quarter * sz.own + i, 1), :] for c in range(3))
        h, m, l = features_of(*rows, (1.0, 3, 4))
        feats = jnp.concatenate([h, h, m, m, h, l, jnp.zeros((BS - DEPTH, BS), F32)], axis=0)
        out_ref[i * BS : (i + 1) * BS, :] = feats.T.astype(BF16)
    out_ref[sz.own * BS :, :] = jnp.zeros((BS, BS), BF16)


def list_kernel(sz, *refs):
    me = sz.me()
    out_ref, count_ref, target, other, place, value, key_column, key_row, entry_row = refs[sz.plane :]
    lines = sz.slots // BS
    at = 2 * lines * sz.devs
    for base in range(0, at, 2 * lines):
        pairs_ref = refs[base // (2 * lines * sz.blks)]
        start = base % (2 * lines * sz.blks)
        rows = pairs_ref[start : start + lines, :]
        cols = pairs_ref[start + lines : start + 2 * lines, :]
        target[base : base + lines, :] = rows
        other[base : base + lines, :] = cols
        target[base + lines : base + 2 * lines, :] = cols
        other[base + lines : base + 2 * lines, :] = rows
    local = target[...] - me * sz.own
    mine = jnp.logical_and(local >= 0, local < sz.own)
    flags = jnp.where(mine, 1.0, 0.0)
    a = lax.broadcasted_iota(jnp.int32, (BS, BS), 0)
    b = lax.broadcasted_iota(jnp.int32, (BS, BS), 1)
    before = jnp.dot(flags.astype(BF16), jnp.where(a < b, 1.0, 0.0).astype(BF16), preferred_element_type=F32)
    totals = jnp.broadcast_to(jnp.sum(flags, axis=1, keepdims=True), (at, BS))
    a = lax.broadcasted_iota(jnp.int32, (at, at), 0)
    b = lax.broadcasted_iota(jnp.int32, (at, at), 1)
    above = jnp.dot(jnp.where(b < a, 1.0, 0.0).astype(BF16), totals.astype(BF16), preferred_element_type=F32)
    place[...] = jnp.where(mine, above + before, -1.0)
    value[...] = (local + 256 * other[...]).astype(F32)
    count = jnp.sum(flags).astype(jnp.int32)
    count_ref[0] = count
    sub = lax.broadcasted_iota(jnp.int32, (BS, BS), 0)
    lane = lax.broadcasted_iota(jnp.int32, (1, BS), 1)

    chunks = lax.shift_right_logical(count + BS - 1, 7)

    def key_of(found, slot):
        entry = jnp.where(slot < count, found.astype(jnp.int32), sz.own)
        return entry.astype(F32), (jnp.bitwise_and(entry, 255) * 65536 + slot).astype(F32)

    def compact(c, unused):
        slot = (sub + c * BS).astype(F32)

        def line(r, total):
            hit = place[pl.ds(r, 1), :] == slot
            return total + jnp.where(hit, value[pl.ds(r, 1), :], 0.0)

        total = lax.fori_loop(0, at, line, jnp.zeros((BS, BS), F32), unroll=4)
        entry, key = key_of(jnp.sum(total.T, axis=0, keepdims=True), lane + c * BS)
        entry_row[pl.ds(c, 1), :] = entry
        key_row[pl.ds(c, 1), :] = key
        unused_entry, key = key_of(jnp.sum(total, axis=1, keepdims=True), sub[:, 0:1] + c * BS)
        key_column[pl.ds(pl.multiple_of(c * BS, BS), BS), :] = jnp.broadcast_to(key, (BS, BS))
        return unused

    lax.fori_loop(0, chunks, compact, 0)

    def rank(c, unused):
        def below(k, total):
            lower = key_column[pl.ds(pl.multiple_of(k * BS, BS), BS), :] < key_row[pl.ds(c, 1), :]
            return total + jnp.where(lower, 1.0, 0.0)

        total = lax.fori_loop(0, chunks, below, jnp.zeros((BS, BS), F32))
        place[pl.ds(c, 1), :] = jnp.sum(total, axis=0, keepdims=True)
        return unused

    lax.fori_loop(0, chunks, rank, 0)

    def arrange(c, unused):
        slot = (sub + c * BS).astype(F32)

        def line(r, total):
            hit = place[pl.ds(r, 1), :] == slot
            return total + jnp.where(hit, entry_row[pl.ds(r, 1), :], 0.0)

        total = lax.fori_loop(0, chunks, line, jnp.zeros((BS, BS), F32))
        out_ref[pl.ds(c, 1), :] = jnp.sum(total.T, axis=0, keepdims=True).astype(jnp.int32)
        return unused

    lax.fori_loop(0, chunks, arrange, 0)


def entry_of(list_ref, k):
    entry = list_ref[k]
    return jnp.bitwise_and(entry, 255), lax.shift_right_logical(entry, 8)


def tile_of(features, other_features):
    squared = jnp.maximum(jnp.dot(features, other_features, preferred_element_type=F32), 1e-20)
    remain = jnp.maximum(4.0 - squared * lax.rsqrt(squared), 0.0)
    twice = remain * remain
    return twice * twice * (5.0 - remain)


def kept_groups(sz, count, at):
    first = at * (sz.kept // UNROLL)
    last = jnp.minimum(lax.div(count + (UNROLL - 1), UNROLL), first + sz.kept // UNROLL)
    return first, jnp.maximum(first, last)


def generate(sz, list_ref, count, lhs_ref, rhs_ref, tile_refs):
    for at, tile_ref in enumerate(tile_refs):

        def group(g, unused, at=at, tile_ref=tile_ref):
            for u in range(UNROLL):
                i, j = entry_of(list_ref, g * UNROLL + u)
                start = pl.multiple_of((g * UNROLL + u - at * sz.kept) * BS, BS)
                tile_ref[pl.ds(start, BS), :] = tile_of(
                    lhs_ref[pl.ds(pl.multiple_of(i * BS, BS), BS), :DEPTH],
                    rhs_ref[pl.ds(pl.multiple_of(j * DEPTH, DEPTH), DEPTH), :],
                )
            return unused

        lax.fori_loop(*kept_groups(sz, count, at), group, 0)


def sweep(sz, list_ref, count, tile_refs, vec_ref, acc, acc_ones, remake):
    accs = [acc] if acc_ones is None else [acc, acc_ones]
    for ref in accs:
        ref[...] = jnp.zeros_like(ref)
    carry = (jnp.int32(-1),) + tuple(jnp.zeros((BS, BS), F32) for unused in accs)
    for at, tile_ref in enumerate(tile_refs):

        def group(g, carry, at=at, tile_ref=tile_ref):
            before, *sums = carry
            for u in range(UNROLL):
                i, j = entry_of(list_ref, g * UNROLL + u)
                keep = jnp.where(i == before, 1.0, 0.0)
                start = pl.multiple_of((g * UNROLL + u - at * sz.kept) * BS, BS)
                tile = tile_ref[pl.ds(start, BS), :]
                terms = [tile * vec_ref[pl.ds(j, 1), :], tile]
                sums = [total * keep + term for total, term in zip(sums, terms)]
                for ref, total in zip(accs, sums):
                    ref[pl.ds(pl.multiple_of(i * BS, BS), BS), :] = total
                before = i
            return (before, *sums)

        carry = lax.fori_loop(*kept_groups(sz, count, at), group, carry)

    def extra(k, unused):
        i, j = entry_of(list_ref, k)
        tile = tile_of(*remake(i, j))
        rows = pl.ds(pl.multiple_of(i * BS, BS), BS)
        acc[rows, :] += tile * vec_ref[pl.ds(j, 1), :]
        if acc_ones is not None:
            acc_ones[rows, :] += tile
        return unused

    kept = sz.kept * len(tile_refs)
    lax.fori_loop(kept, jnp.maximum(count, kept), extra, 0)


def finish(sz, acc, out_ref):
    unit = jnp.ones((8, BS), BF16)
    across = (((1,), (1,)), ((), ()))
    for i in range(sz.own):
        whole = acc[i * BS : (i + 1) * BS, :]
        high = whole.astype(BF16)
        low = (whole - high.astype(F32)).astype(BF16)
        y = lax.dot_general(unit, high, across, preferred_element_type=F32)
        y = y + lax.dot_general(unit, low, across, preferred_element_type=F32)
        out_ref[i : i + 1, :] = y[0:1, :] * sz.scale


def total_of(x):
    return jnp.sum(jnp.sum(x, axis=0, keepdims=True), axis=1, keepdims=True)


def place_block(piece_ref, part, first, obs_ref, rhs_ref):
    obs_ref[pl.ds(first, part), :] = piece_ref[3 * part : 4 * part, :]

    def one(k, unused):
        h, m, l = features_of(*(piece_ref[pl.ds(c * part + k, 1), :] for c in range(3)), (-2.0, 4, 3))
        feats = jnp.concatenate([h, m, h, m, l, h], axis=0).astype(BF16)
        rhs_ref[pl.ds(pl.multiple_of((first + k) * DEPTH, DEPTH), DEPTH), :] = feats
        return unused

    lax.fori_loop(0, part, one, 0, unroll=4)


def first_kernel(sz, *refs):
    list_ref, count_ref, lhs_ref, nugget_ref, home_ref = refs[:5]
    coord_refs = refs[4 : 5 + (sz.blks - 1) * sz.reps]
    refs = refs[5 + (sz.blks - 1) * sz.reps :]
    tile_refs = refs[:ARRAYS]
    spare_ref, obs_ref, diag_ref, mapped_ref, norm_ref, rhs_ref, acc, acc_ones, total_row, done = refs[ARRAYS:]
    blk, rep = lax.axis_index("blk"), lax.axis_index("rep")
    for at, piece_ref in enumerate(coord_refs[1:]):
        code, turn = at // sz.reps + 1, at % sz.reps
        part = sz.local_blocks // sz.reps
        first = jnp.bitwise_xor(blk, code) * sz.local_blocks + jnp.bitwise_xor(rep, turn) * part
        place_block(piece_ref, part, pl.multiple_of(first, 8), obs_ref, rhs_ref)
    place_block(home_ref, sz.local_blocks, pl.multiple_of(blk * sz.local_blocks, 8), obs_ref, rhs_ref)
    count = count_ref[0]
    generate(sz, list_ref, count, lhs_ref, rhs_ref, tile_refs)

    def remake(i, j):
        features = lhs_ref[pl.ds(pl.multiple_of(i * BS, BS), BS), :DEPTH]
        return features, rhs_ref[pl.ds(pl.multiple_of(j * DEPTH, DEPTH), DEPTH), :]

    sweep(sz, list_ref, count, tile_refs, obs_ref, acc, acc_ones, remake)

    @pl.when(count > sz.kept * ARRAYS)
    def save():
        copy = pltpu.make_async_copy(rhs_ref, spare_ref, done)
        copy.start()
        copy.wait()

    finish(sz, acc_ones, total_row)
    finish(sz, acc, mapped_ref)
    quarter = lax.axis_index("col") * sz.reps + rep
    own = pl.ds(pl.multiple_of(sz.me() * sz.own, 8), sz.own)
    diag = nugget_ref[pl.ds(pl.multiple_of(quarter * sz.own, 8), sz.own), :] + total_row[...]
    diag_ref[...] = diag
    mapped_ref[...] += diag * obs_ref[own, :]
    norm_ref[...] = jnp.broadcast_to(total_of(obs_ref[...] * obs_ref[...]), (8, BS))


def step_kernel(sz, last, *refs):
    list_ref, count_ref, lhs_ref, spare_ref, diag_ref, norm_ref, field_ref, resid_ref, dirn_ref = refs[:9]
    pieces = refs[9 : 9 + sz.plane]
    tile_refs = refs[9 + sz.plane : 9 + sz.plane + ARRAYS]
    rest = refs[9 + sz.plane + ARRAYS :]
    mapped_ref, next_norm_ref, next_field_ref, next_resid_ref, next_dirn_ref = rest[:5]
    if last:
        dot_ref, dirn = rest[5:7]
    else:
        dirn = next_dirn_ref
    mapped, acc, features, others, done = rest[-5:]
    me = sz.me()
    assemble(sz, pieces, sz.own, mapped)
    norm = norm_ref[0:1, 0:1]
    step = norm / total_of(dirn_ref[...] * mapped[...])
    resid = resid_ref[...] - step * mapped[...]
    next_norm = total_of(resid * resid)
    dirn[...] = resid + (next_norm / norm) * dirn_ref[...]
    next_norm_ref[...] = jnp.broadcast_to(next_norm, (8, BS))
    home = pl.ds(pl.multiple_of(lax.axis_index("blk") * sz.local_blocks, 8), sz.local_blocks)
    own = pl.ds(pl.multiple_of(me * sz.own, 8), sz.own)
    field = step * dirn_ref[home, :]
    if last:
        next_field_ref[...] = field_ref[...] + field
        next_resid_ref[...] = resid_ref[home, :] - step * mapped[home, :]
        next_dirn_ref[...] = dirn[home, :]
    else:
        next_field_ref[...] = field
        next_resid_ref[...] = resid

    def remake(i, j):
        for source, start, size, target in ((lhs_ref, i, BS, features), (spare_ref, j, DEPTH, others)):
            copy = pltpu.make_async_copy(source.at[pl.ds(pl.multiple_of(start * size, size), size), :], target, done)
            copy.start()
            copy.wait()
        return features[:, :DEPTH], others[...]

    sweep(sz, list_ref, count_ref[0], tile_refs, dirn, acc, None, remake)
    finish(sz, acc, mapped_ref)
    ours = mapped_ref[...] + diag_ref[...] * dirn[own, :]
    mapped_ref[...] = ours
    if last:
        dot_ref[...] = jnp.broadcast_to(total_of(ours * dirn[own, :]), dot_ref.shape)


def last_kernel(sz, *refs):
    norm_ref, field_ref, resid_ref, dirn_ref = refs[:4]
    pieces = refs[4 : 4 + sz.plane]
    out_field_ref, out_resid_ref = refs[4 + sz.plane :]
    product = jnp.zeros((8, BS), F32)
    for ref in pieces:
        for z in range(sz.blks):
            product = product + ref[sz.own + 8 * z : sz.own + 8 * (z + 1), :]
    step = norm_ref[0:1, :] / product[0:1, :]
    out_field_ref[...] = field_ref[...] + step * dirn_ref[...]
    quarter = lax.axis_index("col") * sz.reps + lax.axis_index("rep")
    for k, ref in enumerate(pieces):
        rows = pl.ds(pl.multiple_of(jnp.bitwise_xor(quarter, k) * sz.own, 8), sz.own)
        out_resid_ref[rows, :] = resid_ref[rows, :] - step * ref[: sz.own, :]


def call(kernel, mib, in_specs, shapes, out_specs, scratch, flops, *args):
    return pl.pallas_call(
        kernel,
        in_specs=in_specs,
        out_shape=shapes,
        out_specs=out_specs,
        scratch_shapes=scratch,
        compiler_params=pltpu.CompilerParams(vmem_limit_bytes=mib * MIB),
        cost_estimate=pl.CostEstimate(flops=flops, bytes_accessed=1 << 20, transcendentals=0),
    )(*args)


def array(*shape, dtype=F32):
    return jax.ShapeDtypeStruct(shape, dtype)


def local(coords, observations, nugget, tile_pairs, tile_live):
    sz = Sizes(observations.shape[0], tile_pairs.shape[1])
    own, blocks, home = sz.own, sz.blocks, sz.local_blocks
    alive = jnp.arange(sz.slots, dtype=jnp.int32) < tile_live[0]
    pairs = jnp.where(alive, tile_pairs, -1).reshape(2 * sz.slots // BS, BS)
    rep = lax.axis_index("rep")
    part = home // sz.reps
    rows = jnp.concatenate([coords, observations[None]], axis=0).reshape(4, home, BS)
    half = lax.dynamic_slice_in_dim(rows, rep * part, part, axis=1).reshape(4 * part, BS)
    rows = rows.reshape(4 * home, BS)
    nears = [swap(half, "blk", z) for z in range(1, sz.blks)]
    pair_arrays = over_plane(along_blk(pairs))

    lhs = call(
        functools.partial(lhs_kernel, sz),
        12,
        [VMEM],
        array((own + 1) * BS, BS, dtype=BF16),
        VMEM,
        [],
        10_000_000,
        rows,
    )
    lines = 2 * sz.slots // BS * sz.devs
    table, count = call(
        functools.partial(list_kernel, sz),
        12,
        [VMEM] * sz.plane,
        (array(sz.capacity // BS, BS, dtype=jnp.int32), array(1, dtype=jnp.int32)),
        (VMEM, SMEM),
        [pltpu.VMEM((lines, BS), jnp.int32)] * 2
        + [pltpu.VMEM((lines, BS), F32)] * 2
        + [pltpu.VMEM((sz.capacity, BS), F32)]
        + [pltpu.VMEM((sz.capacity // BS, BS), F32)] * 2,
        10_000_000,
        *pair_arrays,
    )
    table, lhs, *nears = lax.optimization_barrier((table.reshape(sz.capacity), lhs, *nears))
    coord_arrays = []
    for near in nears:
        coord_arrays += [near] + [swap(near, "rep", r) for r in range(1, sz.reps)]
    tall = pltpu.VMEM(((own + 1) * BS, BS), F32)
    kept = [pltpu.VMEM((sz.kept * BS, BS), F32)] * ARRAYS
    *tiles, spare, obs, diag, mapped, norm = call(
        functools.partial(first_kernel, sz),
        sz.first_mib,
        [SMEM, SMEM] + [VMEM] * (3 + len(coord_arrays)),
        kept
        + [
            pltpu.HBM((blocks * DEPTH, BS), BF16),
            array(blocks, BS),
            array(own, BS),
            array(own, BS),
            array(8, BS),
        ],
        [VMEM] * ARRAYS + [ANY] + [VMEM] * 4,
        [
            pltpu.VMEM((blocks * DEPTH, BS), BF16),
            tall,
            tall,
            pltpu.VMEM((own, BS), F32),
            pltpu.SemaphoreType.DMA,
        ],
        100_000_000,
        table,
        count,
        lhs,
        nugget.reshape(home, BS),
        rows,
        *coord_arrays,
    )
    tiles = [pltpu.with_memory_space_constraint(tile, pltpu.VMEM) for tile in tiles]
    spare = pltpu.with_memory_space_constraint(spare, pltpu.HBM)
    field, resid, dirn = norm, obs, obs
    for sweep_index in range(1, ITERS):
        last = sweep_index + 1 == ITERS
        span = home if last else blocks
        outs = [array(own, BS), array(8, BS), array(home, BS), array(span, BS), array(span, BS)]
        mapped, norm, field, resid, dirn, *dot = call(
            functools.partial(step_kernel, sz, last),
            5,
            [SMEM, SMEM, ANY, ANY] + [VMEM] * (5 + sz.plane + ARRAYS),
            outs + [array(8, BS)] * last,
            [VMEM] * (len(outs) + last),
            [pltpu.VMEM((blocks, BS), F32)] * (1 + last)
            + [tall, pltpu.VMEM((BS, BS), BF16), pltpu.VMEM((DEPTH, BS), BF16), pltpu.SemaphoreType.DMA],
            100_000_000,
            table,
            count,
            lhs,
            spare,
            diag,
            norm,
            field,
            resid,
            dirn,
            *over_plane(along_blk(mapped)),
            *tiles,
        )
    ends = over_plane(jnp.concatenate([mapped, along_blk(dot[0])], axis=0))
    field, resid = call(
        functools.partial(last_kernel, sz),
        4,
        [VMEM] * (4 + sz.plane),
        (array(home, BS), array(home, BS)),
        (VMEM, VMEM),
        [],
        100_000,
        norm,
        field,
        resid,
        dirn,
        *ends,
    )
    return field.reshape(sz.points), resid.reshape(sz.points)


def solution(mesh):
    in_specs = (
        P(None, ("grp", "blk")),
        P(("grp", "blk")),
        P(("grp", "blk")),
        P(None, ("grp", "blk", "col", "rep")),
        P(("grp", "blk", "col", "rep")),
    )
    out_specs = (P(("grp", "blk")), P(("grp", "blk")))
    return jax.shard_map(local, mesh=mesh, in_specs=in_specs, out_specs=out_specs, check_vma=False)
```

```python
import functools

import jax
import jax.numpy as jnp
from jax import lax
from jax.experimental import pallas as pl
from jax.experimental.pallas import tpu as pltpu
from jax.sharding import PartitionSpec as P

BS = 128
ITERS = 3
SUPPORT = 0.3
DEPTH = 48
UNROLL = 4
ARRAYS = 4
MIB = 1024 * 1024
VMEM = pl.BlockSpec(memory_space=pltpu.VMEM)
SMEM = pl.BlockSpec(memory_space=pltpu.SMEM)
ANY = pl.BlockSpec(memory_space=pl.ANY)
BF16 = jnp.bfloat16
F32 = jnp.float32


class Sizes:
    def __init__(self, points, slots):
        self.blks = lax.axis_size("blk")
        self.reps = lax.axis_size("rep")
        self.plane = lax.axis_size("col") * self.reps
        self.devs = self.blks * self.plane
        self.points = points
        self.slots = slots
        self.local_blocks = points // BS
        self.blocks = self.local_blocks * self.blks
        self.own = self.local_blocks // self.plane
        self.capacity = 2 * self.plane * slots
        per_row = slots * self.devs // self.blocks
        self.first_mib = 6 + self.blocks * DEPTH * BS * 2 // MIB
        self.kept = min(448, (48 - self.first_mib) * 16) // ARRAYS
        self.scale = 16.0 / (BS * per_row) / 256.0

    def me(self):
        return (lax.axis_index("blk") * lax.axis_size("col") + lax.axis_index("col")) * self.reps + lax.axis_index(
            "rep"
        )


def swap(x, axis, code):
    return lax.ppermute(x, axis, [(i, i ^ code) for i in range(lax.axis_size(axis))])


def along_blk(x):
    return jnp.concatenate([x] + [swap(x, "blk", k) for k in range(1, lax.axis_size("blk"))], axis=0)


def over_plane(x):
    reps = lax.axis_size("rep")
    found = {0: x}
    for c in range(1, lax.axis_size("col")):
        found[c * reps] = swap(x, "col", c)
    for start in sorted(found):
        for r in range(1, reps):
            found[start + r] = swap(found[start], "rep", r)
    return [found[k] for k in sorted(found)]


def assemble(sz, refs, rows, target):
    me = sz.me()
    for k, ref in enumerate(refs):
        for z in range(ref.shape[0] // rows):
            start = pl.multiple_of(jnp.bitwise_xor(me, z * sz.plane + k) * rows, 8)
            target[pl.ds(start, rows), :] = ref[z * rows : (z + 1) * rows, :]


def features_of(x_row, y_row, z_row, order):
    feature = lax.broadcasted_iota(jnp.int32, (8, BS), 0)
    x, y, z = ((row - 0.5) * (4.0 / SUPPORT) for row in (x_row, y_row, z_row))
    factor, unit, norm = order
    feats = jnp.where(feature == unit, 1.0, 0.0)
    for place, row in ((0, factor * x), (1, factor * y), (2, factor * z), (norm, x * x + y * y + z * z)):
        feats = jnp.where(feature == place, row, feats)
    return split3(feats)


def split3(x):
    high = x.astype(BF16).astype(F32)
    rest = x - high
    middle = rest.astype(BF16).astype(F32)
    return high, middle, rest - middle


def block_row(ref, c, part, k):
    return ref[c, pl.ds(k, 1), :] if len(ref.shape) == 3 else ref[pl.ds(c * part + k, 1), :]


def lhs_kernel(sz, home_ref, out_ref):
    quarter = lax.axis_index("col") * sz.reps + lax.axis_index("rep")
    for i in range(sz.own):
        rows = (block_row(home_ref, c, None, quarter * sz.own + i) for c in range(3))
        h, m, l = features_of(*rows, (1.0, 3, 4))
        feats = jnp.concatenate([h, h, m, m, h, l, jnp.zeros((BS - DEPTH, BS), F32)], axis=0)
        out_ref[i * BS : (i + 1) * BS, :] = feats.T.astype(BF16)
    out_ref[sz.own * BS :, :] = jnp.zeros((BS, BS), BF16)


def list_kernel(sz, *refs):
    me = sz.me()
    out_ref, count_ref, target, other, place, value, key_column, key_row, entry_row = refs[sz.plane :]
    lines = sz.slots // BS
    at = 2 * lines * sz.devs
    for base in range(0, at, 2 * lines):
        pairs_ref = refs[base // (2 * lines * sz.blks)]
        start = base % (2 * lines * sz.blks)
        rows = pairs_ref[start : start + lines, :]
        cols = pairs_ref[start + lines : start + 2 * lines, :]
        target[base : base + lines, :] = rows
        other[base : base + lines, :] = cols
        target[base + lines : base + 2 * lines, :] = cols
        other[base + lines : base + 2 * lines, :] = rows
    local = target[...] - me * sz.own
    mine = jnp.logical_and(local >= 0, local < sz.own)
    flags = jnp.where(mine, 1.0, 0.0)
    a = lax.broadcasted_iota(jnp.int32, (BS, BS), 0)
    b = lax.broadcasted_iota(jnp.int32, (BS, BS), 1)
    before = jnp.dot(flags.astype(BF16), jnp.where(a < b, 1.0, 0.0).astype(BF16), preferred_element_type=F32)
    totals = jnp.broadcast_to(jnp.sum(flags, axis=1, keepdims=True), (at, BS))
    a = lax.broadcasted_iota(jnp.int32, (at, at), 0)
    b = lax.broadcasted_iota(jnp.int32, (at, at), 1)
    above = jnp.dot(jnp.where(b < a, 1.0, 0.0).astype(BF16), totals.astype(BF16), preferred_element_type=F32)
    place[...] = jnp.where(mine, above + before, -1.0)
    value[...] = (local + 256 * other[...]).astype(F32)
    count = jnp.sum(flags).astype(jnp.int32)
    count_ref[0] = count
    sub = lax.broadcasted_iota(jnp.int32, (BS, BS), 0)
    lane = lax.broadcasted_iota(jnp.int32, (1, BS), 1)

    chunks = jnp.maximum(lax.shift_right_logical(count + BS - 1, 7), 1)

    def key_of(found, slot):
        entry = jnp.where(slot < count, found.astype(jnp.int32), sz.own)
        return entry.astype(F32), (jnp.bitwise_and(entry, 255) * 65536 + slot).astype(F32)

    def compact(c, unused):
        slot = (sub + c * BS).astype(F32)

        def line(r, total):
            hit = place[pl.ds(r, 1), :] == slot
            return total + jnp.where(hit, value[pl.ds(r, 1), :], 0.0)

        total = lax.fori_loop(0, at, line, jnp.zeros((BS, BS), F32), unroll=4)
        entry, key = key_of(jnp.sum(total.T, axis=0, keepdims=True), lane + c * BS)
        entry_row[pl.ds(c, 1), :] = entry
        key_row[pl.ds(c, 1), :] = key
        unused_entry, key = key_of(jnp.sum(total, axis=1, keepdims=True), sub[:, 0:1] + c * BS)
        key_column[pl.ds(pl.multiple_of(c * BS, BS), BS), :] = jnp.broadcast_to(key, (BS, BS))
        return unused

    lax.fori_loop(0, chunks, compact, 0)

    def rank(c, unused):
        def below(k, total):
            lower = key_column[pl.ds(pl.multiple_of(k * BS, BS), BS), :] < key_row[pl.ds(c, 1), :]
            return total + jnp.where(lower, 1.0, 0.0)

        total = lax.fori_loop(0, chunks, below, jnp.zeros((BS, BS), F32))
        place[pl.ds(c, 1), :] = jnp.sum(total, axis=0, keepdims=True)
        return unused

    lax.fori_loop(0, chunks, rank, 0)

    def arrange(c, unused):
        slot = (sub + c * BS).astype(F32)

        def line(r, total):
            hit = place[pl.ds(r, 1), :] == slot
            return total + jnp.where(hit, entry_row[pl.ds(r, 1), :], 0.0)

        total = lax.fori_loop(0, chunks, line, jnp.zeros((BS, BS), F32))
        out_ref[pl.ds(c, 1), :] = jnp.sum(total.T, axis=0, keepdims=True).astype(jnp.int32)
        return unused

    lax.fori_loop(0, chunks, arrange, 0)


def entry_of(list_ref, k):
    entry = list_ref[k]
    return jnp.bitwise_and(entry, 255), lax.shift_right_logical(entry, 8)


def squared_of(features, other_features):
    return jnp.dot(features, other_features, preferred_element_type=F32)


def taper_of(squared):
    squared = jnp.maximum(squared, 1e-20)
    remain = jnp.maximum(4.0 - squared * lax.rsqrt(squared), 0.0)
    twice = remain * remain
    return twice * twice * (5.0 - remain)


def kept_groups(sz, count, at):
    first = at * (sz.kept // UNROLL)
    last = jnp.minimum(lax.div(count + (UNROLL - 1), UNROLL), first + sz.kept // UNROLL)
    return first, jnp.maximum(first, last)


def generate(sz, list_ref, count, lhs_ref, rhs_ref, tile_refs, squares):
    top = jnp.maximum(lax.div(count + (UNROLL - 1), UNROLL) - 1, 0)

    def squared(g, u):
        i, j = entry_of(list_ref, jnp.minimum(g, top) * UNROLL + u)
        return squared_of(
            lhs_ref[pl.ds(pl.multiple_of(i * BS, BS), BS), :DEPTH],
            rhs_ref[pl.ds(pl.multiple_of(j * DEPTH, DEPTH), DEPTH), :],
        )

    for u in range(UNROLL):
        squares[u * BS : (u + 1) * BS, :] = squared(0, u)
    for at, tile_ref in enumerate(tile_refs):

        def group(g, unused, at=at, tile_ref=tile_ref):
            for u in range(UNROLL):
                here = slice(u * BS, (u + 1) * BS)
                tile = taper_of(squares[here, :])
                squares[here, :] = squared(g + 1, u)
                start = pl.multiple_of((g * UNROLL + u - at * sz.kept) * BS, BS)
                tile_ref[pl.ds(start, BS), :] = tile
            return unused

        lax.fori_loop(*kept_groups(sz, count, at), group, 0)


def sweep(sz, list_ref, count, tile_refs, vec_ref, acc, acc_ones, remake):
    accs = [acc] if acc_ones is None else [acc, acc_ones]
    for ref in accs:
        ref[...] = jnp.zeros_like(ref)
    carry = (jnp.int32(-1),) + tuple(jnp.zeros((BS, BS), F32) for unused in accs)
    for at, tile_ref in enumerate(tile_refs):

        def group(g, carry, at=at, tile_ref=tile_ref):
            before, *sums = carry
            for u in range(UNROLL):
                i, j = entry_of(list_ref, g * UNROLL + u)
                keep = jnp.where(i == before, 1.0, 0.0)
                start = pl.multiple_of((g * UNROLL + u - at * sz.kept) * BS, BS)
                tile = tile_ref[pl.ds(start, BS), :]
                terms = [tile * vec_ref[pl.ds(j, 1), :], tile]
                sums = [total * keep + term for total, term in zip(sums, terms)]
                for ref, total in zip(accs, sums):
                    ref[pl.ds(pl.multiple_of(i * BS, BS), BS), :] = total
                before = i
            return (before, *sums)

        carry = lax.fori_loop(*kept_groups(sz, count, at), group, carry)

    def extra(k, unused):
        i, j = entry_of(list_ref, k)
        tile = taper_of(squared_of(*remake(i, j)))
        rows = pl.ds(pl.multiple_of(i * BS, BS), BS)
        acc[rows, :] += tile * vec_ref[pl.ds(j, 1), :]
        if acc_ones is not None:
            acc_ones[rows, :] += tile
        return unused

    kept = sz.kept * len(tile_refs)
    lax.fori_loop(kept, jnp.maximum(count, kept), extra, 0)


def finish(sz, acc, out_ref):
    unit = jnp.ones((8, BS), BF16)
    across = (((1,), (1,)), ((), ()))
    for i in range(sz.own):
        whole = acc[i * BS : (i + 1) * BS, :]
        high = whole.astype(BF16)
        low = (whole - high.astype(F32)).astype(BF16)
        y = lax.dot_general(unit, high, across, preferred_element_type=F32)
        y = y + lax.dot_general(unit, low, across, preferred_element_type=F32)
        out_ref[i : i + 1, :] = y[0:1, :] * sz.scale


def total_of(x):
    return jnp.sum(jnp.sum(x, axis=0, keepdims=True), axis=1, keepdims=True)


def place_block(piece_ref, part, first, rhs_ref):
    def one(k, unused):
        h, m, l = features_of(*(block_row(piece_ref, c, part, k) for c in range(3)), (-2.0, 4, 3))
        feats = jnp.concatenate([h, m, h, m, l, h], axis=0).astype(BF16)
        rhs_ref[pl.ds(pl.multiple_of((first + k) * DEPTH, DEPTH), DEPTH), :] = feats
        return unused

    lax.fori_loop(0, part, one, 0, unroll=4)


def first_kernel(sz, *refs):
    list_ref, count_ref, lhs_ref, nugget_any, obs_any, home_ref = refs[:6]
    coord_refs = refs[6 : 6 + (sz.blks - 1) * sz.reps]
    refs = refs[6 + (sz.blks - 1) * sz.reps :]
    tile_refs = refs[:ARRAYS]
    spare_ref, obs_ref, diag_ref, mapped_ref, norm_ref = refs[ARRAYS : ARRAYS + 5]
    rhs_ref, acc, acc_ones, total_row, squares, nugget_ref, done, fetched = refs[ARRAYS + 5 :]
    blk, rep = lax.axis_index("blk"), lax.axis_index("rep")
    home = pl.ds(pl.multiple_of(blk * sz.local_blocks, 8), sz.local_blocks)
    fetch = pltpu.make_async_copy(nugget_any, nugget_ref, fetched.at[0])
    fetch_obs = pltpu.make_async_copy(obs_any, obs_ref.at[home, :], fetched.at[1])
    fetch.start()
    fetch_obs.start()
    for at, piece_ref in enumerate(coord_refs):
        code, turn = at // sz.reps + 1, at % sz.reps
        part = sz.local_blocks // sz.reps
        first = jnp.bitwise_xor(blk, code) * sz.local_blocks + jnp.bitwise_xor(rep, turn) * part
        first = pl.multiple_of(first, 8)
        place_block(piece_ref, part, first, rhs_ref)
        obs_ref[pl.ds(first, part), :] = piece_ref[3 * part : 4 * part, :]
    place_block(home_ref, sz.local_blocks, blk * sz.local_blocks, rhs_ref)
    count = count_ref[0]
    generate(sz, list_ref, count, lhs_ref, rhs_ref, tile_refs, squares)

    def remake(i, j):
        features = lhs_ref[pl.ds(pl.multiple_of(i * BS, BS), BS), :DEPTH]
        return features, rhs_ref[pl.ds(pl.multiple_of(j * DEPTH, DEPTH), DEPTH), :]

    fetch_obs.wait()
    sweep(sz, list_ref, count, tile_refs, obs_ref, acc, acc_ones, remake)

    @pl.when(count > sz.kept * ARRAYS)
    def save():
        copy = pltpu.make_async_copy(rhs_ref, spare_ref, done)
        copy.start()
        copy.wait()

    finish(sz, acc_ones, total_row)
    finish(sz, acc, mapped_ref)
    quarter = lax.axis_index("col") * sz.reps + rep
    own = pl.ds(pl.multiple_of(sz.me() * sz.own, 8), sz.own)
    fetch.wait()
    diag = nugget_ref[pl.ds(pl.multiple_of(quarter * sz.own, 8), sz.own), :] + total_row[...]
    diag_ref[...] = diag
    mapped_ref[...] += diag * obs_ref[own, :]
    norm_ref[...] = jnp.broadcast_to(total_of(obs_ref[...] * obs_ref[...]), (8, BS))


def step_kernel(sz, last, *refs):
    list_ref, count_ref, lhs_ref, spare_ref, diag_ref, norm_ref, field_ref, resid_ref, dirn_ref = refs[:9]
    pieces = refs[9 : 9 + sz.plane]
    tile_refs = refs[9 + sz.plane : 9 + sz.plane + ARRAYS]
    rest = refs[9 + sz.plane + ARRAYS :]
    mapped_ref, next_norm_ref, next_field_ref, next_resid_ref, next_dirn_ref = rest[:5]
    if last:
        dot_ref, dirn = rest[5:7]
    else:
        dirn = next_dirn_ref
    mapped, acc, features, others, done = rest[-5:]
    me = sz.me()
    assemble(sz, pieces, sz.own, mapped)
    norm = norm_ref[0:1, 0:1]
    step = norm / total_of(dirn_ref[...] * mapped[...])
    resid = resid_ref[...] - step * mapped[...]
    next_norm = total_of(resid * resid)
    dirn[...] = resid + (next_norm / norm) * dirn_ref[...]
    next_norm_ref[...] = jnp.broadcast_to(next_norm, (8, BS))
    home = pl.ds(pl.multiple_of(lax.axis_index("blk") * sz.local_blocks, 8), sz.local_blocks)
    own = pl.ds(pl.multiple_of(me * sz.own, 8), sz.own)
    field = step * dirn_ref[home, :]
    if last:
        next_field_ref[...] = field_ref[...] + field
        next_resid_ref[...] = resid_ref[home, :] - step * mapped[home, :]
        next_dirn_ref[...] = dirn[home, :]
    else:
        next_field_ref[...] = field
        next_resid_ref[...] = resid

    def remake(i, j):
        for source, start, size, target in ((lhs_ref, i, BS, features), (spare_ref, j, DEPTH, others)):
            copy = pltpu.make_async_copy(source.at[pl.ds(pl.multiple_of(start * size, size), size), :], target, done)
            copy.start()
            copy.wait()
        return features[:, :DEPTH], others[...]

    sweep(sz, list_ref, count_ref[0], tile_refs, dirn, acc, None, remake)
    finish(sz, acc, mapped_ref)
    ours = mapped_ref[...] + diag_ref[...] * dirn[own, :]
    mapped_ref[...] = ours
    if last:
        dot_ref[...] = jnp.broadcast_to(total_of(ours * dirn[own, :]), dot_ref.shape)


def last_kernel(sz, *refs):
    norm_ref, field_ref, resid_ref, dirn_ref = refs[:4]
    pieces = refs[4 : 4 + sz.plane]
    out_field_ref, out_resid_ref = refs[4 + sz.plane :]
    product = jnp.zeros((8, BS), F32)
    for ref in pieces:
        for z in range(sz.blks):
            product = product + ref[sz.own + 8 * z : sz.own + 8 * (z + 1), :]
    step = norm_ref[0:1, :] / product[0:1, :]
    out_field_ref[...] = field_ref[...] + step * dirn_ref[...]
    quarter = lax.axis_index("col") * sz.reps + lax.axis_index("rep")
    for k, ref in enumerate(pieces):
        rows = pl.ds(pl.multiple_of(jnp.bitwise_xor(quarter, k) * sz.own, 8), sz.own)
        out_resid_ref[rows, :] = resid_ref[rows, :] - step * ref[: sz.own, :]


def call(kernel, mib, in_specs, shapes, out_specs, scratch, flops, *args):
    return pl.pallas_call(
        kernel,
        in_specs=in_specs,
        out_shape=shapes,
        out_specs=out_specs,
        scratch_shapes=scratch,
        compiler_params=pltpu.CompilerParams(vmem_limit_bytes=mib * MIB),
        cost_estimate=pl.CostEstimate(flops=flops, bytes_accessed=1 << 20, transcendentals=0),
    )(*args)


def array(*shape, dtype=F32):
    return jax.ShapeDtypeStruct(shape, dtype)


def local(coords, observations, nugget, tile_pairs, tile_live):
    sz = Sizes(observations.shape[0], tile_pairs.shape[1])
    own, blocks, home = sz.own, sz.blocks, sz.local_blocks
    alive = jnp.arange(sz.slots, dtype=jnp.int32) < tile_live[0]
    pairs = jnp.where(alive, tile_pairs, -1).reshape(2 * sz.slots // BS, BS)
    rep = lax.axis_index("rep")
    part = home // sz.reps
    obs_rows = observations.reshape(home, BS)
    rows = coords.reshape(3, home, BS)
    half = lax.dynamic_slice_in_dim(jnp.concatenate([rows, obs_rows[None]], axis=0), rep * part, part, axis=1)
    half = half.reshape(4 * part, BS)
    nears = [swap(half, "blk", z) for z in range(1, sz.blks)]
    pair_arrays = over_plane(along_blk(pairs))

    lhs = call(
        functools.partial(lhs_kernel, sz),
        12,
        [VMEM],
        array((own + 1) * BS, BS, dtype=BF16),
        VMEM,
        [],
        10_000_000,
        rows,
    )
    lines = 2 * sz.slots // BS * sz.devs
    table, count = call(
        functools.partial(list_kernel, sz),
        12,
        [VMEM] * sz.plane,
        (array(sz.capacity // BS, BS, dtype=jnp.int32), array(1, dtype=jnp.int32)),
        (VMEM, SMEM),
        [pltpu.VMEM((lines, BS), jnp.int32)] * 2
        + [pltpu.VMEM((lines, BS), F32)] * 2
        + [pltpu.VMEM((sz.capacity, BS), F32)]
        + [pltpu.VMEM((sz.capacity // BS, BS), F32)] * 2,
        10_000_000,
        *pair_arrays,
    )
    table, lhs, *nears = lax.optimization_barrier((table.reshape(sz.capacity), lhs, *nears))
    coord_arrays = []
    for near in nears:
        coord_arrays += [near] + [swap(near, "rep", r) for r in range(1, sz.reps)]
    tall = pltpu.VMEM(((own + 1) * BS, BS), F32)
    kept = [pltpu.VMEM((sz.kept * BS, BS), F32)] * ARRAYS
    *tiles, spare, obs, diag, mapped, norm = call(
        functools.partial(first_kernel, sz),
        sz.first_mib,
        [SMEM, SMEM, VMEM, ANY, ANY] + [VMEM] * (1 + len(coord_arrays)),
        kept
        + [
            pltpu.HBM((blocks * DEPTH, BS), BF16),
            array(blocks, BS),
            array(own, BS),
            array(own, BS),
            array(8, BS),
        ],
        [VMEM] * ARRAYS + [ANY] + [VMEM] * 4,
        [
            pltpu.VMEM((blocks * DEPTH, BS), BF16),
            tall,
            tall,
            pltpu.VMEM((own, BS), F32),
            pltpu.VMEM((UNROLL * BS, BS), F32),
            pltpu.VMEM((home, BS), F32),
            pltpu.SemaphoreType.DMA,
            pltpu.SemaphoreType.DMA((2,)),
        ],
        100_000_000,
        table,
        count,
        lhs,
        pltpu.with_memory_space_constraint(nugget.reshape(home, BS), pltpu.HBM),
        pltpu.with_memory_space_constraint(obs_rows, pltpu.HBM),
        rows,
        *coord_arrays,
    )
    tiles = [pltpu.with_memory_space_constraint(tile, pltpu.VMEM) for tile in tiles]
    spare = pltpu.with_memory_space_constraint(spare, pltpu.HBM)
    field, resid, dirn = norm, obs, obs
    for sweep_index in range(1, ITERS):
        last = sweep_index + 1 == ITERS
        span = home if last else blocks
        outs = [array(own, BS), array(8, BS), array(home, BS), array(span, BS), array(span, BS)]
        mapped, norm, field, resid, dirn, *dot = call(
            functools.partial(step_kernel, sz, last),
            5,
            [SMEM, SMEM, ANY, ANY] + [VMEM] * (5 + sz.plane + ARRAYS),
            outs + [array(8, BS)] * last,
            [VMEM] * (len(outs) + last),
            [pltpu.VMEM((blocks, BS), F32)] * (1 + last)
            + [tall, pltpu.VMEM((BS, BS), BF16), pltpu.VMEM((DEPTH, BS), BF16), pltpu.SemaphoreType.DMA],
            100_000_000,
            table,
            count,
            lhs,
            spare,
            diag,
            norm,
            field,
            resid,
            dirn,
            *over_plane(along_blk(mapped)),
            *tiles,
        )
    ends = over_plane(jnp.concatenate([mapped, along_blk(dot[0])], axis=0))
    field, resid = call(
        functools.partial(last_kernel, sz),
        4,
        [VMEM] * (4 + sz.plane),
        (array(home, BS), array(home, BS)),
        (VMEM, VMEM),
        [],
        100_000,
        norm,
        field,
        resid,
        dirn,
        *ends,
    )
    return field.reshape(sz.points), resid.reshape(sz.points)


def solution(mesh):
    in_specs = (
        P(None, ("grp", "blk")),
        P(("grp", "blk")),
        P(("grp", "blk")),
        P(None, ("grp", "blk", "col", "rep")),
        P(("grp", "blk", "col", "rep")),
    )
    out_specs = (P(("grp", "blk")), P(("grp", "blk")))
    return jax.shard_map(local, mesh=mesh, in_specs=in_specs, out_specs=out_specs, check_vma=False)
```

```python
import functools

import jax
import jax.numpy as jnp
from jax import lax
from jax.experimental import pallas as pl
from jax.experimental.pallas import tpu as pltpu
from jax.sharding import PartitionSpec as P

BS = 128
ITERS = 3
SUPPORT = 0.3
DEPTH = 48
UNROLL = 4
ARRAYS = 4
MIB = 1024 * 1024
VMEM = pl.BlockSpec(memory_space=pltpu.VMEM)
SMEM = pl.BlockSpec(memory_space=pltpu.SMEM)
ANY = pl.BlockSpec(memory_space=pl.ANY)
BF16 = jnp.bfloat16
F32 = jnp.float32


class Sizes:
    def __init__(self, points, slots):
        self.blks = lax.axis_size("blk")
        self.reps = lax.axis_size("rep")
        self.plane = lax.axis_size("col") * self.reps
        self.devs = self.blks * self.plane
        self.points = points
        self.slots = slots
        self.local_blocks = points // BS
        self.blocks = self.local_blocks * self.blks
        self.own = self.local_blocks // self.plane
        self.capacity = 2 * self.plane * slots
        per_row = slots * self.devs // self.blocks
        self.first_mib = 6 + self.blocks * DEPTH * BS * 2 // MIB
        self.kept = min(448, (48 - self.first_mib) * 16) // ARRAYS
        self.scale = 16.0 / (BS * per_row) / 256.0

    def me(self):
        return (lax.axis_index("blk") * lax.axis_size("col") + lax.axis_index("col")) * self.reps + lax.axis_index(
            "rep"
        )


def swap(x, axis, code):
    return lax.ppermute(x, axis, [(i, i ^ code) for i in range(lax.axis_size(axis))])


def along_blk(x):
    return jnp.concatenate([x] + [swap(x, "blk", k) for k in range(1, lax.axis_size("blk"))], axis=0)


def over_plane(x):
    reps = lax.axis_size("rep")
    found = {0: x}
    for c in range(1, lax.axis_size("col")):
        found[c * reps] = swap(x, "col", c)
    for start in sorted(found):
        for r in range(1, reps):
            found[start + r] = swap(found[start], "rep", r)
    return [found[k] for k in sorted(found)]


def assemble(sz, refs, rows, target):
    me = sz.me()
    for k, ref in enumerate(refs):
        for z in range(ref.shape[0] // rows):
            start = pl.multiple_of(jnp.bitwise_xor(me, z * sz.plane + k) * rows, 8)
            target[pl.ds(start, rows), :] = ref[z * rows : (z + 1) * rows, :]


def features_of(x_row, y_row, z_row, order):
    feature = lax.broadcasted_iota(jnp.int32, (8, BS), 0)
    x, y, z = ((row - 0.5) * (4.0 / SUPPORT) for row in (x_row, y_row, z_row))
    factor, unit, norm = order
    feats = jnp.where(feature == unit, 1.0, 0.0)
    for place, row in ((0, factor * x), (1, factor * y), (2, factor * z), (norm, x * x + y * y + z * z)):
        feats = jnp.where(feature == place, row, feats)
    return split3(feats)


def split3(x):
    high = x.astype(BF16).astype(F32)
    rest = x - high
    middle = rest.astype(BF16).astype(F32)
    return high, middle, rest - middle


def block_row(ref, c, part, k):
    return ref[c, pl.ds(k, 1), :] if len(ref.shape) == 3 else ref[pl.ds(c * part + k, 1), :]


def lhs_kernel(sz, home_ref, out_ref):
    quarter = lax.axis_index("col") * sz.reps + lax.axis_index("rep")
    for i in range(sz.own):
        rows = (block_row(home_ref, c, None, quarter * sz.own + i) for c in range(3))
        h, m, l = features_of(*rows, (1.0, 3, 4))
        feats = jnp.concatenate([h, h, m, m, h, l, jnp.zeros((BS - DEPTH, BS), F32)], axis=0)
        out_ref[i * BS : (i + 1) * BS, :] = feats.T.astype(BF16)
    out_ref[sz.own * BS :, :] = jnp.zeros((BS, BS), BF16)


def list_kernel(sz, *refs):
    me = sz.me()
    out_ref, count_ref, target, other, place, value, key_column, key_row, entry_row = refs[sz.plane :]
    lines = sz.slots // BS
    at = 2 * lines * sz.devs
    for base in range(0, at, 2 * lines):
        pairs_ref = refs[base // (2 * lines * sz.blks)]
        start = base % (2 * lines * sz.blks)
        rows = pairs_ref[start : start + lines, :]
        cols = pairs_ref[start + lines : start + 2 * lines, :]
        target[base : base + lines, :] = rows
        other[base : base + lines, :] = cols
        target[base + lines : base + 2 * lines, :] = cols
        other[base + lines : base + 2 * lines, :] = rows
    local = target[...] - me * sz.own
    mine = jnp.logical_and(local >= 0, local < sz.own)
    flags = jnp.where(mine, 1.0, 0.0)
    a = lax.broadcasted_iota(jnp.int32, (BS, BS), 0)
    b = lax.broadcasted_iota(jnp.int32, (BS, BS), 1)
    before = jnp.dot(flags.astype(BF16), jnp.where(a < b, 1.0, 0.0).astype(BF16), preferred_element_type=F32)
    totals = jnp.broadcast_to(jnp.sum(flags, axis=1, keepdims=True), (at, BS))
    a = lax.broadcasted_iota(jnp.int32, (at, at), 0)
    b = lax.broadcasted_iota(jnp.int32, (at, at), 1)
    above = jnp.dot(jnp.where(b < a, 1.0, 0.0).astype(BF16), totals.astype(BF16), preferred_element_type=F32)
    place[...] = jnp.where(mine, above + before, -1.0)
    value[...] = (local + 256 * other[...]).astype(F32)
    count = jnp.sum(flags).astype(jnp.int32)
    count_ref[0] = count
    sub = lax.broadcasted_iota(jnp.int32, (BS, BS), 0)
    lane = lax.broadcasted_iota(jnp.int32, (1, BS), 1)

    chunks = jnp.maximum(lax.shift_right_logical(count + BS - 1, 7), 1)

    def key_of(found, slot):
        entry = jnp.where(slot < count, found.astype(jnp.int32), sz.own)
        return entry.astype(F32), (jnp.bitwise_and(entry, 255) * 65536 + slot).astype(F32)

    def compact(c, unused):
        slot = (sub + c * BS).astype(F32)

        def line(r, total):
            hit = place[pl.ds(r, 1), :] == slot
            return total + jnp.where(hit, value[pl.ds(r, 1), :], 0.0)

        total = lax.fori_loop(0, at, line, jnp.zeros((BS, BS), F32), unroll=4)
        entry, key = key_of(jnp.sum(total.T, axis=0, keepdims=True), lane + c * BS)
        entry_row[pl.ds(c, 1), :] = entry
        key_row[pl.ds(c, 1), :] = key
        unused_entry, key = key_of(jnp.sum(total, axis=1, keepdims=True), sub[:, 0:1] + c * BS)
        key_column[pl.ds(pl.multiple_of(c * BS, BS), BS), :] = jnp.broadcast_to(key, (BS, BS))
        return unused

    lax.fori_loop(0, chunks, compact, 0)

    def rank(c, unused):
        def below(k, total):
            lower = key_column[pl.ds(pl.multiple_of(k * BS, BS), BS), :] < key_row[pl.ds(c, 1), :]
            return total + jnp.where(lower, 1.0, 0.0)

        total = lax.fori_loop(0, chunks, below, jnp.zeros((BS, BS), F32))
        place[pl.ds(c, 1), :] = jnp.sum(total, axis=0, keepdims=True)
        return unused

    lax.fori_loop(0, chunks, rank, 0)

    def arrange(c, unused):
        slot = (sub + c * BS).astype(F32)

        def line(r, total):
            hit = place[pl.ds(r, 1), :] == slot
            return total + jnp.where(hit, entry_row[pl.ds(r, 1), :], 0.0)

        total = lax.fori_loop(0, chunks, line, jnp.zeros((BS, BS), F32))
        out_ref[pl.ds(c, 1), :] = jnp.sum(total.T, axis=0, keepdims=True).astype(jnp.int32)
        return unused

    lax.fori_loop(0, chunks, arrange, 0)


def entry_of(list_ref, k):
    entry = list_ref[k]
    return jnp.bitwise_and(entry, 255), lax.shift_right_logical(entry, 8)


def squared_of(features, other_features):
    return jnp.dot(features, other_features, preferred_element_type=F32)


def taper_of(squared):
    squared = jnp.maximum(squared, 1e-20)
    remain = jnp.maximum(4.0 - jnp.exp(0.5 * jnp.log(squared)), 0.0)
    twice = remain * remain
    return twice * twice * (5.0 - remain)


def kept_groups(sz, count, at):
    first = at * (sz.kept // UNROLL)
    last = jnp.minimum(lax.div(count + (UNROLL - 1), UNROLL), first + sz.kept // UNROLL)
    return first, jnp.maximum(first, last)


def generate(sz, list_ref, count, lhs_ref, rhs_ref, tile_refs, squares):
    top = jnp.maximum(lax.div(count + (UNROLL - 1), UNROLL) - 1, 0)

    def squared(g, u):
        i, j = entry_of(list_ref, jnp.minimum(g, top) * UNROLL + u)
        return squared_of(
            lhs_ref[pl.ds(pl.multiple_of(i * BS, BS), BS), :DEPTH],
            rhs_ref[pl.ds(pl.multiple_of(j * DEPTH, DEPTH), DEPTH), :],
        )

    for u in range(UNROLL):
        squares[u * BS : (u + 1) * BS, :] = squared(0, u)
    for at, tile_ref in enumerate(tile_refs):

        def group(g, unused, at=at, tile_ref=tile_ref):
            for u in range(UNROLL):
                here = slice(u * BS, (u + 1) * BS)
                tile = taper_of(squares[here, :])
                squares[here, :] = squared(g + 1, u)
                start = pl.multiple_of((g * UNROLL + u - at * sz.kept) * BS, BS)
                tile_ref[pl.ds(start, BS), :] = tile
            return unused

        lax.fori_loop(*kept_groups(sz, count, at), group, 0)


def sweep(sz, list_ref, count, tile_refs, vec_ref, acc, acc_ones, remake):
    accs = [acc] if acc_ones is None else [acc, acc_ones]
    for ref in accs:
        ref[...] = jnp.zeros_like(ref)
    carry = (jnp.int32(-1),) + tuple(jnp.zeros((BS, BS), F32) for unused in accs)
    for at, tile_ref in enumerate(tile_refs):

        def group(g, carry, at=at, tile_ref=tile_ref):
            before, *sums = carry
            for u in range(UNROLL):
                i, j = entry_of(list_ref, g * UNROLL + u)
                keep = jnp.where(i == before, 1.0, 0.0)
                start = pl.multiple_of((g * UNROLL + u - at * sz.kept) * BS, BS)
                tile = tile_ref[pl.ds(start, BS), :]
                terms = [tile * vec_ref[pl.ds(j, 1), :], tile]
                sums = [total * keep + term for total, term in zip(sums, terms)]
                for ref, total in zip(accs, sums):
                    ref[pl.ds(pl.multiple_of(i * BS, BS), BS), :] = total
                before = i
            return (before, *sums)

        carry = lax.fori_loop(*kept_groups(sz, count, at), group, carry)

    def extra(k, unused):
        i, j = entry_of(list_ref, k)
        tile = taper_of(squared_of(*remake(i, j)))
        rows = pl.ds(pl.multiple_of(i * BS, BS), BS)
        acc[rows, :] += tile * vec_ref[pl.ds(j, 1), :]
        if acc_ones is not None:
            acc_ones[rows, :] += tile
        return unused

    kept = sz.kept * len(tile_refs)
    lax.fori_loop(kept, jnp.maximum(count, kept), extra, 0)


def finish(sz, acc, out_ref):
    unit = jnp.ones((8, BS), BF16)
    across = (((1,), (1,)), ((), ()))
    for i in range(sz.own):
        whole = acc[i * BS : (i + 1) * BS, :]
        high = whole.astype(BF16)
        low = (whole - high.astype(F32)).astype(BF16)
        y = lax.dot_general(unit, high, across, preferred_element_type=F32)
        y = y + lax.dot_general(unit, low, across, preferred_element_type=F32)
        out_ref[i : i + 1, :] = y[0:1, :] * sz.scale


def total_of(x):
    return jnp.sum(jnp.sum(x, axis=0, keepdims=True), axis=1, keepdims=True)


def place_block(piece_ref, part, first, rhs_ref):
    def one(k, unused):
        h, m, l = features_of(*(block_row(piece_ref, c, part, k) for c in range(3)), (-2.0, 4, 3))
        feats = jnp.concatenate([h, m, h, m, l, h], axis=0).astype(BF16)
        rhs_ref[pl.ds(pl.multiple_of((first + k) * DEPTH, DEPTH), DEPTH), :] = feats
        return unused

    lax.fori_loop(0, part, one, 0, unroll=4)


def first_kernel(sz, *refs):
    list_ref, count_ref, lhs_ref, nugget_any, obs_any, home_ref = refs[:6]
    coord_refs = refs[6 : 6 + (sz.blks - 1) * sz.reps]
    refs = refs[6 + (sz.blks - 1) * sz.reps :]
    tile_refs = refs[:ARRAYS]
    spare_ref, obs_ref, diag_ref, mapped_ref, norm_ref = refs[ARRAYS : ARRAYS + 5]
    rhs_ref, acc, acc_ones, total_row, squares, nugget_ref, done, fetched = refs[ARRAYS + 5 :]
    blk, rep = lax.axis_index("blk"), lax.axis_index("rep")
    home = pl.ds(pl.multiple_of(blk * sz.local_blocks, 8), sz.local_blocks)
    fetch = pltpu.make_async_copy(nugget_any, nugget_ref, fetched.at[0])
    fetch_obs = pltpu.make_async_copy(obs_any, obs_ref.at[home, :], fetched.at[1])
    fetch.start()
    fetch_obs.start()
    for at, piece_ref in enumerate(coord_refs):
        code, turn = at // sz.reps + 1, at % sz.reps
        part = sz.local_blocks // sz.reps
        first = jnp.bitwise_xor(blk, code) * sz.local_blocks + jnp.bitwise_xor(rep, turn) * part
        first = pl.multiple_of(first, 8)
        place_block(piece_ref, part, first, rhs_ref)
        obs_ref[pl.ds(first, part), :] = piece_ref[3 * part : 4 * part, :]
    place_block(home_ref, sz.local_blocks, blk * sz.local_blocks, rhs_ref)
    count = count_ref[0]
    generate(sz, list_ref, count, lhs_ref, rhs_ref, tile_refs, squares)

    def remake(i, j):
        features = lhs_ref[pl.ds(pl.multiple_of(i * BS, BS), BS), :DEPTH]
        return features, rhs_ref[pl.ds(pl.multiple_of(j * DEPTH, DEPTH), DEPTH), :]

    fetch_obs.wait()
    sweep(sz, list_ref, count, tile_refs, obs_ref, acc, acc_ones, remake)

    @pl.when(count > sz.kept * ARRAYS)
    def save():
        copy = pltpu.make_async_copy(rhs_ref, spare_ref, done)
        copy.start()
        copy.wait()

    finish(sz, acc_ones, total_row)
    finish(sz, acc, mapped_ref)
    quarter = lax.axis_index("col") * sz.reps + rep
    own = pl.ds(pl.multiple_of(sz.me() * sz.own, 8), sz.own)
    fetch.wait()
    diag = nugget_ref[pl.ds(pl.multiple_of(quarter * sz.own, 8), sz.own), :] + total_row[...]
    diag_ref[...] = diag
    mapped_ref[...] += diag * obs_ref[own, :]
    norm_ref[...] = jnp.broadcast_to(total_of(obs_ref[...] * obs_ref[...]), (8, BS))


def step_kernel(sz, last, *refs):
    list_ref, count_ref, lhs_ref, spare_ref, diag_ref, norm_ref, field_ref, resid_ref, dirn_ref = refs[:9]
    pieces = refs[9 : 9 + sz.plane]
    tile_refs = refs[9 + sz.plane : 9 + sz.plane + ARRAYS]
    rest = refs[9 + sz.plane + ARRAYS :]
    mapped_ref, next_norm_ref, next_field_ref, next_resid_ref, next_dirn_ref = rest[:5]
    if last:
        dot_ref, dirn = rest[5:7]
    else:
        dirn = next_dirn_ref
    mapped, acc, features, others, done = rest[-5:]
    me = sz.me()
    assemble(sz, pieces, sz.own, mapped)
    norm = norm_ref[0:1, 0:1]
    step = norm / total_of(dirn_ref[...] * mapped[...])
    resid = resid_ref[...] - step * mapped[...]
    next_norm = total_of(resid * resid)
    dirn[...] = resid + (next_norm / norm) * dirn_ref[...]
    next_norm_ref[...] = jnp.broadcast_to(next_norm, (8, BS))
    home = pl.ds(pl.multiple_of(lax.axis_index("blk") * sz.local_blocks, 8), sz.local_blocks)
    own = pl.ds(pl.multiple_of(me * sz.own, 8), sz.own)
    field = step * dirn_ref[home, :]
    if last:
        next_field_ref[...] = field_ref[...] + field
        next_resid_ref[...] = resid_ref[home, :] - step * mapped[home, :]
        next_dirn_ref[...] = dirn[home, :]
    else:
        next_field_ref[...] = field
        next_resid_ref[...] = resid

    def remake(i, j):
        for source, start, size, target in ((lhs_ref, i, BS, features), (spare_ref, j, DEPTH, others)):
            copy = pltpu.make_async_copy(source.at[pl.ds(pl.multiple_of(start * size, size), size), :], target, done)
            copy.start()
            copy.wait()
        return features[:, :DEPTH], others[...]

    sweep(sz, list_ref, count_ref[0], tile_refs, dirn, acc, None, remake)
    finish(sz, acc, mapped_ref)
    ours = mapped_ref[...] + diag_ref[...] * dirn[own, :]
    mapped_ref[...] = ours
    if last:
        dot_ref[...] = jnp.broadcast_to(total_of(ours * dirn[own, :]), dot_ref.shape)


def last_kernel(sz, *refs):
    norm_ref, field_ref, resid_ref, dirn_ref = refs[:4]
    pieces = refs[4 : 4 + sz.plane]
    out_field_ref, out_resid_ref = refs[4 + sz.plane :]
    product = jnp.zeros((8, BS), F32)
    for ref in pieces:
        for z in range(sz.blks):
            product = product + ref[sz.own + 8 * z : sz.own + 8 * (z + 1), :]
    step = norm_ref[0:1, :] / product[0:1, :]
    out_field_ref[...] = field_ref[...] + step * dirn_ref[...]
    quarter = lax.axis_index("col") * sz.reps + lax.axis_index("rep")
    for k, ref in enumerate(pieces):
        rows = pl.ds(pl.multiple_of(jnp.bitwise_xor(quarter, k) * sz.own, 8), sz.own)
        out_resid_ref[rows, :] = resid_ref[rows, :] - step * ref[: sz.own, :]


def call(kernel, mib, in_specs, shapes, out_specs, scratch, flops, *args):
    return pl.pallas_call(
        kernel,
        in_specs=in_specs,
        out_shape=shapes,
        out_specs=out_specs,
        scratch_shapes=scratch,
        compiler_params=pltpu.CompilerParams(vmem_limit_bytes=mib * MIB),
        cost_estimate=pl.CostEstimate(flops=flops, bytes_accessed=1 << 20, transcendentals=0),
    )(*args)


def array(*shape, dtype=F32):
    return jax.ShapeDtypeStruct(shape, dtype)


def local(coords, observations, nugget, tile_pairs, tile_live):
    sz = Sizes(observations.shape[0], tile_pairs.shape[1])
    own, blocks, home = sz.own, sz.blocks, sz.local_blocks
    alive = jnp.arange(sz.slots, dtype=jnp.int32) < tile_live[0]
    pairs = jnp.where(alive, tile_pairs, -1).reshape(2 * sz.slots // BS, BS)
    rep = lax.axis_index("rep")
    part = home // sz.reps
    obs_rows = observations.reshape(home, BS)
    rows = coords.reshape(3, home, BS)
    half = lax.dynamic_slice_in_dim(jnp.concatenate([rows, obs_rows[None]], axis=0), rep * part, part, axis=1)
    half = half.reshape(4 * part, BS)
    nears = [swap(half, "blk", z) for z in range(1, sz.blks)]
    pair_arrays = over_plane(along_blk(pairs))

    lhs = call(
        functools.partial(lhs_kernel, sz),
        12,
        [VMEM],
        array((own + 1) * BS, BS, dtype=BF16),
        VMEM,
        [],
        10_000_000,
        rows,
    )
    lines = 2 * sz.slots // BS * sz.devs
    table, count = call(
        functools.partial(list_kernel, sz),
        12,
        [VMEM] * sz.plane,
        (array(sz.capacity // BS, BS, dtype=jnp.int32), array(1, dtype=jnp.int32)),
        (VMEM, SMEM),
        [pltpu.VMEM((lines, BS), jnp.int32)] * 2
        + [pltpu.VMEM((lines, BS), F32)] * 2
        + [pltpu.VMEM((sz.capacity, BS), F32)]
        + [pltpu.VMEM((sz.capacity // BS, BS), F32)] * 2,
        10_000_000,
        *pair_arrays,
    )
    table, lhs, *nears = lax.optimization_barrier((table.reshape(sz.capacity), lhs, *nears))
    coord_arrays = []
    for near in nears:
        coord_arrays += [near] + [swap(near, "rep", r) for r in range(1, sz.reps)]
    tall = pltpu.VMEM(((own + 1) * BS, BS), F32)
    kept = [pltpu.VMEM((sz.kept * BS, BS), F32)] * ARRAYS
    *tiles, spare, obs, diag, mapped, norm = call(
        functools.partial(first_kernel, sz),
        sz.first_mib,
        [SMEM, SMEM, VMEM, ANY, ANY] + [VMEM] * (1 + len(coord_arrays)),
        kept
        + [
            pltpu.HBM((blocks * DEPTH, BS), BF16),
            array(blocks, BS),
            array(own, BS),
            array(own, BS),
            array(8, BS),
        ],
        [VMEM] * ARRAYS + [ANY] + [VMEM] * 4,
        [
            pltpu.VMEM((blocks * DEPTH, BS), BF16),
            tall,
            tall,
            pltpu.VMEM((own, BS), F32),
            pltpu.VMEM((UNROLL * BS, BS), F32),
            pltpu.VMEM((home, BS), F32),
            pltpu.SemaphoreType.DMA,
            pltpu.SemaphoreType.DMA((2,)),
        ],
        100_000_000,
        table,
        count,
        lhs,
        pltpu.with_memory_space_constraint(nugget.reshape(home, BS), pltpu.HBM),
        pltpu.with_memory_space_constraint(obs_rows, pltpu.HBM),
        rows,
        *coord_arrays,
    )
    tiles = [pltpu.with_memory_space_constraint(tile, pltpu.VMEM) for tile in tiles]
    spare = pltpu.with_memory_space_constraint(spare, pltpu.HBM)
    field, resid, dirn = norm, obs, obs
    for sweep_index in range(1, ITERS):
        last = sweep_index + 1 == ITERS
        span = home if last else blocks
        outs = [array(own, BS), array(8, BS), array(home, BS), array(span, BS), array(span, BS)]
        mapped, norm, field, resid, dirn, *dot = call(
            functools.partial(step_kernel, sz, last),
            5,
            [SMEM, SMEM, ANY, ANY] + [VMEM] * (5 + sz.plane + ARRAYS),
            outs + [array(8, BS)] * last,
            [VMEM] * (len(outs) + last),
            [pltpu.VMEM((blocks, BS), F32)] * (1 + last)
            + [tall, pltpu.VMEM((BS, BS), BF16), pltpu.VMEM((DEPTH, BS), BF16), pltpu.SemaphoreType.DMA],
            100_000_000,
            table,
            count,
            lhs,
            spare,
            diag,
            norm,
            field,
            resid,
            dirn,
            *over_plane(along_blk(mapped)),
            *tiles,
        )
    ends = over_plane(jnp.concatenate([mapped, along_blk(dot[0])], axis=0))
    field, resid = call(
        functools.partial(last_kernel, sz),
        4,
        [VMEM] * (4 + sz.plane),
        (array(home, BS), array(home, BS)),
        (VMEM, VMEM),
        [],
        100_000,
        norm,
        field,
        resid,
        dirn,
        *ends,
    )
    return field.reshape(sz.points), resid.reshape(sz.points)


def solution(mesh):
    in_specs = (
        P(None, ("grp", "blk")),
        P(("grp", "blk")),
        P(("grp", "blk")),
        P(None, ("grp", "blk", "col", "rep")),
        P(("grp", "blk", "col", "rep")),
    )
    out_specs = (P(("grp", "blk")), P(("grp", "blk")))
    return jax.shard_map(local, mesh=mesh, in_specs=in_specs, out_specs=out_specs, check_vma=False)
```

```python
import functools

import jax
import jax.numpy as jnp
from jax import lax
from jax.experimental import pallas as pl
from jax.experimental.pallas import tpu as pltpu
from jax.sharding import PartitionSpec as P

BS = 128
ITERS = 3
SUPPORT = 0.3
DEPTH = 32
UNROLL = 4
ARRAYS = 4
MIB = 1024 * 1024
VMEM = pl.BlockSpec(memory_space=pltpu.VMEM)
SMEM = pl.BlockSpec(memory_space=pltpu.SMEM)
ANY = pl.BlockSpec(memory_space=pl.ANY)
BF16 = jnp.bfloat16
F32 = jnp.float32


class Sizes:
    def __init__(self, points, slots):
        self.blks = lax.axis_size("blk")
        self.reps = lax.axis_size("rep")
        self.plane = lax.axis_size("col") * self.reps
        self.devs = self.blks * self.plane
        self.points = points
        self.slots = slots
        self.local_blocks = points // BS
        self.blocks = self.local_blocks * self.blks
        self.own = self.local_blocks // self.plane
        self.capacity = 2 * self.plane * slots + 1024
        per_row = slots * self.devs // self.blocks
        self.first_mib = 6 + self.blocks * DEPTH * BS * 4 // MIB
        self.kept = min(448, (48 - self.first_mib) * 16) // ARRAYS
        self.scale = 16.0 / (BS * per_row) / 256.0

    def me(self):
        return (lax.axis_index("blk") * lax.axis_size("col") + lax.axis_index("col")) * self.reps + lax.axis_index(
            "rep"
        )


def swap(x, axis, code):
    return lax.ppermute(x, axis, [(i, i ^ code) for i in range(lax.axis_size(axis))])


def along_blk(x):
    return jnp.concatenate([x] + [swap(x, "blk", k) for k in range(1, lax.axis_size("blk"))], axis=0)


def over_plane(x):
    reps = lax.axis_size("rep")
    found = {0: x}
    for c in range(1, lax.axis_size("col")):
        found[c * reps] = swap(x, "col", c)
    for start in sorted(found):
        for r in range(1, reps):
            found[start + r] = swap(found[start], "rep", r)
    return [found[k] for k in sorted(found)]


def assemble(sz, refs, rows, target):
    me = sz.me()
    for k, ref in enumerate(refs):
        for z in range(ref.shape[0] // rows):
            start = pl.multiple_of(jnp.bitwise_xor(me, z * sz.plane + k) * rows, 8)
            target[pl.ds(start, rows), :] = ref[z * rows : (z + 1) * rows, :]


def split3(x):
    high = x.astype(BF16).astype(F32)
    rest = x - high
    middle = rest.astype(BF16).astype(F32)
    return high, middle, rest - middle


def store_features(target, block, x, y, z, own):
    places = [(row - 0.5) * (4.0 / SUPPORT) for row in (x, y, z)]
    norm = split3(sum(row * row for row in places))
    high, middle, low = zip(*(split3(row if own else -2.0 * row) for row in places))
    unit = [jnp.ones((8, BS), F32)] * 3
    if own:
        rows = [*high, *high, *middle, *middle, *high, *low, *middle, *low, *unit, *norm]
    else:
        rows = [*high, *middle, *high, *middle, *low, *high, *low, *middle, *norm, *unit]
    for at, row in enumerate(rows + [jnp.zeros((8, BS), F32)] * (DEPTH - len(rows))):
        target[pl.ds(block * DEPTH + at, 8, stride=DEPTH), :] = row


def eight_rows(ref, c, part, k):
    if len(ref.shape) == 3:
        return ref[c, pl.ds(pl.multiple_of(k, 8), 8), :]
    return ref[pl.ds(pl.multiple_of(c * part + k, 8), 8), :]


def lhs_kernel(sz, home_ref, out_ref, feats):
    quarter = lax.axis_index("col") * sz.reps + lax.axis_index("rep")
    for i in range(0, sz.own, 8):
        store_features(feats, i, *(eight_rows(home_ref, c, None, quarter * sz.own + i) for c in range(3)), True)
    for i in range(sz.own):
        wide = jnp.concatenate([feats[i * DEPTH : (i + 1) * DEPTH, :], jnp.zeros((BS - DEPTH, BS), F32)], axis=0)
        out_ref[i * BS : (i + 1) * BS, :] = wide.T.astype(BF16)
    out_ref[sz.own * BS :, :] = jnp.zeros((BS, BS), BF16)


def list_kernel(sz, *refs):
    me = sz.me()
    out_ref, count_ref, target, other, place, value, key_column, key_row, entry_row = refs[sz.plane :]
    lines = sz.slots // BS
    at = 2 * lines * sz.devs
    for base in range(0, at, 2 * lines):
        pairs_ref = refs[base // (2 * lines * sz.blks)]
        start = base % (2 * lines * sz.blks)
        rows = pairs_ref[start : start + lines, :]
        cols = pairs_ref[start + lines : start + 2 * lines, :]
        target[base : base + lines, :] = rows
        other[base : base + lines, :] = cols
        target[base + lines : base + 2 * lines, :] = cols
        other[base + lines : base + 2 * lines, :] = rows
    local = target[...] - me * sz.own
    mine = jnp.logical_and(local >= 0, local < sz.own)
    flags = jnp.where(mine, 1.0, 0.0)
    a = lax.broadcasted_iota(jnp.int32, (BS, BS), 0)
    b = lax.broadcasted_iota(jnp.int32, (BS, BS), 1)
    ahead = jnp.where(a < b, 1.0, 0.0).astype(BF16)
    before = jnp.dot(flags.astype(BF16), ahead, preferred_element_type=F32)
    totals = jnp.broadcast_to(jnp.sum(flags, axis=1, keepdims=True), (at, BS))
    a = lax.broadcasted_iota(jnp.int32, (at, at), 0)
    b = lax.broadcasted_iota(jnp.int32, (at, at), 1)
    above = jnp.dot(jnp.where(b < a, 1.0, 0.0).astype(BF16), totals.astype(BF16), preferred_element_type=F32)
    place[...] = jnp.where(mine, above + before, -1.0)
    value[...] = (local + 256 * other[...]).astype(F32)
    count = jnp.sum(flags).astype(jnp.int32)
    sub = lax.broadcasted_iota(jnp.int32, (BS, BS), 0)
    lane = lax.broadcasted_iota(jnp.int32, (1, BS), 1)

    chunks = jnp.maximum(lax.shift_right_logical(count + BS - 1, 7), 1)

    def key_of(found, slot):
        entry = jnp.where(slot < count, found.astype(jnp.int32), sz.own)
        return entry.astype(F32), (jnp.bitwise_and(entry, 255) * 65536 + slot).astype(F32)

    def compact(c, unused):
        slot = (sub + c * BS).astype(F32)

        def line(r, total):
            hit = place[pl.ds(r, 1), :] == slot
            return total + jnp.where(hit, value[pl.ds(r, 1), :], 0.0)

        total = lax.fori_loop(0, at, line, jnp.zeros((BS, BS), F32), unroll=4)
        entry, key = key_of(jnp.sum(total.T, axis=0, keepdims=True), lane + c * BS)
        entry_row[pl.ds(c, 1), :] = entry
        key_row[pl.ds(c, 1), :] = key
        unused_entry, key = key_of(jnp.sum(total, axis=1, keepdims=True), sub[:, 0:1] + c * BS)
        key_column[pl.ds(pl.multiple_of(c * BS, BS), BS), :] = jnp.broadcast_to(key, (BS, BS))
        return unused

    lax.fori_loop(0, chunks, compact, 0)

    bound = lane.astype(F32) * 65536.0

    def tally(c, carry):
        keys = key_column[pl.ds(pl.multiple_of(c * BS, BS), BS), :]
        from_here, after = carry
        return from_here + jnp.where(keys >= bound, 1.0, 0.0), after + jnp.where(keys >= bound + 65536.0, 1.0, 0.0)

    zero = jnp.zeros((BS, BS), F32)
    from_here, after = lax.fori_loop(0, chunks, tally, (zero, zero))
    from_here = jnp.sum(from_here, axis=0, keepdims=True)
    each = from_here - jnp.sum(after, axis=0, keepdims=True)
    odd = jnp.where(lane < sz.own, each - 2.0 * jnp.floor(0.5 * each), 0.0)
    wide_odd = jnp.broadcast_to(odd, (BS, BS))
    odd_column = wide_odd.T
    odd_before = jnp.dot(wide_odd.astype(BF16), ahead, preferred_element_type=F32)[0:1, :]
    start = (chunks * BS).astype(F32) - from_here + odd_before
    null_place = jnp.where(odd > 0.0, start + each, -1.0)
    null_entry = (lane + 256 * sz.blocks).astype(F32)
    full = count + jnp.sum(odd).astype(jnp.int32)
    count_ref[0] = full

    def rank(c, unused):
        keys = key_row[pl.ds(c, 1), :]

        def below(k, total):
            lower = key_column[pl.ds(pl.multiple_of(k * BS, BS), BS), :] < keys
            return total + jnp.where(lower, 1.0, 0.0)

        past = (sub + 1).astype(F32) * 65536.0 <= keys
        total = lax.fori_loop(0, chunks, below, jnp.where(past, odd_column, 0.0))
        place[pl.ds(c, 1), :] = jnp.sum(total, axis=0, keepdims=True)
        return unused

    lax.fori_loop(0, chunks, rank, 0)

    def arrange(c, unused):
        slot = (sub + c * BS).astype(F32)

        def line(r, total):
            hit = place[pl.ds(r, 1), :] == slot
            return total + jnp.where(hit, entry_row[pl.ds(r, 1), :], 0.0)

        total = lax.fori_loop(0, chunks, line, jnp.where(null_place == slot, null_entry, 0.0))
        found = jnp.sum(total.T, axis=0, keepdims=True).astype(jnp.int32)
        out_ref[pl.ds(c, 1), :] = jnp.where(lane + c * BS < full, found, sz.own)
        return unused

    lax.fori_loop(0, jnp.maximum(lax.shift_right_logical(full + BS - 1, 7), 1), arrange, 0)


def entry_of(list_ref, k):
    entry = list_ref[k]
    return jnp.bitwise_and(entry, 255), lax.shift_right_logical(entry, 8)


def squared_of(features, *others):
    return jnp.dot(features, jnp.concatenate(others, axis=1).astype(BF16), preferred_element_type=F32)


def taper_of(squared):
    squared = jnp.maximum(squared, 1e-20)
    remain = jnp.maximum(4.0 - jnp.exp(0.5 * jnp.log(squared)), 0.0)
    twice = remain * remain
    return twice * twice * (5.0 - remain)


def kept_groups(sz, count, at):
    first = at * (sz.kept // UNROLL)
    last = jnp.minimum(lax.div(count + (UNROLL - 1), UNROLL), first + sz.kept // UNROLL)
    return first, jnp.maximum(first, last)


def vector_row(vec_ref, j):
    return vec_ref[pl.ds(jnp.minimum(j, vec_ref.shape[0] - 1), 1), :]


def own_features(lhs_ref, i):
    return lhs_ref[pl.ds(pl.multiple_of(i * BS, BS), BS), :DEPTH]


def other_features(rhs_ref, j):
    return rhs_ref[pl.ds(pl.multiple_of(j * DEPTH, DEPTH), DEPTH), :]


def clear(*accs):
    for acc in accs:
        acc[...] = jnp.zeros_like(acc)


def generate(sz, list_ref, count, lhs_ref, rhs_ref, tile_refs, vec_ref, acc, acc_ones, squares):
    clear(acc, acc_ones)
    top = jnp.maximum(lax.div(count + (UNROLL - 1), UNROLL) - 1, 0)

    def fill(g, u):
        k = jnp.minimum(g, top) * UNROLL + u
        i, j = entry_of(list_ref, k)
        unused, twin = entry_of(list_ref, k + 1)
        squared = squared_of(own_features(lhs_ref, i), other_features(rhs_ref, j), other_features(rhs_ref, twin))
        squares[u * BS : (u + 1) * BS, :] = squared[:, :BS]
        squares[(u + 1) * BS : (u + 2) * BS, :] = squared[:, BS:]

    for u in range(0, UNROLL, 2):
        fill(0, u)
    carry = (jnp.int32(-1), jnp.zeros((BS, BS), F32), jnp.zeros((BS, BS), F32))
    for at, tile_ref in enumerate(tile_refs):

        def group(g, carry, at=at, tile_ref=tile_ref):
            before, total, total_ones = carry
            for u in range(0, UNROLL, 2):
                i, j = entry_of(list_ref, g * UNROLL + u)
                unused, twin = entry_of(list_ref, g * UNROLL + u + 1)
                keep = jnp.where(i == before, 1.0, 0.0)
                tile = taper_of(squares[u * BS : (u + 1) * BS, :])
                twin_tile = taper_of(squares[(u + 1) * BS : (u + 2) * BS, :])
                fill(g + 1, u)
                start = (g * UNROLL + u - at * sz.kept) * BS
                tile_ref[pl.ds(pl.multiple_of(start, BS), BS), :] = tile
                tile_ref[pl.ds(pl.multiple_of(start + BS, BS), BS), :] = twin_tile
                total_ones = total_ones * keep + (tile + twin_tile)
                total = total * keep + (tile * vector_row(vec_ref, j) + twin_tile * vector_row(vec_ref, twin))
                rows = pl.ds(pl.multiple_of(i * BS, BS), BS)
                acc_ones[rows, :] = total_ones
                acc[rows, :] = total
                before = i
            return before, total, total_ones

        carry = lax.fori_loop(*kept_groups(sz, count, at), group, carry)


def sweep(sz, list_ref, count, tile_refs, vec_ref, acc):
    clear(acc)
    carry = (jnp.int32(-1), jnp.zeros((BS, BS), F32))
    for at, tile_ref in enumerate(tile_refs):

        def group(g, carry, at=at, tile_ref=tile_ref):
            before, total = carry
            for u in range(0, UNROLL, 2):
                i, j = entry_of(list_ref, g * UNROLL + u)
                unused, twin = entry_of(list_ref, g * UNROLL + u + 1)
                keep = jnp.where(i == before, 1.0, 0.0)
                start = (g * UNROLL + u - at * sz.kept) * BS
                tile = tile_ref[pl.ds(pl.multiple_of(start, BS), BS), :]
                twin_tile = tile_ref[pl.ds(pl.multiple_of(start + BS, BS), BS), :]
                total = total * keep + (tile * vector_row(vec_ref, j) + twin_tile * vector_row(vec_ref, twin))
                acc[pl.ds(pl.multiple_of(i * BS, BS), BS), :] = total
                before = i
            return before, total

        carry = lax.fori_loop(*kept_groups(sz, count, at), group, carry)


def extras(sz, list_ref, count, vec_ref, acc, acc_ones, remake):
    def extra(k, unused):
        i, j = entry_of(list_ref, k)
        tile = taper_of(squared_of(*remake(i, j)))
        rows = pl.ds(pl.multiple_of(i * BS, BS), BS)
        acc[rows, :] += tile * vector_row(vec_ref, j)
        if acc_ones is not None:
            acc_ones[rows, :] += tile
        return unused

    kept = sz.kept * ARRAYS
    lax.fori_loop(kept, jnp.maximum(count, kept), extra, 0)


def finish(sz, acc, out_ref):
    unit = jnp.ones((8, BS), BF16)
    across = (((1,), (1,)), ((), ()))
    for i in range(sz.own):
        whole = acc[i * BS : (i + 1) * BS, :]
        high = whole.astype(BF16)
        low = (whole - high.astype(F32)).astype(BF16)
        y = lax.dot_general(unit, high, across, preferred_element_type=F32)
        y = y + lax.dot_general(unit, low, across, preferred_element_type=F32)
        out_ref[i : i + 1, :] = y[0:1, :] * sz.scale


def total_of(x):
    return jnp.sum(jnp.sum(x, axis=0, keepdims=True), axis=1, keepdims=True)


def place_block(piece_ref, part, first, rhs_ref):
    def eight(k, unused):
        store_features(rhs_ref, first + 8 * k, *(eight_rows(piece_ref, c, part, 8 * k) for c in range(3)), False)
        return unused

    lax.fori_loop(0, part // 8, eight, 0)


def first_kernel(sz, *refs):
    list_ref, count_ref, lhs_ref, nugget_any, obs_any, home_ref = refs[:6]
    coord_refs = refs[6 : 6 + (sz.blks - 1) * sz.reps]
    refs = refs[6 + (sz.blks - 1) * sz.reps :]
    tile_refs = refs[:ARRAYS]
    spare_ref, obs_ref, diag_ref, mapped_ref, norm_ref = refs[ARRAYS : ARRAYS + 5]
    rhs_ref, acc, acc_ones, total_row, squares, nugget_ref, done, fetched = refs[ARRAYS + 5 :]
    blk, rep = lax.axis_index("blk"), lax.axis_index("rep")
    home = pl.ds(pl.multiple_of(blk * sz.local_blocks, 8), sz.local_blocks)
    fetch = pltpu.make_async_copy(nugget_any, nugget_ref, fetched.at[0])
    fetch_obs = pltpu.make_async_copy(obs_any, obs_ref.at[home, :], fetched.at[1])
    fetch.start()
    fetch_obs.start()
    for at, piece_ref in enumerate(coord_refs):
        code, turn = at // sz.reps + 1, at % sz.reps
        part = sz.local_blocks // sz.reps
        first = jnp.bitwise_xor(blk, code) * sz.local_blocks + jnp.bitwise_xor(rep, turn) * part
        first = pl.multiple_of(first, 8)
        place_block(piece_ref, part, first, rhs_ref)
        obs_ref[pl.ds(first, part), :] = piece_ref[3 * part : 4 * part, :]
    place_block(home_ref, sz.local_blocks, blk * sz.local_blocks, rhs_ref)
    far = lax.broadcasted_iota(jnp.int32, (DEPTH, BS), 0) == 24
    rhs_ref[sz.blocks * DEPTH :, :] = jnp.where(far, 1e6, 0.0)
    count = count_ref[0]
    fetch_obs.wait()
    generate(sz, list_ref, count, lhs_ref, rhs_ref, tile_refs, obs_ref, acc, acc_ones, squares)
    extras(
        sz,
        list_ref,
        count,
        obs_ref,
        acc,
        acc_ones,
        lambda i, j: (own_features(lhs_ref, i), other_features(rhs_ref, j)),
    )

    @pl.when(count > sz.kept * ARRAYS)
    def save():
        copy = pltpu.make_async_copy(rhs_ref, spare_ref, done)
        copy.start()
        copy.wait()

    finish(sz, acc_ones, total_row)
    finish(sz, acc, mapped_ref)
    quarter = lax.axis_index("col") * sz.reps + rep
    own = pl.ds(pl.multiple_of(sz.me() * sz.own, 8), sz.own)
    fetch.wait()
    diag = nugget_ref[pl.ds(pl.multiple_of(quarter * sz.own, 8), sz.own), :] + total_row[...]
    diag_ref[...] = diag
    mapped_ref[...] += diag * obs_ref[own, :]
    norm_ref[...] = jnp.broadcast_to(total_of(obs_ref[...] * obs_ref[...]), (8, BS))


def step_kernel(sz, last, *refs):
    list_ref, count_ref, lhs_ref, spare_ref, diag_ref, norm_ref, field_ref, resid_ref, dirn_ref = refs[:9]
    pieces = refs[9 : 9 + sz.plane]
    tile_refs = refs[9 + sz.plane : 9 + sz.plane + ARRAYS]
    rest = refs[9 + sz.plane + ARRAYS :]
    mapped_ref, next_norm_ref, next_field_ref, next_resid_ref, next_dirn_ref = rest[:5]
    if last:
        dot_ref, dirn = rest[5:7]
    else:
        dirn = next_dirn_ref
    mapped, acc, features, others, done = rest[-5:]
    me = sz.me()
    assemble(sz, pieces, sz.own, mapped)
    norm = norm_ref[0:1, 0:1]
    step = norm / total_of(dirn_ref[...] * mapped[...])
    resid = resid_ref[...] - step * mapped[...]
    next_norm = total_of(resid * resid)
    dirn[...] = resid + (next_norm / norm) * dirn_ref[...]
    next_norm_ref[...] = jnp.broadcast_to(next_norm, (8, BS))
    home = pl.ds(pl.multiple_of(lax.axis_index("blk") * sz.local_blocks, 8), sz.local_blocks)
    own = pl.ds(pl.multiple_of(me * sz.own, 8), sz.own)
    field = step * dirn_ref[home, :]
    if last:
        next_field_ref[...] = field_ref[...] + field
        next_resid_ref[...] = resid_ref[home, :] - step * mapped[home, :]
        next_dirn_ref[...] = dirn[home, :]
    else:
        next_field_ref[...] = field
        next_resid_ref[...] = resid

    def remake(i, j):
        for source, start, size, target in ((lhs_ref, i, BS, features), (spare_ref, j, DEPTH, others)):
            copy = pltpu.make_async_copy(source.at[pl.ds(pl.multiple_of(start * size, size), size), :], target, done)
            copy.start()
            copy.wait()
        return features[:, :DEPTH], others[...]

    sweep(sz, list_ref, count_ref[0], tile_refs, dirn, acc)
    extras(sz, list_ref, count_ref[0], dirn, acc, None, remake)
    finish(sz, acc, mapped_ref)
    ours = mapped_ref[...] + diag_ref[...] * dirn[own, :]
    mapped_ref[...] = ours
    if last:
        dot_ref[...] = jnp.broadcast_to(total_of(ours * dirn[own, :]), dot_ref.shape)


def last_kernel(sz, *refs):
    norm_ref, field_ref, resid_ref, dirn_ref = refs[:4]
    pieces = refs[4 : 4 + sz.plane]
    out_field_ref, out_resid_ref = refs[4 + sz.plane :]
    product = jnp.zeros((8, BS), F32)
    for ref in pieces:
        for z in range(sz.blks):
            product = product + ref[sz.own + 8 * z : sz.own + 8 * (z + 1), :]
    step = norm_ref[0:1, :] / product[0:1, :]
    out_field_ref[...] = field_ref[...] + step * dirn_ref[...]
    quarter = lax.axis_index("col") * sz.reps + lax.axis_index("rep")
    for k, ref in enumerate(pieces):
        rows = pl.ds(pl.multiple_of(jnp.bitwise_xor(quarter, k) * sz.own, 8), sz.own)
        out_resid_ref[rows, :] = resid_ref[rows, :] - step * ref[: sz.own, :]


def call(kernel, mib, in_specs, shapes, out_specs, scratch, flops, *args):
    return pl.pallas_call(
        kernel,
        in_specs=in_specs,
        out_shape=shapes,
        out_specs=out_specs,
        scratch_shapes=scratch,
        compiler_params=pltpu.CompilerParams(vmem_limit_bytes=mib * MIB),
        cost_estimate=pl.CostEstimate(flops=flops, bytes_accessed=1 << 20, transcendentals=0),
    )(*args)


def array(*shape, dtype=F32):
    return jax.ShapeDtypeStruct(shape, dtype)


def local(coords, observations, nugget, tile_pairs, tile_live):
    sz = Sizes(observations.shape[0], tile_pairs.shape[1])
    own, blocks, home = sz.own, sz.blocks, sz.local_blocks
    alive = jnp.arange(sz.slots, dtype=jnp.int32) < tile_live[0]
    pairs = jnp.where(alive, tile_pairs, -1).reshape(2 * sz.slots // BS, BS)
    rep = lax.axis_index("rep")
    part = home // sz.reps
    obs_rows = observations.reshape(home, BS)
    rows = coords.reshape(3, home, BS)
    half = lax.dynamic_slice_in_dim(jnp.concatenate([rows, obs_rows[None]], axis=0), rep * part, part, axis=1)
    half = half.reshape(4 * part, BS)
    nears = [swap(half, "blk", z) for z in range(1, sz.blks)]
    pair_arrays = over_plane(along_blk(pairs))

    lhs = call(
        functools.partial(lhs_kernel, sz),
        12,
        [VMEM],
        array((own + 1) * BS, BS, dtype=BF16),
        VMEM,
        [pltpu.VMEM((own * DEPTH, BS), F32)],
        10_000_000,
        rows,
    )
    lines = 2 * sz.slots // BS * sz.devs
    table, count = call(
        functools.partial(list_kernel, sz),
        12,
        [VMEM] * sz.plane,
        (array(sz.capacity // BS, BS, dtype=jnp.int32), array(1, dtype=jnp.int32)),
        (VMEM, SMEM),
        [pltpu.VMEM((lines, BS), jnp.int32)] * 2
        + [pltpu.VMEM((lines, BS), F32)] * 2
        + [pltpu.VMEM((sz.capacity, BS), F32)]
        + [pltpu.VMEM((sz.capacity // BS, BS), F32)] * 2,
        10_000_000,
        *pair_arrays,
    )
    table, lhs, *nears = lax.optimization_barrier((table.reshape(sz.capacity), lhs, *nears))
    coord_arrays = []
    for near in nears:
        coord_arrays += [near] + [swap(near, "rep", r) for r in range(1, sz.reps)]
    tall = pltpu.VMEM(((own + 1) * BS, BS), F32)
    kept = [pltpu.VMEM((sz.kept * BS, BS), F32)] * ARRAYS
    *tiles, spare, obs, diag, mapped, norm = call(
        functools.partial(first_kernel, sz),
        sz.first_mib,
        [SMEM, SMEM, VMEM, ANY, ANY] + [VMEM] * (1 + len(coord_arrays)),
        kept
        + [
            pltpu.HBM(((blocks + 1) * DEPTH, BS), F32),
            array(blocks, BS),
            array(own, BS),
            array(own, BS),
            array(8, BS),
        ],
        [VMEM] * ARRAYS + [ANY] + [VMEM] * 4,
        [
            pltpu.VMEM(((blocks + 1) * DEPTH, BS), F32),
            tall,
            tall,
            pltpu.VMEM((own, BS), F32),
            pltpu.VMEM((UNROLL * BS, BS), F32),
            pltpu.VMEM((home, BS), F32),
            pltpu.SemaphoreType.DMA,
            pltpu.SemaphoreType.DMA((2,)),
        ],
        100_000_000,
        table,
        count,
        lhs,
        pltpu.with_memory_space_constraint(nugget.reshape(home, BS), pltpu.HBM),
        pltpu.with_memory_space_constraint(obs_rows, pltpu.HBM),
        rows,
        *coord_arrays,
    )
    tiles = [pltpu.with_memory_space_constraint(tile, pltpu.VMEM) for tile in tiles]
    spare = pltpu.with_memory_space_constraint(spare, pltpu.HBM)
    field, resid, dirn = norm, obs, obs
    for sweep_index in range(1, ITERS):
        last = sweep_index + 1 == ITERS
        span = home if last else blocks
        outs = [array(own, BS), array(8, BS), array(home, BS), array(span, BS), array(span, BS)]
        mapped, norm, field, resid, dirn, *dot = call(
            functools.partial(step_kernel, sz, last),
            5,
            [SMEM, SMEM, ANY, ANY] + [VMEM] * (5 + sz.plane + ARRAYS),
            outs + [array(8, BS)] * last,
            [VMEM] * (len(outs) + last),
            [pltpu.VMEM((blocks, BS), F32)] * (1 + last)
            + [tall, pltpu.VMEM((BS, BS), BF16), pltpu.VMEM((DEPTH, BS), F32), pltpu.SemaphoreType.DMA],
            100_000_000,
            table,
            count,
            lhs,
            spare,
            diag,
            norm,
            field,
            resid,
            dirn,
            *over_plane(along_blk(mapped)),
            *tiles,
        )
    ends = over_plane(jnp.concatenate([mapped, along_blk(dot[0])], axis=0))
    field, resid = call(
        functools.partial(last_kernel, sz),
        4,
        [VMEM] * (4 + sz.plane),
        (array(home, BS), array(home, BS)),
        (VMEM, VMEM),
        [],
        100_000,
        norm,
        field,
        resid,
        dirn,
        *ends,
    )
    return field.reshape(sz.points), resid.reshape(sz.points)


def solution(mesh):
    in_specs = (
        P(None, ("grp", "blk")),
        P(("grp", "blk")),
        P(("grp", "blk")),
        P(None, ("grp", "blk", "col", "rep")),
        P(("grp", "blk", "col", "rep")),
    )
    out_specs = (P(("grp", "blk")), P(("grp", "blk")))
    return jax.shard_map(local, mesh=mesh, in_specs=in_specs, out_specs=out_specs, check_vma=False)
```

```python
import functools

import jax
import jax.numpy as jnp
from jax import lax
from jax.experimental import pallas as pl
from jax.experimental.pallas import tpu as pltpu
from jax.sharding import PartitionSpec as P

BS = 128
ITERS = 3
SUPPORT = 0.3
HALF_LOG2E = 0.7213475204444817
DEPTH = 48
UNROLL = 4
ARRAYS = 4
MIB = 1024 * 1024
VMEM = pl.BlockSpec(memory_space=pltpu.VMEM)
SMEM = pl.BlockSpec(memory_space=pltpu.SMEM)
ANY = pl.BlockSpec(memory_space=pl.ANY)
BF16 = jnp.bfloat16
F32 = jnp.float32


class Sizes:
    def __init__(self, points, slots):
        self.blks = lax.axis_size("blk")
        self.reps = lax.axis_size("rep")
        self.plane = lax.axis_size("col") * self.reps
        self.devs = self.blks * self.plane
        self.points = points
        self.slots = slots
        self.local_blocks = points // BS
        self.blocks = self.local_blocks * self.blks
        self.own = self.local_blocks // self.plane
        self.capacity = 2 * self.plane * slots + 1024
        per_row = slots * self.devs // self.blocks
        self.first_mib = 6 + self.blocks * DEPTH * BS * 2 // MIB
        self.kept = min(448, (48 - self.first_mib) * 16) // ARRAYS
        self.scale = 16.0 / (BS * per_row) / 256.0

    def me(self):
        return (lax.axis_index("blk") * lax.axis_size("col") + lax.axis_index("col")) * self.reps + lax.axis_index(
            "rep"
        )


def swap(x, axis, code):
    return lax.ppermute(x, axis, [(i, i ^ code) for i in range(lax.axis_size(axis))])


def along_blk(x):
    return jnp.concatenate([x] + [swap(x, "blk", k) for k in range(1, lax.axis_size("blk"))], axis=0)


def over_plane(x):
    reps = lax.axis_size("rep")
    found = {0: x}
    for c in range(1, lax.axis_size("col")):
        found[c * reps] = swap(x, "col", c)
    for start in sorted(found):
        for r in range(1, reps):
            found[start + r] = swap(found[start], "rep", r)
    return [found[k] for k in sorted(found)]


def assemble(sz, refs, rows, target):
    me = sz.me()
    for k, ref in enumerate(refs):
        for z in range(ref.shape[0] // rows):
            start = pl.multiple_of(jnp.bitwise_xor(me, z * sz.plane + k) * rows, 8)
            target[pl.ds(start, rows), :] = ref[z * rows : (z + 1) * rows, :]


def split3(x):
    high = x.astype(BF16).astype(F32)
    rest = x - high
    middle = rest.astype(BF16).astype(F32)
    return high, middle, rest - middle


def features_of(rows, factor, unit, norm):
    feature = lax.broadcasted_iota(jnp.int32, (8, BS), 0)
    x, y, z = ((row - 0.5) * (4.0 / SUPPORT) for row in rows)
    feats = jnp.where(feature == unit, 1.0, 0.0)
    for place, row in ((0, factor * x), (1, factor * y), (2, factor * z), (norm, x * x + y * y + z * z)):
        feats = jnp.where(feature == place, row, feats)
    return split3(feats)


def block_row(ref, c, part, k):
    return ref[c, pl.ds(k, 1), :] if len(ref.shape) == 3 else ref[pl.ds(c * part + k, 1), :]


def lhs_kernel(sz, home_ref, out_ref):
    quarter = lax.axis_index("col") * sz.reps + lax.axis_index("rep")
    for i in range(sz.own):
        h, m, l = features_of([block_row(home_ref, c, None, quarter * sz.own + i) for c in range(3)], 1.0, 3, 4)
        feats = jnp.concatenate([h, h, m, m, h, l, jnp.zeros((BS - DEPTH, BS), F32)], axis=0)
        out_ref[i * BS : (i + 1) * BS, :] = feats.T.astype(BF16)
    out_ref[sz.own * BS :, :] = jnp.zeros((BS, BS), BF16)


def list_kernel(sz, *refs):
    me = sz.me()
    out_ref, count_ref, target, other, place, value, key_column, key_row, entry_row = refs[sz.plane :]
    lines = sz.slots // BS
    at = 2 * lines * sz.devs
    for base in range(0, at, 2 * lines):
        pairs_ref = refs[base // (2 * lines * sz.blks)]
        start = base % (2 * lines * sz.blks)
        rows = pairs_ref[start : start + lines, :]
        cols = pairs_ref[start + lines : start + 2 * lines, :]
        target[base : base + lines, :] = rows
        other[base : base + lines, :] = cols
        target[base + lines : base + 2 * lines, :] = cols
        other[base + lines : base + 2 * lines, :] = rows
    local = target[...] - me * sz.own
    mine = jnp.logical_and(local >= 0, local < sz.own)
    flags = jnp.where(mine, 1.0, 0.0)
    a = lax.broadcasted_iota(jnp.int32, (BS, BS), 0)
    b = lax.broadcasted_iota(jnp.int32, (BS, BS), 1)
    ahead = jnp.where(a < b, 1.0, 0.0).astype(BF16)
    before = jnp.dot(flags.astype(BF16), ahead, preferred_element_type=F32)
    totals = jnp.broadcast_to(jnp.sum(flags, axis=1, keepdims=True), (at, BS))
    a = lax.broadcasted_iota(jnp.int32, (at, at), 0)
    b = lax.broadcasted_iota(jnp.int32, (at, at), 1)
    above = jnp.dot(jnp.where(b < a, 1.0, 0.0).astype(BF16), totals.astype(BF16), preferred_element_type=F32)
    place[...] = jnp.where(mine, above + before, -1.0)
    ends = jnp.sum(jnp.where(lax.broadcasted_iota(jnp.int32, (at, BS), 1) == 0, above + totals, 0.0), axis=1, keepdims=True)
    starts = ends - totals[:, 0:1]
    value[...] = (local + 256 * other[...]).astype(F32)
    count = jnp.sum(flags).astype(jnp.int32)
    sub = lax.broadcasted_iota(jnp.int32, (BS, BS), 0)
    lane = lax.broadcasted_iota(jnp.int32, (1, BS), 1)

    chunks = jnp.maximum(lax.shift_right_logical(count + BS - 1, 7), 1)

    def key_of(found, slot):
        entry = jnp.where(slot < count, found.astype(jnp.int32), sz.own)
        return entry.astype(F32), (jnp.bitwise_and(entry, 255) * 65536 + slot).astype(F32)

    def compact(c, unused):
        slot = (sub + c * BS).astype(F32)
        base = (c * BS).astype(F32)
        first = jnp.sum(jnp.where(ends <= base, 1.0, 0.0)).astype(jnp.int32)
        last = jnp.sum(jnp.where(starts < base + BS, 1.0, 0.0)).astype(jnp.int32)
        first = jnp.minimum(lax.shift_right_logical(first, 2), at // 4)
        last = lax.shift_right_logical(last + 3, 2)

        def lines(g, total):
            for u in range(4):
                r = 4 * g + u
                hit = place[pl.ds(r, 1), :] == slot
                total = jnp.where(hit, value[pl.ds(r, 1), :], total)
            return total

        total = lax.fori_loop(first, last, lines, jnp.zeros((BS, BS), F32))
        entry, key = key_of(jnp.sum(total.T, axis=0, keepdims=True), lane + c * BS)
        entry_row[pl.ds(c, 1), :] = entry
        key_row[pl.ds(c, 1), :] = key
        unused_entry, key = key_of(jnp.sum(total, axis=1, keepdims=True), sub[:, 0:1] + c * BS)
        key_column[pl.ds(pl.multiple_of(c * BS, BS), BS), :] = jnp.broadcast_to(key, (BS, BS))
        return unused

    lax.fori_loop(0, chunks, compact, 0)

    bound = lane.astype(F32) * 65536.0

    def tally(c, carry):
        keys = key_column[pl.ds(pl.multiple_of(c * BS, BS), BS), :]
        from_here, after = carry
        return from_here + jnp.where(keys >= bound, 1.0, 0.0), after + jnp.where(keys >= bound + 65536.0, 1.0, 0.0)

    zero = jnp.zeros((BS, BS), F32)
    from_here, after = lax.fori_loop(0, chunks, tally, (zero, zero))
    from_here = jnp.sum(from_here, axis=0, keepdims=True)
    each = from_here - jnp.sum(after, axis=0, keepdims=True)
    odd = jnp.where(lane < sz.own, each - 2.0 * jnp.floor(0.5 * each), 0.0)
    wide_odd = jnp.broadcast_to(odd, (BS, BS))
    odd_column = wide_odd.T
    odd_before = jnp.dot(wide_odd.astype(BF16), ahead, preferred_element_type=F32)[0:1, :]
    start = (chunks * BS).astype(F32) - from_here + odd_before
    null_place = jnp.where(odd > 0.0, start + each, -1.0)
    null_entry = (lane + 256 * sz.blocks).astype(F32)
    full = count + jnp.sum(odd).astype(jnp.int32)
    count_ref[0] = full

    def rank(c, unused):
        keys = key_row[pl.ds(c, 1), :]

        def below(k, total):
            lower = key_column[pl.ds(pl.multiple_of(k * BS, BS), BS), :] < keys
            return total + jnp.where(lower, 1.0, 0.0)

        past = (sub + 1).astype(F32) * 65536.0 <= keys
        total = lax.fori_loop(0, chunks, below, jnp.where(past, odd_column, 0.0))
        place[pl.ds(c, 1), :] = jnp.sum(total, axis=0, keepdims=True)
        return unused

    lax.fori_loop(0, chunks, rank, 0)

    def arrange(c, unused):
        slot = (sub + c * BS).astype(F32)

        def line(r, total):
            hit = place[pl.ds(r, 1), :] == slot
            return total + jnp.where(hit, entry_row[pl.ds(r, 1), :], 0.0)

        total = lax.fori_loop(0, chunks, line, jnp.where(null_place == slot, null_entry, 0.0))
        found = jnp.sum(total.T, axis=0, keepdims=True).astype(jnp.int32)
        out_ref[pl.ds(c, 1), :] = jnp.where(lane + c * BS < full, found, sz.own)
        return unused

    lax.fori_loop(0, jnp.maximum(lax.shift_right_logical(full + BS - 1, 7), 1), arrange, 0)


def entry_of(list_ref, k):
    entry = list_ref[k]
    return jnp.bitwise_and(entry, 255), lax.shift_right_logical(entry, 8)


def squared_of(features, *others):
    return jnp.dot(features, jnp.concatenate(others, axis=1), preferred_element_type=F32)


def taper_of(squared):
    squared = jnp.maximum(squared, 1e-20)
    remain = jnp.maximum(4.0 - jnp.exp2(jnp.log(squared) * HALF_LOG2E), 0.0)
    twice = remain * remain
    return twice * twice * (5.0 - remain)


def kept_groups(sz, count, at):
    first = at * (sz.kept // UNROLL)
    last = jnp.minimum(lax.div(count + (UNROLL - 1), UNROLL), first + sz.kept // UNROLL)
    return first, jnp.maximum(first, last)


def vector_row(vec_ref, j):
    return vec_ref[pl.ds(jnp.minimum(j, vec_ref.shape[0] - 1), 1), :]


def own_features(lhs_ref, i):
    return lhs_ref[pl.ds(pl.multiple_of(i * BS, BS), BS), :DEPTH]


def other_features(rhs_ref, j):
    return rhs_ref[pl.ds(pl.multiple_of(j * DEPTH, DEPTH), DEPTH), :]


def clear(*accs):
    for acc in accs:
        acc[...] = jnp.zeros_like(acc)


def generate(sz, list_ref, count, lhs_ref, rhs_ref, tile_refs, squares):
    top = jnp.maximum(lax.div(count + (UNROLL - 1), UNROLL) - 1, 0)

    def squared(g, u):
        k = jnp.minimum(g, top) * UNROLL + u
        i, j = entry_of(list_ref, k)
        unused, twin = entry_of(list_ref, k + 1)
        return squared_of(own_features(lhs_ref, i), other_features(rhs_ref, j), other_features(rhs_ref, twin))

    def fill(u, both):
        squares[u * BS : (u + 1) * BS, :] = both[:, :BS]
        squares[(u + 1) * BS : (u + 2) * BS, :] = both[:, BS:]

    for u in range(0, UNROLL, 2):
        fill(u, squared(0, u))
    for at, tile_ref in enumerate(tile_refs):

        def group(g, unused, at=at, tile_ref=tile_ref):
            for u in range(0, UNROLL, 2):
                tiles = taper_of(squares[u * BS : (u + 2) * BS, :])
                fill(u, squared(g + 1, u))
                start = pl.multiple_of((g * UNROLL + u - at * sz.kept) * BS, BS)
                tile_ref[pl.ds(start, 2 * BS), :] = tiles
            return unused

        lax.fori_loop(*kept_groups(sz, count, at), group, 0)


def sweep(sz, list_ref, count, tile_refs, vec_ref, acc, acc_ones=None):
    accs = [acc] if acc_ones is None else [acc, acc_ones]
    clear(*accs)
    carry = (jnp.int32(-1),) + tuple(jnp.zeros((BS, BS), F32) for unused in accs)
    for at, tile_ref in enumerate(tile_refs):

        def group(g, carry, at=at, tile_ref=tile_ref):
            before, *totals = carry
            for u in range(0, UNROLL, 2):
                i, j = entry_of(list_ref, g * UNROLL + u)
                unused, twin = entry_of(list_ref, g * UNROLL + u + 1)
                keep = jnp.where(i == before, 1.0, 0.0)
                start = (g * UNROLL + u - at * sz.kept) * BS
                tile = tile_ref[pl.ds(pl.multiple_of(start, BS), BS), :]
                twin_tile = tile_ref[pl.ds(pl.multiple_of(start + BS, BS), BS), :]
                terms = [tile * vector_row(vec_ref, j) + twin_tile * vector_row(vec_ref, twin), tile + twin_tile]
                totals = [total * keep + term for total, term in zip(totals, terms)]
                for ref, total in zip(accs, totals):
                    ref[pl.ds(pl.multiple_of(i * BS, BS), BS), :] = total
                before = i
            return (before, *totals)

        carry = lax.fori_loop(*kept_groups(sz, count, at), group, carry)


def extras(sz, list_ref, count, vec_ref, acc, acc_ones, remake):
    def extra(k, unused):
        i, j = entry_of(list_ref, k)
        tile = taper_of(squared_of(*remake(i, j)))
        rows = pl.ds(pl.multiple_of(i * BS, BS), BS)
        acc[rows, :] += tile * vector_row(vec_ref, j)
        if acc_ones is not None:
            acc_ones[rows, :] += tile
        return unused

    kept = sz.kept * ARRAYS
    lax.fori_loop(kept, jnp.maximum(count, kept), extra, 0)


def finish(sz, acc, out_ref):
    unit = jnp.ones((8, BS), BF16)
    across = (((1,), (1,)), ((), ()))
    for i in range(sz.own):
        whole = acc[i * BS : (i + 1) * BS, :]
        high = whole.astype(BF16)
        low = (whole - high.astype(F32)).astype(BF16)
        y = lax.dot_general(unit, high, across, preferred_element_type=F32)
        y = y + lax.dot_general(unit, low, across, preferred_element_type=F32)
        out_ref[i : i + 1, :] = y[0:1, :] * sz.scale


def total_of(x):
    return jnp.sum(jnp.sum(x, axis=0, keepdims=True), axis=1, keepdims=True)


def place_block(piece_ref, part, first, rhs_ref):
    def one(k, unused):
        h, m, l = features_of([block_row(piece_ref, c, part, k) for c in range(3)], -2.0, 4, 3)
        feats = jnp.concatenate([h, m, h, m, l, h], axis=0).astype(BF16)
        rhs_ref[pl.ds(pl.multiple_of((first + k) * DEPTH, DEPTH), DEPTH), :] = feats
        return unused

    lax.fori_loop(0, part, one, 0, unroll=4)


def first_kernel(sz, *refs):
    list_ref, count_ref, lhs_ref, nugget_any, obs_any, home_ref = refs[:6]
    coord_refs = refs[6 : 6 + (sz.blks - 1) * sz.reps]
    refs = refs[6 + (sz.blks - 1) * sz.reps :]
    tile_refs = refs[:ARRAYS]
    spare_ref, obs_ref, diag_ref, mapped_ref, norm_ref = refs[ARRAYS : ARRAYS + 5]
    rhs_ref, acc, acc_ones, total_row, squares, nugget_ref, done, fetched = refs[ARRAYS + 5 :]
    blk, rep = lax.axis_index("blk"), lax.axis_index("rep")
    home = pl.ds(pl.multiple_of(blk * sz.local_blocks, 8), sz.local_blocks)
    fetch = pltpu.make_async_copy(nugget_any, nugget_ref, fetched.at[0])
    fetch_obs = pltpu.make_async_copy(obs_any, obs_ref.at[home, :], fetched.at[1])
    fetch.start()
    fetch_obs.start()
    for at, piece_ref in enumerate(coord_refs):
        code, turn = at // sz.reps + 1, at % sz.reps
        part = sz.local_blocks // sz.reps
        first = jnp.bitwise_xor(blk, code) * sz.local_blocks + jnp.bitwise_xor(rep, turn) * part
        first = pl.multiple_of(first, 8)
        place_block(piece_ref, part, first, rhs_ref)
        obs_ref[pl.ds(first, part), :] = piece_ref[3 * part : 4 * part, :]
    place_block(home_ref, sz.local_blocks, blk * sz.local_blocks, rhs_ref)
    far = lax.broadcasted_iota(jnp.int32, (DEPTH, BS), 0) == 3
    rhs_ref[sz.blocks * DEPTH :, :] = jnp.where(far, 1e6, 0.0).astype(BF16)
    count = count_ref[0]
    generate(sz, list_ref, count, lhs_ref, rhs_ref, tile_refs, squares)
    fetch_obs.wait()
    sweep(sz, list_ref, count, tile_refs, obs_ref, acc, acc_ones)
    extras(
        sz,
        list_ref,
        count,
        obs_ref,
        acc,
        acc_ones,
        lambda i, j: (own_features(lhs_ref, i), other_features(rhs_ref, j)),
    )

    @pl.when(count > sz.kept * ARRAYS)
    def save():
        copy = pltpu.make_async_copy(rhs_ref, spare_ref, done)
        copy.start()
        copy.wait()

    finish(sz, acc_ones, total_row)
    finish(sz, acc, mapped_ref)
    quarter = lax.axis_index("col") * sz.reps + rep
    own = pl.ds(pl.multiple_of(sz.me() * sz.own, 8), sz.own)
    fetch.wait()
    diag = nugget_ref[pl.ds(pl.multiple_of(quarter * sz.own, 8), sz.own), :] + total_row[...]
    diag_ref[...] = diag
    mapped_ref[...] += diag * obs_ref[own, :]
    norm_ref[...] = jnp.broadcast_to(total_of(obs_ref[...] * obs_ref[...]), (8, BS))


def step_kernel(sz, last, *refs):
    list_ref, count_ref, lhs_ref, spare_ref, diag_ref, norm_ref, field_ref, resid_ref, dirn_ref = refs[:9]
    pieces = refs[9 : 9 + sz.plane]
    tile_refs = refs[9 + sz.plane : 9 + sz.plane + ARRAYS]
    rest = refs[9 + sz.plane + ARRAYS :]
    mapped_ref, next_norm_ref, next_field_ref, next_resid_ref, next_dirn_ref = rest[:5]
    if last:
        dot_ref, dirn = rest[5:7]
    else:
        dirn = next_dirn_ref
    mapped, acc, features, others, done = rest[-5:]
    me = sz.me()
    assemble(sz, pieces, sz.own, mapped)
    norm = norm_ref[0:1, 0:1]
    step = norm / total_of(dirn_ref[...] * mapped[...])
    resid = resid_ref[...] - step * mapped[...]
    next_norm = total_of(resid * resid)
    dirn[...] = resid + (next_norm / norm) * dirn_ref[...]
    next_norm_ref[...] = jnp.broadcast_to(next_norm, (8, BS))
    home = pl.ds(pl.multiple_of(lax.axis_index("blk") * sz.local_blocks, 8), sz.local_blocks)
    own = pl.ds(pl.multiple_of(me * sz.own, 8), sz.own)
    field = step * dirn_ref[home, :]
    if last:
        next_field_ref[...] = field_ref[...] + field
        next_resid_ref[...] = resid_ref[home, :] - step * mapped[home, :]
        next_dirn_ref[...] = dirn[home, :]
    else:
        next_field_ref[...] = field
        next_resid_ref[...] = resid

    def remake(i, j):
        for source, start, size, target in ((lhs_ref, i, BS, features), (spare_ref, j, DEPTH, others)):
            copy = pltpu.make_async_copy(source.at[pl.ds(pl.multiple_of(start * size, size), size), :], target, done)
            copy.start()
            copy.wait()
        return features[:, :DEPTH], others[...]

    sweep(sz, list_ref, count_ref[0], tile_refs, dirn, acc)
    extras(sz, list_ref, count_ref[0], dirn, acc, None, remake)
    finish(sz, acc, mapped_ref)
    ours = mapped_ref[...] + diag_ref[...] * dirn[own, :]
    mapped_ref[...] = ours
    if last:
        dot_ref[...] = jnp.broadcast_to(total_of(ours * dirn[own, :]), dot_ref.shape)


def last_kernel(sz, *refs):
    norm_ref, field_ref, resid_ref, dirn_ref = refs[:4]
    pieces = refs[4 : 4 + sz.plane]
    out_field_ref, out_resid_ref = refs[4 + sz.plane :]
    product = jnp.zeros((8, BS), F32)
    for ref in pieces:
        for z in range(sz.blks):
            product = product + ref[sz.own + 8 * z : sz.own + 8 * (z + 1), :]
    step = norm_ref[0:1, :] / product[0:1, :]
    out_field_ref[...] = field_ref[...] + step * dirn_ref[...]
    quarter = lax.axis_index("col") * sz.reps + lax.axis_index("rep")
    for k, ref in enumerate(pieces):
        rows = pl.ds(pl.multiple_of(jnp.bitwise_xor(quarter, k) * sz.own, 8), sz.own)
        out_resid_ref[rows, :] = resid_ref[rows, :] - step * ref[: sz.own, :]


def call(kernel, mib, in_specs, shapes, out_specs, scratch, flops, *args):
    return pl.pallas_call(
        kernel,
        in_specs=in_specs,
        out_shape=shapes,
        out_specs=out_specs,
        scratch_shapes=scratch,
        compiler_params=pltpu.CompilerParams(vmem_limit_bytes=mib * MIB),
        cost_estimate=pl.CostEstimate(flops=flops, bytes_accessed=1 << 20, transcendentals=0),
    )(*args)


def array(*shape, dtype=F32):
    return jax.ShapeDtypeStruct(shape, dtype)


def local(coords, observations, nugget, tile_pairs, tile_live):
    sz = Sizes(observations.shape[0], tile_pairs.shape[1])
    own, blocks, home = sz.own, sz.blocks, sz.local_blocks
    alive = jnp.arange(sz.slots, dtype=jnp.int32) < tile_live[0]
    pairs = jnp.where(alive, tile_pairs, -1).reshape(2 * sz.slots // BS, BS)
    rep = lax.axis_index("rep")
    part = home // sz.reps
    obs_rows = observations.reshape(home, BS)
    rows = coords.reshape(3, home, BS)
    half = lax.dynamic_slice_in_dim(jnp.concatenate([rows, obs_rows[None]], axis=0), rep * part, part, axis=1)
    half = half.reshape(4 * part, BS)
    nears = [swap(half, "blk", z) for z in range(1, sz.blks)]
    pair_arrays = over_plane(along_blk(pairs))

    lhs = call(
        functools.partial(lhs_kernel, sz),
        12,
        [VMEM],
        array((own + 1) * BS, BS, dtype=BF16),
        VMEM,
        [],
        10_000_000,
        rows,
    )
    lines = 2 * sz.slots // BS * sz.devs
    table, count = call(
        functools.partial(list_kernel, sz),
        12,
        [VMEM] * sz.plane,
        (array(sz.capacity // BS, BS, dtype=jnp.int32), array(1, dtype=jnp.int32)),
        (VMEM, SMEM),
        [pltpu.VMEM((lines, BS), jnp.int32)] * 2
        + [pltpu.VMEM((lines, BS), F32)] * 2
        + [pltpu.VMEM((sz.capacity, BS), F32)]
        + [pltpu.VMEM((sz.capacity // BS, BS), F32)] * 2,
        10_000_000,
        *pair_arrays,
    )
    table, lhs, *nears = lax.optimization_barrier((table.reshape(sz.capacity), lhs, *nears))
    coord_arrays = []
    for near in nears:
        coord_arrays += [near] + [swap(near, "rep", r) for r in range(1, sz.reps)]
    tall = pltpu.VMEM(((own + 1) * BS, BS), F32)
    kept = [pltpu.VMEM((sz.kept * BS, BS), F32)] * ARRAYS
    *tiles, spare, obs, diag, mapped, norm = call(
        functools.partial(first_kernel, sz),
        sz.first_mib,
        [SMEM, SMEM, VMEM, ANY, ANY] + [VMEM] * (1 + len(coord_arrays)),
        kept
        + [
            pltpu.HBM(((blocks + 1) * DEPTH, BS), BF16),
            array(blocks, BS),
            array(own, BS),
            array(own, BS),
            array(8, BS),
        ],
        [VMEM] * ARRAYS + [ANY] + [VMEM] * 4,
        [
            pltpu.VMEM(((blocks + 1) * DEPTH, BS), BF16),
            tall,
            tall,
            pltpu.VMEM((own, BS), F32),
            pltpu.VMEM((UNROLL * BS, BS), F32),
            pltpu.VMEM((home, BS), F32),
            pltpu.SemaphoreType.DMA,
            pltpu.SemaphoreType.DMA((2,)),
        ],
        100_000_000,
        table,
        count,
        lhs,
        pltpu.with_memory_space_constraint(nugget.reshape(home, BS), pltpu.HBM),
        pltpu.with_memory_space_constraint(obs_rows, pltpu.HBM),
        rows,
        *coord_arrays,
    )
    tiles = [pltpu.with_memory_space_constraint(tile, pltpu.VMEM) for tile in tiles]
    spare = pltpu.with_memory_space_constraint(spare, pltpu.HBM)
    field, resid, dirn = norm, obs, obs
    for sweep_index in range(1, ITERS):
        last = sweep_index + 1 == ITERS
        span = home if last else blocks
        outs = [array(own, BS), array(8, BS), array(home, BS), array(span, BS), array(span, BS)]
        mapped, norm, field, resid, dirn, *dot = call(
            functools.partial(step_kernel, sz, last),
            5,
            [SMEM, SMEM, ANY, ANY] + [VMEM] * (5 + sz.plane + ARRAYS),
            outs + [array(8, BS)] * last,
            [VMEM] * (len(outs) + last),
            [pltpu.VMEM((blocks, BS), F32)] * (1 + last)
            + [tall, pltpu.VMEM((BS, BS), BF16), pltpu.VMEM((DEPTH, BS), BF16), pltpu.SemaphoreType.DMA],
            100_000_000,
            table,
            count,
            lhs,
            spare,
            diag,
            norm,
            field,
            resid,
            dirn,
            *over_plane(along_blk(mapped)),
            *tiles,
        )
    ends = over_plane(jnp.concatenate([mapped, along_blk(dot[0])], axis=0))
    field, resid = call(
        functools.partial(last_kernel, sz),
        4,
        [VMEM] * (4 + sz.plane),
        (array(home, BS), array(home, BS)),
        (VMEM, VMEM),
        [],
        100_000,
        norm,
        field,
        resid,
        dirn,
        *ends,
    )
    return field.reshape(sz.points), resid.reshape(sz.points)


def solution(mesh):
    in_specs = (
        P(None, ("grp", "blk")),
        P(("grp", "blk")),
        P(("grp", "blk")),
        P(None, ("grp", "blk", "col", "rep")),
        P(("grp", "blk", "col", "rep")),
    )
    out_specs = (P(("grp", "blk")), P(("grp", "blk")))
    return jax.shard_map(local, mesh=mesh, in_specs=in_specs, out_specs=out_specs, check_vma=False)
```

```python
import functools

import jax
import jax.numpy as jnp
from jax import lax
from jax.experimental import pallas as pl
from jax.experimental.pallas import tpu as pltpu
from jax.sharding import PartitionSpec as P

BS = 128
ITERS = 3
SUPPORT = 0.3
HALF_LOG2E = 0.7213475204444817
DEPTH = 48
UNROLL = 4
ARRAYS = 4
MIB = 1024 * 1024
VMEM = pl.BlockSpec(memory_space=pltpu.VMEM)
SMEM = pl.BlockSpec(memory_space=pltpu.SMEM)
ANY = pl.BlockSpec(memory_space=pl.ANY)
BF16 = jnp.bfloat16
F32 = jnp.float32


class Sizes:
    def __init__(self, points, slots):
        self.blks = lax.axis_size("blk")
        self.reps = lax.axis_size("rep")
        self.plane = lax.axis_size("col") * self.reps
        self.devs = self.blks * self.plane
        self.points = points
        self.slots = slots
        self.local_blocks = points // BS
        self.blocks = self.local_blocks * self.blks
        self.own = self.local_blocks // self.plane
        self.capacity = 2 * self.plane * slots + 1024
        per_row = slots * self.devs // self.blocks
        self.first_mib = 6 + self.blocks * DEPTH * BS * 2 // MIB
        self.kept = min(448, (48 - self.first_mib) * 16) // ARRAYS
        self.scale = 16.0 / (BS * per_row) / 256.0

    def me(self):
        return (lax.axis_index("blk") * lax.axis_size("col") + lax.axis_index("col")) * self.reps + lax.axis_index(
            "rep"
        )


def swap(x, axis, code):
    return lax.ppermute(x, axis, [(i, i ^ code) for i in range(lax.axis_size(axis))])


def along_blk(x):
    return jnp.concatenate([x] + [swap(x, "blk", k) for k in range(1, lax.axis_size("blk"))], axis=0)


def over_plane(x):
    reps = lax.axis_size("rep")
    found = {0: x}
    for c in range(1, lax.axis_size("col")):
        found[c * reps] = swap(x, "col", c)
    for start in sorted(found):
        for r in range(1, reps):
            found[start + r] = swap(found[start], "rep", r)
    return [found[k] for k in sorted(found)]


def assemble(sz, refs, rows, target):
    me = sz.me()
    for k, ref in enumerate(refs):
        for z in range(ref.shape[0] // rows):
            start = pl.multiple_of(jnp.bitwise_xor(me, z * sz.plane + k) * rows, 8)
            target[pl.ds(start, rows), :] = ref[z * rows : (z + 1) * rows, :]


def split3(x):
    high = x.astype(BF16).astype(F32)
    rest = x - high
    middle = rest.astype(BF16).astype(F32)
    return high, middle, rest - middle


def features_of(rows, factor, unit, norm):
    feature = lax.broadcasted_iota(jnp.int32, (8, BS), 0)
    x, y, z = ((row - 0.5) * (4.0 / SUPPORT) for row in rows)
    feats = jnp.where(feature == unit, 1.0, 0.0)
    for place, row in ((0, factor * x), (1, factor * y), (2, factor * z), (norm, x * x + y * y + z * z)):
        feats = jnp.where(feature == place, row, feats)
    return split3(feats)


def block_row(ref, c, part, k):
    return ref[c, pl.ds(k, 1), :] if len(ref.shape) == 3 else ref[pl.ds(c * part + k, 1), :]


def lhs_kernel(sz, home_ref, out_ref):
    quarter = lax.axis_index("col") * sz.reps + lax.axis_index("rep")
    for i in range(sz.own):
        h, m, l = features_of([block_row(home_ref, c, None, quarter * sz.own + i) for c in range(3)], 1.0, 3, 4)
        feats = jnp.concatenate([h, h, m, m, h, l, jnp.zeros((BS - DEPTH, BS), F32)], axis=0)
        out_ref[i * BS : (i + 1) * BS, :] = feats.T.astype(BF16)
    out_ref[sz.own * BS :, :] = jnp.zeros((BS, BS), BF16)


def list_kernel(sz, *refs):
    me = sz.me()
    out_ref, count_ref, target, other, place, value, key_column, key_row, entry_row = refs[sz.plane :]
    lines = sz.slots // BS
    at = 2 * lines * sz.devs
    for base in range(0, at, 2 * lines):
        pairs_ref = refs[base // (2 * lines * sz.blks)]
        start = base % (2 * lines * sz.blks)
        rows = pairs_ref[start : start + lines, :]
        cols = pairs_ref[start + lines : start + 2 * lines, :]
        target[base : base + lines, :] = rows
        other[base : base + lines, :] = cols
        target[base + lines : base + 2 * lines, :] = cols
        other[base + lines : base + 2 * lines, :] = rows
    local = target[...] - me * sz.own
    mine = jnp.logical_and(local >= 0, local < sz.own)
    flags = jnp.where(mine, 1.0, 0.0)
    a = lax.broadcasted_iota(jnp.int32, (BS, BS), 0)
    b = lax.broadcasted_iota(jnp.int32, (BS, BS), 1)
    ahead = jnp.where(a < b, 1.0, 0.0).astype(BF16)
    before = jnp.dot(flags.astype(BF16), ahead, preferred_element_type=F32)
    totals = jnp.broadcast_to(jnp.sum(flags, axis=1, keepdims=True), (at, BS))
    a = lax.broadcasted_iota(jnp.int32, (at, at), 0)
    b = lax.broadcasted_iota(jnp.int32, (at, at), 1)
    above = jnp.dot(jnp.where(b < a, 1.0, 0.0).astype(BF16), totals.astype(BF16), preferred_element_type=F32)
    place[...] = jnp.where(mine, above + before, -1.0)
    ends = jnp.sum(jnp.where(lax.broadcasted_iota(jnp.int32, (at, BS), 1) == 0, above + totals, 0.0), axis=1, keepdims=True)
    starts = ends - totals[:, 0:1]
    value[...] = (local + 256 * other[...]).astype(F32)
    count = jnp.sum(flags).astype(jnp.int32)
    sub = lax.broadcasted_iota(jnp.int32, (BS, BS), 0)
    lane = lax.broadcasted_iota(jnp.int32, (1, BS), 1)

    chunks = jnp.maximum(lax.shift_right_logical(count + BS - 1, 7), 1)

    def key_of(found, slot):
        entry = jnp.where(slot < count, found.astype(jnp.int32), sz.own)
        return entry.astype(F32), (jnp.bitwise_and(entry, 255) * 65536 + slot).astype(F32)

    def compact(c, unused):
        slot = (sub + c * BS).astype(F32)
        base = (c * BS).astype(F32)
        first = jnp.sum(jnp.where(ends <= base, 1.0, 0.0)).astype(jnp.int32)
        last = jnp.sum(jnp.where(starts < base + BS, 1.0, 0.0)).astype(jnp.int32)
        first = jnp.minimum(lax.shift_right_logical(first, 2), at // 4)
        last = lax.shift_right_logical(last + 3, 2)

        def lines(g, total):
            for u in range(4):
                r = 4 * g + u
                hit = place[pl.ds(r, 1), :] == slot
                total = jnp.where(hit, value[pl.ds(r, 1), :], total)
            return total

        total = lax.fori_loop(first, last, lines, jnp.zeros((BS, BS), F32))
        entry, key = key_of(jnp.sum(total.T, axis=0, keepdims=True), lane + c * BS)
        entry_row[pl.ds(c, 1), :] = entry
        key_row[pl.ds(c, 1), :] = key
        unused_entry, key = key_of(jnp.sum(total, axis=1, keepdims=True), sub[:, 0:1] + c * BS)
        key_column[pl.ds(pl.multiple_of(c * BS, BS), BS), :] = jnp.broadcast_to(key, (BS, BS))
        return unused

    lax.fori_loop(0, chunks, compact, 0)

    bound = lane.astype(F32) * 65536.0

    def tally(c, carry):
        keys = key_column[pl.ds(pl.multiple_of(c * BS, BS), BS), :]
        from_here, after = carry
        return from_here + jnp.where(keys >= bound, 1.0, 0.0), after + jnp.where(keys >= bound + 65536.0, 1.0, 0.0)

    zero = jnp.zeros((BS, BS), F32)
    from_here, after = lax.fori_loop(0, chunks, tally, (zero, zero))
    from_here = jnp.sum(from_here, axis=0, keepdims=True)
    each = from_here - jnp.sum(after, axis=0, keepdims=True)
    odd = jnp.where(lane < sz.own, each - 2.0 * jnp.floor(0.5 * each), 0.0)
    wide_odd = jnp.broadcast_to(odd, (BS, BS))
    odd_column = wide_odd.T
    odd_before = jnp.dot(wide_odd.astype(BF16), ahead, preferred_element_type=F32)[0:1, :]
    start = (chunks * BS).astype(F32) - from_here + odd_before
    null_place = jnp.where(odd > 0.0, start + each, -1.0)
    null_entry = (lane + 256 * sz.blocks).astype(F32)
    full = count + jnp.sum(odd).astype(jnp.int32)
    count_ref[0] = full

    def rank(c, unused):
        keys = key_row[pl.ds(c, 1), :]

        def below(k, total):
            lower = key_column[pl.ds(pl.multiple_of(k * BS, BS), BS), :] < keys
            return total + jnp.where(lower, 1.0, 0.0)

        past = (sub + 1).astype(F32) * 65536.0 <= keys
        total = lax.fori_loop(0, chunks, below, jnp.where(past, odd_column, 0.0))
        place[pl.ds(c, 1), :] = jnp.sum(total, axis=0, keepdims=True)
        return unused

    lax.fori_loop(0, chunks, rank, 0)

    def arrange(c, unused):
        slot = (sub + c * BS).astype(F32)

        def line(r, total):
            hit = place[pl.ds(r, 1), :] == slot
            return total + jnp.where(hit, entry_row[pl.ds(r, 1), :], 0.0)

        total = lax.fori_loop(0, chunks, line, jnp.where(null_place == slot, null_entry, 0.0))
        found = jnp.sum(total.T, axis=0, keepdims=True).astype(jnp.int32)
        out_ref[pl.ds(c, 1), :] = jnp.where(lane + c * BS < full, found, sz.own)
        return unused

    lax.fori_loop(0, jnp.maximum(lax.shift_right_logical(full + BS - 1, 7), 1), arrange, 0)


def entry_of(list_ref, k):
    entry = list_ref[k]
    return jnp.bitwise_and(entry, 255), lax.shift_right_logical(entry, 8)


def squared_of(features, others):
    return jnp.dot(features, others, preferred_element_type=F32)


def taper_of(squared):
    squared = jnp.maximum(squared, 1e-20)
    remain = jnp.maximum(4.0 - jnp.exp2(jnp.log(squared) * HALF_LOG2E), 0.0)
    twice = remain * remain
    return twice * twice * (5.0 - remain)


def kept_groups(sz, count, at):
    first = at * (sz.kept // UNROLL)
    last = jnp.minimum(lax.div(count + (UNROLL - 1), UNROLL), first + sz.kept // UNROLL)
    return first, jnp.maximum(first, last)


def vector_row(vec_ref, j):
    return vec_ref[pl.ds(jnp.minimum(j, vec_ref.shape[0] - 1), 1), :]


def own_features(lhs_ref, i):
    return lhs_ref[pl.ds(pl.multiple_of(i * BS, BS), BS), :DEPTH]


def other_features(rhs_ref, j):
    return rhs_ref[pl.ds(pl.multiple_of(j * DEPTH, DEPTH), DEPTH), :]


def clear(*accs):
    for acc in accs:
        acc[...] = jnp.zeros_like(acc)


def generate(sz, list_ref, count, lhs_ref, rhs_ref, tile_refs, squares):
    top = jnp.maximum(lax.div(count + (UNROLL - 1), UNROLL) - 1, 0)

    def squared(g, u):
        i, j = entry_of(list_ref, jnp.minimum(g, top) * UNROLL + u)
        return squared_of(own_features(lhs_ref, i), other_features(rhs_ref, j))

    for u in range(UNROLL):
        squares[u * BS : (u + 1) * BS, :] = squared(0, u)
    for at, tile_ref in enumerate(tile_refs):

        def group(g, unused, at=at, tile_ref=tile_ref):
            for u in range(UNROLL):
                following = squared(g + 1, u)
                start = pl.multiple_of((g * UNROLL + u - at * sz.kept) * BS, BS)
                for r in range(0, BS, 8):
                    here = slice(u * BS + r, u * BS + r + 8)
                    tile_ref[pl.ds(start + r, 8), :] = taper_of(squares[here, :])
                    squares[here, :] = following[r : r + 8, :]
            return unused

        lax.fori_loop(*kept_groups(sz, count, at), group, 0)


def sweep(sz, list_ref, count, tile_refs, vec_ref, acc, acc_ones=None):
    accs = [acc] if acc_ones is None else [acc, acc_ones]
    clear(*accs)
    zero = jnp.zeros((8, BS), F32)
    carry = (jnp.int32(-1),) + ((zero,) * (BS // 8),) * len(accs)
    for at, tile_ref in enumerate(tile_refs):

        def group(g, carry, at=at, tile_ref=tile_ref):
            before, *totals = carry
            totals = [list(total) for total in totals]
            for u in range(0, UNROLL, 2):
                i, j = entry_of(list_ref, g * UNROLL + u)
                unused, twin = entry_of(list_ref, g * UNROLL + u + 1)
                keep = jnp.where(i == before, 1.0, 0.0)
                start = pl.multiple_of((g * UNROLL + u - at * sz.kept) * BS, BS)
                base = pl.multiple_of(i * BS, BS)
                row = jnp.broadcast_to(vector_row(vec_ref, j), (8, BS))
                twin_row = jnp.broadcast_to(vector_row(vec_ref, twin), (8, BS))
                for k in range(BS // 8):
                    tile = tile_ref[pl.ds(start + 8 * k, 8), :]
                    twin_tile = tile_ref[pl.ds(start + BS + 8 * k, 8), :]
                    for ref, total, term in zip(accs, totals, (tile * row + twin_tile * twin_row, tile + twin_tile)):
                        total[k] = total[k] * keep + term
                        ref[pl.ds(base + 8 * k, 8), :] = total[k]
                before = i
            return (before, *(tuple(total) for total in totals))

        carry = lax.fori_loop(*kept_groups(sz, count, at), group, carry)


def extras(sz, list_ref, count, vec_ref, acc, acc_ones, remake):
    def extra(k, unused):
        i, j = entry_of(list_ref, k)
        tile = taper_of(squared_of(*remake(i, j)))
        rows = pl.ds(pl.multiple_of(i * BS, BS), BS)
        acc[rows, :] += tile * vector_row(vec_ref, j)
        if acc_ones is not None:
            acc_ones[rows, :] += tile
        return unused

    kept = sz.kept * ARRAYS
    lax.fori_loop(kept, jnp.maximum(count, kept), extra, 0)


def finish(sz, acc, out_ref):
    unit = jnp.ones((8, BS), BF16)
    across = (((1,), (1,)), ((), ()))
    for i in range(sz.own):
        whole = acc[i * BS : (i + 1) * BS, :]
        high = whole.astype(BF16)
        low = (whole - high.astype(F32)).astype(BF16)
        y = lax.dot_general(unit, high, across, preferred_element_type=F32)
        y = y + lax.dot_general(unit, low, across, preferred_element_type=F32)
        out_ref[i : i + 1, :] = y[0:1, :] * sz.scale


def total_of(x):
    return jnp.sum(jnp.sum(x, axis=0, keepdims=True), axis=1, keepdims=True)


def place_block(piece_ref, part, first, rhs_ref):
    def one(k, unused):
        h, m, l = features_of([block_row(piece_ref, c, part, k) for c in range(3)], -2.0, 4, 3)
        feats = jnp.concatenate([h, m, h, m, l, h], axis=0).astype(BF16)
        rhs_ref[pl.ds(pl.multiple_of((first + k) * DEPTH, DEPTH), DEPTH), :] = feats
        return unused

    lax.fori_loop(0, part, one, 0, unroll=4)


def first_kernel(sz, *refs):
    list_ref, count_ref, lhs_ref, nugget_any, obs_any, home_ref = refs[:6]
    coord_refs = refs[6 : 6 + (sz.blks - 1) * sz.reps]
    refs = refs[6 + (sz.blks - 1) * sz.reps :]
    tile_refs = refs[:ARRAYS]
    spare_ref, obs_ref, diag_ref, mapped_ref, norm_ref = refs[ARRAYS : ARRAYS + 5]
    rhs_ref, acc, acc_ones, total_row, squares, nugget_ref, done, fetched = refs[ARRAYS + 5 :]
    blk, rep = lax.axis_index("blk"), lax.axis_index("rep")
    home = pl.ds(pl.multiple_of(blk * sz.local_blocks, 8), sz.local_blocks)
    fetch = pltpu.make_async_copy(nugget_any, nugget_ref, fetched.at[0])
    fetch_obs = pltpu.make_async_copy(obs_any, obs_ref.at[home, :], fetched.at[1])
    fetch.start()
    fetch_obs.start()
    for at, piece_ref in enumerate(coord_refs):
        code, turn = at // sz.reps + 1, at % sz.reps
        part = sz.local_blocks // sz.reps
        first = jnp.bitwise_xor(blk, code) * sz.local_blocks + jnp.bitwise_xor(rep, turn) * part
        first = pl.multiple_of(first, 8)
        place_block(piece_ref, part, first, rhs_ref)
        obs_ref[pl.ds(first, part), :] = piece_ref[3 * part : 4 * part, :]
    place_block(home_ref, sz.local_blocks, blk * sz.local_blocks, rhs_ref)
    far = lax.broadcasted_iota(jnp.int32, (DEPTH, BS), 0) == 3
    rhs_ref[sz.blocks * DEPTH :, :] = jnp.where(far, 1e6, 0.0).astype(BF16)
    count = count_ref[0]
    generate(sz, list_ref, count, lhs_ref, rhs_ref, tile_refs, squares)
    fetch_obs.wait()
    sweep(sz, list_ref, count, tile_refs, obs_ref, acc, acc_ones)
    extras(
        sz,
        list_ref,
        count,
        obs_ref,
        acc,
        acc_ones,
        lambda i, j: (own_features(lhs_ref, i), other_features(rhs_ref, j)),
    )

    @pl.when(count > sz.kept * ARRAYS)
    def save():
        copy = pltpu.make_async_copy(rhs_ref, spare_ref, done)
        copy.start()
        copy.wait()

    finish(sz, acc_ones, total_row)
    finish(sz, acc, mapped_ref)
    quarter = lax.axis_index("col") * sz.reps + rep
    own = pl.ds(pl.multiple_of(sz.me() * sz.own, 8), sz.own)
    fetch.wait()
    diag = nugget_ref[pl.ds(pl.multiple_of(quarter * sz.own, 8), sz.own), :] + total_row[...]
    diag_ref[...] = diag
    mapped_ref[...] += diag * obs_ref[own, :]
    norm_ref[...] = jnp.broadcast_to(total_of(obs_ref[...] * obs_ref[...]), (8, BS))


def step_kernel(sz, last, *refs):
    list_ref, count_ref, lhs_ref, spare_ref, diag_ref, norm_ref, field_ref, resid_ref, dirn_ref = refs[:9]
    pieces = refs[9 : 9 + sz.plane]
    tile_refs = refs[9 + sz.plane : 9 + sz.plane + ARRAYS]
    rest = refs[9 + sz.plane + ARRAYS :]
    mapped_ref, next_norm_ref, next_field_ref, next_resid_ref, next_dirn_ref = rest[:5]
    if last:
        dot_ref, dirn = rest[5:7]
    else:
        dirn = next_dirn_ref
    mapped, acc, features, others, done = rest[-5:]
    me = sz.me()
    assemble(sz, pieces, sz.own, mapped)
    norm = norm_ref[0:1, 0:1]
    step = norm / total_of(dirn_ref[...] * mapped[...])
    resid = resid_ref[...] - step * mapped[...]
    next_norm = total_of(resid * resid)
    dirn[...] = resid + (next_norm / norm) * dirn_ref[...]
    next_norm_ref[...] = jnp.broadcast_to(next_norm, (8, BS))
    home = pl.ds(pl.multiple_of(lax.axis_index("blk") * sz.local_blocks, 8), sz.local_blocks)
    own = pl.ds(pl.multiple_of(me * sz.own, 8), sz.own)
    field = step * dirn_ref[home, :]
    if last:
        next_field_ref[...] = field_ref[...] + field
        next_resid_ref[...] = resid_ref[home, :] - step * mapped[home, :]
        next_dirn_ref[...] = dirn[home, :]
    else:
        next_field_ref[...] = field
        next_resid_ref[...] = resid

    def remake(i, j):
        for source, start, size, target in ((lhs_ref, i, BS, features), (spare_ref, j, DEPTH, others)):
            copy = pltpu.make_async_copy(source.at[pl.ds(pl.multiple_of(start * size, size), size), :], target, done)
            copy.start()
            copy.wait()
        return features[:, :DEPTH], others[...]

    sweep(sz, list_ref, count_ref[0], tile_refs, dirn, acc)
    extras(sz, list_ref, count_ref[0], dirn, acc, None, remake)
    finish(sz, acc, mapped_ref)
    ours = mapped_ref[...] + diag_ref[...] * dirn[own, :]
    mapped_ref[...] = ours
    if last:
        dot_ref[...] = jnp.broadcast_to(total_of(ours * dirn[own, :]), dot_ref.shape)


def last_kernel(sz, *refs):
    norm_ref, field_ref, resid_ref, dirn_ref = refs[:4]
    pieces = refs[4 : 4 + sz.plane]
    out_field_ref, out_resid_ref = refs[4 + sz.plane :]
    product = jnp.zeros((8, BS), F32)
    for ref in pieces:
        for z in range(sz.blks):
            product = product + ref[sz.own + 8 * z : sz.own + 8 * (z + 1), :]
    step = norm_ref[0:1, :] / product[0:1, :]
    out_field_ref[...] = field_ref[...] + step * dirn_ref[...]
    quarter = lax.axis_index("col") * sz.reps + lax.axis_index("rep")
    for k, ref in enumerate(pieces):
        rows = pl.ds(pl.multiple_of(jnp.bitwise_xor(quarter, k) * sz.own, 8), sz.own)
        out_resid_ref[rows, :] = resid_ref[rows, :] - step * ref[: sz.own, :]


def call(kernel, mib, in_specs, shapes, out_specs, scratch, flops, *args):
    return pl.pallas_call(
        kernel,
        in_specs=in_specs,
        out_shape=shapes,
        out_specs=out_specs,
        scratch_shapes=scratch,
        compiler_params=pltpu.CompilerParams(vmem_limit_bytes=mib * MIB),
        cost_estimate=pl.CostEstimate(flops=flops, bytes_accessed=1 << 20, transcendentals=0),
    )(*args)


def array(*shape, dtype=F32):
    return jax.ShapeDtypeStruct(shape, dtype)


def local(coords, observations, nugget, tile_pairs, tile_live):
    sz = Sizes(observations.shape[0], tile_pairs.shape[1])
    own, blocks, home = sz.own, sz.blocks, sz.local_blocks
    alive = jnp.arange(sz.slots, dtype=jnp.int32) < tile_live[0]
    pairs = jnp.where(alive, tile_pairs, -1).reshape(2 * sz.slots // BS, BS)
    rep = lax.axis_index("rep")
    part = home // sz.reps
    obs_rows = observations.reshape(home, BS)
    rows = coords.reshape(3, home, BS)
    half = lax.dynamic_slice_in_dim(jnp.concatenate([rows, obs_rows[None]], axis=0), rep * part, part, axis=1)
    half = half.reshape(4 * part, BS)
    nears = [swap(half, "blk", z) for z in range(1, sz.blks)]
    pair_arrays = over_plane(along_blk(pairs))

    lhs = call(
        functools.partial(lhs_kernel, sz),
        12,
        [VMEM],
        array((own + 1) * BS, BS, dtype=BF16),
        VMEM,
        [],
        10_000_000,
        rows,
    )
    lines = 2 * sz.slots // BS * sz.devs
    table, count = call(
        functools.partial(list_kernel, sz),
        12,
        [VMEM] * sz.plane,
        (array(sz.capacity // BS, BS, dtype=jnp.int32), array(1, dtype=jnp.int32)),
        (VMEM, SMEM),
        [pltpu.VMEM((lines, BS), jnp.int32)] * 2
        + [pltpu.VMEM((lines, BS), F32)] * 2
        + [pltpu.VMEM((sz.capacity, BS), F32)]
        + [pltpu.VMEM((sz.capacity // BS, BS), F32)] * 2,
        10_000_000,
        *pair_arrays,
    )
    table, lhs, *nears = lax.optimization_barrier((table.reshape(sz.capacity), lhs, *nears))
    coord_arrays = []
    for near in nears:
        coord_arrays += [near] + [swap(near, "rep", r) for r in range(1, sz.reps)]
    tall = pltpu.VMEM(((own + 1) * BS, BS), F32)
    kept = [pltpu.VMEM((sz.kept * BS, BS), F32)] * ARRAYS
    *tiles, spare, obs, diag, mapped, norm = call(
        functools.partial(first_kernel, sz),
        sz.first_mib,
        [SMEM, SMEM, VMEM, ANY, ANY] + [VMEM] * (1 + len(coord_arrays)),
        kept
        + [
            pltpu.HBM(((blocks + 1) * DEPTH, BS), BF16),
            array(blocks, BS),
            array(own, BS),
            array(own, BS),
            array(8, BS),
        ],
        [VMEM] * ARRAYS + [ANY] + [VMEM] * 4,
        [
            pltpu.VMEM(((blocks + 1) * DEPTH, BS), BF16),
            tall,
            tall,
            pltpu.VMEM((own, BS), F32),
            pltpu.VMEM((UNROLL * BS, BS), F32),
            pltpu.VMEM((home, BS), F32),
            pltpu.SemaphoreType.DMA,
            pltpu.SemaphoreType.DMA((2,)),
        ],
        100_000_000,
        table,
        count,
        lhs,
        pltpu.with_memory_space_constraint(nugget.reshape(home, BS), pltpu.HBM),
        pltpu.with_memory_space_constraint(obs_rows, pltpu.HBM),
        rows,
        *coord_arrays,
    )
    tiles = [pltpu.with_memory_space_constraint(tile, pltpu.VMEM) for tile in tiles]
    spare = pltpu.with_memory_space_constraint(spare, pltpu.HBM)
    field, resid, dirn = norm, obs, obs
    for sweep_index in range(1, ITERS):
        last = sweep_index + 1 == ITERS
        span = home if last else blocks
        outs = [array(own, BS), array(8, BS), array(home, BS), array(span, BS), array(span, BS)]
        mapped, norm, field, resid, dirn, *dot = call(
            functools.partial(step_kernel, sz, last),
            5,
            [SMEM, SMEM, ANY, ANY] + [VMEM] * (5 + sz.plane + ARRAYS),
            outs + [array(8, BS)] * last,
            [VMEM] * (len(outs) + last),
            [pltpu.VMEM((blocks, BS), F32)] * (1 + last)
            + [tall, pltpu.VMEM((BS, BS), BF16), pltpu.VMEM((DEPTH, BS), BF16), pltpu.SemaphoreType.DMA],
            100_000_000,
            table,
            count,
            lhs,
            spare,
            diag,
            norm,
            field,
            resid,
            dirn,
            *over_plane(along_blk(mapped)),
            *tiles,
        )
    ends = over_plane(jnp.concatenate([mapped, along_blk(dot[0])], axis=0))
    field, resid = call(
        functools.partial(last_kernel, sz),
        4,
        [VMEM] * (4 + sz.plane),
        (array(home, BS), array(home, BS)),
        (VMEM, VMEM),
        [],
        100_000,
        norm,
        field,
        resid,
        dirn,
        *ends,
    )
    return field.reshape(sz.points), resid.reshape(sz.points)


def solution(mesh):
    in_specs = (
        P(None, ("grp", "blk")),
        P(("grp", "blk")),
        P(("grp", "blk")),
        P(None, ("grp", "blk", "col", "rep")),
        P(("grp", "blk", "col", "rep")),
    )
    out_specs = (P(("grp", "blk")), P(("grp", "blk")))
    return jax.shard_map(local, mesh=mesh, in_specs=in_specs, out_specs=out_specs, check_vma=False)
```

```python
import functools

import jax
import jax.numpy as jnp
from jax import lax
from jax.experimental import pallas as pl
from jax.experimental.pallas import tpu as pltpu
from jax.sharding import PartitionSpec as P

BS = 128
ITERS = 3
SUPPORT = 0.3
HALF_LOG2E = 0.7213475204444817
DEPTH = 48
UNROLL = 8
ARRAYS = 4
MIB = 1024 * 1024
VMEM = pl.BlockSpec(memory_space=pltpu.VMEM)
SMEM = pl.BlockSpec(memory_space=pltpu.SMEM)
ANY = pl.BlockSpec(memory_space=pl.ANY)
BF16 = jnp.bfloat16
F32 = jnp.float32


class Sizes:
    def __init__(self, points, slots):
        self.blks = lax.axis_size("blk")
        self.reps = lax.axis_size("rep")
        self.plane = lax.axis_size("col") * self.reps
        self.devs = self.blks * self.plane
        self.points = points
        self.slots = slots
        self.local_blocks = points // BS
        self.blocks = self.local_blocks * self.blks
        self.own = self.local_blocks // self.plane
        self.capacity = 2 * self.plane * slots + 1024
        per_row = slots * self.devs // self.blocks
        self.first_mib = 6 + self.blocks * DEPTH * BS * 2 // MIB
        self.kept = min(448, (48 - self.first_mib) * 16) // ARRAYS
        self.scale = 16.0 / (BS * per_row) / 256.0

    def me(self):
        return (lax.axis_index("blk") * lax.axis_size("col") + lax.axis_index("col")) * self.reps + lax.axis_index(
            "rep"
        )


def swap(x, axis, code):
    return lax.ppermute(x, axis, [(i, i ^ code) for i in range(lax.axis_size(axis))])


def along_blk(x):
    return jnp.concatenate([x] + [swap(x, "blk", k) for k in range(1, lax.axis_size("blk"))], axis=0)


def over_plane(x):
    reps = lax.axis_size("rep")
    found = {0: x}
    for c in range(1, lax.axis_size("col")):
        found[c * reps] = swap(x, "col", c)
    for start in sorted(found):
        for r in range(1, reps):
            found[start + r] = swap(found[start], "rep", r)
    return [found[k] for k in sorted(found)]


def assemble(sz, refs, rows, target):
    me = sz.me()
    for k, ref in enumerate(refs):
        for z in range(ref.shape[0] // rows):
            start = pl.multiple_of(jnp.bitwise_xor(me, z * sz.plane + k) * rows, 8)
            target[pl.ds(start, rows), :] = ref[z * rows : (z + 1) * rows, :]


def split3(x):
    high = x.astype(BF16).astype(F32)
    rest = x - high
    middle = rest.astype(BF16).astype(F32)
    return high, middle, rest - middle


def features_of(rows, factor, unit, norm):
    feature = lax.broadcasted_iota(jnp.int32, (8, BS), 0)
    x, y, z = ((row - 0.5) * (4.0 / SUPPORT) for row in rows)
    feats = jnp.where(feature == unit, 1.0, 0.0)
    for place, row in ((0, factor * x), (1, factor * y), (2, factor * z), (norm, x * x + y * y + z * z)):
        feats = jnp.where(feature == place, row, feats)
    return split3(feats)


def block_row(ref, c, part, k):
    return ref[c, pl.ds(k, 1), :] if len(ref.shape) == 3 else ref[pl.ds(c * part + k, 1), :]


def lhs_kernel(sz, home_ref, out_ref):
    quarter = lax.axis_index("col") * sz.reps + lax.axis_index("rep")
    for i in range(sz.own):
        h, m, l = features_of([block_row(home_ref, c, None, quarter * sz.own + i) for c in range(3)], 1.0, 3, 4)
        feats = jnp.concatenate([h, h, m, m, h, l, jnp.zeros((BS - DEPTH, BS), F32)], axis=0)
        out_ref[i * BS : (i + 1) * BS, :] = feats.T.astype(BF16)
    out_ref[sz.own * BS :, :] = jnp.zeros((BS, BS), BF16)


def list_kernel(sz, *refs):
    me = sz.me()
    out_ref, count_ref, target, other, place, value, key_column, key_row, entry_row = refs[sz.plane :]
    lines = sz.slots // BS
    at = 2 * lines * sz.devs
    for base in range(0, at, 2 * lines):
        pairs_ref = refs[base // (2 * lines * sz.blks)]
        start = base % (2 * lines * sz.blks)
        rows = pairs_ref[start : start + lines, :]
        cols = pairs_ref[start + lines : start + 2 * lines, :]
        target[base : base + lines, :] = rows
        other[base : base + lines, :] = cols
        target[base + lines : base + 2 * lines, :] = cols
        other[base + lines : base + 2 * lines, :] = rows
    local = target[...] - me * sz.own
    mine = jnp.logical_and(local >= 0, local < sz.own)
    flags = jnp.where(mine, 1.0, 0.0)
    a = lax.broadcasted_iota(jnp.int32, (BS, BS), 0)
    b = lax.broadcasted_iota(jnp.int32, (BS, BS), 1)
    ahead = jnp.where(a < b, 1.0, 0.0).astype(BF16)
    before = jnp.dot(flags.astype(BF16), ahead, preferred_element_type=F32)
    totals = jnp.broadcast_to(jnp.sum(flags, axis=1, keepdims=True), (at, BS))
    a = lax.broadcasted_iota(jnp.int32, (at, at), 0)
    b = lax.broadcasted_iota(jnp.int32, (at, at), 1)
    above = jnp.dot(jnp.where(b < a, 1.0, 0.0).astype(BF16), totals.astype(BF16), preferred_element_type=F32)
    place[...] = jnp.where(mine, above + before, -1.0)
    ends = jnp.sum(jnp.where(lax.broadcasted_iota(jnp.int32, (at, BS), 1) == 0, above + totals, 0.0), axis=1, keepdims=True)
    starts = ends - totals[:, 0:1]
    value[...] = (local + 256 * other[...]).astype(F32)
    count = jnp.sum(flags).astype(jnp.int32)
    sub = lax.broadcasted_iota(jnp.int32, (BS, BS), 0)
    lane = lax.broadcasted_iota(jnp.int32, (1, BS), 1)

    chunks = jnp.maximum(lax.shift_right_logical(count + BS - 1, 7), 1)

    def key_of(found, slot):
        entry = jnp.where(slot < count, found.astype(jnp.int32), sz.own)
        return entry.astype(F32), (jnp.bitwise_and(entry, 255) * 65536 + slot).astype(F32)

    def compact(c, unused):
        slot = (sub + c * BS).astype(F32)
        base = (c * BS).astype(F32)
        first = jnp.sum(jnp.where(ends <= base, 1.0, 0.0)).astype(jnp.int32)
        last = jnp.sum(jnp.where(starts < base + BS, 1.0, 0.0)).astype(jnp.int32)
        first = jnp.minimum(lax.shift_right_logical(first, 2), at // 4)
        last = lax.shift_right_logical(last + 3, 2)

        def lines(g, total):
            for u in range(4):
                r = 4 * g + u
                hit = place[pl.ds(r, 1), :] == slot
                total = jnp.where(hit, value[pl.ds(r, 1), :], total)
            return total

        total = lax.fori_loop(first, last, lines, jnp.zeros((BS, BS), F32))
        entry, key = key_of(jnp.sum(total.T, axis=0, keepdims=True), lane + c * BS)
        entry_row[pl.ds(c, 1), :] = entry
        key_row[pl.ds(c, 1), :] = key
        unused_entry, key = key_of(jnp.sum(total, axis=1, keepdims=True), sub[:, 0:1] + c * BS)
        key_column[pl.ds(pl.multiple_of(c * BS, BS), BS), :] = jnp.broadcast_to(key, (BS, BS))
        return unused

    lax.fori_loop(0, chunks, compact, 0)

    bound = lane.astype(F32) * 65536.0

    def tally(c, carry):
        keys = key_column[pl.ds(pl.multiple_of(c * BS, BS), BS), :]
        from_here, after = carry
        return from_here + jnp.where(keys >= bound, 1.0, 0.0), after + jnp.where(keys >= bound + 65536.0, 1.0, 0.0)

    zero = jnp.zeros((BS, BS), F32)
    from_here, after = lax.fori_loop(0, chunks, tally, (zero, zero))
    from_here = jnp.sum(from_here, axis=0, keepdims=True)
    each = from_here - jnp.sum(after, axis=0, keepdims=True)
    odd = jnp.where(lane < sz.own, each - 2.0 * jnp.floor(0.5 * each), 0.0)
    wide_odd = jnp.broadcast_to(odd, (BS, BS))
    odd_column = wide_odd.T
    odd_before = jnp.dot(wide_odd.astype(BF16), ahead, preferred_element_type=F32)[0:1, :]
    start = (chunks * BS).astype(F32) - from_here + odd_before
    null_place = jnp.where(odd > 0.0, start + each, -1.0)
    null_entry = (lane + 256 * sz.blocks).astype(F32)
    full = count + jnp.sum(odd).astype(jnp.int32)
    count_ref[0] = full

    def rank(c, unused):
        keys = key_row[pl.ds(c, 1), :]

        def below(k, total):
            lower = key_column[pl.ds(pl.multiple_of(k * BS, BS), BS), :] < keys
            return total + jnp.where(lower, 1.0, 0.0)

        past = (sub + 1).astype(F32) * 65536.0 <= keys
        total = lax.fori_loop(0, chunks, below, jnp.where(past, odd_column, 0.0))
        place[pl.ds(c, 1), :] = jnp.sum(total, axis=0, keepdims=True)
        return unused

    lax.fori_loop(0, chunks, rank, 0)

    def arrange(c, unused):
        slot = (sub + c * BS).astype(F32)

        def line(r, total):
            hit = place[pl.ds(r, 1), :] == slot
            return total + jnp.where(hit, entry_row[pl.ds(r, 1), :], 0.0)

        total = lax.fori_loop(0, chunks, line, jnp.where(null_place == slot, null_entry, 0.0))
        found = jnp.sum(total.T, axis=0, keepdims=True).astype(jnp.int32)
        out_ref[pl.ds(c, 1), :] = jnp.where(lane + c * BS < full, found, sz.own)
        return unused

    lax.fori_loop(0, jnp.maximum(lax.shift_right_logical(full + BS - 1, 7), 1), arrange, 0)


def entry_of(list_ref, k):
    entry = list_ref[k]
    return jnp.bitwise_and(entry, 255), lax.shift_right_logical(entry, 8)


def squared_of(features, others):
    return jnp.dot(features, others, preferred_element_type=F32)


def taper_of(squared):
    squared = jnp.maximum(squared, 1e-20)
    remain = jnp.maximum(4.0 - jnp.exp2(jnp.log(squared) * HALF_LOG2E), 0.0)
    twice = remain * remain
    return twice * twice * (5.0 - remain)


def kept_groups(sz, count, at):
    first = at * (sz.kept // UNROLL)
    last = jnp.minimum(lax.div(count + (UNROLL - 1), UNROLL), first + sz.kept // UNROLL)
    return first, jnp.maximum(first, last)


def vector_row(vec_ref, j):
    return vec_ref[pl.ds(jnp.minimum(j, vec_ref.shape[0] - 1), 1), :]


def own_features(lhs_ref, i):
    return lhs_ref[pl.ds(pl.multiple_of(i * BS, BS), BS), :DEPTH]


def other_features(rhs_ref, j):
    return rhs_ref[pl.ds(pl.multiple_of(j * DEPTH, DEPTH), DEPTH), :]


def clear(*accs):
    for acc in accs:
        acc[...] = jnp.zeros_like(acc)


def generate(sz, list_ref, count, lhs_ref, rhs_ref, tile_refs, squares):
    top = jnp.maximum(lax.div(count + (UNROLL - 1), UNROLL) - 1, 0)

    def squared(g, u):
        i, j = entry_of(list_ref, jnp.minimum(g, top) * UNROLL + u)
        return squared_of(own_features(lhs_ref, i), other_features(rhs_ref, j))

    for u in range(UNROLL):
        squares[u * BS : (u + 1) * BS, :] = squared(0, u)
    for at, tile_ref in enumerate(tile_refs):

        def group(g, unused, at=at, tile_ref=tile_ref):
            for u in range(UNROLL):
                following = squared(g + 1, u)
                start = pl.multiple_of((g * UNROLL + u - at * sz.kept) * BS, BS)
                for r in range(0, BS, 8):
                    here = slice(u * BS + r, u * BS + r + 8)
                    tile_ref[pl.ds(start + r, 8), :] = taper_of(squares[here, :])
                    squares[here, :] = following[r : r + 8, :]
            return unused

        lax.fori_loop(*kept_groups(sz, count, at), group, 0)


def sweep(sz, list_ref, count, tile_refs, vec_ref, acc, acc_ones=None):
    accs = [acc] if acc_ones is None else [acc, acc_ones]
    clear(*accs)
    zero = jnp.zeros((8, BS), F32)
    carry = (jnp.int32(-1),) + ((zero,) * (BS // 8),) * len(accs)
    for at, tile_ref in enumerate(tile_refs):

        def group(g, carry, at=at, tile_ref=tile_ref):
            before, *totals = carry
            totals = [list(total) for total in totals]
            for u in range(0, UNROLL, 2):
                i, j = entry_of(list_ref, g * UNROLL + u)
                unused, twin = entry_of(list_ref, g * UNROLL + u + 1)
                keep = jnp.where(i == before, 1.0, 0.0)
                start = pl.multiple_of((g * UNROLL + u - at * sz.kept) * BS, BS)
                base = pl.multiple_of(i * BS, BS)
                row = jnp.broadcast_to(vector_row(vec_ref, j), (8, BS))
                twin_row = jnp.broadcast_to(vector_row(vec_ref, twin), (8, BS))
                for k in range(BS // 8):
                    tile = tile_ref[pl.ds(start + 8 * k, 8), :]
                    twin_tile = tile_ref[pl.ds(start + BS + 8 * k, 8), :]
                    for ref, total, term in zip(accs, totals, (tile * row + twin_tile * twin_row, tile + twin_tile)):
                        total[k] = total[k] * keep + term
                        ref[pl.ds(base + 8 * k, 8), :] = total[k]
                before = i
            return (before, *(tuple(total) for total in totals))

        carry = lax.fori_loop(*kept_groups(sz, count, at), group, carry)


def extras(sz, list_ref, count, vec_ref, acc, acc_ones, remake):
    def extra(k, unused):
        i, j = entry_of(list_ref, k)
        tile = taper_of(squared_of(*remake(i, j)))
        rows = pl.ds(pl.multiple_of(i * BS, BS), BS)
        acc[rows, :] += tile * vector_row(vec_ref, j)
        if acc_ones is not None:
            acc_ones[rows, :] += tile
        return unused

    kept = sz.kept * ARRAYS
    lax.fori_loop(kept, jnp.maximum(count, kept), extra, 0)


def finish(sz, acc, out_ref):
    unit = jnp.ones((8, BS), BF16)
    across = (((1,), (1,)), ((), ()))
    for i in range(sz.own):
        whole = acc[i * BS : (i + 1) * BS, :]
        high = whole.astype(BF16)
        low = (whole - high.astype(F32)).astype(BF16)
        y = lax.dot_general(unit, high, across, preferred_element_type=F32)
        y = y + lax.dot_general(unit, low, across, preferred_element_type=F32)
        out_ref[i : i + 1, :] = y[0:1, :] * sz.scale


def total_of(x):
    return jnp.sum(jnp.sum(x, axis=0, keepdims=True), axis=1, keepdims=True)


def place_block(piece_ref, part, first, rhs_ref):
    def one(k, unused):
        h, m, l = features_of([block_row(piece_ref, c, part, k) for c in range(3)], -2.0, 4, 3)
        feats = jnp.concatenate([h, m, h, m, l, h], axis=0).astype(BF16)
        rhs_ref[pl.ds(pl.multiple_of((first + k) * DEPTH, DEPTH), DEPTH), :] = feats
        return unused

    lax.fori_loop(0, part, one, 0, unroll=4)


def first_kernel(sz, *refs):
    list_ref, count_ref, lhs_ref, nugget_any, obs_any, home_ref = refs[:6]
    coord_refs = refs[6 : 6 + (sz.blks - 1) * sz.reps]
    refs = refs[6 + (sz.blks - 1) * sz.reps :]
    tile_refs = refs[:ARRAYS]
    spare_ref, obs_ref, diag_ref, mapped_ref, norm_ref = refs[ARRAYS : ARRAYS + 5]
    rhs_ref, acc, acc_ones, total_row, squares, nugget_ref, done, fetched = refs[ARRAYS + 5 :]
    blk, rep = lax.axis_index("blk"), lax.axis_index("rep")
    home = pl.ds(pl.multiple_of(blk * sz.local_blocks, 8), sz.local_blocks)
    fetch = pltpu.make_async_copy(nugget_any, nugget_ref, fetched.at[0])
    fetch_obs = pltpu.make_async_copy(obs_any, obs_ref.at[home, :], fetched.at[1])
    fetch.start()
    fetch_obs.start()
    for at, piece_ref in enumerate(coord_refs):
        code, turn = at // sz.reps + 1, at % sz.reps
        part = sz.local_blocks // sz.reps
        first = jnp.bitwise_xor(blk, code) * sz.local_blocks + jnp.bitwise_xor(rep, turn) * part
        first = pl.multiple_of(first, 8)
        place_block(piece_ref, part, first, rhs_ref)
        obs_ref[pl.ds(first, part), :] = piece_ref[3 * part : 4 * part, :]
    place_block(home_ref, sz.local_blocks, blk * sz.local_blocks, rhs_ref)
    far = lax.broadcasted_iota(jnp.int32, (DEPTH, BS), 0) == 3
    rhs_ref[sz.blocks * DEPTH :, :] = jnp.where(far, 1e6, 0.0).astype(BF16)
    count = count_ref[0]
    generate(sz, list_ref, count, lhs_ref, rhs_ref, tile_refs, squares)
    fetch_obs.wait()
    sweep(sz, list_ref, count, tile_refs, obs_ref, acc, acc_ones)
    extras(
        sz,
        list_ref,
        count,
        obs_ref,
        acc,
        acc_ones,
        lambda i, j: (own_features(lhs_ref, i), other_features(rhs_ref, j)),
    )

    @pl.when(count > sz.kept * ARRAYS)
    def save():
        copy = pltpu.make_async_copy(rhs_ref, spare_ref, done)
        copy.start()
        copy.wait()

    finish(sz, acc_ones, total_row)
    finish(sz, acc, mapped_ref)
    quarter = lax.axis_index("col") * sz.reps + rep
    own = pl.ds(pl.multiple_of(sz.me() * sz.own, 8), sz.own)
    fetch.wait()
    diag = nugget_ref[pl.ds(pl.multiple_of(quarter * sz.own, 8), sz.own), :] + total_row[...]
    diag_ref[...] = diag
    mapped_ref[...] += diag * obs_ref[own, :]
    norm_ref[...] = jnp.broadcast_to(total_of(obs_ref[...] * obs_ref[...]), (8, BS))


def step_kernel(sz, last, *refs):
    list_ref, count_ref, lhs_ref, spare_ref, diag_ref, norm_ref, field_ref, resid_ref, dirn_ref = refs[:9]
    pieces = refs[9 : 9 + sz.plane]
    tile_refs = refs[9 + sz.plane : 9 + sz.plane + ARRAYS]
    rest = refs[9 + sz.plane + ARRAYS :]
    mapped_ref, next_norm_ref, next_field_ref, next_resid_ref, next_dirn_ref = rest[:5]
    if last:
        dot_ref, dirn = rest[5:7]
    else:
        dirn = next_dirn_ref
    mapped, acc, features, others, done = rest[-5:]
    me = sz.me()
    assemble(sz, pieces, sz.own, mapped)
    norm = norm_ref[0:1, 0:1]
    step = norm / total_of(dirn_ref[...] * mapped[...])
    resid = resid_ref[...] - step * mapped[...]
    next_norm = total_of(resid * resid)
    dirn[...] = resid + (next_norm / norm) * dirn_ref[...]
    next_norm_ref[...] = jnp.broadcast_to(next_norm, (8, BS))
    home = pl.ds(pl.multiple_of(lax.axis_index("blk") * sz.local_blocks, 8), sz.local_blocks)
    own = pl.ds(pl.multiple_of(me * sz.own, 8), sz.own)
    field = step * dirn_ref[home, :]
    if last:
        next_field_ref[...] = field_ref[...] + field
        next_resid_ref[...] = resid_ref[home, :] - step * mapped[home, :]
        next_dirn_ref[...] = dirn[home, :]
    else:
        next_field_ref[...] = field
        next_resid_ref[...] = resid

    def remake(i, j):
        for source, start, size, target in ((lhs_ref, i, BS, features), (spare_ref, j, DEPTH, others)):
            copy = pltpu.make_async_copy(source.at[pl.ds(pl.multiple_of(start * size, size), size), :], target, done)
            copy.start()
            copy.wait()
        return features[:, :DEPTH], others[...]

    sweep(sz, list_ref, count_ref[0], tile_refs, dirn, acc)
    extras(sz, list_ref, count_ref[0], dirn, acc, None, remake)
    finish(sz, acc, mapped_ref)
    ours = mapped_ref[...] + diag_ref[...] * dirn[own, :]
    mapped_ref[...] = ours
    if last:
        dot_ref[...] = jnp.broadcast_to(total_of(ours * dirn[own, :]), dot_ref.shape)


def last_kernel(sz, *refs):
    norm_ref, field_ref, resid_ref, dirn_ref = refs[:4]
    pieces = refs[4 : 4 + sz.plane]
    out_field_ref, out_resid_ref = refs[4 + sz.plane :]
    product = jnp.zeros((8, BS), F32)
    for ref in pieces:
        for z in range(sz.blks):
            product = product + ref[sz.own + 8 * z : sz.own + 8 * (z + 1), :]
    step = norm_ref[0:1, :] / product[0:1, :]
    out_field_ref[...] = field_ref[...] + step * dirn_ref[...]
    quarter = lax.axis_index("col") * sz.reps + lax.axis_index("rep")
    for k, ref in enumerate(pieces):
        rows = pl.ds(pl.multiple_of(jnp.bitwise_xor(quarter, k) * sz.own, 8), sz.own)
        out_resid_ref[rows, :] = resid_ref[rows, :] - step * ref[: sz.own, :]


def call(kernel, mib, in_specs, shapes, out_specs, scratch, flops, *args):
    return pl.pallas_call(
        kernel,
        in_specs=in_specs,
        out_shape=shapes,
        out_specs=out_specs,
        scratch_shapes=scratch,
        compiler_params=pltpu.CompilerParams(vmem_limit_bytes=mib * MIB),
        cost_estimate=pl.CostEstimate(flops=flops, bytes_accessed=1 << 20, transcendentals=0),
    )(*args)


def array(*shape, dtype=F32):
    return jax.ShapeDtypeStruct(shape, dtype)


def local(coords, observations, nugget, tile_pairs, tile_live):
    sz = Sizes(observations.shape[0], tile_pairs.shape[1])
    own, blocks, home = sz.own, sz.blocks, sz.local_blocks
    alive = jnp.arange(sz.slots, dtype=jnp.int32) < tile_live[0]
    pairs = jnp.where(alive, tile_pairs, -1).reshape(2 * sz.slots // BS, BS)
    rep = lax.axis_index("rep")
    part = home // sz.reps
    obs_rows = observations.reshape(home, BS)
    rows = coords.reshape(3, home, BS)
    half = lax.dynamic_slice_in_dim(jnp.concatenate([rows, obs_rows[None]], axis=0), rep * part, part, axis=1)
    half = half.reshape(4 * part, BS)
    nears = [swap(half, "blk", z) for z in range(1, sz.blks)]
    pair_arrays = over_plane(along_blk(pairs))

    lhs = call(
        functools.partial(lhs_kernel, sz),
        12,
        [VMEM],
        array((own + 1) * BS, BS, dtype=BF16),
        VMEM,
        [],
        10_000_000,
        rows,
    )
    lines = 2 * sz.slots // BS * sz.devs
    table, count = call(
        functools.partial(list_kernel, sz),
        12,
        [VMEM] * sz.plane,
        (array(sz.capacity // BS, BS, dtype=jnp.int32), array(1, dtype=jnp.int32)),
        (VMEM, SMEM),
        [pltpu.VMEM((lines, BS), jnp.int32)] * 2
        + [pltpu.VMEM((lines, BS), F32)] * 2
        + [pltpu.VMEM((sz.capacity, BS), F32)]
        + [pltpu.VMEM((sz.capacity // BS, BS), F32)] * 2,
        10_000_000,
        *pair_arrays,
    )
    table, lhs, *nears = lax.optimization_barrier((table.reshape(sz.capacity), lhs, *nears))
    coord_arrays = []
    for near in nears:
        coord_arrays += [near] + [swap(near, "rep", r) for r in range(1, sz.reps)]
    tall = pltpu.VMEM(((own + 1) * BS, BS), F32)
    kept = [pltpu.VMEM((sz.kept * BS, BS), F32)] * ARRAYS
    *tiles, spare, obs, diag, mapped, norm = call(
        functools.partial(first_kernel, sz),
        sz.first_mib,
        [SMEM, SMEM, VMEM, ANY, ANY] + [VMEM] * (1 + len(coord_arrays)),
        kept
        + [
            pltpu.HBM(((blocks + 1) * DEPTH, BS), BF16),
            array(blocks, BS),
            array(own, BS),
            array(own, BS),
            array(8, BS),
        ],
        [VMEM] * ARRAYS + [ANY] + [VMEM] * 4,
        [
            pltpu.VMEM(((blocks + 1) * DEPTH, BS), BF16),
            tall,
            tall,
            pltpu.VMEM((own, BS), F32),
            pltpu.VMEM((UNROLL * BS, BS), F32),
            pltpu.VMEM((home, BS), F32),
            pltpu.SemaphoreType.DMA,
            pltpu.SemaphoreType.DMA((2,)),
        ],
        100_000_000,
        table,
        count,
        lhs,
        pltpu.with_memory_space_constraint(nugget.reshape(home, BS), pltpu.HBM),
        pltpu.with_memory_space_constraint(obs_rows, pltpu.HBM),
        rows,
        *coord_arrays,
    )
    tiles = [pltpu.with_memory_space_constraint(tile, pltpu.VMEM) for tile in tiles]
    spare = pltpu.with_memory_space_constraint(spare, pltpu.HBM)
    field, resid, dirn = norm, obs, obs
    for sweep_index in range(1, ITERS):
        last = sweep_index + 1 == ITERS
        span = home if last else blocks
        outs = [array(own, BS), array(8, BS), array(home, BS), array(span, BS), array(span, BS)]
        mapped, norm, field, resid, dirn, *dot = call(
            functools.partial(step_kernel, sz, last),
            5,
            [SMEM, SMEM, ANY, ANY] + [VMEM] * (5 + sz.plane + ARRAYS),
            outs + [array(8, BS)] * last,
            [VMEM] * (len(outs) + last),
            [pltpu.VMEM((blocks, BS), F32)] * (1 + last)
            + [tall, pltpu.VMEM((BS, BS), BF16), pltpu.VMEM((DEPTH, BS), BF16), pltpu.SemaphoreType.DMA],
            100_000_000,
            table,
            count,
            lhs,
            spare,
            diag,
            norm,
            field,
            resid,
            dirn,
            *over_plane(along_blk(mapped)),
            *tiles,
        )
    ends = over_plane(jnp.concatenate([mapped, along_blk(dot[0])], axis=0))
    field, resid = call(
        functools.partial(last_kernel, sz),
        4,
        [VMEM] * (4 + sz.plane),
        (array(home, BS), array(home, BS)),
        (VMEM, VMEM),
        [],
        100_000,
        norm,
        field,
        resid,
        dirn,
        *ends,
    )
    return field.reshape(sz.points), resid.reshape(sz.points)


def solution(mesh):
    in_specs = (
        P(None, ("grp", "blk")),
        P(("grp", "blk")),
        P(("grp", "blk")),
        P(None, ("grp", "blk", "col", "rep")),
        P(("grp", "blk", "col", "rep")),
    )
    out_specs = (P(("grp", "blk")), P(("grp", "blk")))
    return jax.shard_map(local, mesh=mesh, in_specs=in_specs, out_specs=out_specs, check_vma=False)
```

```python
import functools

import jax
import jax.numpy as jnp
from jax import lax
from jax.experimental import pallas as pl
from jax.experimental.pallas import tpu as pltpu
from jax.sharding import PartitionSpec as P

BS = 128
ITERS = 3
SUPPORT = 0.3
HALF_LOG2E = 0.7213475204444817
DEPTH = 48
UNROLL = 16
ARRAYS = 4
MIB = 1024 * 1024
VMEM = pl.BlockSpec(memory_space=pltpu.VMEM)
SMEM = pl.BlockSpec(memory_space=pltpu.SMEM)
ANY = pl.BlockSpec(memory_space=pl.ANY)
BF16 = jnp.bfloat16
F32 = jnp.float32


class Sizes:
    def __init__(self, points, slots):
        self.blks = lax.axis_size("blk")
        self.reps = lax.axis_size("rep")
        self.plane = lax.axis_size("col") * self.reps
        self.devs = self.blks * self.plane
        self.points = points
        self.slots = slots
        self.local_blocks = points // BS
        self.blocks = self.local_blocks * self.blks
        self.own = self.local_blocks // self.plane
        self.capacity = 2 * self.plane * slots + 1024
        per_row = slots * self.devs // self.blocks
        self.first_mib = 6 + self.blocks * DEPTH * BS * 2 // MIB
        self.kept = min(448, (48 - self.first_mib) * 16) // (ARRAYS * UNROLL) * UNROLL
        self.scale = 16.0 / (BS * per_row) / 256.0

    def me(self):
        return (lax.axis_index("blk") * lax.axis_size("col") + lax.axis_index("col")) * self.reps + lax.axis_index(
            "rep"
        )


def swap(x, axis, code):
    return lax.ppermute(x, axis, [(i, i ^ code) for i in range(lax.axis_size(axis))])


def along_blk(x):
    return jnp.concatenate([x] + [swap(x, "blk", k) for k in range(1, lax.axis_size("blk"))], axis=0)


def over_plane(x):
    reps = lax.axis_size("rep")
    found = {0: x}
    for c in range(1, lax.axis_size("col")):
        found[c * reps] = swap(x, "col", c)
    for start in sorted(found):
        for r in range(1, reps):
            found[start + r] = swap(found[start], "rep", r)
    return [found[k] for k in sorted(found)]


def assemble(sz, refs, rows, target):
    me = sz.me()
    for k, ref in enumerate(refs):
        for z in range(ref.shape[0] // rows):
            start = pl.multiple_of(jnp.bitwise_xor(me, z * sz.plane + k) * rows, 8)
            target[pl.ds(start, rows), :] = ref[z * rows : (z + 1) * rows, :]


def split3(x):
    high = x.astype(BF16).astype(F32)
    rest = x - high
    middle = rest.astype(BF16).astype(F32)
    return high, middle, rest - middle


def features_of(rows, factor, unit, norm):
    feature = lax.broadcasted_iota(jnp.int32, (8, BS), 0)
    x, y, z = ((row - 0.5) * (4.0 / SUPPORT) for row in rows)
    feats = jnp.where(feature == unit, 1.0, 0.0)
    for place, row in ((0, factor * x), (1, factor * y), (2, factor * z), (norm, x * x + y * y + z * z)):
        feats = jnp.where(feature == place, row, feats)
    return split3(feats)


def block_row(ref, c, part, k):
    return ref[c, pl.ds(k, 1), :] if len(ref.shape) == 3 else ref[pl.ds(c * part + k, 1), :]


def lhs_kernel(sz, home_ref, out_ref):
    quarter = lax.axis_index("col") * sz.reps + lax.axis_index("rep")
    for i in range(sz.own):
        h, m, l = features_of([block_row(home_ref, c, None, quarter * sz.own + i) for c in range(3)], 1.0, 3, 4)
        feats = jnp.concatenate([h, h, m, m, h, l, jnp.zeros((BS - DEPTH, BS), F32)], axis=0)
        out_ref[i * BS : (i + 1) * BS, :] = feats.T.astype(BF16)
    out_ref[sz.own * BS :, :] = jnp.zeros((BS, BS), BF16)


def list_kernel(sz, *refs):
    me = sz.me()
    out_ref, count_ref, target, other, place, value, key_column, key_row, entry_row = refs[sz.plane :]
    lines = sz.slots // BS
    at = 2 * lines * sz.devs
    for base in range(0, at, 2 * lines):
        pairs_ref = refs[base // (2 * lines * sz.blks)]
        start = base % (2 * lines * sz.blks)
        rows = pairs_ref[start : start + lines, :]
        cols = pairs_ref[start + lines : start + 2 * lines, :]
        target[base : base + lines, :] = rows
        other[base : base + lines, :] = cols
        target[base + lines : base + 2 * lines, :] = cols
        other[base + lines : base + 2 * lines, :] = rows
    local = target[...] - me * sz.own
    mine = jnp.logical_and(local >= 0, local < sz.own)
    flags = jnp.where(mine, 1.0, 0.0)
    a = lax.broadcasted_iota(jnp.int32, (BS, BS), 0)
    b = lax.broadcasted_iota(jnp.int32, (BS, BS), 1)
    ahead = jnp.where(a < b, 1.0, 0.0).astype(BF16)
    before = jnp.dot(flags.astype(BF16), ahead, preferred_element_type=F32)
    totals = jnp.broadcast_to(jnp.sum(flags, axis=1, keepdims=True), (at, BS))
    a = lax.broadcasted_iota(jnp.int32, (at, at), 0)
    b = lax.broadcasted_iota(jnp.int32, (at, at), 1)
    above = jnp.dot(jnp.where(b < a, 1.0, 0.0).astype(BF16), totals.astype(BF16), preferred_element_type=F32)
    place[...] = jnp.where(mine, above + before, -1.0)
    ends = jnp.sum(jnp.where(lax.broadcasted_iota(jnp.int32, (at, BS), 1) == 0, above + totals, 0.0), axis=1, keepdims=True)
    starts = ends - totals[:, 0:1]
    value[...] = (local + 256 * other[...]).astype(F32)
    count = jnp.sum(flags).astype(jnp.int32)
    sub = lax.broadcasted_iota(jnp.int32, (BS, BS), 0)
    lane = lax.broadcasted_iota(jnp.int32, (1, BS), 1)

    chunks = jnp.maximum(lax.shift_right_logical(count + BS - 1, 7), 1)

    def key_of(found, slot):
        entry = jnp.where(slot < count, found.astype(jnp.int32), sz.own)
        return entry.astype(F32), (jnp.bitwise_and(entry, 255) * 65536 + slot).astype(F32)

    def compact(c, unused):
        slot = (sub + c * BS).astype(F32)
        base = (c * BS).astype(F32)
        first = jnp.sum(jnp.where(ends <= base, 1.0, 0.0)).astype(jnp.int32)
        last = jnp.sum(jnp.where(starts < base + BS, 1.0, 0.0)).astype(jnp.int32)
        first = jnp.minimum(lax.shift_right_logical(first, 2), at // 4)
        last = lax.shift_right_logical(last + 3, 2)

        def lines(g, total):
            for u in range(4):
                r = 4 * g + u
                hit = place[pl.ds(r, 1), :] == slot
                total = jnp.where(hit, value[pl.ds(r, 1), :], total)
            return total

        total = lax.fori_loop(first, last, lines, jnp.zeros((BS, BS), F32))
        entry, key = key_of(jnp.sum(total.T, axis=0, keepdims=True), lane + c * BS)
        entry_row[pl.ds(c, 1), :] = entry
        key_row[pl.ds(c, 1), :] = key
        unused_entry, key = key_of(jnp.sum(total, axis=1, keepdims=True), sub[:, 0:1] + c * BS)
        key_column[pl.ds(pl.multiple_of(c * BS, BS), BS), :] = jnp.broadcast_to(key, (BS, BS))
        return unused

    lax.fori_loop(0, chunks, compact, 0)

    bound = lane.astype(F32) * 65536.0

    def tally(c, carry):
        keys = key_column[pl.ds(pl.multiple_of(c * BS, BS), BS), :]
        from_here, after = carry
        return from_here + jnp.where(keys >= bound, 1.0, 0.0), after + jnp.where(keys >= bound + 65536.0, 1.0, 0.0)

    zero = jnp.zeros((BS, BS), F32)
    from_here, after = lax.fori_loop(0, chunks, tally, (zero, zero))
    from_here = jnp.sum(from_here, axis=0, keepdims=True)
    each = from_here - jnp.sum(after, axis=0, keepdims=True)
    odd = jnp.where(lane < sz.own, each - 2.0 * jnp.floor(0.5 * each), 0.0)
    wide_odd = jnp.broadcast_to(odd, (BS, BS))
    odd_column = wide_odd.T
    odd_before = jnp.dot(wide_odd.astype(BF16), ahead, preferred_element_type=F32)[0:1, :]
    start = (chunks * BS).astype(F32) - from_here + odd_before
    null_place = jnp.where(odd > 0.0, start + each, -1.0)
    null_entry = (lane + 256 * sz.blocks).astype(F32)
    full = count + jnp.sum(odd).astype(jnp.int32)
    count_ref[0] = full

    def rank(c, unused):
        keys = key_row[pl.ds(c, 1), :]

        def below(k, total):
            lower = key_column[pl.ds(pl.multiple_of(k * BS, BS), BS), :] < keys
            return total + jnp.where(lower, 1.0, 0.0)

        past = (sub + 1).astype(F32) * 65536.0 <= keys
        total = lax.fori_loop(0, chunks, below, jnp.where(past, odd_column, 0.0))
        place[pl.ds(c, 1), :] = jnp.sum(total, axis=0, keepdims=True)
        return unused

    lax.fori_loop(0, chunks, rank, 0)

    def arrange(c, unused):
        slot = (sub + c * BS).astype(F32)

        def line(r, total):
            hit = place[pl.ds(r, 1), :] == slot
            return total + jnp.where(hit, entry_row[pl.ds(r, 1), :], 0.0)

        total = lax.fori_loop(0, chunks, line, jnp.where(null_place == slot, null_entry, 0.0))
        found = jnp.sum(total.T, axis=0, keepdims=True).astype(jnp.int32)
        out_ref[pl.ds(c, 1), :] = jnp.where(lane + c * BS < full, found, sz.own)
        return unused

    lax.fori_loop(0, jnp.maximum(lax.shift_right_logical(full + BS - 1, 7), 1), arrange, 0)


def entry_of(list_ref, k):
    entry = list_ref[k]
    return jnp.bitwise_and(entry, 255), lax.shift_right_logical(entry, 8)


def squared_of(features, others):
    return jnp.dot(features, others, preferred_element_type=F32)


def taper_of(squared):
    squared = jnp.maximum(squared, 1e-20)
    remain = jnp.maximum(4.0 - jnp.exp2(jnp.log(squared) * HALF_LOG2E), 0.0)
    twice = remain * remain
    return twice * twice * (5.0 - remain)


def kept_groups(sz, count, at):
    first = at * (sz.kept // UNROLL)
    last = jnp.minimum(lax.div(count + (UNROLL - 1), UNROLL), first + sz.kept // UNROLL)
    return first, jnp.maximum(first, last)


def vector_row(vec_ref, j):
    return vec_ref[pl.ds(jnp.minimum(j, vec_ref.shape[0] - 1), 1), :]


def own_features(lhs_ref, i):
    return lhs_ref[pl.ds(pl.multiple_of(i * BS, BS), BS), :DEPTH]


def other_features(rhs_ref, j):
    return rhs_ref[pl.ds(pl.multiple_of(j * DEPTH, DEPTH), DEPTH), :]


def clear(*accs):
    for acc in accs:
        acc[...] = jnp.zeros_like(acc)


def generate(sz, list_ref, count, lhs_ref, rhs_ref, tile_refs, squares):
    top = jnp.maximum(lax.div(count + (UNROLL - 1), UNROLL) - 1, 0)

    def squared(g, u):
        k = jnp.minimum(g, top) * UNROLL + u
        i, j = entry_of(list_ref, k)
        unused, twin = entry_of(list_ref, k + 1)
        both = jnp.concatenate([other_features(rhs_ref, j), other_features(rhs_ref, twin)], axis=1)
        return squared_of(own_features(lhs_ref, i), both)

    for u in range(0, UNROLL, 2):
        squares[u // 2 * BS : (u // 2 + 1) * BS, :] = squared(0, u)
    for at, tile_ref in enumerate(tile_refs):

        def group(g, unused, at=at, tile_ref=tile_ref):
            for u in range(0, UNROLL, 2):
                following = squared(g + 1, u)
                start = pl.multiple_of((g * UNROLL + u - at * sz.kept) * BS, BS)
                for r in range(0, BS, 8):
                    here = slice(u // 2 * BS + r, u // 2 * BS + r + 8)
                    tile_ref[pl.ds(start + r, 8), :] = taper_of(squares[here, :BS])
                    tile_ref[pl.ds(start + BS + r, 8), :] = taper_of(squares[here, BS:])
                    squares[here, :] = following[r : r + 8, :]
            return unused

        lax.fori_loop(*kept_groups(sz, count, at), group, 0)


def sweep(sz, list_ref, count, tile_refs, vec_ref, acc, acc_ones=None):
    accs = [acc] if acc_ones is None else [acc, acc_ones]
    clear(*accs)
    zero = jnp.zeros((8, BS), F32)
    carry = (jnp.int32(-1),) + ((zero,) * (BS // 8),) * len(accs)
    for at, tile_ref in enumerate(tile_refs):

        def group(g, carry, at=at, tile_ref=tile_ref):
            before, *totals = carry
            totals = [list(total) for total in totals]
            for u in range(0, UNROLL, 2):
                i, j = entry_of(list_ref, g * UNROLL + u)
                unused, twin = entry_of(list_ref, g * UNROLL + u + 1)
                keep = jnp.where(i == before, 1.0, 0.0)
                start = pl.multiple_of((g * UNROLL + u - at * sz.kept) * BS, BS)
                base = pl.multiple_of(i * BS, BS)
                row = jnp.broadcast_to(vector_row(vec_ref, j), (8, BS))
                twin_row = jnp.broadcast_to(vector_row(vec_ref, twin), (8, BS))
                for k in range(BS // 8):
                    tile = tile_ref[pl.ds(start + 8 * k, 8), :]
                    twin_tile = tile_ref[pl.ds(start + BS + 8 * k, 8), :]
                    for ref, total, term in zip(accs, totals, (tile * row + twin_tile * twin_row, tile + twin_tile)):
                        total[k] = total[k] * keep + term
                        ref[pl.ds(base + 8 * k, 8), :] = total[k]
                before = i
            return (before, *(tuple(total) for total in totals))

        carry = lax.fori_loop(*kept_groups(sz, count, at), group, carry)


def extras(sz, list_ref, count, vec_ref, acc, acc_ones, remake):
    def extra(k, unused):
        i, j = entry_of(list_ref, k)
        tile = taper_of(squared_of(*remake(i, j)))
        rows = pl.ds(pl.multiple_of(i * BS, BS), BS)
        acc[rows, :] += tile * vector_row(vec_ref, j)
        if acc_ones is not None:
            acc_ones[rows, :] += tile
        return unused

    kept = sz.kept * ARRAYS
    lax.fori_loop(kept, jnp.maximum(count, kept), extra, 0)


def finish(sz, acc, out_ref):
    unit = jnp.ones((8, BS), BF16)
    across = (((1,), (1,)), ((), ()))
    for i in range(sz.own):
        whole = acc[i * BS : (i + 1) * BS, :]
        high = whole.astype(BF16)
        low = (whole - high.astype(F32)).astype(BF16)
        y = lax.dot_general(unit, high, across, preferred_element_type=F32)
        y = y + lax.dot_general(unit, low, across, preferred_element_type=F32)
        out_ref[i : i + 1, :] = y[0:1, :] * sz.scale


def total_of(x):
    return jnp.sum(jnp.sum(x, axis=0, keepdims=True), axis=1, keepdims=True)


def place_block(piece_ref, part, first, rhs_ref):
    def one(k, unused):
        h, m, l = features_of([block_row(piece_ref, c, part, k) for c in range(3)], -2.0, 4, 3)
        feats = jnp.concatenate([h, m, h, m, l, h], axis=0).astype(BF16)
        rhs_ref[pl.ds(pl.multiple_of((first + k) * DEPTH, DEPTH), DEPTH), :] = feats
        return unused

    lax.fori_loop(0, part, one, 0, unroll=4)


def first_kernel(sz, *refs):
    list_ref, count_ref, lhs_ref, nugget_any, obs_any, home_ref = refs[:6]
    coord_refs = refs[6 : 6 + (sz.blks - 1) * sz.reps]
    refs = refs[6 + (sz.blks - 1) * sz.reps :]
    tile_refs = refs[:ARRAYS]
    spare_ref, obs_ref, diag_ref, mapped_ref, norm_ref = refs[ARRAYS : ARRAYS + 5]
    rhs_ref, acc, acc_ones, total_row, squares, nugget_ref, done, fetched = refs[ARRAYS + 5 :]
    blk, rep = lax.axis_index("blk"), lax.axis_index("rep")
    home = pl.ds(pl.multiple_of(blk * sz.local_blocks, 8), sz.local_blocks)
    fetch = pltpu.make_async_copy(nugget_any, nugget_ref, fetched.at[0])
    fetch_obs = pltpu.make_async_copy(obs_any, obs_ref.at[home, :], fetched.at[1])
    fetch.start()
    fetch_obs.start()
    for at, piece_ref in enumerate(coord_refs):
        code, turn = at // sz.reps + 1, at % sz.reps
        part = sz.local_blocks // sz.reps
        first = jnp.bitwise_xor(blk, code) * sz.local_blocks + jnp.bitwise_xor(rep, turn) * part
        first = pl.multiple_of(first, 8)
        place_block(piece_ref, part, first, rhs_ref)
        obs_ref[pl.ds(first, part), :] = piece_ref[3 * part : 4 * part, :]
    place_block(home_ref, sz.local_blocks, blk * sz.local_blocks, rhs_ref)
    far = lax.broadcasted_iota(jnp.int32, (DEPTH, BS), 0) == 3
    rhs_ref[sz.blocks * DEPTH :, :] = jnp.where(far, 1e6, 0.0).astype(BF16)
    count = count_ref[0]
    generate(sz, list_ref, count, lhs_ref, rhs_ref, tile_refs, squares)
    fetch_obs.wait()
    sweep(sz, list_ref, count, tile_refs, obs_ref, acc, acc_ones)
    extras(
        sz,
        list_ref,
        count,
        obs_ref,
        acc,
        acc_ones,
        lambda i, j: (own_features(lhs_ref, i), other_features(rhs_ref, j)),
    )

    @pl.when(count > sz.kept * ARRAYS)
    def save():
        copy = pltpu.make_async_copy(rhs_ref, spare_ref, done)
        copy.start()
        copy.wait()

    finish(sz, acc_ones, total_row)
    finish(sz, acc, mapped_ref)
    quarter = lax.axis_index("col") * sz.reps + rep
    own = pl.ds(pl.multiple_of(sz.me() * sz.own, 8), sz.own)
    fetch.wait()
    diag = nugget_ref[pl.ds(pl.multiple_of(quarter * sz.own, 8), sz.own), :] + total_row[...]
    diag_ref[...] = diag
    mapped_ref[...] += diag * obs_ref[own, :]
    norm_ref[...] = jnp.broadcast_to(total_of(obs_ref[...] * obs_ref[...]), (8, BS))


def step_kernel(sz, last, *refs):
    list_ref, count_ref, lhs_ref, spare_ref, diag_ref, norm_ref, field_ref, resid_ref, dirn_ref = refs[:9]
    pieces = refs[9 : 9 + sz.plane]
    tile_refs = refs[9 + sz.plane : 9 + sz.plane + ARRAYS]
    rest = refs[9 + sz.plane + ARRAYS :]
    mapped_ref, next_norm_ref, next_field_ref, next_resid_ref, next_dirn_ref = rest[:5]
    if last:
        dot_ref, dirn = rest[5:7]
    else:
        dirn = next_dirn_ref
    mapped, acc, features, others, done = rest[-5:]
    me = sz.me()
    assemble(sz, pieces, sz.own, mapped)
    norm = norm_ref[0:1, 0:1]
    step = norm / total_of(dirn_ref[...] * mapped[...])
    resid = resid_ref[...] - step * mapped[...]
    next_norm = total_of(resid * resid)
    dirn[...] = resid + (next_norm / norm) * dirn_ref[...]
    next_norm_ref[...] = jnp.broadcast_to(next_norm, (8, BS))
    home = pl.ds(pl.multiple_of(lax.axis_index("blk") * sz.local_blocks, 8), sz.local_blocks)
    own = pl.ds(pl.multiple_of(me * sz.own, 8), sz.own)
    field = step * dirn_ref[home, :]
    if last:
        next_field_ref[...] = field_ref[...] + field
        next_resid_ref[...] = resid_ref[home, :] - step * mapped[home, :]
        next_dirn_ref[...] = dirn[home, :]
    else:
        next_field_ref[...] = field
        next_resid_ref[...] = resid

    def remake(i, j):
        for source, start, size, target in ((lhs_ref, i, BS, features), (spare_ref, j, DEPTH, others)):
            copy = pltpu.make_async_copy(source.at[pl.ds(pl.multiple_of(start * size, size), size), :], target, done)
            copy.start()
            copy.wait()
        return features[:, :DEPTH], others[...]

    sweep(sz, list_ref, count_ref[0], tile_refs, dirn, acc)
    extras(sz, list_ref, count_ref[0], dirn, acc, None, remake)
    finish(sz, acc, mapped_ref)
    ours = mapped_ref[...] + diag_ref[...] * dirn[own, :]
    mapped_ref[...] = ours
    if last:
        dot_ref[...] = jnp.broadcast_to(total_of(ours * dirn[own, :]), dot_ref.shape)


def last_kernel(sz, *refs):
    norm_ref, field_ref, resid_ref, dirn_ref = refs[:4]
    pieces = refs[4 : 4 + sz.plane]
    out_field_ref, out_resid_ref = refs[4 + sz.plane :]
    product = jnp.zeros((8, BS), F32)
    for ref in pieces:
        for z in range(sz.blks):
            product = product + ref[sz.own + 8 * z : sz.own + 8 * (z + 1), :]
    step = norm_ref[0:1, :] / product[0:1, :]
    out_field_ref[...] = field_ref[...] + step * dirn_ref[...]
    quarter = lax.axis_index("col") * sz.reps + lax.axis_index("rep")
    for k, ref in enumerate(pieces):
        rows = pl.ds(pl.multiple_of(jnp.bitwise_xor(quarter, k) * sz.own, 8), sz.own)
        out_resid_ref[rows, :] = resid_ref[rows, :] - step * ref[: sz.own, :]


def call(kernel, mib, in_specs, shapes, out_specs, scratch, flops, *args):
    return pl.pallas_call(
        kernel,
        in_specs=in_specs,
        out_shape=shapes,
        out_specs=out_specs,
        scratch_shapes=scratch,
        compiler_params=pltpu.CompilerParams(vmem_limit_bytes=mib * MIB),
        cost_estimate=pl.CostEstimate(flops=flops, bytes_accessed=1 << 20, transcendentals=0),
    )(*args)


def array(*shape, dtype=F32):
    return jax.ShapeDtypeStruct(shape, dtype)


def local(coords, observations, nugget, tile_pairs, tile_live):
    sz = Sizes(observations.shape[0], tile_pairs.shape[1])
    own, blocks, home = sz.own, sz.blocks, sz.local_blocks
    alive = jnp.arange(sz.slots, dtype=jnp.int32) < tile_live[0]
    pairs = jnp.where(alive, tile_pairs, -1).reshape(2 * sz.slots // BS, BS)
    rep = lax.axis_index("rep")
    part = home // sz.reps
    obs_rows = observations.reshape(home, BS)
    rows = coords.reshape(3, home, BS)
    half = lax.dynamic_slice_in_dim(jnp.concatenate([rows, obs_rows[None]], axis=0), rep * part, part, axis=1)
    half = half.reshape(4 * part, BS)
    nears = [swap(half, "blk", z) for z in range(1, sz.blks)]
    pair_arrays = over_plane(along_blk(pairs))

    lhs = call(
        functools.partial(lhs_kernel, sz),
        12,
        [VMEM],
        array((own + 1) * BS, BS, dtype=BF16),
        VMEM,
        [],
        10_000_000,
        rows,
    )
    lines = 2 * sz.slots // BS * sz.devs
    table, count = call(
        functools.partial(list_kernel, sz),
        12,
        [VMEM] * sz.plane,
        (array(sz.capacity // BS, BS, dtype=jnp.int32), array(1, dtype=jnp.int32)),
        (VMEM, SMEM),
        [pltpu.VMEM((lines, BS), jnp.int32)] * 2
        + [pltpu.VMEM((lines, BS), F32)] * 2
        + [pltpu.VMEM((sz.capacity, BS), F32)]
        + [pltpu.VMEM((sz.capacity // BS, BS), F32)] * 2,
        10_000_000,
        *pair_arrays,
    )
    table, lhs, *nears = lax.optimization_barrier((table.reshape(sz.capacity), lhs, *nears))
    coord_arrays = []
    for near in nears:
        coord_arrays += [near] + [swap(near, "rep", r) for r in range(1, sz.reps)]
    tall = pltpu.VMEM(((own + 1) * BS, BS), F32)
    kept = [pltpu.VMEM((sz.kept * BS, BS), F32)] * ARRAYS
    *tiles, spare, obs, diag, mapped, norm = call(
        functools.partial(first_kernel, sz),
        sz.first_mib,
        [SMEM, SMEM, VMEM, ANY, ANY] + [VMEM] * (1 + len(coord_arrays)),
        kept
        + [
            pltpu.HBM(((blocks + 1) * DEPTH, BS), BF16),
            array(blocks, BS),
            array(own, BS),
            array(own, BS),
            array(8, BS),
        ],
        [VMEM] * ARRAYS + [ANY] + [VMEM] * 4,
        [
            pltpu.VMEM(((blocks + 1) * DEPTH, BS), BF16),
            tall,
            tall,
            pltpu.VMEM((own, BS), F32),
            pltpu.VMEM((UNROLL // 2 * BS, 2 * BS), F32),
            pltpu.VMEM((home, BS), F32),
            pltpu.SemaphoreType.DMA,
            pltpu.SemaphoreType.DMA((2,)),
        ],
        100_000_000,
        table,
        count,
        lhs,
        pltpu.with_memory_space_constraint(nugget.reshape(home, BS), pltpu.HBM),
        pltpu.with_memory_space_constraint(obs_rows, pltpu.HBM),
        rows,
        *coord_arrays,
    )
    tiles = [pltpu.with_memory_space_constraint(tile, pltpu.VMEM) for tile in tiles]
    spare = pltpu.with_memory_space_constraint(spare, pltpu.HBM)
    field, resid, dirn = norm, obs, obs
    for sweep_index in range(1, ITERS):
        last = sweep_index + 1 == ITERS
        span = home if last else blocks
        outs = [array(own, BS), array(8, BS), array(home, BS), array(span, BS), array(span, BS)]
        mapped, norm, field, resid, dirn, *dot = call(
            functools.partial(step_kernel, sz, last),
            8,
            [SMEM, SMEM, ANY, ANY] + [VMEM] * (5 + sz.plane + ARRAYS),
            outs + [array(8, BS)] * last,
            [VMEM] * (len(outs) + last),
            [pltpu.VMEM((blocks, BS), F32)] * (1 + last)
            + [tall, pltpu.VMEM((BS, BS), BF16), pltpu.VMEM((DEPTH, BS), BF16), pltpu.SemaphoreType.DMA],
            100_000_000,
            table,
            count,
            lhs,
            spare,
            diag,
            norm,
            field,
            resid,
            dirn,
            *over_plane(along_blk(mapped)),
            *tiles,
        )
    ends = over_plane(jnp.concatenate([mapped, along_blk(dot[0])], axis=0))
    field, resid = call(
        functools.partial(last_kernel, sz),
        4,
        [VMEM] * (4 + sz.plane),
        (array(home, BS), array(home, BS)),
        (VMEM, VMEM),
        [],
        100_000,
        norm,
        field,
        resid,
        dirn,
        *ends,
    )
    return field.reshape(sz.points), resid.reshape(sz.points)


def solution(mesh):
    in_specs = (
        P(None, ("grp", "blk")),
        P(("grp", "blk")),
        P(("grp", "blk")),
        P(None, ("grp", "blk", "col", "rep")),
        P(("grp", "blk", "col", "rep")),
    )
    out_specs = (P(("grp", "blk")), P(("grp", "blk")))
    return jax.shard_map(local, mesh=mesh, in_specs=in_specs, out_specs=out_specs, check_vma=False)
```

```python
import functools

import jax
import jax.numpy as jnp
from jax import lax
from jax.experimental import pallas as pl
from jax.experimental.pallas import tpu as pltpu
from jax.sharding import PartitionSpec as P

BS = 128
ITERS = 3
SUPPORT = 0.3
DEPTH = 48
UNROLL = 16
ARRAYS = 4
MIB = 1024 * 1024
VMEM = pl.BlockSpec(memory_space=pltpu.VMEM)
SMEM = pl.BlockSpec(memory_space=pltpu.SMEM)
ANY = pl.BlockSpec(memory_space=pl.ANY)
BF16 = jnp.bfloat16
F32 = jnp.float32


class Sizes:
    def __init__(self, points, slots):
        self.blks = lax.axis_size("blk")
        self.reps = lax.axis_size("rep")
        self.plane = lax.axis_size("col") * self.reps
        self.devs = self.blks * self.plane
        self.points = points
        self.slots = slots
        self.local_blocks = points // BS
        self.blocks = self.local_blocks * self.blks
        self.own = self.local_blocks // self.plane
        self.capacity = 2 * self.plane * slots + 1024
        per_row = slots * self.devs // self.blocks
        self.first_mib = 6 + self.blocks * DEPTH * BS * 2 // MIB
        self.kept = min(448, (48 - self.first_mib) * 16) // (ARRAYS * UNROLL) * UNROLL
        self.scale = 16.0 / (BS * per_row) / 256.0

    def me(self):
        return (lax.axis_index("blk") * lax.axis_size("col") + lax.axis_index("col")) * self.reps + lax.axis_index(
            "rep"
        )


def swap(x, axis, code):
    return lax.ppermute(x, axis, [(i, i ^ code) for i in range(lax.axis_size(axis))])


def along_blk(x):
    return jnp.concatenate([x] + [swap(x, "blk", k) for k in range(1, lax.axis_size("blk"))], axis=0)


def over_plane(x):
    reps = lax.axis_size("rep")
    found = {0: x}
    for c in range(1, lax.axis_size("col")):
        found[c * reps] = swap(x, "col", c)
    for start in sorted(found):
        for r in range(1, reps):
            found[start + r] = swap(found[start], "rep", r)
    return [found[k] for k in sorted(found)]


def assemble(sz, refs, rows, target):
    me = sz.me()
    for k, ref in enumerate(refs):
        for z in range(ref.shape[0] // rows):
            start = pl.multiple_of(jnp.bitwise_xor(me, z * sz.plane + k) * rows, 8)
            target[pl.ds(start, rows), :] = ref[z * rows : (z + 1) * rows, :]


def split3(x):
    high = x.astype(BF16).astype(F32)
    rest = x - high
    middle = rest.astype(BF16).astype(F32)
    return high, middle, rest - middle


def features_of(rows, factor, unit, norm):
    feature = lax.broadcasted_iota(jnp.int32, (8, BS), 0)
    x, y, z = ((row - 0.5) * (4.0 / SUPPORT) for row in rows)
    feats = jnp.where(feature == unit, 1.0, 0.0)
    for place, row in ((0, factor * x), (1, factor * y), (2, factor * z), (norm, x * x + y * y + z * z)):
        feats = jnp.where(feature == place, row, feats)
    return split3(feats)


def block_row(ref, c, part, k):
    return ref[c, pl.ds(k, 1), :] if len(ref.shape) == 3 else ref[pl.ds(c * part + k, 1), :]


def lhs_kernel(sz, home_ref, out_ref):
    quarter = lax.axis_index("col") * sz.reps + lax.axis_index("rep")
    for i in range(sz.own):
        h, m, l = features_of([block_row(home_ref, c, None, quarter * sz.own + i) for c in range(3)], 1.0, 3, 4)
        feats = jnp.concatenate([h, h, m, m, h, l, jnp.zeros((BS - DEPTH, BS), F32)], axis=0)
        out_ref[i * BS : (i + 1) * BS, :] = feats.T.astype(BF16)
    out_ref[sz.own * BS :, :] = jnp.zeros((BS, BS), BF16)


def list_kernel(sz, *refs):
    me = sz.me()
    out_ref, count_ref, target, other, place, value, key_column, key_row, entry_row = refs[sz.plane :]
    lines = sz.slots // BS
    at = 2 * lines * sz.devs
    for base in range(0, at, 2 * lines):
        pairs_ref = refs[base // (2 * lines * sz.blks)]
        start = base % (2 * lines * sz.blks)
        rows = pairs_ref[start : start + lines, :]
        cols = pairs_ref[start + lines : start + 2 * lines, :]
        target[base : base + lines, :] = rows
        other[base : base + lines, :] = cols
        target[base + lines : base + 2 * lines, :] = cols
        other[base + lines : base + 2 * lines, :] = rows
    local = target[...] - me * sz.own
    mine = jnp.logical_and(local >= 0, local < sz.own)
    flags = jnp.where(mine, 1.0, 0.0)
    a = lax.broadcasted_iota(jnp.int32, (BS, BS), 0)
    b = lax.broadcasted_iota(jnp.int32, (BS, BS), 1)
    ahead = jnp.where(a < b, 1.0, 0.0).astype(BF16)
    before = jnp.dot(flags.astype(BF16), ahead, preferred_element_type=F32)
    totals = jnp.broadcast_to(jnp.sum(flags, axis=1, keepdims=True), (at, BS))
    a = lax.broadcasted_iota(jnp.int32, (at, at), 0)
    b = lax.broadcasted_iota(jnp.int32, (at, at), 1)
    above = jnp.dot(jnp.where(b < a, 1.0, 0.0).astype(BF16), totals.astype(BF16), preferred_element_type=F32)
    place[...] = jnp.where(mine, above + before, -1.0)
    ends = jnp.sum(jnp.where(lax.broadcasted_iota(jnp.int32, (at, BS), 1) == 0, above + totals, 0.0), axis=1, keepdims=True)
    starts = ends - totals[:, 0:1]
    value[...] = (local + 256 * other[...]).astype(F32)
    count = jnp.sum(flags).astype(jnp.int32)
    sub = lax.broadcasted_iota(jnp.int32, (BS, BS), 0)
    lane = lax.broadcasted_iota(jnp.int32, (1, BS), 1)

    chunks = jnp.maximum(lax.shift_right_logical(count + BS - 1, 7), 1)

    def key_of(found, slot):
        entry = jnp.where(slot < count, found.astype(jnp.int32), sz.own)
        return entry.astype(F32), (jnp.bitwise_and(entry, 255) * 65536 + slot).astype(F32)

    def compact(c, unused):
        slot = (sub + c * BS).astype(F32)
        base = (c * BS).astype(F32)
        first = jnp.sum(jnp.where(ends <= base, 1.0, 0.0)).astype(jnp.int32)
        last = jnp.sum(jnp.where(starts < base + BS, 1.0, 0.0)).astype(jnp.int32)
        first = jnp.minimum(lax.shift_right_logical(first, 2), at // 4)
        last = lax.shift_right_logical(last + 3, 2)

        def lines(g, total):
            for u in range(4):
                r = 4 * g + u
                hit = place[pl.ds(r, 1), :] == slot
                total = jnp.where(hit, value[pl.ds(r, 1), :], total)
            return total

        total = lax.fori_loop(first, last, lines, jnp.zeros((BS, BS), F32))
        entry, key = key_of(jnp.sum(total.T, axis=0, keepdims=True), lane + c * BS)
        entry_row[pl.ds(c, 1), :] = entry
        key_row[pl.ds(c, 1), :] = key
        unused_entry, key = key_of(jnp.sum(total, axis=1, keepdims=True), sub[:, 0:1] + c * BS)
        key_column[pl.ds(pl.multiple_of(c * BS, BS), BS), :] = jnp.broadcast_to(key, (BS, BS))
        return unused

    lax.fori_loop(0, chunks, compact, 0)

    bound = lane.astype(F32) * 65536.0

    def tally(c, carry):
        keys = key_column[pl.ds(pl.multiple_of(c * BS, BS), BS), :]
        from_here, after = carry
        return from_here + jnp.where(keys >= bound, 1.0, 0.0), after + jnp.where(keys >= bound + 65536.0, 1.0, 0.0)

    zero = jnp.zeros((BS, BS), F32)
    from_here, after = lax.fori_loop(0, chunks, tally, (zero, zero))
    from_here = jnp.sum(from_here, axis=0, keepdims=True)
    each = from_here - jnp.sum(after, axis=0, keepdims=True)
    odd = each - 2.0 * jnp.floor(0.5 * each)
    pad = jnp.where(lane < sz.own, jnp.where(each == 0.0, 2.0, odd), 0.0)
    wide_pad = jnp.broadcast_to(pad, (BS, BS))
    pad_column = wide_pad.T
    pad_before = jnp.dot(wide_pad.astype(BF16), ahead, preferred_element_type=F32)[0:1, :]
    start = (chunks * BS).astype(F32) - from_here + pad_before
    null_places = (jnp.where(pad > 0.0, start + each, -1.0), jnp.where(pad > 1.0, start + 1.0, -1.0))
    null_entry = (lane + 256 * sz.blocks).astype(F32)
    full = count + jnp.sum(pad).astype(jnp.int32)
    count_ref[0] = full

    def rank(c, unused):
        keys = key_row[pl.ds(c, 1), :]

        def below(k, total):
            lower = key_column[pl.ds(pl.multiple_of(k * BS, BS), BS), :] < keys
            return total + jnp.where(lower, 1.0, 0.0)

        past = (sub + 1).astype(F32) * 65536.0 <= keys
        total = lax.fori_loop(0, chunks, below, jnp.where(past, pad_column, 0.0))
        place[pl.ds(c, 1), :] = jnp.sum(total, axis=0, keepdims=True)
        return unused

    lax.fori_loop(0, chunks, rank, 0)

    def arrange(c, unused):
        slot = (sub + c * BS).astype(F32)

        def line(r, total):
            hit = place[pl.ds(r, 1), :] == slot
            return total + jnp.where(hit, entry_row[pl.ds(r, 1), :], 0.0)

        nulls = jnp.logical_or(null_places[0] == slot, null_places[1] == slot)
        total = lax.fori_loop(0, chunks, line, jnp.where(nulls, null_entry, 0.0))
        found = jnp.sum(total.T, axis=0, keepdims=True).astype(jnp.int32)
        out_ref[pl.ds(c, 1), :] = jnp.where(lane + c * BS < full, found, sz.own)
        return unused

    lax.fori_loop(0, jnp.maximum(lax.shift_right_logical(full + BS - 1, 7), 1), arrange, 0)


def entry_of(list_ref, k):
    entry = list_ref[k]
    return jnp.bitwise_and(entry, 255), lax.shift_right_logical(entry, 8)


def squared_of(features, others):
    return jnp.dot(features, others, preferred_element_type=F32)


def taper_of(squared):
    squared = jnp.maximum(squared, 1e-20)
    remain = jnp.maximum(4.0 - squared * lax.rsqrt(squared), 0.0)
    twice = remain * remain
    return twice * twice * (5.0 - remain)


def kept_groups(sz, count, at):
    first = at * (sz.kept // UNROLL)
    last = jnp.minimum(lax.div(count + (UNROLL - 1), UNROLL), first + sz.kept // UNROLL)
    return first, jnp.maximum(first, last)


def vector_row(vec_ref, j):
    return vec_ref[pl.ds(jnp.minimum(j, vec_ref.shape[0] - 1), 1), :]


def own_features(lhs_ref, i):
    return lhs_ref[pl.ds(pl.multiple_of(i * BS, BS), BS), :DEPTH]


def other_features(rhs_ref, j):
    return rhs_ref[pl.ds(pl.multiple_of(j * DEPTH, DEPTH), DEPTH), :]


def generate(sz, list_ref, count, lhs_ref, rhs_ref, tile_refs, squares):
    top = jnp.maximum(lax.div(count + (UNROLL - 1), UNROLL) - 1, 0)

    def squared(g, u):
        k = jnp.minimum(g, top) * UNROLL + u
        i, j = entry_of(list_ref, k)
        unused, twin = entry_of(list_ref, k + 1)
        both = jnp.concatenate([other_features(rhs_ref, j), other_features(rhs_ref, twin)], axis=1)
        return squared_of(own_features(lhs_ref, i), both)

    for u in range(0, UNROLL, 2):
        squares[u // 2 * BS : (u // 2 + 1) * BS, :] = squared(0, u)
    for at, tile_ref in enumerate(tile_refs):

        def group(g, unused, at=at, tile_ref=tile_ref):
            for u in range(0, UNROLL, 2):
                following = squared(g + 1, u)
                start = pl.multiple_of((g * UNROLL + u - at * sz.kept) * BS, BS)
                for r in range(0, BS, 8):
                    here = slice(u // 2 * BS + r, u // 2 * BS + r + 8)
                    tile_ref[pl.ds(start + r, 8), :] = taper_of(squares[here, :BS])
                    tile_ref[pl.ds(start + BS + r, 8), :] = taper_of(squares[here, BS:])
                    squares[here, :] = following[r : r + 8, :]
            return unused

        lax.fori_loop(*kept_groups(sz, count, at), group, 0)


def sweep(sz, list_ref, count, tile_refs, vec_ref, acc, acc_ones=None):
    accs = [acc] if acc_ones is None else [acc, acc_ones]

    @pl.when(count > sz.kept * len(tile_refs))
    def some_targets_are_extra():
        for ref in accs:
            ref[...] = jnp.zeros_like(ref)

    zero = jnp.zeros((8, BS), F32)
    carry = (jnp.int32(-1),) + ((zero,) * (BS // 8),) * len(accs)
    for at, tile_ref in enumerate(tile_refs):

        def group(g, carry, at=at, tile_ref=tile_ref):
            before, *totals = carry
            totals = [list(total) for total in totals]
            for u in range(0, UNROLL, 2):
                i, j = entry_of(list_ref, g * UNROLL + u)
                unused, twin = entry_of(list_ref, g * UNROLL + u + 1)
                keep = jnp.where(i == before, 1.0, 0.0)
                start = pl.multiple_of((g * UNROLL + u - at * sz.kept) * BS, BS)
                base = pl.multiple_of(i * BS, BS)
                row = jnp.broadcast_to(vector_row(vec_ref, j), (8, BS))
                twin_row = jnp.broadcast_to(vector_row(vec_ref, twin), (8, BS))
                for k in range(BS // 8):
                    tile = tile_ref[pl.ds(start + 8 * k, 8), :]
                    twin_tile = tile_ref[pl.ds(start + BS + 8 * k, 8), :]
                    for ref, total, term in zip(accs, totals, (tile * row + twin_tile * twin_row, tile + twin_tile)):
                        total[k] = total[k] * keep + term
                        ref[pl.ds(base + 8 * k, 8), :] = total[k]
                before = i
            return (before, *(tuple(total) for total in totals))

        carry = lax.fori_loop(*kept_groups(sz, count, at), group, carry)


def extras(sz, list_ref, count, vec_ref, acc, acc_ones, remake):
    def extra(k, unused):
        i, j = entry_of(list_ref, k)
        tile = taper_of(squared_of(*remake(i, j)))
        rows = pl.ds(pl.multiple_of(i * BS, BS), BS)
        acc[rows, :] += tile * vector_row(vec_ref, j)
        if acc_ones is not None:
            acc_ones[rows, :] += tile
        return unused

    kept = sz.kept * ARRAYS
    lax.fori_loop(kept, jnp.maximum(count, kept), extra, 0)


def finish(sz, acc, out_ref):
    unit = jnp.ones((8, BS), BF16)
    across = (((1,), (1,)), ((), ()))
    for i in range(sz.own):
        whole = acc[i * BS : (i + 1) * BS, :]
        high = whole.astype(BF16)
        low = (whole - high.astype(F32)).astype(BF16)
        y = lax.dot_general(unit, high, across, preferred_element_type=F32)
        y = y + lax.dot_general(unit, low, across, preferred_element_type=F32)
        out_ref[i : i + 1, :] = y[0:1, :] * sz.scale


def total_of(x):
    return jnp.sum(jnp.sum(x, axis=0, keepdims=True), axis=1, keepdims=True)


def place_block(piece_ref, part, first, rhs_ref):
    def one(k, unused):
        h, m, l = features_of([block_row(piece_ref, c, part, k) for c in range(3)], -2.0, 4, 3)
        feats = jnp.concatenate([h, m, h, m, l, h], axis=0).astype(BF16)
        rhs_ref[pl.ds(pl.multiple_of((first + k) * DEPTH, DEPTH), DEPTH), :] = feats
        return unused

    lax.fori_loop(0, part, one, 0, unroll=4)


def first_kernel(sz, *refs):
    list_ref, count_ref, lhs_ref, nugget_any, obs_any, home_ref = refs[:6]
    coord_refs = refs[6 : 6 + (sz.blks - 1) * sz.reps]
    refs = refs[6 + (sz.blks - 1) * sz.reps :]
    tile_refs = refs[:ARRAYS]
    spare_ref, obs_ref, diag_ref, mapped_ref, norm_ref = refs[ARRAYS : ARRAYS + 5]
    rhs_ref, acc, acc_ones, total_row, squares, nugget_ref, done, fetched = refs[ARRAYS + 5 :]
    blk, rep = lax.axis_index("blk"), lax.axis_index("rep")
    home = pl.ds(pl.multiple_of(blk * sz.local_blocks, 8), sz.local_blocks)
    fetch = pltpu.make_async_copy(nugget_any, nugget_ref, fetched.at[0])
    fetch_obs = pltpu.make_async_copy(obs_any, obs_ref.at[home, :], fetched.at[1])
    fetch.start()
    fetch_obs.start()
    for at, piece_ref in enumerate(coord_refs):
        code, turn = at // sz.reps + 1, at % sz.reps
        part = sz.local_blocks // sz.reps
        first = jnp.bitwise_xor(blk, code) * sz.local_blocks + jnp.bitwise_xor(rep, turn) * part
        first = pl.multiple_of(first, 8)
        place_block(piece_ref, part, first, rhs_ref)
        obs_ref[pl.ds(first, part), :] = piece_ref[3 * part : 4 * part, :]
    place_block(home_ref, sz.local_blocks, blk * sz.local_blocks, rhs_ref)
    far = lax.broadcasted_iota(jnp.int32, (DEPTH, BS), 0) == 3
    rhs_ref[sz.blocks * DEPTH :, :] = jnp.where(far, 1e6, 0.0).astype(BF16)
    count = count_ref[0]
    generate(sz, list_ref, count, lhs_ref, rhs_ref, tile_refs, squares)
    fetch_obs.wait()
    sweep(sz, list_ref, count, tile_refs, obs_ref, acc, acc_ones)
    extras(
        sz,
        list_ref,
        count,
        obs_ref,
        acc,
        acc_ones,
        lambda i, j: (own_features(lhs_ref, i), other_features(rhs_ref, j)),
    )

    @pl.when(count > sz.kept * ARRAYS)
    def save():
        copy = pltpu.make_async_copy(rhs_ref, spare_ref, done)
        copy.start()
        copy.wait()

    finish(sz, acc_ones, total_row)
    finish(sz, acc, mapped_ref)
    quarter = lax.axis_index("col") * sz.reps + rep
    own = pl.ds(pl.multiple_of(sz.me() * sz.own, 8), sz.own)
    fetch.wait()
    diag = nugget_ref[pl.ds(pl.multiple_of(quarter * sz.own, 8), sz.own), :] + total_row[...]
    diag_ref[...] = diag
    mapped_ref[...] += diag * obs_ref[own, :]
    norm_ref[...] = jnp.broadcast_to(total_of(obs_ref[...] * obs_ref[...]), (8, BS))


def step_kernel(sz, last, *refs):
    list_ref, count_ref, lhs_ref, spare_ref, diag_ref, norm_ref, field_ref, resid_ref, dirn_ref = refs[:9]
    pieces = refs[9 : 9 + sz.plane]
    tile_refs = refs[9 + sz.plane : 9 + sz.plane + ARRAYS]
    rest = refs[9 + sz.plane + ARRAYS :]
    mapped_ref, next_norm_ref, next_field_ref, next_resid_ref, next_dirn_ref = rest[:5]
    if last:
        dot_ref, dirn = rest[5:7]
    else:
        dirn = next_dirn_ref
    mapped, acc, features, others, done = rest[-5:]
    me = sz.me()
    assemble(sz, pieces, sz.own, mapped)
    norm = norm_ref[0:1, 0:1]
    step = norm / total_of(dirn_ref[...] * mapped[...])
    resid = resid_ref[...] - step * mapped[...]
    next_norm = total_of(resid * resid)
    dirn[...] = resid + (next_norm / norm) * dirn_ref[...]
    next_norm_ref[...] = jnp.broadcast_to(next_norm, (8, BS))
    home = pl.ds(pl.multiple_of(lax.axis_index("blk") * sz.local_blocks, 8), sz.local_blocks)
    own = pl.ds(pl.multiple_of(me * sz.own, 8), sz.own)
    field = step * dirn_ref[home, :]
    if last:
        next_field_ref[...] = field_ref[...] + field
        next_resid_ref[...] = resid_ref[home, :] - step * mapped[home, :]
        next_dirn_ref[...] = dirn[home, :]
    else:
        next_field_ref[...] = field
        next_resid_ref[...] = resid

    def remake(i, j):
        for source, start, size, target in ((lhs_ref, i, BS, features), (spare_ref, j, DEPTH, others)):
            copy = pltpu.make_async_copy(source.at[pl.ds(pl.multiple_of(start * size, size), size), :], target, done)
            copy.start()
            copy.wait()
        return features[:, :DEPTH], others[...]

    sweep(sz, list_ref, count_ref[0], tile_refs, dirn, acc)
    extras(sz, list_ref, count_ref[0], dirn, acc, None, remake)
    finish(sz, acc, mapped_ref)
    ours = mapped_ref[...] + diag_ref[...] * dirn[own, :]
    mapped_ref[...] = ours
    if last:
        dot_ref[...] = jnp.broadcast_to(total_of(ours * dirn[own, :]), dot_ref.shape)


def last_kernel(sz, *refs):
    norm_ref, field_ref, resid_ref, dirn_ref = refs[:4]
    pieces = refs[4 : 4 + sz.plane]
    out_field_ref, out_resid_ref = refs[4 + sz.plane :]
    product = jnp.zeros((8, BS), F32)
    for ref in pieces:
        for z in range(sz.blks):
            product = product + ref[sz.own + 8 * z : sz.own + 8 * (z + 1), :]
    step = norm_ref[0:1, :] / product[0:1, :]
    out_field_ref[...] = field_ref[...] + step * dirn_ref[...]
    quarter = lax.axis_index("col") * sz.reps + lax.axis_index("rep")
    for k, ref in enumerate(pieces):
        rows = pl.ds(pl.multiple_of(jnp.bitwise_xor(quarter, k) * sz.own, 8), sz.own)
        out_resid_ref[rows, :] = resid_ref[rows, :] - step * ref[: sz.own, :]


def call(kernel, mib, in_specs, shapes, out_specs, scratch, flops, *args):
    return pl.pallas_call(
        kernel,
        in_specs=in_specs,
        out_shape=shapes,
        out_specs=out_specs,
        scratch_shapes=scratch,
        compiler_params=pltpu.CompilerParams(vmem_limit_bytes=mib * MIB),
        cost_estimate=pl.CostEstimate(flops=flops, bytes_accessed=1 << 20, transcendentals=0),
    )(*args)


def array(*shape, dtype=F32):
    return jax.ShapeDtypeStruct(shape, dtype)


def local(coords, observations, nugget, tile_pairs, tile_live):
    sz = Sizes(observations.shape[0], tile_pairs.shape[1])
    own, blocks, home = sz.own, sz.blocks, sz.local_blocks
    alive = jnp.arange(sz.slots, dtype=jnp.int32) < tile_live[0]
    pairs = jnp.where(alive, tile_pairs, -1).reshape(2 * sz.slots // BS, BS)
    rep = lax.axis_index("rep")
    part = home // sz.reps
    obs_rows = observations.reshape(home, BS)
    rows = coords.reshape(3, home, BS)
    half = lax.dynamic_slice_in_dim(jnp.concatenate([rows, obs_rows[None]], axis=0), rep * part, part, axis=1)
    half = half.reshape(4 * part, BS)
    nears = [swap(half, "blk", z) for z in range(1, sz.blks)]
    pair_arrays = over_plane(along_blk(pairs))

    lhs = call(
        functools.partial(lhs_kernel, sz),
        12,
        [VMEM],
        array((own + 1) * BS, BS, dtype=BF16),
        VMEM,
        [],
        10_000_000,
        rows,
    )
    lines = 2 * sz.slots // BS * sz.devs
    table, count = call(
        functools.partial(list_kernel, sz),
        12,
        [VMEM] * sz.plane,
        (array(sz.capacity // BS, BS, dtype=jnp.int32), array(1, dtype=jnp.int32)),
        (VMEM, SMEM),
        [pltpu.VMEM((lines, BS), jnp.int32)] * 2
        + [pltpu.VMEM((lines, BS), F32)] * 2
        + [pltpu.VMEM((sz.capacity, BS), F32)]
        + [pltpu.VMEM((sz.capacity // BS, BS), F32)] * 2,
        10_000_000,
        *pair_arrays,
    )
    table, lhs, *nears = lax.optimization_barrier((table.reshape(sz.capacity), lhs, *nears))
    coord_arrays = []
    for near in nears:
        coord_arrays += [near] + [swap(near, "rep", r) for r in range(1, sz.reps)]
    tall = pltpu.VMEM(((own + 1) * BS, BS), F32)
    kept = [pltpu.VMEM((sz.kept * BS, BS), F32)] * ARRAYS
    *tiles, spare, obs, diag, mapped, norm = call(
        functools.partial(first_kernel, sz),
        sz.first_mib,
        [SMEM, SMEM, VMEM, ANY, ANY] + [VMEM] * (1 + len(coord_arrays)),
        kept
        + [
            pltpu.HBM(((blocks + 1) * DEPTH, BS), BF16),
            array(blocks, BS),
            array(own, BS),
            array(own, BS),
            array(8, BS),
        ],
        [VMEM] * ARRAYS + [ANY] + [VMEM] * 4,
        [
            pltpu.VMEM(((blocks + 1) * DEPTH, BS), BF16),
            tall,
            tall,
            pltpu.VMEM((own, BS), F32),
            pltpu.VMEM((UNROLL // 2 * BS, 2 * BS), F32),
            pltpu.VMEM((home, BS), F32),
            pltpu.SemaphoreType.DMA,
            pltpu.SemaphoreType.DMA((2,)),
        ],
        100_000_000,
        table,
        count,
        lhs,
        pltpu.with_memory_space_constraint(nugget.reshape(home, BS), pltpu.HBM),
        pltpu.with_memory_space_constraint(obs_rows, pltpu.HBM),
        rows,
        *coord_arrays,
    )
    tiles = [pltpu.with_memory_space_constraint(tile, pltpu.VMEM) for tile in tiles]
    spare = pltpu.with_memory_space_constraint(spare, pltpu.HBM)
    field, resid, dirn = norm, obs, obs
    for sweep_index in range(1, ITERS):
        last = sweep_index + 1 == ITERS
        span = home if last else blocks
        outs = [array(own, BS), array(8, BS), array(home, BS), array(span, BS), array(span, BS)]
        mapped, norm, field, resid, dirn, *dot = call(
            functools.partial(step_kernel, sz, last),
            8,
            [SMEM, SMEM, ANY, ANY] + [VMEM] * (5 + sz.plane + ARRAYS),
            outs + [array(8, BS)] * last,
            [VMEM] * (len(outs) + last),
            [pltpu.VMEM((blocks, BS), F32)] * (1 + last)
            + [tall, pltpu.VMEM((BS, BS), BF16), pltpu.VMEM((DEPTH, BS), BF16), pltpu.SemaphoreType.DMA],
            100_000_000,
            table,
            count,
            lhs,
            spare,
            diag,
            norm,
            field,
            resid,
            dirn,
            *over_plane(along_blk(mapped)),
            *tiles,
        )
    ends = over_plane(jnp.concatenate([mapped, along_blk(dot[0])], axis=0))
    field, resid = call(
        functools.partial(last_kernel, sz),
        4,
        [VMEM] * (4 + sz.plane),
        (array(home, BS), array(home, BS)),
        (VMEM, VMEM),
        [],
        100_000,
        norm,
        field,
        resid,
        dirn,
        *ends,
    )
    return field.reshape(sz.points), resid.reshape(sz.points)


def solution(mesh):
    in_specs = (
        P(None, ("grp", "blk")),
        P(("grp", "blk")),
        P(("grp", "blk")),
        P(None, ("grp", "blk", "col", "rep")),
        P(("grp", "blk", "col", "rep")),
    )
    out_specs = (P(("grp", "blk")), P(("grp", "blk")))
    return jax.shard_map(local, mesh=mesh, in_specs=in_specs, out_specs=out_specs, check_vma=False)
```

```python
import functools

import jax
import jax.numpy as jnp
from jax import lax
from jax.experimental import pallas as pl
from jax.experimental.pallas import tpu as pltpu
from jax.sharding import PartitionSpec as P

BS = 128
ITERS = 3
SUPPORT = 0.3
DEPTH = 48
UNROLL = 16
ARRAYS = 4
MIB = 1024 * 1024
VMEM = pl.BlockSpec(memory_space=pltpu.VMEM)
SMEM = pl.BlockSpec(memory_space=pltpu.SMEM)
ANY = pl.BlockSpec(memory_space=pl.ANY)
BF16 = jnp.bfloat16
F32 = jnp.float32


class Sizes:
    def __init__(self, points, slots):
        self.blks = lax.axis_size("blk")
        self.reps = lax.axis_size("rep")
        self.plane = lax.axis_size("col") * self.reps
        self.devs = self.blks * self.plane
        self.points = points
        self.slots = slots
        self.local_blocks = points // BS
        self.blocks = self.local_blocks * self.blks
        self.own = self.local_blocks // self.plane
        self.capacity = 2 * self.plane * slots + 1024
        per_row = slots * self.devs // self.blocks
        self.first_mib = 6 + self.blocks * DEPTH * BS * 2 // MIB
        self.kept = min(448, (48 - self.first_mib) * 16) // (ARRAYS * UNROLL) * UNROLL
        self.scale = 16.0 / (BS * per_row) / 256.0

    def me(self):
        return (lax.axis_index("blk") * lax.axis_size("col") + lax.axis_index("col")) * self.reps + lax.axis_index(
            "rep"
        )


def swap(x, axis, code):
    return lax.ppermute(x, axis, [(i, i ^ code) for i in range(lax.axis_size(axis))])


def along_blk(x):
    return jnp.concatenate([x] + [swap(x, "blk", k) for k in range(1, lax.axis_size("blk"))], axis=0)


def over_plane(x):
    reps = lax.axis_size("rep")
    found = {0: x}
    for c in range(1, lax.axis_size("col")):
        found[c * reps] = swap(x, "col", c)
    for start in sorted(found):
        for r in range(1, reps):
            found[start + r] = swap(found[start], "rep", r)
    return [found[k] for k in sorted(found)]


def assemble(sz, refs, rows, target):
    me = sz.me()
    for k, ref in enumerate(refs):
        for z in range(ref.shape[0] // rows):
            start = pl.multiple_of(jnp.bitwise_xor(me, z * sz.plane + k) * rows, 8)
            target[pl.ds(start, rows), :] = ref[z * rows : (z + 1) * rows, :]


def split3(x):
    high = x.astype(BF16).astype(F32)
    rest = x - high
    middle = rest.astype(BF16).astype(F32)
    return high, middle, rest - middle


def features_of(rows, factor, unit, norm):
    feature = lax.broadcasted_iota(jnp.int32, (8, BS), 0)
    x, y, z = ((row - 0.5) * (4.0 / SUPPORT) for row in rows)
    feats = jnp.where(feature == unit, 1.0, 0.0)
    for place, row in ((0, factor * x), (1, factor * y), (2, factor * z), (norm, x * x + y * y + z * z)):
        feats = jnp.where(feature == place, row, feats)
    return split3(feats)


def block_row(ref, c, part, k):
    return ref[c, pl.ds(k, 1), :] if len(ref.shape) == 3 else ref[pl.ds(c * part + k, 1), :]


def lhs_kernel(sz, home_ref, out_ref):
    quarter = lax.axis_index("col") * sz.reps + lax.axis_index("rep")
    for i in range(sz.own):
        h, m, l = features_of([block_row(home_ref, c, None, quarter * sz.own + i) for c in range(3)], 1.0, 3, 4)
        feats = jnp.concatenate([h, h, m, m, h, l, jnp.zeros((BS - DEPTH, BS), F32)], axis=0)
        out_ref[i * BS : (i + 1) * BS, :] = feats.T.astype(BF16)
    out_ref[sz.own * BS :, :] = jnp.zeros((BS, BS), BF16)


def list_kernel(sz, *refs):
    me = sz.me()
    out_ref, count_ref, target, other, place, value, key_column, key_row, entry_row = refs[sz.plane :]
    lines = sz.slots // BS
    at = 2 * lines * sz.devs
    for base in range(0, at, 2 * lines):
        pairs_ref = refs[base // (2 * lines * sz.blks)]
        start = base % (2 * lines * sz.blks)
        rows = pairs_ref[start : start + lines, :]
        cols = pairs_ref[start + lines : start + 2 * lines, :]
        target[base : base + lines, :] = rows
        other[base : base + lines, :] = cols
        target[base + lines : base + 2 * lines, :] = cols
        other[base + lines : base + 2 * lines, :] = rows
    local = target[...] - me * sz.own
    mine = jnp.logical_and(local >= 0, local < sz.own)
    flags = jnp.where(mine, 1.0, 0.0)
    a = lax.broadcasted_iota(jnp.int32, (BS, BS), 0)
    b = lax.broadcasted_iota(jnp.int32, (BS, BS), 1)
    ahead = jnp.where(a < b, 1.0, 0.0).astype(BF16)
    before = jnp.dot(flags.astype(BF16), ahead, preferred_element_type=F32)
    totals = jnp.broadcast_to(jnp.sum(flags, axis=1, keepdims=True), (at, BS))
    a = lax.broadcasted_iota(jnp.int32, (at, at), 0)
    b = lax.broadcasted_iota(jnp.int32, (at, at), 1)
    above = jnp.dot(jnp.where(b < a, 1.0, 0.0).astype(BF16), totals.astype(BF16), preferred_element_type=F32)
    place[...] = jnp.where(mine, above + before, -1.0)
    ends = jnp.sum(jnp.where(lax.broadcasted_iota(jnp.int32, (at, BS), 1) == 0, above + totals, 0.0), axis=1, keepdims=True)
    starts = ends - totals[:, 0:1]
    value[...] = (local + 256 * other[...]).astype(F32)
    count = jnp.sum(flags).astype(jnp.int32)
    sub = lax.broadcasted_iota(jnp.int32, (BS, BS), 0)
    lane = lax.broadcasted_iota(jnp.int32, (1, BS), 1)

    chunks = jnp.maximum(lax.shift_right_logical(count + BS - 1, 7), 1)

    def key_of(found, slot):
        entry = jnp.where(slot < count, found.astype(jnp.int32), sz.own)
        return entry.astype(F32), (jnp.bitwise_and(entry, 255) * 65536 + slot).astype(F32)

    def compact(c, unused):
        slot = (sub + c * BS).astype(F32)
        base = (c * BS).astype(F32)
        first = jnp.sum(jnp.where(ends <= base, 1.0, 0.0)).astype(jnp.int32)
        last = jnp.sum(jnp.where(starts < base + BS, 1.0, 0.0)).astype(jnp.int32)
        first = jnp.minimum(lax.shift_right_logical(first, 2), at // 4)
        last = lax.shift_right_logical(last + 3, 2)

        def lines(g, total):
            for u in range(4):
                r = 4 * g + u
                hit = place[pl.ds(r, 1), :] == slot
                total = jnp.where(hit, value[pl.ds(r, 1), :], total)
            return total

        total = lax.fori_loop(first, last, lines, jnp.zeros((BS, BS), F32))
        entry, key = key_of(jnp.sum(total.T, axis=0, keepdims=True), lane + c * BS)
        entry_row[pl.ds(c, 1), :] = entry
        key_row[pl.ds(c, 1), :] = key
        unused_entry, key = key_of(jnp.sum(total, axis=1, keepdims=True), sub[:, 0:1] + c * BS)
        key_column[pl.ds(pl.multiple_of(c * BS, BS), BS), :] = jnp.broadcast_to(key, (BS, BS))
        return unused

    lax.fori_loop(0, chunks, compact, 0)

    bound = lane.astype(F32) * 65536.0

    def tally(c, carry):
        keys = key_column[pl.ds(pl.multiple_of(c * BS, BS), BS), :]
        from_here, after = carry
        return from_here + jnp.where(keys >= bound, 1.0, 0.0), after + jnp.where(keys >= bound + 65536.0, 1.0, 0.0)

    zero = jnp.zeros((BS, BS), F32)
    from_here, after = lax.fori_loop(0, chunks, tally, (zero, zero))
    from_here = jnp.sum(from_here, axis=0, keepdims=True)
    each = from_here - jnp.sum(after, axis=0, keepdims=True)
    odd = each - 2.0 * jnp.floor(0.5 * each)
    pad = jnp.where(lane < sz.own, jnp.where(each == 0.0, 2.0, odd), 0.0)
    wide_pad = jnp.broadcast_to(pad, (BS, BS))
    pad_column = wide_pad.T
    pad_before = jnp.dot(wide_pad.astype(BF16), ahead, preferred_element_type=F32)[0:1, :]
    start = (chunks * BS).astype(F32) - from_here + pad_before
    null_places = (jnp.where(pad > 0.0, start + each, -1.0), jnp.where(pad > 1.0, start + 1.0, -1.0))
    null_entry = (lane + 256 * sz.blocks).astype(F32)
    full = count + jnp.sum(pad).astype(jnp.int32)
    count_ref[0] = full

    def rank(c, unused):
        keys = key_row[pl.ds(c, 1), :]

        def below(k, total):
            lower = key_column[pl.ds(pl.multiple_of(k * BS, BS), BS), :] < keys
            return total + jnp.where(lower, 1.0, 0.0)

        past = (sub + 1).astype(F32) * 65536.0 <= keys
        total = lax.fori_loop(0, chunks, below, jnp.where(past, pad_column, 0.0))
        place[pl.ds(c, 1), :] = jnp.sum(total, axis=0, keepdims=True)
        return unused

    lax.fori_loop(0, chunks, rank, 0)

    def arrange(c, unused):
        slot = (sub + c * BS).astype(F32)

        def line(r, total):
            hit = place[pl.ds(r, 1), :] == slot
            return total + jnp.where(hit, entry_row[pl.ds(r, 1), :], 0.0)

        nulls = jnp.logical_or(null_places[0] == slot, null_places[1] == slot)
        total = lax.fori_loop(0, chunks, line, jnp.where(nulls, null_entry, 0.0))
        found = jnp.sum(total.T, axis=0, keepdims=True).astype(jnp.int32)
        out_ref[pl.ds(c, 1), :] = jnp.where(lane + c * BS < full, found, sz.own)
        return unused

    lax.fori_loop(0, jnp.maximum(lax.shift_right_logical(full + BS - 1, 7), 1), arrange, 0)


def entry_of(list_ref, k):
    entry = list_ref[k]
    return jnp.bitwise_and(entry, 255), lax.shift_right_logical(entry, 8)


def squared_of(features, others):
    return jnp.dot(features, others, preferred_element_type=F32)


def taper_of(squared):
    squared = jnp.maximum(squared, 1e-20)
    remain = jnp.maximum(4.0 - squared * lax.rsqrt(squared), 0.0)
    twice = remain * remain
    return twice * twice * (5.0 - remain)


def kept_groups(sz, count, at):
    first = at * (sz.kept // UNROLL)
    last = jnp.minimum(lax.div(count + (UNROLL - 1), UNROLL), first + sz.kept // UNROLL)
    return first, jnp.maximum(first, last)


def vector_row(vec_ref, j):
    return vec_ref[pl.ds(jnp.minimum(j, vec_ref.shape[0] - 1), 1), :]


def own_features(lhs_ref, i):
    return lhs_ref[pl.ds(pl.multiple_of(i * BS, BS), BS), :DEPTH]


def other_features(rhs_ref, j):
    return rhs_ref[pl.ds(pl.multiple_of(j * DEPTH, DEPTH), DEPTH), :]


def clear_if_extra(sz, count, accs):
    @pl.when(count > sz.kept * ARRAYS)
    def clear():
        for ref in accs:
            ref[...] = jnp.zeros_like(ref)


def generate(sz, list_ref, count, lhs_ref, rhs_ref, tile_refs, squares, vec_ref, acc, acc_ones):
    clear_if_extra(sz, count, (acc, acc_ones))
    top = jnp.maximum(lax.div(count + (UNROLL - 1), UNROLL) - 1, 0)

    def squared(g, u):
        k = jnp.minimum(g, top) * UNROLL + u
        i, j = entry_of(list_ref, k)
        unused, twin = entry_of(list_ref, k + 1)
        both = jnp.concatenate([other_features(rhs_ref, j), other_features(rhs_ref, twin)], axis=1)
        return squared_of(own_features(lhs_ref, i), both)

    for u in range(0, UNROLL, 2):
        squares[u // 2 * BS : (u // 2 + 1) * BS, :] = squared(0, u)
    zero = jnp.zeros((8, BS), F32)
    carry = (jnp.int32(-1), (zero,) * (BS // 8), (zero,) * (BS // 8))
    for at, tile_ref in enumerate(tile_refs):

        def group(g, carry, at=at, tile_ref=tile_ref):
            before, totals, ones = carry
            totals, ones = list(totals), list(ones)
            for u in range(0, UNROLL, 2):
                following = squared(g + 1, u)
                i, j = entry_of(list_ref, g * UNROLL + u)
                unused, twin = entry_of(list_ref, g * UNROLL + u + 1)
                keep = jnp.where(i == before, 1.0, 0.0)
                before = i
                start = pl.multiple_of((g * UNROLL + u - at * sz.kept) * BS, BS)
                base = pl.multiple_of(i * BS, BS)
                row = jnp.broadcast_to(vector_row(vec_ref, j), (8, BS))
                twin_row = jnp.broadcast_to(vector_row(vec_ref, twin), (8, BS))
                for k in range(BS // 8):
                    r = 8 * k
                    here = slice(u // 2 * BS + r, u // 2 * BS + r + 8)
                    tile = taper_of(squares[here, :BS])
                    twin_tile = taper_of(squares[here, BS:])
                    tile_ref[pl.ds(start + r, 8), :] = tile
                    tile_ref[pl.ds(start + BS + r, 8), :] = twin_tile
                    squares[here, :] = following[r : r + 8, :]
                    totals[k] = totals[k] * keep + (tile * row + twin_tile * twin_row)
                    ones[k] = ones[k] * keep + (tile + twin_tile)
                    acc[pl.ds(base + r, 8), :] = totals[k]
                    acc_ones[pl.ds(base + r, 8), :] = ones[k]
            return before, tuple(totals), tuple(ones)

        carry = lax.fori_loop(*kept_groups(sz, count, at), group, carry)


def sweep(sz, list_ref, count, tile_refs, vec_ref, acc):
    clear_if_extra(sz, count, (acc,))
    zero = jnp.zeros((8, BS), F32)
    carry = (jnp.int32(-1), (zero,) * (BS // 8))
    for at, tile_ref in enumerate(tile_refs):

        def group(g, carry, at=at, tile_ref=tile_ref):
            before, totals = carry
            totals = list(totals)
            for u in range(0, UNROLL, 2):
                i, j = entry_of(list_ref, g * UNROLL + u)
                unused, twin = entry_of(list_ref, g * UNROLL + u + 1)
                keep = jnp.where(i == before, 1.0, 0.0)
                before = i
                start = pl.multiple_of((g * UNROLL + u - at * sz.kept) * BS, BS)
                base = pl.multiple_of(i * BS, BS)
                row = jnp.broadcast_to(vector_row(vec_ref, j), (8, BS))
                twin_row = jnp.broadcast_to(vector_row(vec_ref, twin), (8, BS))
                for k in range(BS // 8):
                    tile = tile_ref[pl.ds(start + 8 * k, 8), :]
                    twin_tile = tile_ref[pl.ds(start + BS + 8 * k, 8), :]
                    totals[k] = totals[k] * keep + (tile * row + twin_tile * twin_row)
                    acc[pl.ds(base + 8 * k, 8), :] = totals[k]
            return before, tuple(totals)

        carry = lax.fori_loop(*kept_groups(sz, count, at), group, carry)


def extras(sz, list_ref, count, vec_ref, acc, acc_ones, remake):
    def extra(k, unused):
        i, j = entry_of(list_ref, k)
        tile = taper_of(squared_of(*remake(i, j)))
        rows = pl.ds(pl.multiple_of(i * BS, BS), BS)
        acc[rows, :] += tile * vector_row(vec_ref, j)
        if acc_ones is not None:
            acc_ones[rows, :] += tile
        return unused

    kept = sz.kept * ARRAYS
    lax.fori_loop(kept, jnp.maximum(count, kept), extra, 0)


def finish(sz, acc, out_ref):
    unit = jnp.ones((8, BS), BF16)
    across = (((1,), (1,)), ((), ()))
    for i in range(sz.own):
        whole = acc[i * BS : (i + 1) * BS, :]
        high = whole.astype(BF16)
        low = (whole - high.astype(F32)).astype(BF16)
        y = lax.dot_general(unit, high, across, preferred_element_type=F32)
        y = y + lax.dot_general(unit, low, across, preferred_element_type=F32)
        out_ref[i : i + 1, :] = y[0:1, :] * sz.scale


def total_of(x):
    return jnp.sum(jnp.sum(x, axis=0, keepdims=True), axis=1, keepdims=True)


def place_block(piece_ref, part, first, rhs_ref):
    def one(k, unused):
        h, m, l = features_of([block_row(piece_ref, c, part, k) for c in range(3)], -2.0, 4, 3)
        feats = jnp.concatenate([h, m, h, m, l, h], axis=0).astype(BF16)
        rhs_ref[pl.ds(pl.multiple_of((first + k) * DEPTH, DEPTH), DEPTH), :] = feats
        return unused

    lax.fori_loop(0, part, one, 0, unroll=4)


def first_kernel(sz, *refs):
    list_ref, count_ref, lhs_ref, nugget_any, obs_any, home_ref = refs[:6]
    coord_refs = refs[6 : 6 + (sz.blks - 1) * sz.reps]
    refs = refs[6 + (sz.blks - 1) * sz.reps :]
    tile_refs = refs[:ARRAYS]
    spare_ref, obs_ref, diag_ref, mapped_ref, norm_ref = refs[ARRAYS : ARRAYS + 5]
    rhs_ref, acc, acc_ones, total_row, squares, nugget_ref, done, fetched = refs[ARRAYS + 5 :]
    blk, rep = lax.axis_index("blk"), lax.axis_index("rep")
    home = pl.ds(pl.multiple_of(blk * sz.local_blocks, 8), sz.local_blocks)
    fetch = pltpu.make_async_copy(nugget_any, nugget_ref, fetched.at[0])
    fetch_obs = pltpu.make_async_copy(obs_any, obs_ref.at[home, :], fetched.at[1])
    fetch.start()
    fetch_obs.start()
    for at, piece_ref in enumerate(coord_refs):
        code, turn = at // sz.reps + 1, at % sz.reps
        part = sz.local_blocks // sz.reps
        first = jnp.bitwise_xor(blk, code) * sz.local_blocks + jnp.bitwise_xor(rep, turn) * part
        first = pl.multiple_of(first, 8)
        place_block(piece_ref, part, first, rhs_ref)
        obs_ref[pl.ds(first, part), :] = piece_ref[3 * part : 4 * part, :]
    place_block(home_ref, sz.local_blocks, blk * sz.local_blocks, rhs_ref)
    far = lax.broadcasted_iota(jnp.int32, (DEPTH, BS), 0) == 3
    rhs_ref[sz.blocks * DEPTH :, :] = jnp.where(far, 1e6, 0.0).astype(BF16)
    count = count_ref[0]
    fetch_obs.wait()
    generate(sz, list_ref, count, lhs_ref, rhs_ref, tile_refs, squares, obs_ref, acc, acc_ones)
    extras(
        sz,
        list_ref,
        count,
        obs_ref,
        acc,
        acc_ones,
        lambda i, j: (own_features(lhs_ref, i), other_features(rhs_ref, j)),
    )

    @pl.when(count > sz.kept * ARRAYS)
    def save():
        copy = pltpu.make_async_copy(rhs_ref, spare_ref, done)
        copy.start()
        copy.wait()

    finish(sz, acc_ones, total_row)
    finish(sz, acc, mapped_ref)
    quarter = lax.axis_index("col") * sz.reps + rep
    own = pl.ds(pl.multiple_of(sz.me() * sz.own, 8), sz.own)
    fetch.wait()
    diag = nugget_ref[pl.ds(pl.multiple_of(quarter * sz.own, 8), sz.own), :] + total_row[...]
    diag_ref[...] = diag
    mapped_ref[...] += diag * obs_ref[own, :]
    norm_ref[...] = jnp.broadcast_to(total_of(obs_ref[...] * obs_ref[...]), (8, BS))


def step_kernel(sz, last, *refs):
    list_ref, count_ref, lhs_ref, spare_ref, diag_ref, norm_ref, field_ref, resid_ref, dirn_ref = refs[:9]
    pieces = refs[9 : 9 + sz.plane]
    tile_refs = refs[9 + sz.plane : 9 + sz.plane + ARRAYS]
    rest = refs[9 + sz.plane + ARRAYS :]
    mapped_ref, next_norm_ref, next_field_ref, next_resid_ref, next_dirn_ref = rest[:5]
    if last:
        dot_ref, dirn = rest[5:7]
    else:
        dirn = next_dirn_ref
    mapped, acc, features, others, done = rest[-5:]
    me = sz.me()
    assemble(sz, pieces, sz.own, mapped)
    norm = norm_ref[0:1, 0:1]
    step = norm / total_of(dirn_ref[...] * mapped[...])
    resid = resid_ref[...] - step * mapped[...]
    next_norm = total_of(resid * resid)
    dirn[...] = resid + (next_norm / norm) * dirn_ref[...]
    next_norm_ref[...] = jnp.broadcast_to(next_norm, (8, BS))
    home = pl.ds(pl.multiple_of(lax.axis_index("blk") * sz.local_blocks, 8), sz.local_blocks)
    own = pl.ds(pl.multiple_of(me * sz.own, 8), sz.own)
    field = step * dirn_ref[home, :]
    if last:
        next_field_ref[...] = field_ref[...] + field
        next_resid_ref[...] = resid_ref[home, :] - step * mapped[home, :]
        next_dirn_ref[...] = dirn[home, :]
    else:
        next_field_ref[...] = field
        next_resid_ref[...] = resid

    def remake(i, j):
        for source, start, size, target in ((lhs_ref, i, BS, features), (spare_ref, j, DEPTH, others)):
            copy = pltpu.make_async_copy(source.at[pl.ds(pl.multiple_of(start * size, size), size), :], target, done)
            copy.start()
            copy.wait()
        return features[:, :DEPTH], others[...]

    sweep(sz, list_ref, count_ref[0], tile_refs, dirn, acc)
    extras(sz, list_ref, count_ref[0], dirn, acc, None, remake)
    finish(sz, acc, mapped_ref)
    ours = mapped_ref[...] + diag_ref[...] * dirn[own, :]
    mapped_ref[...] = ours
    if last:
        dot_ref[...] = jnp.broadcast_to(total_of(ours * dirn[own, :]), dot_ref.shape)


def last_kernel(sz, *refs):
    norm_ref, field_ref, resid_ref, dirn_ref = refs[:4]
    pieces = refs[4 : 4 + sz.plane]
    out_field_ref, out_resid_ref = refs[4 + sz.plane :]
    product = jnp.zeros((8, BS), F32)
    for ref in pieces:
        for z in range(sz.blks):
            product = product + ref[sz.own + 8 * z : sz.own + 8 * (z + 1), :]
    step = norm_ref[0:1, :] / product[0:1, :]
    out_field_ref[...] = field_ref[...] + step * dirn_ref[...]
    quarter = lax.axis_index("col") * sz.reps + lax.axis_index("rep")
    for k, ref in enumerate(pieces):
        rows = pl.ds(pl.multiple_of(jnp.bitwise_xor(quarter, k) * sz.own, 8), sz.own)
        out_resid_ref[rows, :] = resid_ref[rows, :] - step * ref[: sz.own, :]


def call(kernel, mib, in_specs, shapes, out_specs, scratch, flops, *args):
    return pl.pallas_call(
        kernel,
        in_specs=in_specs,
        out_shape=shapes,
        out_specs=out_specs,
        scratch_shapes=scratch,
        compiler_params=pltpu.CompilerParams(vmem_limit_bytes=mib * MIB),
        cost_estimate=pl.CostEstimate(flops=flops, bytes_accessed=1 << 20, transcendentals=0),
    )(*args)


def array(*shape, dtype=F32):
    return jax.ShapeDtypeStruct(shape, dtype)


def local(coords, observations, nugget, tile_pairs, tile_live):
    sz = Sizes(observations.shape[0], tile_pairs.shape[1])
    own, blocks, home = sz.own, sz.blocks, sz.local_blocks
    alive = jnp.arange(sz.slots, dtype=jnp.int32) < tile_live[0]
    pairs = jnp.where(alive, tile_pairs, -1).reshape(2 * sz.slots // BS, BS)
    rep = lax.axis_index("rep")
    part = home // sz.reps
    obs_rows = observations.reshape(home, BS)
    rows = coords.reshape(3, home, BS)
    half = lax.dynamic_slice_in_dim(jnp.concatenate([rows, obs_rows[None]], axis=0), rep * part, part, axis=1)
    half = half.reshape(4 * part, BS)
    nears = [swap(half, "blk", z) for z in range(1, sz.blks)]
    pair_arrays = over_plane(along_blk(pairs))

    lhs = call(
        functools.partial(lhs_kernel, sz),
        12,
        [VMEM],
        array((own + 1) * BS, BS, dtype=BF16),
        VMEM,
        [],
        10_000_000,
        rows,
    )
    lines = 2 * sz.slots // BS * sz.devs
    table, count = call(
        functools.partial(list_kernel, sz),
        12,
        [VMEM] * sz.plane,
        (array(sz.capacity // BS, BS, dtype=jnp.int32), array(1, dtype=jnp.int32)),
        (VMEM, SMEM),
        [pltpu.VMEM((lines, BS), jnp.int32)] * 2
        + [pltpu.VMEM((lines, BS), F32)] * 2
        + [pltpu.VMEM((sz.capacity, BS), F32)]
        + [pltpu.VMEM((sz.capacity // BS, BS), F32)] * 2,
        10_000_000,
        *pair_arrays,
    )
    table, lhs, *nears = lax.optimization_barrier((table.reshape(sz.capacity), lhs, *nears))
    coord_arrays = []
    for near in nears:
        coord_arrays += [near] + [swap(near, "rep", r) for r in range(1, sz.reps)]
    tall = pltpu.VMEM(((own + 1) * BS, BS), F32)
    kept = [pltpu.VMEM((sz.kept * BS, BS), F32)] * ARRAYS
    *tiles, spare, obs, diag, mapped, norm = call(
        functools.partial(first_kernel, sz),
        sz.first_mib,
        [SMEM, SMEM, VMEM, ANY, ANY] + [VMEM] * (1 + len(coord_arrays)),
        kept
        + [
            pltpu.HBM(((blocks + 1) * DEPTH, BS), BF16),
            array(blocks, BS),
            array(own, BS),
            array(own, BS),
            array(8, BS),
        ],
        [VMEM] * ARRAYS + [ANY] + [VMEM] * 4,
        [
            pltpu.VMEM(((blocks + 1) * DEPTH, BS), BF16),
            tall,
            tall,
            pltpu.VMEM((own, BS), F32),
            pltpu.VMEM((UNROLL // 2 * BS, 2 * BS), F32),
            pltpu.VMEM((home, BS), F32),
            pltpu.SemaphoreType.DMA,
            pltpu.SemaphoreType.DMA((2,)),
        ],
        100_000_000,
        table,
        count,
        lhs,
        pltpu.with_memory_space_constraint(nugget.reshape(home, BS), pltpu.HBM),
        pltpu.with_memory_space_constraint(obs_rows, pltpu.HBM),
        rows,
        *coord_arrays,
    )
    tiles = [pltpu.with_memory_space_constraint(tile, pltpu.VMEM) for tile in tiles]
    spare = pltpu.with_memory_space_constraint(spare, pltpu.HBM)
    field, resid, dirn = norm, obs, obs
    for sweep_index in range(1, ITERS):
        last = sweep_index + 1 == ITERS
        span = home if last else blocks
        outs = [array(own, BS), array(8, BS), array(home, BS), array(span, BS), array(span, BS)]
        mapped, norm, field, resid, dirn, *dot = call(
            functools.partial(step_kernel, sz, last),
            8,
            [SMEM, SMEM, ANY, ANY] + [VMEM] * (5 + sz.plane + ARRAYS),
            outs + [array(8, BS)] * last,
            [VMEM] * (len(outs) + last),
            [pltpu.VMEM((blocks, BS), F32)] * (1 + last)
            + [tall, pltpu.VMEM((BS, BS), BF16), pltpu.VMEM((DEPTH, BS), BF16), pltpu.SemaphoreType.DMA],
            100_000_000,
            table,
            count,
            lhs,
            spare,
            diag,
            norm,
            field,
            resid,
            dirn,
            *over_plane(along_blk(mapped)),
            *tiles,
        )
    ends = over_plane(jnp.concatenate([mapped, along_blk(dot[0])], axis=0))
    field, resid = call(
        functools.partial(last_kernel, sz),
        4,
        [VMEM] * (4 + sz.plane),
        (array(home, BS), array(home, BS)),
        (VMEM, VMEM),
        [],
        100_000,
        norm,
        field,
        resid,
        dirn,
        *ends,
    )
    return field.reshape(sz.points), resid.reshape(sz.points)


def solution(mesh):
    in_specs = (
        P(None, ("grp", "blk")),
        P(("grp", "blk")),
        P(("grp", "blk")),
        P(None, ("grp", "blk", "col", "rep")),
        P(("grp", "blk", "col", "rep")),
    )
    out_specs = (P(("grp", "blk")), P(("grp", "blk")))
    return jax.shard_map(local, mesh=mesh, in_specs=in_specs, out_specs=out_specs, check_vma=False)
```

```python
import functools

import jax
import jax.numpy as jnp
from jax import lax
from jax.experimental import pallas as pl
from jax.experimental.pallas import tpu as pltpu
from jax.sharding import PartitionSpec as P

BS = 128
ITERS = 3
SUPPORT = 0.3
DEPTH = 48
UNROLL = 16
ARRAYS = 4
MIB = 1024 * 1024
VMEM = pl.BlockSpec(memory_space=pltpu.VMEM)
SMEM = pl.BlockSpec(memory_space=pltpu.SMEM)
ANY = pl.BlockSpec(memory_space=pl.ANY)
BF16 = jnp.bfloat16
F32 = jnp.float32


class Sizes:
    def __init__(self, points, slots):
        self.blks = lax.axis_size("blk")
        self.reps = lax.axis_size("rep")
        self.plane = lax.axis_size("col") * self.reps
        self.devs = self.blks * self.plane
        self.points = points
        self.slots = slots
        self.local_blocks = points // BS
        self.blocks = self.local_blocks * self.blks
        self.own = self.local_blocks // self.plane
        self.capacity = 2 * self.plane * slots + 1024
        per_row = slots * self.devs // self.blocks
        self.first_mib = 6 + self.blocks * DEPTH * BS * 2 // MIB
        self.kept = min(448, (48 - self.first_mib) * 16) // (ARRAYS * UNROLL) * UNROLL
        self.scale = 16.0 / (BS * per_row) / 256.0

    def me(self):
        return (lax.axis_index("blk") * lax.axis_size("col") + lax.axis_index("col")) * self.reps + lax.axis_index(
            "rep"
        )


def swap(x, axis, code):
    return lax.ppermute(x, axis, [(i, i ^ code) for i in range(lax.axis_size(axis))])


def along_blk(x):
    return jnp.concatenate([x] + [swap(x, "blk", k) for k in range(1, lax.axis_size("blk"))], axis=0)


def over_plane(x):
    reps = lax.axis_size("rep")
    found = {0: x}
    for c in range(1, lax.axis_size("col")):
        found[c * reps] = swap(x, "col", c)
    for start in sorted(found):
        for r in range(1, reps):
            found[start + r] = swap(found[start], "rep", r)
    return [found[k] for k in sorted(found)]


def assemble(sz, refs, rows, target):
    me = sz.me()
    for k, ref in enumerate(refs):
        for z in range(ref.shape[0] // rows):
            start = pl.multiple_of(jnp.bitwise_xor(me, z * sz.plane + k) * rows, 8)
            target[pl.ds(start, rows), :] = ref[z * rows : (z + 1) * rows, :]


def split3(x):
    high = x.astype(BF16).astype(F32)
    rest = x - high
    middle = rest.astype(BF16).astype(F32)
    return high, middle, rest - middle


def features_of(rows, factor, unit, norm):
    feature = lax.broadcasted_iota(jnp.int32, (8, BS), 0)
    x, y, z = ((row - 0.5) * (4.0 / SUPPORT) for row in rows)
    feats = jnp.where(feature == unit, 1.0, 0.0)
    for place, row in ((0, factor * x), (1, factor * y), (2, factor * z), (norm, x * x + y * y + z * z)):
        feats = jnp.where(feature == place, row, feats)
    return split3(feats)


def block_row(ref, c, part, k):
    return ref[c, pl.ds(k, 1), :] if len(ref.shape) == 3 else ref[pl.ds(c * part + k, 1), :]


def lhs_kernel(sz, home_ref, out_ref):
    quarter = lax.axis_index("col") * sz.reps + lax.axis_index("rep")
    for i in range(sz.own):
        h, m, l = features_of([block_row(home_ref, c, None, quarter * sz.own + i) for c in range(3)], 1.0, 3, 4)
        feats = jnp.concatenate([h, h, m, m, h, l, jnp.zeros((BS - DEPTH, BS), F32)], axis=0)
        out_ref[i * BS : (i + 1) * BS, :] = feats.T.astype(BF16)
    out_ref[sz.own * BS :, :] = jnp.zeros((BS, BS), BF16)


def list_kernel(sz, *refs):
    me = sz.me()
    out_ref, count_ref, target, other, place, value, key_column, key_row, entry_row = refs[sz.plane :]
    lines = sz.slots // BS
    at = 2 * lines * sz.devs
    for base in range(0, at, 2 * lines):
        pairs_ref = refs[base // (2 * lines * sz.blks)]
        start = base % (2 * lines * sz.blks)
        rows = pairs_ref[start : start + lines, :]
        cols = pairs_ref[start + lines : start + 2 * lines, :]
        target[base : base + lines, :] = rows
        other[base : base + lines, :] = cols
        target[base + lines : base + 2 * lines, :] = cols
        other[base + lines : base + 2 * lines, :] = rows
    local = target[...] - me * sz.own
    mine = jnp.logical_and(local >= 0, local < sz.own)
    flags = jnp.where(mine, 1.0, 0.0)
    a = lax.broadcasted_iota(jnp.int32, (BS, BS), 0)
    b = lax.broadcasted_iota(jnp.int32, (BS, BS), 1)
    ahead = jnp.where(a < b, 1.0, 0.0).astype(BF16)
    before = jnp.dot(flags.astype(BF16), ahead, preferred_element_type=F32)
    totals = jnp.broadcast_to(jnp.sum(flags, axis=1, keepdims=True), (at, BS))
    a = lax.broadcasted_iota(jnp.int32, (at, at), 0)
    b = lax.broadcasted_iota(jnp.int32, (at, at), 1)
    above = jnp.dot(jnp.where(b < a, 1.0, 0.0).astype(BF16), totals.astype(BF16), preferred_element_type=F32)
    place[...] = jnp.where(mine, above + before, -1.0)
    ends = jnp.sum(jnp.where(lax.broadcasted_iota(jnp.int32, (at, BS), 1) == 0, above + totals, 0.0), axis=1, keepdims=True)
    starts = ends - totals[:, 0:1]
    value[...] = (local + 256 * other[...]).astype(F32)
    count = jnp.sum(flags).astype(jnp.int32)
    sub = lax.broadcasted_iota(jnp.int32, (BS, BS), 0)
    lane = lax.broadcasted_iota(jnp.int32, (1, BS), 1)

    chunks = jnp.maximum(lax.shift_right_logical(count + BS - 1, 7), 1)

    def key_of(found, slot):
        entry = jnp.where(slot < count, found.astype(jnp.int32), sz.own)
        return entry.astype(F32), (jnp.bitwise_and(entry, 255) * 65536 + slot).astype(F32)

    def compact(c, unused):
        slot = (sub + c * BS).astype(F32)
        base = (c * BS).astype(F32)
        bounds = jnp.where(ends <= base, 1.0, 0.0) + jnp.where(starts < base + BS, 1024.0, 0.0)
        bounds = jnp.sum(bounds).astype(jnp.int32)
        first = jnp.minimum(lax.shift_right_logical(jnp.bitwise_and(bounds, 1023), 2), at // 4)
        last = lax.shift_right_logical(lax.shift_right_logical(bounds, 10) + 3, 2)

        def lines(g, total):
            for u in range(4):
                r = 4 * g + u
                hit = place[pl.ds(r, 1), :] == slot
                total = jnp.where(hit, value[pl.ds(r, 1), :], total)
            return total

        total = lax.fori_loop(first, last, lines, jnp.zeros((BS, BS), F32))
        entry, key = key_of(jnp.sum(total.T, axis=0, keepdims=True), lane + c * BS)
        entry_row[pl.ds(c, 1), :] = entry
        key_row[pl.ds(c, 1), :] = key
        unused_entry, key = key_of(jnp.sum(total, axis=1, keepdims=True), sub[:, 0:1] + c * BS)
        key_column[pl.ds(pl.multiple_of(c * BS, BS), BS), :] = jnp.broadcast_to(key, (BS, BS))
        return unused

    lax.fori_loop(0, chunks, compact, 0)

    bound = lane.astype(F32) * 65536.0

    def tally(c, carry):
        keys = key_column[pl.ds(pl.multiple_of(c * BS, BS), BS), :]
        from_here, after = carry
        return from_here + jnp.where(keys >= bound, 1.0, 0.0), after + jnp.where(keys >= bound + 65536.0, 1.0, 0.0)

    zero = jnp.zeros((BS, BS), F32)
    from_here, after = lax.fori_loop(0, chunks, tally, (zero, zero))
    from_here = jnp.sum(from_here, axis=0, keepdims=True)
    each = from_here - jnp.sum(after, axis=0, keepdims=True)
    odd = each - 2.0 * jnp.floor(0.5 * each)
    pad = jnp.where(lane < sz.own, jnp.where(each == 0.0, 2.0, odd), 0.0)
    wide_pad = jnp.broadcast_to(pad, (BS, BS))
    pad_column = wide_pad.T
    pad_before = jnp.dot(wide_pad.astype(BF16), ahead, preferred_element_type=F32)[0:1, :]
    start = (chunks * BS).astype(F32) - from_here + pad_before
    null_places = (jnp.where(pad > 0.0, start + each, -1.0), jnp.where(pad > 1.0, start + 1.0, -1.0))
    null_entry = (lane + 256 * sz.blocks).astype(F32)
    full = count + jnp.sum(pad).astype(jnp.int32)
    count_ref[0] = full

    def rank(c, unused):
        keys = key_row[pl.ds(c, 1), :]

        def below(k, total):
            lower = key_column[pl.ds(pl.multiple_of(k * BS, BS), BS), :] < keys
            return total + jnp.where(lower, 1.0, 0.0)

        past = (sub + 1).astype(F32) * 65536.0 <= keys
        total = lax.fori_loop(0, chunks, below, jnp.where(past, pad_column, 0.0))
        place[pl.ds(c, 1), :] = jnp.sum(total, axis=0, keepdims=True)
        return unused

    lax.fori_loop(0, chunks, rank, 0)

    def arrange(c, unused):
        slot = (sub + c * BS).astype(F32)

        def line(r, total):
            hit = place[pl.ds(r, 1), :] == slot
            return total + jnp.where(hit, entry_row[pl.ds(r, 1), :], 0.0)

        nulls = jnp.logical_or(null_places[0] == slot, null_places[1] == slot)
        total = lax.fori_loop(0, chunks, line, jnp.where(nulls, null_entry, 0.0))
        found = jnp.sum(total.T, axis=0, keepdims=True).astype(jnp.int32)
        out_ref[pl.ds(c, 1), :] = jnp.where(lane + c * BS < full, found, sz.own)
        return unused

    lax.fori_loop(0, jnp.maximum(lax.shift_right_logical(full + BS - 1, 7), 1), arrange, 0)


def entry_of(list_ref, k):
    entry = list_ref[k]
    return jnp.bitwise_and(entry, 255), lax.shift_right_logical(entry, 8)


def squared_of(features, others):
    return jnp.dot(features, others, preferred_element_type=F32)


def taper_of(squared):
    squared = jnp.maximum(squared, 1e-20)
    remain = jnp.maximum(4.0 - squared * lax.rsqrt(squared), 0.0)
    twice = remain * remain
    return twice * twice * (5.0 - remain)


def kept_groups(sz, count, at):
    first = at * (sz.kept // UNROLL)
    last = jnp.minimum(lax.div(count + (UNROLL - 1), UNROLL), first + sz.kept // UNROLL)
    return first, jnp.maximum(first, last)


def vector_row(vec_ref, j):
    return vec_ref[pl.ds(jnp.minimum(j, vec_ref.shape[0] - 1), 1), :]


def own_features(lhs_ref, i):
    return lhs_ref[pl.ds(pl.multiple_of(i * BS, BS), BS), :DEPTH]


def other_features(rhs_ref, j):
    return rhs_ref[pl.ds(pl.multiple_of(j * DEPTH, DEPTH), DEPTH), :]


def clear_if_extra(sz, count, accs):
    @pl.when(count > sz.kept * ARRAYS)
    def clear():
        for ref in accs:
            ref[...] = jnp.zeros_like(ref)


def generate(sz, list_ref, count, lhs_ref, rhs_ref, tile_refs, squares, vec_ref, acc, acc_ones):
    clear_if_extra(sz, count, (acc, acc_ones))
    top = jnp.maximum(lax.div(count + (UNROLL - 1), UNROLL) - 1, 0)

    def squared(g, u):
        k = jnp.minimum(g, top) * UNROLL + u
        i, j = entry_of(list_ref, k)
        unused, twin = entry_of(list_ref, k + 1)
        both = jnp.concatenate([other_features(rhs_ref, j), other_features(rhs_ref, twin)], axis=1)
        return squared_of(own_features(lhs_ref, i), both)

    for u in range(0, UNROLL, 2):
        squares[u // 2 * BS : (u // 2 + 1) * BS, :] = squared(0, u)
    zero = jnp.zeros((8, BS), F32)
    carry = (jnp.int32(-1), (zero,) * (BS // 8), (zero,) * (BS // 8))
    for at, tile_ref in enumerate(tile_refs):

        def group(g, carry, at=at, tile_ref=tile_ref):
            before, totals, ones = carry
            totals, ones = list(totals), list(ones)
            for u in range(0, UNROLL, 2):
                following = squared(g + 1, u)
                i, j = entry_of(list_ref, g * UNROLL + u)
                unused, twin = entry_of(list_ref, g * UNROLL + u + 1)
                keep = jnp.where(i == before, 1.0, 0.0)
                before = i
                start = pl.multiple_of((g * UNROLL + u - at * sz.kept) * BS, BS)
                base = pl.multiple_of(i * BS, BS)
                row = jnp.broadcast_to(vector_row(vec_ref, j), (8, BS))
                twin_row = jnp.broadcast_to(vector_row(vec_ref, twin), (8, BS))
                for k in range(BS // 8):
                    r = 8 * k
                    here = slice(u // 2 * BS + r, u // 2 * BS + r + 8)
                    tile = taper_of(squares[here, :BS])
                    twin_tile = taper_of(squares[here, BS:])
                    tile_ref[pl.ds(start + r, 8), :] = tile
                    tile_ref[pl.ds(start + BS + r, 8), :] = twin_tile
                    squares[here, :] = following[r : r + 8, :]
                    totals[k] = totals[k] * keep + (tile * row + twin_tile * twin_row)
                    ones[k] = ones[k] * keep + (tile + twin_tile)
                    acc[pl.ds(base + r, 8), :] = totals[k]
                    acc_ones[pl.ds(base + r, 8), :] = ones[k]
            return before, tuple(totals), tuple(ones)

        carry = lax.fori_loop(*kept_groups(sz, count, at), group, carry)


def sweep(sz, list_ref, count, tile_refs, vec_ref, acc):
    clear_if_extra(sz, count, (acc,))
    zero = jnp.zeros((8, BS), F32)
    carry = (jnp.int32(-1), (zero,) * (BS // 8))
    for at, tile_ref in enumerate(tile_refs):

        def group(g, carry, at=at, tile_ref=tile_ref):
            before, totals = carry
            totals = list(totals)
            for u in range(0, UNROLL, 2):
                i, j = entry_of(list_ref, g * UNROLL + u)
                unused, twin = entry_of(list_ref, g * UNROLL + u + 1)
                keep = jnp.where(i == before, 1.0, 0.0)
                before = i
                start = pl.multiple_of((g * UNROLL + u - at * sz.kept) * BS, BS)
                base = pl.multiple_of(i * BS, BS)
                row = jnp.broadcast_to(vector_row(vec_ref, j), (8, BS))
                twin_row = jnp.broadcast_to(vector_row(vec_ref, twin), (8, BS))
                for k in range(BS // 8):
                    tile = tile_ref[pl.ds(start + 8 * k, 8), :]
                    twin_tile = tile_ref[pl.ds(start + BS + 8 * k, 8), :]
                    totals[k] = totals[k] * keep + (tile * row + twin_tile * twin_row)
                    acc[pl.ds(base + 8 * k, 8), :] = totals[k]
            return before, tuple(totals)

        carry = lax.fori_loop(*kept_groups(sz, count, at), group, carry)


def extras(sz, list_ref, count, vec_ref, acc, acc_ones, remake):
    def extra(k, unused):
        i, j = entry_of(list_ref, k)
        tile = taper_of(squared_of(*remake(i, j)))
        rows = pl.ds(pl.multiple_of(i * BS, BS), BS)
        acc[rows, :] += tile * vector_row(vec_ref, j)
        if acc_ones is not None:
            acc_ones[rows, :] += tile
        return unused

    kept = sz.kept * ARRAYS
    lax.fori_loop(kept, jnp.maximum(count, kept), extra, 0)


def finish(sz, acc, out_ref):
    unit = jnp.ones((8, 2 * BS), BF16)
    across = (((1,), (1,)), ((), ()))
    for i in range(sz.own):
        whole = acc[i * BS : (i + 1) * BS, :]
        high = whole.astype(BF16)
        low = (whole - high.astype(F32)).astype(BF16)
        y = lax.dot_general(unit, jnp.concatenate([high, low], axis=1), across, preferred_element_type=F32)
        out_ref[i : i + 1, :] = y[0:1, :] * sz.scale


def total_of(x):
    return jnp.sum(jnp.sum(x, axis=0, keepdims=True), axis=1, keepdims=True)


def place_block(piece_ref, part, first, rhs_ref):
    def one(k, unused):
        h, m, l = features_of([block_row(piece_ref, c, part, k) for c in range(3)], -2.0, 4, 3)
        feats = jnp.concatenate([h, m, h, m, l, h], axis=0).astype(BF16)
        rhs_ref[pl.ds(pl.multiple_of((first + k) * DEPTH, DEPTH), DEPTH), :] = feats
        return unused

    lax.fori_loop(0, part, one, 0, unroll=4)


def first_kernel(sz, *refs):
    list_ref, count_ref, lhs_ref, nugget_any, obs_any, home_ref = refs[:6]
    coord_refs = refs[6 : 6 + (sz.blks - 1) * sz.reps]
    refs = refs[6 + (sz.blks - 1) * sz.reps :]
    tile_refs = refs[:ARRAYS]
    spare_ref, obs_ref, diag_ref, mapped_ref, norm_ref = refs[ARRAYS : ARRAYS + 5]
    rhs_ref, acc, acc_ones, total_row, squares, nugget_ref, done, fetched = refs[ARRAYS + 5 :]
    blk, rep = lax.axis_index("blk"), lax.axis_index("rep")
    home = pl.ds(pl.multiple_of(blk * sz.local_blocks, 8), sz.local_blocks)
    fetch = pltpu.make_async_copy(nugget_any, nugget_ref, fetched.at[0])
    fetch_obs = pltpu.make_async_copy(obs_any, obs_ref.at[home, :], fetched.at[1])
    fetch.start()
    fetch_obs.start()
    for at, piece_ref in enumerate(coord_refs):
        code, turn = at // sz.reps + 1, at % sz.reps
        part = sz.local_blocks // sz.reps
        first = jnp.bitwise_xor(blk, code) * sz.local_blocks + jnp.bitwise_xor(rep, turn) * part
        first = pl.multiple_of(first, 8)
        place_block(piece_ref, part, first, rhs_ref)
        obs_ref[pl.ds(first, part), :] = piece_ref[3 * part : 4 * part, :]
    place_block(home_ref, sz.local_blocks, blk * sz.local_blocks, rhs_ref)
    far = lax.broadcasted_iota(jnp.int32, (DEPTH, BS), 0) == 3
    rhs_ref[sz.blocks * DEPTH :, :] = jnp.where(far, 1e6, 0.0).astype(BF16)
    count = count_ref[0]
    fetch_obs.wait()
    generate(sz, list_ref, count, lhs_ref, rhs_ref, tile_refs, squares, obs_ref, acc, acc_ones)
    extras(
        sz,
        list_ref,
        count,
        obs_ref,
        acc,
        acc_ones,
        lambda i, j: (own_features(lhs_ref, i), other_features(rhs_ref, j)),
    )

    @pl.when(count > sz.kept * ARRAYS)
    def save():
        copy = pltpu.make_async_copy(rhs_ref, spare_ref, done)
        copy.start()
        copy.wait()

    finish(sz, acc_ones, total_row)
    finish(sz, acc, mapped_ref)
    quarter = lax.axis_index("col") * sz.reps + rep
    own = pl.ds(pl.multiple_of(sz.me() * sz.own, 8), sz.own)
    fetch.wait()
    diag = nugget_ref[pl.ds(pl.multiple_of(quarter * sz.own, 8), sz.own), :] + total_row[...]
    diag_ref[...] = diag
    mapped_ref[...] += diag * obs_ref[own, :]
    norm_ref[...] = jnp.broadcast_to(total_of(obs_ref[...] * obs_ref[...]), (8, BS))


def step_kernel(sz, last, *refs):
    list_ref, count_ref, lhs_ref, spare_ref, diag_ref, norm_ref, field_ref, resid_ref, dirn_ref = refs[:9]
    pieces = refs[9 : 9 + sz.plane]
    tile_refs = refs[9 + sz.plane : 9 + sz.plane + ARRAYS]
    rest = refs[9 + sz.plane + ARRAYS :]
    mapped_ref, next_norm_ref, next_field_ref, next_resid_ref, next_dirn_ref = rest[:5]
    if last:
        dot_ref, dirn = rest[5:7]
    else:
        dirn = next_dirn_ref
    mapped, acc, features, others, done = rest[-5:]
    me = sz.me()
    assemble(sz, pieces, sz.own, mapped)
    norm = norm_ref[0:1, 0:1]
    step = norm / total_of(dirn_ref[...] * mapped[...])
    resid = resid_ref[...] - step * mapped[...]
    next_norm = total_of(resid * resid)
    dirn[...] = resid + (next_norm / norm) * dirn_ref[...]
    next_norm_ref[...] = jnp.broadcast_to(next_norm, (8, BS))
    home = pl.ds(pl.multiple_of(lax.axis_index("blk") * sz.local_blocks, 8), sz.local_blocks)
    own = pl.ds(pl.multiple_of(me * sz.own, 8), sz.own)
    field = step * dirn_ref[home, :]
    if last:
        next_field_ref[...] = field_ref[...] + field
        next_resid_ref[...] = resid_ref[home, :] - step * mapped[home, :]
        next_dirn_ref[...] = dirn[home, :]
    else:
        next_field_ref[...] = field
        next_resid_ref[...] = resid

    def remake(i, j):
        for source, start, size, target in ((lhs_ref, i, BS, features), (spare_ref, j, DEPTH, others)):
            copy = pltpu.make_async_copy(source.at[pl.ds(pl.multiple_of(start * size, size), size), :], target, done)
            copy.start()
            copy.wait()
        return features[:, :DEPTH], others[...]

    sweep(sz, list_ref, count_ref[0], tile_refs, dirn, acc)
    extras(sz, list_ref, count_ref[0], dirn, acc, None, remake)
    finish(sz, acc, mapped_ref)
    ours = mapped_ref[...] + diag_ref[...] * dirn[own, :]
    mapped_ref[...] = ours
    if last:
        dot_ref[...] = jnp.broadcast_to(total_of(ours * dirn[own, :]), dot_ref.shape)


def last_kernel(sz, *refs):
    norm_ref, field_ref, resid_ref, dirn_ref = refs[:4]
    pieces = refs[4 : 4 + sz.plane]
    out_field_ref, out_resid_ref = refs[4 + sz.plane :]
    product = jnp.zeros((8, BS), F32)
    for ref in pieces:
        for z in range(sz.blks):
            product = product + ref[sz.own + 8 * z : sz.own + 8 * (z + 1), :]
    step = norm_ref[0:1, :] / product[0:1, :]
    out_field_ref[...] = field_ref[...] + step * dirn_ref[...]
    quarter = lax.axis_index("col") * sz.reps + lax.axis_index("rep")
    for k, ref in enumerate(pieces):
        rows = pl.ds(pl.multiple_of(jnp.bitwise_xor(quarter, k) * sz.own, 8), sz.own)
        out_resid_ref[rows, :] = resid_ref[rows, :] - step * ref[: sz.own, :]


def call(kernel, mib, in_specs, shapes, out_specs, scratch, flops, *args):
    return pl.pallas_call(
        kernel,
        in_specs=in_specs,
        out_shape=shapes,
        out_specs=out_specs,
        scratch_shapes=scratch,
        compiler_params=pltpu.CompilerParams(vmem_limit_bytes=mib * MIB),
        cost_estimate=pl.CostEstimate(flops=flops, bytes_accessed=1 << 20, transcendentals=0),
    )(*args)


def array(*shape, dtype=F32):
    return jax.ShapeDtypeStruct(shape, dtype)


def local(coords, observations, nugget, tile_pairs, tile_live):
    sz = Sizes(observations.shape[0], tile_pairs.shape[1])
    own, blocks, home = sz.own, sz.blocks, sz.local_blocks
    alive = jnp.arange(sz.slots, dtype=jnp.int32) < tile_live[0]
    pairs = jnp.where(alive, tile_pairs, -1).reshape(2 * sz.slots // BS, BS)
    rep = lax.axis_index("rep")
    part = home // sz.reps
    obs_rows = observations.reshape(home, BS)
    rows = coords.reshape(3, home, BS)
    half = lax.dynamic_slice_in_dim(jnp.concatenate([rows, obs_rows[None]], axis=0), rep * part, part, axis=1)
    half = half.reshape(4 * part, BS)
    nears = [swap(half, "blk", z) for z in range(1, sz.blks)]
    pair_arrays = over_plane(along_blk(pairs))

    lhs = call(
        functools.partial(lhs_kernel, sz),
        12,
        [VMEM],
        array((own + 1) * BS, BS, dtype=BF16),
        VMEM,
        [],
        10_000_000,
        rows,
    )
    lines = 2 * sz.slots // BS * sz.devs
    table, count = call(
        functools.partial(list_kernel, sz),
        12,
        [VMEM] * sz.plane,
        (array(sz.capacity // BS, BS, dtype=jnp.int32), array(1, dtype=jnp.int32)),
        (VMEM, SMEM),
        [pltpu.VMEM((lines, BS), jnp.int32)] * 2
        + [pltpu.VMEM((lines, BS), F32)] * 2
        + [pltpu.VMEM((sz.capacity, BS), F32)]
        + [pltpu.VMEM((sz.capacity // BS, BS), F32)] * 2,
        10_000_000,
        *pair_arrays,
    )
    table, lhs, *nears = lax.optimization_barrier((table.reshape(sz.capacity), lhs, *nears))
    coord_arrays = []
    for near in nears:
        coord_arrays += [near] + [swap(near, "rep", r) for r in range(1, sz.reps)]
    tall = pltpu.VMEM(((own + 1) * BS, BS), F32)
    kept = [pltpu.VMEM((sz.kept * BS, BS), F32)] * ARRAYS
    *tiles, spare, obs, diag, mapped, norm = call(
        functools.partial(first_kernel, sz),
        sz.first_mib,
        [SMEM, SMEM, VMEM, ANY, ANY] + [VMEM] * (1 + len(coord_arrays)),
        kept
        + [
            pltpu.HBM(((blocks + 1) * DEPTH, BS), BF16),
            array(blocks, BS),
            array(own, BS),
            array(own, BS),
            array(8, BS),
        ],
        [VMEM] * ARRAYS + [ANY] + [VMEM] * 4,
        [
            pltpu.VMEM(((blocks + 1) * DEPTH, BS), BF16),
            tall,
            tall,
            pltpu.VMEM((own, BS), F32),
            pltpu.VMEM((UNROLL // 2 * BS, 2 * BS), F32),
            pltpu.VMEM((home, BS), F32),
            pltpu.SemaphoreType.DMA,
            pltpu.SemaphoreType.DMA((2,)),
        ],
        100_000_000,
        table,
        count,
        lhs,
        pltpu.with_memory_space_constraint(nugget.reshape(home, BS), pltpu.HBM),
        pltpu.with_memory_space_constraint(obs_rows, pltpu.HBM),
        rows,
        *coord_arrays,
    )
    tiles = [pltpu.with_memory_space_constraint(tile, pltpu.VMEM) for tile in tiles]
    spare = pltpu.with_memory_space_constraint(spare, pltpu.HBM)
    field, resid, dirn = norm, obs, obs
    for sweep_index in range(1, ITERS):
        last = sweep_index + 1 == ITERS
        span = home if last else blocks
        outs = [array(own, BS), array(8, BS), array(home, BS), array(span, BS), array(span, BS)]
        mapped, norm, field, resid, dirn, *dot = call(
            functools.partial(step_kernel, sz, last),
            8,
            [SMEM, SMEM, ANY, ANY] + [VMEM] * (5 + sz.plane + ARRAYS),
            outs + [array(8, BS)] * last,
            [VMEM] * (len(outs) + last),
            [pltpu.VMEM((blocks, BS), F32)] * (1 + last)
            + [tall, pltpu.VMEM((BS, BS), BF16), pltpu.VMEM((DEPTH, BS), BF16), pltpu.SemaphoreType.DMA],
            100_000_000,
            table,
            count,
            lhs,
            spare,
            diag,
            norm,
            field,
            resid,
            dirn,
            *over_plane(along_blk(mapped)),
            *tiles,
        )
    ends = over_plane(jnp.concatenate([mapped, along_blk(dot[0])], axis=0))
    field, resid = call(
        functools.partial(last_kernel, sz),
        4,
        [VMEM] * (4 + sz.plane),
        (array(home, BS), array(home, BS)),
        (VMEM, VMEM),
        [],
        100_000,
        norm,
        field,
        resid,
        dirn,
        *ends,
    )
    return field.reshape(sz.points), resid.reshape(sz.points)


def solution(mesh):
    in_specs = (
        P(None, ("grp", "blk")),
        P(("grp", "blk")),
        P(("grp", "blk")),
        P(None, ("grp", "blk", "col", "rep")),
        P(("grp", "blk", "col", "rep")),
    )
    out_specs = (P(("grp", "blk")), P(("grp", "blk")))
    return jax.shard_map(local, mesh=mesh, in_specs=in_specs, out_specs=out_specs, check_vma=False)
```

```python
import functools

import jax
import jax.numpy as jnp
from jax import lax
from jax.experimental import pallas as pl
from jax.experimental.pallas import tpu as pltpu
from jax.sharding import PartitionSpec as P

BS = 128
ITERS = 3
SUPPORT = 0.3
DEPTH = 48
UNROLL = 16
ARRAYS = 4
MIB = 1024 * 1024
VMEM = pl.BlockSpec(memory_space=pltpu.VMEM)
SMEM = pl.BlockSpec(memory_space=pltpu.SMEM)
ANY = pl.BlockSpec(memory_space=pl.ANY)
BF16 = jnp.bfloat16
F32 = jnp.float32


class Sizes:
    def __init__(self, points, slots):
        self.blks = lax.axis_size("blk")
        self.reps = lax.axis_size("rep")
        self.plane = lax.axis_size("col") * self.reps
        self.devs = self.blks * self.plane
        self.points = points
        self.slots = slots
        self.local_blocks = points // BS
        self.blocks = self.local_blocks * self.blks
        self.own = self.local_blocks // self.plane
        self.capacity = 2 * self.plane * slots + 1024
        per_row = slots * self.devs // self.blocks
        self.first_mib = 6 + self.blocks * DEPTH * BS * 2 // MIB
        self.kept = min(448, (48 - self.first_mib) * 16) // (ARRAYS * UNROLL) * UNROLL
        self.scale = 16.0 / (BS * per_row) / 256.0

    def me(self):
        return (lax.axis_index("blk") * lax.axis_size("col") + lax.axis_index("col")) * self.reps + lax.axis_index(
            "rep"
        )


def swap(x, axis, code):
    return lax.ppermute(x, axis, [(i, i ^ code) for i in range(lax.axis_size(axis))])


def along_blk(x):
    return jnp.concatenate([x] + [swap(x, "blk", k) for k in range(1, lax.axis_size("blk"))], axis=0)


def over_plane(x):
    reps = lax.axis_size("rep")
    found = {0: x}
    for c in range(1, lax.axis_size("col")):
        found[c * reps] = swap(x, "col", c)
    for start in sorted(found):
        for r in range(1, reps):
            found[start + r] = swap(found[start], "rep", r)
    return [found[k] for k in sorted(found)]


def assemble(sz, refs, rows, target):
    me = sz.me()
    for k, ref in enumerate(refs):
        for z in range(ref.shape[0] // rows):
            start = pl.multiple_of(jnp.bitwise_xor(me, z * sz.plane + k) * rows, 8)
            target[pl.ds(start, rows), :] = ref[z * rows : (z + 1) * rows, :]


def split3(x):
    high = x.astype(BF16).astype(F32)
    rest = x - high
    middle = rest.astype(BF16).astype(F32)
    return high, middle, rest - middle


def features_of(rows, factor, unit, norm):
    feature = lax.broadcasted_iota(jnp.int32, (8, BS), 0)
    x, y, z = ((row - 0.5) * (4.0 / SUPPORT) for row in rows)
    feats = jnp.where(feature == unit, 1.0, 0.0)
    for place, row in ((0, factor * x), (1, factor * y), (2, factor * z), (norm, x * x + y * y + z * z)):
        feats = jnp.where(feature == place, row, feats)
    return split3(feats)


def block_row(ref, c, part, k):
    return ref[c, pl.ds(k, 1), :] if len(ref.shape) == 3 else ref[pl.ds(c * part + k, 1), :]


def lhs_kernel(sz, home_ref, out_ref):
    quarter = lax.axis_index("col") * sz.reps + lax.axis_index("rep")
    for i in range(sz.own):
        h, m, l = features_of([block_row(home_ref, c, None, quarter * sz.own + i) for c in range(3)], 1.0, 3, 4)
        feats = jnp.concatenate([h, h, m, m, h, l, jnp.zeros((BS - DEPTH, BS), F32)], axis=0)
        out_ref[i * BS : (i + 1) * BS, :] = feats.T.astype(BF16)
    out_ref[sz.own * BS :, :] = jnp.zeros((BS, BS), BF16)


def list_kernel(sz, *refs):
    me = sz.me()
    out_ref, count_ref, target, other, place, value, key_column, key_row, entry_row = refs[sz.plane :]
    lines = sz.slots // BS
    at = 2 * lines * sz.devs
    for base in range(0, at, 2 * lines):
        pairs_ref = refs[base // (2 * lines * sz.blks)]
        start = base % (2 * lines * sz.blks)
        rows = pairs_ref[start : start + lines, :]
        cols = pairs_ref[start + lines : start + 2 * lines, :]
        target[base : base + lines, :] = rows
        other[base : base + lines, :] = cols
        target[base + lines : base + 2 * lines, :] = cols
        other[base + lines : base + 2 * lines, :] = rows
    local = target[...] - me * sz.own
    mine = jnp.logical_and(local >= 0, local < sz.own)
    flags = jnp.where(mine, 1.0, 0.0)
    a = lax.broadcasted_iota(jnp.int32, (BS, BS), 0)
    b = lax.broadcasted_iota(jnp.int32, (BS, BS), 1)
    ahead = jnp.where(a < b, 1.0, 0.0).astype(BF16)
    before = jnp.dot(flags.astype(BF16), ahead, preferred_element_type=F32)
    totals = jnp.broadcast_to(jnp.sum(flags, axis=1, keepdims=True), (at, BS))
    a = lax.broadcasted_iota(jnp.int32, (at, at), 0)
    b = lax.broadcasted_iota(jnp.int32, (at, at), 1)
    above = jnp.dot(jnp.where(b < a, 1.0, 0.0).astype(BF16), totals.astype(BF16), preferred_element_type=F32)
    place[...] = jnp.where(mine, above + before, -1.0)
    ends = jnp.sum(jnp.where(lax.broadcasted_iota(jnp.int32, (at, BS), 1) == 0, above + totals, 0.0), axis=1, keepdims=True)
    starts = ends - totals[:, 0:1]
    value[...] = (local + 256 * other[...]).astype(F32)
    count = jnp.sum(flags).astype(jnp.int32)
    sub = lax.broadcasted_iota(jnp.int32, (BS, BS), 0)
    lane = lax.broadcasted_iota(jnp.int32, (1, BS), 1)

    chunks = jnp.maximum(lax.shift_right_logical(count + BS - 1, 7), 1)

    def key_of(found, slot):
        entry = jnp.where(slot < count, found.astype(jnp.int32), sz.own)
        return entry.astype(F32), (jnp.bitwise_and(entry, 255) * 65536 + slot).astype(F32)

    def compact(c, unused):
        slot = (sub + c * BS).astype(F32)
        base = (c * BS).astype(F32)
        bounds = jnp.where(ends <= base, 1.0, 0.0) + jnp.where(starts < base + BS, 1024.0, 0.0)
        bounds = jnp.sum(bounds).astype(jnp.int32)
        first = jnp.minimum(lax.shift_right_logical(jnp.bitwise_and(bounds, 1023), 3), at // 8)
        last = lax.shift_right_logical(lax.shift_right_logical(bounds, 10) + 7, 3)

        def lines(g, total):
            for u in range(8):
                r = 8 * g + u
                hit = place[pl.ds(r, 1), :] == slot
                total = jnp.where(hit, value[pl.ds(r, 1), :], total)
            return total

        total = lax.fori_loop(first, last, lines, jnp.zeros((BS, BS), F32))
        entry, key = key_of(jnp.sum(total.T, axis=0, keepdims=True), lane + c * BS)
        entry_row[pl.ds(c, 1), :] = entry
        key_row[pl.ds(c, 1), :] = key
        unused_entry, key = key_of(jnp.sum(total, axis=1, keepdims=True), sub[:, 0:1] + c * BS)
        key_column[pl.ds(pl.multiple_of(c * BS, BS), BS), :] = jnp.broadcast_to(key, (BS, BS))
        return unused

    lax.fori_loop(0, chunks, compact, 0)

    bound = lane.astype(F32) * 65536.0

    def tally(c, carry):
        keys = key_column[pl.ds(pl.multiple_of(c * BS, BS), BS), :]
        from_here, after = carry
        return from_here + jnp.where(keys >= bound, 1.0, 0.0), after + jnp.where(keys >= bound + 65536.0, 1.0, 0.0)

    zero = jnp.zeros((BS, BS), F32)
    from_here, after = lax.fori_loop(0, chunks, tally, (zero, zero))
    from_here = jnp.sum(from_here, axis=0, keepdims=True)
    each = from_here - jnp.sum(after, axis=0, keepdims=True)
    odd = each - 2.0 * jnp.floor(0.5 * each)
    pad = jnp.where(lane < sz.own, jnp.where(each == 0.0, 2.0, odd), 0.0)
    wide_pad = jnp.broadcast_to(pad, (BS, BS))
    pad_column = wide_pad.T
    pad_before = jnp.dot(wide_pad.astype(BF16), ahead, preferred_element_type=F32)[0:1, :]
    start = (chunks * BS).astype(F32) - from_here + pad_before
    null_places = (jnp.where(pad > 0.0, start + each, -1.0), jnp.where(pad > 1.0, start + 1.0, -1.0))
    null_entry = (lane + 256 * sz.blocks).astype(F32)
    full = count + jnp.sum(pad).astype(jnp.int32)
    count_ref[0] = full

    def rank(c, unused):
        keys = key_row[pl.ds(c, 1), :]

        def below(k, total):
            lower = key_column[pl.ds(pl.multiple_of(k * BS, BS), BS), :] < keys
            return total + jnp.where(lower, 1.0, 0.0)

        past = (sub + 1).astype(F32) * 65536.0 <= keys
        total = lax.fori_loop(0, chunks, below, jnp.where(past, pad_column, 0.0))
        place[pl.ds(c, 1), :] = jnp.sum(total, axis=0, keepdims=True)
        return unused

    lax.fori_loop(0, chunks, rank, 0)

    def arrange(c, unused):
        slot = (sub + c * BS).astype(F32)

        def line(r, total):
            hit = place[pl.ds(r, 1), :] == slot
            return total + jnp.where(hit, entry_row[pl.ds(r, 1), :], 0.0)

        nulls = jnp.logical_or(null_places[0] == slot, null_places[1] == slot)
        total = lax.fori_loop(0, chunks, line, jnp.where(nulls, null_entry, 0.0))
        found = jnp.sum(total.T, axis=0, keepdims=True).astype(jnp.int32)
        out_ref[pl.ds(c, 1), :] = jnp.where(lane + c * BS < full, found, sz.own)
        return unused

    lax.fori_loop(0, jnp.maximum(lax.shift_right_logical(full + BS - 1, 7), 1), arrange, 0)


def entry_of(list_ref, k):
    entry = list_ref[k]
    return jnp.bitwise_and(entry, 255), lax.shift_right_logical(entry, 8)


def squared_of(features, others):
    return jnp.dot(features, others, preferred_element_type=F32)


def taper_of(squared):
    squared = jnp.maximum(squared, 1e-20)
    remain = jnp.maximum(4.0 - squared * lax.rsqrt(squared), 0.0)
    twice = remain * remain
    return twice * twice * (5.0 - remain)


def kept_groups(sz, count, at):
    first = at * (sz.kept // UNROLL)
    last = jnp.minimum(lax.div(count + (UNROLL - 1), UNROLL), first + sz.kept // UNROLL)
    return first, jnp.maximum(first, last)


def vector_row(vec_ref, j):
    return vec_ref[pl.ds(jnp.minimum(j, vec_ref.shape[0] - 1), 1), :]


def own_features(lhs_ref, i):
    return lhs_ref[pl.ds(pl.multiple_of(i * BS, BS), BS), :DEPTH]


def other_features(rhs_ref, j):
    return rhs_ref[pl.ds(pl.multiple_of(j * DEPTH, DEPTH), DEPTH), :]


def clear_if_extra(sz, count, accs):
    @pl.when(count > sz.kept * ARRAYS)
    def clear():
        for ref in accs:
            ref[...] = jnp.zeros_like(ref)


def generate(sz, list_ref, count, lhs_ref, rhs_ref, tile_refs, squares, vec_ref, acc, acc_ones):
    clear_if_extra(sz, count, (acc, acc_ones))
    top = jnp.maximum(lax.div(count + (UNROLL - 1), UNROLL) - 1, 0)

    def squared(g, u):
        k = jnp.minimum(g, top) * UNROLL + u
        i, j = entry_of(list_ref, k)
        unused, twin = entry_of(list_ref, k + 1)
        both = jnp.concatenate([other_features(rhs_ref, j), other_features(rhs_ref, twin)], axis=1)
        return squared_of(own_features(lhs_ref, i), both)

    for u in range(0, UNROLL, 2):
        squares[u // 2 * BS : (u // 2 + 1) * BS, :] = squared(0, u)
    zero = jnp.zeros((8, BS), F32)
    carry = (jnp.int32(-1), (zero,) * (BS // 8), (zero,) * (BS // 8))
    for at, tile_ref in enumerate(tile_refs):

        def group(g, carry, at=at, tile_ref=tile_ref):
            before, totals, ones = carry
            totals, ones = list(totals), list(ones)
            for u in range(0, UNROLL, 2):
                following = squared(g + 1, u)
                i, j = entry_of(list_ref, g * UNROLL + u)
                unused, twin = entry_of(list_ref, g * UNROLL + u + 1)
                keep = jnp.where(i == before, 1.0, 0.0)
                before = i
                start = pl.multiple_of((g * UNROLL + u - at * sz.kept) * BS, BS)
                base = pl.multiple_of(i * BS, BS)
                row = jnp.broadcast_to(vector_row(vec_ref, j), (8, BS))
                twin_row = jnp.broadcast_to(vector_row(vec_ref, twin), (8, BS))
                for k in range(BS // 8):
                    r = 8 * k
                    here = slice(u // 2 * BS + r, u // 2 * BS + r + 8)
                    tile = taper_of(squares[here, :BS])
                    twin_tile = taper_of(squares[here, BS:])
                    tile_ref[pl.ds(start + r, 8), :] = tile
                    tile_ref[pl.ds(start + BS + r, 8), :] = twin_tile
                    squares[here, :] = following[r : r + 8, :]
                    totals[k] = totals[k] * keep + (tile * row + twin_tile * twin_row)
                    ones[k] = ones[k] * keep + (tile + twin_tile)
                    acc[pl.ds(base + r, 8), :] = totals[k]
                    acc_ones[pl.ds(base + r, 8), :] = ones[k]
            return before, tuple(totals), tuple(ones)

        carry = lax.fori_loop(*kept_groups(sz, count, at), group, carry)


def sweep(sz, list_ref, count, tile_refs, vec_ref, acc):
    clear_if_extra(sz, count, (acc,))
    zero = jnp.zeros((8, BS), F32)
    carry = (jnp.int32(-1), (zero,) * (BS // 8))
    for at, tile_ref in enumerate(tile_refs):

        def group(g, carry, at=at, tile_ref=tile_ref):
            before, totals = carry
            totals = list(totals)
            for u in range(0, UNROLL, 2):
                i, j = entry_of(list_ref, g * UNROLL + u)
                unused, twin = entry_of(list_ref, g * UNROLL + u + 1)
                keep = jnp.where(i == before, 1.0, 0.0)
                before = i
                start = pl.multiple_of((g * UNROLL + u - at * sz.kept) * BS, BS)
                base = pl.multiple_of(i * BS, BS)
                row = jnp.broadcast_to(vector_row(vec_ref, j), (8, BS))
                twin_row = jnp.broadcast_to(vector_row(vec_ref, twin), (8, BS))
                for k in range(BS // 8):
                    tile = tile_ref[pl.ds(start + 8 * k, 8), :]
                    twin_tile = tile_ref[pl.ds(start + BS + 8 * k, 8), :]
                    totals[k] = totals[k] * keep + (tile * row + twin_tile * twin_row)
                    acc[pl.ds(base + 8 * k, 8), :] = totals[k]
            return before, tuple(totals)

        carry = lax.fori_loop(*kept_groups(sz, count, at), group, carry)


def extras(sz, list_ref, count, vec_ref, acc, acc_ones, remake):
    def extra(k, unused):
        i, j = entry_of(list_ref, k)
        tile = taper_of(squared_of(*remake(i, j)))
        rows = pl.ds(pl.multiple_of(i * BS, BS), BS)
        acc[rows, :] += tile * vector_row(vec_ref, j)
        if acc_ones is not None:
            acc_ones[rows, :] += tile
        return unused

    kept = sz.kept * ARRAYS
    lax.fori_loop(kept, jnp.maximum(count, kept), extra, 0)


def finish(sz, acc, out_ref):
    unit = jnp.ones((8, 2 * BS), BF16)
    across = (((1,), (1,)), ((), ()))
    for i in range(sz.own):
        whole = acc[i * BS : (i + 1) * BS, :]
        high = whole.astype(BF16)
        low = (whole - high.astype(F32)).astype(BF16)
        y = lax.dot_general(unit, jnp.concatenate([high, low], axis=1), across, preferred_element_type=F32)
        out_ref[i : i + 1, :] = y[0:1, :] * sz.scale


def total_of(x):
    return jnp.sum(jnp.sum(x, axis=0, keepdims=True), axis=1, keepdims=True)


def place_block(sz, piece_ref, part, first, rhs_ref):
    def one(k, unused):
        h, m, l = features_of([block_row(piece_ref, c, part, k) for c in range(3)], -2.0, 4, 3)
        feats = jnp.concatenate([h, m, h, m, l, h], axis=0).astype(BF16)
        rhs_ref[pl.ds(pl.multiple_of((first + k) * DEPTH, DEPTH), DEPTH), :] = feats
        return unused

    lax.fori_loop(0, part, one, 0, unroll=max(4, 64 // sz.blks))


def first_kernel(sz, *refs):
    list_ref, count_ref, lhs_ref, nugget_any, obs_any, home_ref = refs[:6]
    coord_refs = refs[6 : 6 + (sz.blks - 1) * sz.reps]
    refs = refs[6 + (sz.blks - 1) * sz.reps :]
    tile_refs = refs[:ARRAYS]
    spare_ref, obs_ref, diag_ref, mapped_ref, norm_ref = refs[ARRAYS : ARRAYS + 5]
    rhs_ref, acc, acc_ones, total_row, squares, nugget_ref, done, fetched = refs[ARRAYS + 5 :]
    blk, rep = lax.axis_index("blk"), lax.axis_index("rep")
    home = pl.ds(pl.multiple_of(blk * sz.local_blocks, 8), sz.local_blocks)
    fetch = pltpu.make_async_copy(nugget_any, nugget_ref, fetched.at[0])
    fetch_obs = pltpu.make_async_copy(obs_any, obs_ref.at[home, :], fetched.at[1])
    fetch.start()
    fetch_obs.start()
    for at, piece_ref in enumerate(coord_refs):
        code, turn = at // sz.reps + 1, at % sz.reps
        part = sz.local_blocks // sz.reps
        first = jnp.bitwise_xor(blk, code) * sz.local_blocks + jnp.bitwise_xor(rep, turn) * part
        first = pl.multiple_of(first, 8)
        place_block(sz, piece_ref, part, first, rhs_ref)
        obs_ref[pl.ds(first, part), :] = piece_ref[3 * part : 4 * part, :]
    place_block(sz, home_ref, sz.local_blocks, blk * sz.local_blocks, rhs_ref)
    far = lax.broadcasted_iota(jnp.int32, (DEPTH, BS), 0) == 3
    rhs_ref[sz.blocks * DEPTH :, :] = jnp.where(far, 1e6, 0.0).astype(BF16)
    count = count_ref[0]
    fetch_obs.wait()
    generate(sz, list_ref, count, lhs_ref, rhs_ref, tile_refs, squares, obs_ref, acc, acc_ones)
    extras(
        sz,
        list_ref,
        count,
        obs_ref,
        acc,
        acc_ones,
        lambda i, j: (own_features(lhs_ref, i), other_features(rhs_ref, j)),
    )

    @pl.when(count > sz.kept * ARRAYS)
    def save():
        copy = pltpu.make_async_copy(rhs_ref, spare_ref, done)
        copy.start()
        copy.wait()

    finish(sz, acc_ones, total_row)
    finish(sz, acc, mapped_ref)
    quarter = lax.axis_index("col") * sz.reps + rep
    own = pl.ds(pl.multiple_of(sz.me() * sz.own, 8), sz.own)
    fetch.wait()
    diag = nugget_ref[pl.ds(pl.multiple_of(quarter * sz.own, 8), sz.own), :] + total_row[...]
    diag_ref[...] = diag
    mapped_ref[...] += diag * obs_ref[own, :]
    norm_ref[...] = jnp.broadcast_to(total_of(obs_ref[...] * obs_ref[...]), (8, BS))


def step_kernel(sz, last, *refs):
    list_ref, count_ref, lhs_ref, spare_ref, diag_ref, norm_ref, field_ref, resid_ref, dirn_ref = refs[:9]
    pieces = refs[9 : 9 + sz.plane]
    tile_refs = refs[9 + sz.plane : 9 + sz.plane + ARRAYS]
    rest = refs[9 + sz.plane + ARRAYS :]
    mapped_ref, next_norm_ref, next_field_ref, next_resid_ref, next_dirn_ref = rest[:5]
    if last:
        dot_ref, dirn = rest[5:7]
    else:
        dirn = next_dirn_ref
    mapped, acc, features, others, done = rest[-5:]
    me = sz.me()
    assemble(sz, pieces, sz.own, mapped)
    norm = norm_ref[0:1, 0:1]
    step = norm / total_of(dirn_ref[...] * mapped[...])
    resid = resid_ref[...] - step * mapped[...]
    next_norm = total_of(resid * resid)
    dirn[...] = resid + (next_norm / norm) * dirn_ref[...]
    next_norm_ref[...] = jnp.broadcast_to(next_norm, (8, BS))
    home = pl.ds(pl.multiple_of(lax.axis_index("blk") * sz.local_blocks, 8), sz.local_blocks)
    own = pl.ds(pl.multiple_of(me * sz.own, 8), sz.own)
    field = step * dirn_ref[home, :]
    if last:
        next_field_ref[...] = field_ref[...] + field
        next_resid_ref[...] = resid_ref[home, :] - step * mapped[home, :]
        next_dirn_ref[...] = dirn[home, :]
    else:
        next_field_ref[...] = field
        next_resid_ref[...] = resid

    def remake(i, j):
        for source, start, size, target in ((lhs_ref, i, BS, features), (spare_ref, j, DEPTH, others)):
            copy = pltpu.make_async_copy(source.at[pl.ds(pl.multiple_of(start * size, size), size), :], target, done)
            copy.start()
            copy.wait()
        return features[:, :DEPTH], others[...]

    sweep(sz, list_ref, count_ref[0], tile_refs, dirn, acc)
    extras(sz, list_ref, count_ref[0], dirn, acc, None, remake)
    finish(sz, acc, mapped_ref)
    ours = mapped_ref[...] + diag_ref[...] * dirn[own, :]
    mapped_ref[...] = ours
    if last:
        dot_ref[...] = jnp.broadcast_to(total_of(ours * dirn[own, :]), dot_ref.shape)


def last_kernel(sz, *refs):
    norm_ref, field_ref, resid_ref, dirn_ref = refs[:4]
    pieces = refs[4 : 4 + sz.plane]
    out_field_ref, out_resid_ref = refs[4 + sz.plane :]
    product = jnp.zeros((8, BS), F32)
    for ref in pieces:
        for z in range(sz.blks):
            product = product + ref[sz.own + 8 * z : sz.own + 8 * (z + 1), :]
    step = norm_ref[0:1, :] / product[0:1, :]
    out_field_ref[...] = field_ref[...] + step * dirn_ref[...]
    quarter = lax.axis_index("col") * sz.reps + lax.axis_index("rep")
    for k, ref in enumerate(pieces):
        rows = pl.ds(pl.multiple_of(jnp.bitwise_xor(quarter, k) * sz.own, 8), sz.own)
        out_resid_ref[rows, :] = resid_ref[rows, :] - step * ref[: sz.own, :]


def call(kernel, mib, in_specs, shapes, out_specs, scratch, flops, *args):
    return pl.pallas_call(
        kernel,
        in_specs=in_specs,
        out_shape=shapes,
        out_specs=out_specs,
        scratch_shapes=scratch,
        compiler_params=pltpu.CompilerParams(vmem_limit_bytes=mib * MIB),
        cost_estimate=pl.CostEstimate(flops=flops, bytes_accessed=1 << 20, transcendentals=0),
    )(*args)


def array(*shape, dtype=F32):
    return jax.ShapeDtypeStruct(shape, dtype)


def local(coords, observations, nugget, tile_pairs, tile_live):
    sz = Sizes(observations.shape[0], tile_pairs.shape[1])
    own, blocks, home = sz.own, sz.blocks, sz.local_blocks
    alive = jnp.arange(sz.slots, dtype=jnp.int32) < tile_live[0]
    pairs = jnp.where(alive, tile_pairs, -1).reshape(2 * sz.slots // BS, BS)
    rep = lax.axis_index("rep")
    part = home // sz.reps
    obs_rows = observations.reshape(home, BS)
    rows = coords.reshape(3, home, BS)
    half = lax.dynamic_slice_in_dim(jnp.concatenate([rows, obs_rows[None]], axis=0), rep * part, part, axis=1)
    half = half.reshape(4 * part, BS)
    nears = [swap(half, "blk", z) for z in range(1, sz.blks)]
    pair_arrays = over_plane(along_blk(pairs))

    lhs = call(
        functools.partial(lhs_kernel, sz),
        12,
        [VMEM],
        array((own + 1) * BS, BS, dtype=BF16),
        VMEM,
        [],
        10_000_000,
        rows,
    )
    lines = 2 * sz.slots // BS * sz.devs
    table, count = call(
        functools.partial(list_kernel, sz),
        12,
        [VMEM] * sz.plane,
        (array(sz.capacity // BS, BS, dtype=jnp.int32), array(1, dtype=jnp.int32)),
        (VMEM, SMEM),
        [pltpu.VMEM((lines, BS), jnp.int32)] * 2
        + [pltpu.VMEM((lines, BS), F32)] * 2
        + [pltpu.VMEM((sz.capacity, BS), F32)]
        + [pltpu.VMEM((sz.capacity // BS, BS), F32)] * 2,
        10_000_000,
        *pair_arrays,
    )
    table, lhs, *nears = lax.optimization_barrier((table.reshape(sz.capacity), lhs, *nears))
    coord_arrays = []
    for near in nears:
        coord_arrays += [near] + [swap(near, "rep", r) for r in range(1, sz.reps)]
    tall = pltpu.VMEM(((own + 1) * BS, BS), F32)
    kept = [pltpu.VMEM((sz.kept * BS, BS), F32)] * ARRAYS
    *tiles, spare, obs, diag, mapped, norm = call(
        functools.partial(first_kernel, sz),
        sz.first_mib,
        [SMEM, SMEM, VMEM, ANY, ANY] + [VMEM] * (1 + len(coord_arrays)),
        kept
        + [
            pltpu.HBM(((blocks + 1) * DEPTH, BS), BF16),
            array(blocks, BS),
            array(own, BS),
            array(own, BS),
            array(8, BS),
        ],
        [VMEM] * ARRAYS + [ANY] + [VMEM] * 4,
        [
            pltpu.VMEM(((blocks + 1) * DEPTH, BS), BF16),
            tall,
            tall,
            pltpu.VMEM((own, BS), F32),
            pltpu.VMEM((UNROLL // 2 * BS, 2 * BS), F32),
            pltpu.VMEM((home, BS), F32),
            pltpu.SemaphoreType.DMA,
            pltpu.SemaphoreType.DMA((2,)),
        ],
        100_000_000,
        table,
        count,
        lhs,
        pltpu.with_memory_space_constraint(nugget.reshape(home, BS), pltpu.HBM),
        pltpu.with_memory_space_constraint(obs_rows, pltpu.HBM),
        rows,
        *coord_arrays,
    )
    tiles = [pltpu.with_memory_space_constraint(tile, pltpu.VMEM) for tile in tiles]
    spare = pltpu.with_memory_space_constraint(spare, pltpu.HBM)
    field, resid, dirn = norm, obs, obs
    for sweep_index in range(1, ITERS):
        last = sweep_index + 1 == ITERS
        span = home if last else blocks
        outs = [array(own, BS), array(8, BS), array(home, BS), array(span, BS), array(span, BS)]
        mapped, norm, field, resid, dirn, *dot = call(
            functools.partial(step_kernel, sz, last),
            8,
            [SMEM, SMEM, ANY, ANY] + [VMEM] * (5 + sz.plane + ARRAYS),
            outs + [array(8, BS)] * last,
            [VMEM] * (len(outs) + last),
            [pltpu.VMEM((blocks, BS), F32)] * (1 + last)
            + [tall, pltpu.VMEM((BS, BS), BF16), pltpu.VMEM((DEPTH, BS), BF16), pltpu.SemaphoreType.DMA],
            100_000_000,
            table,
            count,
            lhs,
            spare,
            diag,
            norm,
            field,
            resid,
            dirn,
            *over_plane(along_blk(mapped)),
            *tiles,
        )
    ends = over_plane(jnp.concatenate([mapped, along_blk(dot[0])], axis=0))
    field, resid = call(
        functools.partial(last_kernel, sz),
        4,
        [VMEM] * (4 + sz.plane),
        (array(home, BS), array(home, BS)),
        (VMEM, VMEM),
        [],
        100_000,
        norm,
        field,
        resid,
        dirn,
        *ends,
    )
    return field.reshape(sz.points), resid.reshape(sz.points)


def solution(mesh):
    in_specs = (
        P(None, ("grp", "blk")),
        P(("grp", "blk")),
        P(("grp", "blk")),
        P(None, ("grp", "blk", "col", "rep")),
        P(("grp", "blk", "col", "rep")),
    )
    out_specs = (P(("grp", "blk")), P(("grp", "blk")))
    return jax.shard_map(local, mesh=mesh, in_specs=in_specs, out_specs=out_specs, check_vma=False)
```

```python
import functools

import jax
import jax.numpy as jnp
from jax import lax
from jax.experimental import pallas as pl
from jax.experimental.pallas import tpu as pltpu
from jax.sharding import PartitionSpec as P

BS = 128
ITERS = 3
SUPPORT = 0.3
DEPTH = 48
UNROLL = 16
ARRAYS = 4
MIB = 1024 * 1024
VMEM = pl.BlockSpec(memory_space=pltpu.VMEM)
SMEM = pl.BlockSpec(memory_space=pltpu.SMEM)
ANY = pl.BlockSpec(memory_space=pl.ANY)
BF16 = jnp.bfloat16
F32 = jnp.float32


class Sizes:
    def __init__(self, points, slots):
        self.blks = lax.axis_size("blk")
        self.reps = lax.axis_size("rep")
        self.plane = lax.axis_size("col") * self.reps
        self.devs = self.blks * self.plane
        self.points = points
        self.slots = slots
        self.local_blocks = points // BS
        self.blocks = self.local_blocks * self.blks
        self.own = self.local_blocks // self.plane
        self.capacity = 2 * self.plane * slots + 1024
        per_row = slots * self.devs // self.blocks
        self.first_mib = 6 + self.blocks * DEPTH * BS * 2 // MIB
        self.kept = min(448, (48 - self.first_mib) * 16) // (ARRAYS * UNROLL) * UNROLL
        self.scale = 16.0 / (BS * per_row) / 256.0

    def me(self):
        return (lax.axis_index("blk") * lax.axis_size("col") + lax.axis_index("col")) * self.reps + lax.axis_index(
            "rep"
        )


def swap(x, axis, code):
    return lax.ppermute(x, axis, [(i, i ^ code) for i in range(lax.axis_size(axis))])


def along_blk(x):
    return jnp.concatenate([x] + [swap(x, "blk", k) for k in range(1, lax.axis_size("blk"))], axis=0)


def over_plane(x):
    reps = lax.axis_size("rep")
    found = {0: x}
    for c in range(1, lax.axis_size("col")):
        found[c * reps] = swap(x, "col", c)
    for start in sorted(found):
        for r in range(1, reps):
            found[start + r] = swap(found[start], "rep", r)
    return [found[k] for k in sorted(found)]


def assemble(sz, refs, rows, target):
    me = sz.me()
    for k, ref in enumerate(refs):
        for z in range(ref.shape[0] // rows):
            start = pl.multiple_of(jnp.bitwise_xor(me, z * sz.plane + k) * rows, 8)
            target[pl.ds(start, rows), :] = ref[z * rows : (z + 1) * rows, :]


def split3(x):
    high = x.astype(BF16).astype(F32)
    rest = x - high
    middle = rest.astype(BF16).astype(F32)
    return high, middle, rest - middle


def features_of(rows, factor, unit, norm):
    feature = lax.broadcasted_iota(jnp.int32, (8, BS), 0)
    x, y, z = ((row - 0.5) * (4.0 / SUPPORT) for row in rows)
    feats = jnp.where(feature == unit, 1.0, 0.0)
    for place, row in ((0, factor * x), (1, factor * y), (2, factor * z), (norm, x * x + y * y + z * z)):
        feats = jnp.where(feature == place, row, feats)
    return split3(feats)


def block_row(ref, c, part, k):
    return ref[c, pl.ds(k, 1), :] if len(ref.shape) == 3 else ref[pl.ds(c * part + k, 1), :]


def lhs_kernel(sz, home_ref, out_ref):
    quarter = lax.axis_index("col") * sz.reps + lax.axis_index("rep")
    for i in range(sz.own):
        h, m, l = features_of([block_row(home_ref, c, None, quarter * sz.own + i) for c in range(3)], 1.0, 3, 4)
        feats = jnp.concatenate([h, h, m, m, h, l, jnp.zeros((BS - DEPTH, BS), F32)], axis=0)
        out_ref[i * BS : (i + 1) * BS, :] = feats.T.astype(BF16)
    out_ref[sz.own * BS :, :] = jnp.zeros((BS, BS), BF16)


def list_kernel(sz, *refs):
    me = sz.me()
    out_ref, count_ref, target, other, place, value, key_column, key_row, entry_row = refs[sz.plane :]
    lines = sz.slots // BS
    at = 2 * lines * sz.devs
    for base in range(0, at, 2 * lines):
        pairs_ref = refs[base // (2 * lines * sz.blks)]
        start = base % (2 * lines * sz.blks)
        rows = pairs_ref[start : start + lines, :]
        cols = pairs_ref[start + lines : start + 2 * lines, :]
        target[base : base + lines, :] = rows
        other[base : base + lines, :] = cols
        target[base + lines : base + 2 * lines, :] = cols
        other[base + lines : base + 2 * lines, :] = rows
    local = target[...] - me * sz.own
    mine = jnp.logical_and(local >= 0, local < sz.own)
    flags = jnp.where(mine, 1.0, 0.0)
    a = lax.broadcasted_iota(jnp.int32, (BS, BS), 0)
    b = lax.broadcasted_iota(jnp.int32, (BS, BS), 1)
    ahead = jnp.where(a < b, 1.0, 0.0).astype(BF16)
    before = jnp.dot(flags.astype(BF16), ahead, preferred_element_type=F32)
    totals = jnp.broadcast_to(jnp.sum(flags, axis=1, keepdims=True), (at, BS))
    a = lax.broadcasted_iota(jnp.int32, (at, at), 0)
    b = lax.broadcasted_iota(jnp.int32, (at, at), 1)
    above = jnp.dot(jnp.where(b < a, 1.0, 0.0).astype(BF16), totals.astype(BF16), preferred_element_type=F32)
    place[...] = jnp.where(mine, above + before, -1.0)
    ends = jnp.sum(jnp.where(lax.broadcasted_iota(jnp.int32, (at, BS), 1) == 0, above + totals, 0.0), axis=1, keepdims=True)
    starts = ends - totals[:, 0:1]
    value[...] = (local + 256 * other[...]).astype(F32)
    count = jnp.sum(flags).astype(jnp.int32)
    sub = lax.broadcasted_iota(jnp.int32, (BS, BS), 0)
    lane = lax.broadcasted_iota(jnp.int32, (1, BS), 1)

    chunks = jnp.maximum(lax.shift_right_logical(count + BS - 1, 7), 1)

    def key_of(found, slot):
        entry = jnp.where(slot < count, found.astype(jnp.int32), sz.own)
        return entry.astype(F32), (jnp.bitwise_and(entry, 255) * 65536 + slot).astype(F32)

    def compact(c, unused):
        slot = (sub + c * BS).astype(F32)
        base = (c * BS).astype(F32)
        bounds = jnp.where(ends <= base, 1.0, 0.0) + jnp.where(starts < base + BS, 1024.0, 0.0)
        bounds = jnp.sum(bounds).astype(jnp.int32)
        first = jnp.minimum(lax.shift_right_logical(jnp.bitwise_and(bounds, 1023), 3), at // 8)
        last = lax.shift_right_logical(lax.shift_right_logical(bounds, 10) + 7, 3)

        def lines(g, total):
            for u in range(8):
                r = 8 * g + u
                hit = place[pl.ds(r, 1), :] == slot
                total = jnp.where(hit, value[pl.ds(r, 1), :], total)
            return total

        total = lax.fori_loop(first, last, lines, jnp.zeros((BS, BS), F32))
        entry, key = key_of(jnp.sum(total.T, axis=0, keepdims=True), lane + c * BS)
        entry_row[pl.ds(c, 1), :] = entry
        key_row[pl.ds(c, 1), :] = key
        unused_entry, key = key_of(jnp.sum(total, axis=1, keepdims=True), sub[:, 0:1] + c * BS)
        key_column[pl.ds(pl.multiple_of(c * BS, BS), BS), :] = jnp.broadcast_to(key, (BS, BS))
        return unused

    lax.fori_loop(0, chunks, compact, 0)

    bound = lane.astype(F32) * 65536.0

    def tally(c, carry):
        keys = key_column[pl.ds(pl.multiple_of(c * BS, BS), BS), :]
        from_here, after = carry
        return from_here + jnp.where(keys >= bound, 1.0, 0.0), after + jnp.where(keys >= bound + 65536.0, 1.0, 0.0)

    zero = jnp.zeros((BS, BS), F32)
    from_here, after = lax.fori_loop(0, chunks, tally, (zero, zero))
    from_here = jnp.sum(from_here, axis=0, keepdims=True)
    each = from_here - jnp.sum(after, axis=0, keepdims=True)
    odd = each - 2.0 * jnp.floor(0.5 * each)
    pad = jnp.where(lane < sz.own, jnp.where(each == 0.0, 2.0, odd), 0.0)
    wide_pad = jnp.broadcast_to(pad, (BS, BS))
    pad_column = wide_pad.T
    pad_before = jnp.dot(wide_pad.astype(BF16), ahead, preferred_element_type=F32)[0:1, :]
    start = (chunks * BS).astype(F32) - from_here + pad_before
    null_places = (jnp.where(pad > 0.0, start + each, -1.0), jnp.where(pad > 1.0, start + 1.0, -1.0))
    null_entry = (lane + 256 * sz.blocks).astype(F32)
    full = count + jnp.sum(pad).astype(jnp.int32)
    count_ref[0] = full

    pairs = lax.shift_right_logical(chunks + 1, 1)
    key_column[pl.ds(pl.multiple_of(chunks * BS, BS), BS), :] = jnp.full((BS, BS), 1e9, F32)

    def rank(c, unused):
        keys = key_row[pl.ds(c, 1), :]

        def below(k, total):
            for u in range(2):
                lower = key_column[pl.ds(pl.multiple_of((2 * k + u) * BS, BS), BS), :] < keys
                total = total + jnp.where(lower, 1.0, 0.0)
            return total

        past = (sub + 1).astype(F32) * 65536.0 <= keys
        total = lax.fori_loop(0, pairs, below, jnp.where(past, pad_column, 0.0))
        place[pl.ds(c, 1), :] = jnp.sum(total, axis=0, keepdims=True)
        return unused

    lax.fori_loop(0, chunks, rank, 0)

    place[pl.ds(chunks, 1), :] = jnp.full((1, BS), -1.0, F32)

    def arrange(c, unused):
        slot = (sub + c * BS).astype(F32)

        def line(k, total):
            for u in range(2):
                hit = place[pl.ds(2 * k + u, 1), :] == slot
                total = jnp.where(hit, entry_row[pl.ds(2 * k + u, 1), :], total)
            return total

        nulls = jnp.logical_or(null_places[0] == slot, null_places[1] == slot)
        total = lax.fori_loop(0, pairs, line, jnp.where(nulls, null_entry, 0.0))
        found = jnp.sum(total.T, axis=0, keepdims=True).astype(jnp.int32)
        out_ref[pl.ds(c, 1), :] = jnp.where(lane + c * BS < full, found, sz.own)
        return unused

    lax.fori_loop(0, jnp.maximum(lax.shift_right_logical(full + BS - 1, 7), 1), arrange, 0)


def entry_of(list_ref, k):
    entry = list_ref[k]
    return jnp.bitwise_and(entry, 255), lax.shift_right_logical(entry, 8)


def squared_of(features, others):
    return jnp.dot(features, others, preferred_element_type=F32)


def taper_of(squared):
    squared = jnp.maximum(squared, 1e-20)
    remain = jnp.maximum(4.0 - squared * lax.rsqrt(squared), 0.0)
    twice = remain * remain
    return twice * twice * (5.0 - remain)


def kept_groups(sz, count, at):
    first = at * (sz.kept // UNROLL)
    last = jnp.minimum(lax.div(count + (UNROLL - 1), UNROLL), first + sz.kept // UNROLL)
    return first, jnp.maximum(first, last)


def vector_row(vec_ref, j):
    return vec_ref[pl.ds(jnp.minimum(j, vec_ref.shape[0] - 1), 1), :]


def own_features(lhs_ref, i):
    return lhs_ref[pl.ds(pl.multiple_of(i * BS, BS), BS), :DEPTH]


def other_features(rhs_ref, j):
    return rhs_ref[pl.ds(pl.multiple_of(j * DEPTH, DEPTH), DEPTH), :]


def clear_if_extra(sz, count, accs):
    @pl.when(count > sz.kept * ARRAYS)
    def clear():
        for ref in accs:
            ref[...] = jnp.zeros_like(ref)


def generate(sz, list_ref, count, lhs_ref, rhs_ref, tile_refs, squares, vec_ref, acc, acc_ones):
    clear_if_extra(sz, count, (acc, acc_ones))
    top = jnp.maximum(lax.div(count + (UNROLL - 1), UNROLL) - 1, 0)

    def squared(g, u):
        k = jnp.minimum(g, top) * UNROLL + u
        i, j = entry_of(list_ref, k)
        unused, twin = entry_of(list_ref, k + 1)
        both = jnp.concatenate([other_features(rhs_ref, j), other_features(rhs_ref, twin)], axis=1)
        return squared_of(own_features(lhs_ref, i), both)

    for u in range(0, UNROLL, 2):
        squares[u // 2 * BS : (u // 2 + 1) * BS, :] = squared(0, u)
    zero = jnp.zeros((8, BS), F32)
    carry = (jnp.int32(-1), (zero,) * (BS // 8), (zero,) * (BS // 8))
    for at, tile_ref in enumerate(tile_refs):

        def group(g, carry, at=at, tile_ref=tile_ref):
            before, totals, ones = carry
            totals, ones = list(totals), list(ones)
            for u in range(0, UNROLL, 2):
                following = squared(g + 1, u)
                i, j = entry_of(list_ref, g * UNROLL + u)
                unused, twin = entry_of(list_ref, g * UNROLL + u + 1)
                keep = jnp.where(i == before, 1.0, 0.0)
                before = i
                start = pl.multiple_of((g * UNROLL + u - at * sz.kept) * BS, BS)
                base = pl.multiple_of(i * BS, BS)
                row = jnp.broadcast_to(vector_row(vec_ref, j), (8, BS))
                twin_row = jnp.broadcast_to(vector_row(vec_ref, twin), (8, BS))
                for k in range(BS // 8):
                    r = 8 * k
                    here = slice(u // 2 * BS + r, u // 2 * BS + r + 8)
                    tile = taper_of(squares[here, :BS])
                    twin_tile = taper_of(squares[here, BS:])
                    tile_ref[pl.ds(start + r, 8), :] = tile
                    tile_ref[pl.ds(start + BS + r, 8), :] = twin_tile
                    squares[here, :] = following[r : r + 8, :]
                    totals[k] = totals[k] * keep + (tile * row + twin_tile * twin_row)
                    ones[k] = ones[k] * keep + (tile + twin_tile)
                    acc[pl.ds(base + r, 8), :] = totals[k]
                    acc_ones[pl.ds(base + r, 8), :] = ones[k]
            return before, tuple(totals), tuple(ones)

        carry = lax.fori_loop(*kept_groups(sz, count, at), group, carry)


def sweep(sz, list_ref, count, tile_refs, vec_ref, acc):
    clear_if_extra(sz, count, (acc,))
    zero = jnp.zeros((8, BS), F32)
    carry = (jnp.int32(-1), (zero,) * (BS // 8))
    for at, tile_ref in enumerate(tile_refs):

        def group(g, carry, at=at, tile_ref=tile_ref):
            before, totals = carry
            totals = list(totals)
            for u in range(0, UNROLL, 2):
                i, j = entry_of(list_ref, g * UNROLL + u)
                unused, twin = entry_of(list_ref, g * UNROLL + u + 1)
                keep = jnp.where(i == before, 1.0, 0.0)
                before = i
                start = pl.multiple_of((g * UNROLL + u - at * sz.kept) * BS, BS)
                base = pl.multiple_of(i * BS, BS)
                row = jnp.broadcast_to(vector_row(vec_ref, j), (8, BS))
                twin_row = jnp.broadcast_to(vector_row(vec_ref, twin), (8, BS))
                for k in range(BS // 8):
                    tile = tile_ref[pl.ds(start + 8 * k, 8), :]
                    twin_tile = tile_ref[pl.ds(start + BS + 8 * k, 8), :]
                    totals[k] = totals[k] * keep + (tile * row + twin_tile * twin_row)
                    acc[pl.ds(base + 8 * k, 8), :] = totals[k]
            return before, tuple(totals)

        carry = lax.fori_loop(*kept_groups(sz, count, at), group, carry)


def extras(sz, list_ref, count, vec_ref, acc, acc_ones, remake):
    def extra(k, unused):
        i, j = entry_of(list_ref, k)
        tile = taper_of(squared_of(*remake(i, j)))
        rows = pl.ds(pl.multiple_of(i * BS, BS), BS)
        acc[rows, :] += tile * vector_row(vec_ref, j)
        if acc_ones is not None:
            acc_ones[rows, :] += tile
        return unused

    kept = sz.kept * ARRAYS
    lax.fori_loop(kept, jnp.maximum(count, kept), extra, 0)


def finish(sz, acc, out_ref):
    unit = jnp.ones((8, 2 * BS), BF16)
    across = (((1,), (1,)), ((), ()))
    for i in range(sz.own):
        whole = acc[i * BS : (i + 1) * BS, :]
        high = whole.astype(BF16)
        low = (whole - high.astype(F32)).astype(BF16)
        y = lax.dot_general(unit, jnp.concatenate([high, low], axis=1), across, preferred_element_type=F32)
        out_ref[i : i + 1, :] = y[0:1, :] * sz.scale


def total_of(x):
    return jnp.sum(jnp.sum(x, axis=0, keepdims=True), axis=1, keepdims=True)


def place_block(sz, piece_ref, part, first, rhs_ref):
    def one(k, unused):
        h, m, l = features_of([block_row(piece_ref, c, part, k) for c in range(3)], -2.0, 4, 3)
        feats = jnp.concatenate([h, m, h, m, l, h], axis=0).astype(BF16)
        rhs_ref[pl.ds(pl.multiple_of((first + k) * DEPTH, DEPTH), DEPTH), :] = feats
        return unused

    lax.fori_loop(0, part, one, 0, unroll=max(4, 64 // sz.blks))


def first_kernel(sz, *refs):
    list_ref, count_ref, lhs_ref, nugget_any, obs_any, home_ref = refs[:6]
    coord_refs = refs[6 : 6 + (sz.blks - 1) * sz.reps]
    refs = refs[6 + (sz.blks - 1) * sz.reps :]
    tile_refs = refs[:ARRAYS]
    spare_ref, obs_ref, diag_ref, mapped_ref, norm_ref = refs[ARRAYS : ARRAYS + 5]
    rhs_ref, acc, acc_ones, total_row, squares, nugget_ref, done, fetched = refs[ARRAYS + 5 :]
    blk, rep = lax.axis_index("blk"), lax.axis_index("rep")
    home = pl.ds(pl.multiple_of(blk * sz.local_blocks, 8), sz.local_blocks)
    fetch = pltpu.make_async_copy(nugget_any, nugget_ref, fetched.at[0])
    fetch_obs = pltpu.make_async_copy(obs_any, obs_ref.at[home, :], fetched.at[1])
    fetch.start()
    fetch_obs.start()
    for at, piece_ref in enumerate(coord_refs):
        code, turn = at // sz.reps + 1, at % sz.reps
        part = sz.local_blocks // sz.reps
        first = jnp.bitwise_xor(blk, code) * sz.local_blocks + jnp.bitwise_xor(rep, turn) * part
        first = pl.multiple_of(first, 8)
        place_block(sz, piece_ref, part, first, rhs_ref)
        obs_ref[pl.ds(first, part), :] = piece_ref[3 * part : 4 * part, :]
    place_block(sz, home_ref, sz.local_blocks, blk * sz.local_blocks, rhs_ref)
    far = lax.broadcasted_iota(jnp.int32, (DEPTH, BS), 0) == 3
    rhs_ref[sz.blocks * DEPTH :, :] = jnp.where(far, 1e6, 0.0).astype(BF16)
    count = count_ref[0]
    fetch_obs.wait()
    generate(sz, list_ref, count, lhs_ref, rhs_ref, tile_refs, squares, obs_ref, acc, acc_ones)
    extras(
        sz,
        list_ref,
        count,
        obs_ref,
        acc,
        acc_ones,
        lambda i, j: (own_features(lhs_ref, i), other_features(rhs_ref, j)),
    )

    @pl.when(count > sz.kept * ARRAYS)
    def save():
        copy = pltpu.make_async_copy(rhs_ref, spare_ref, done)
        copy.start()
        copy.wait()

    finish(sz, acc_ones, total_row)
    finish(sz, acc, mapped_ref)
    quarter = lax.axis_index("col") * sz.reps + rep
    own = pl.ds(pl.multiple_of(sz.me() * sz.own, 8), sz.own)
    fetch.wait()
    diag = nugget_ref[pl.ds(pl.multiple_of(quarter * sz.own, 8), sz.own), :] + total_row[...]
    diag_ref[...] = diag
    mapped_ref[...] += diag * obs_ref[own, :]
    norm_ref[...] = jnp.broadcast_to(total_of(obs_ref[...] * obs_ref[...]), (8, BS))


def step_kernel(sz, last, *refs):
    list_ref, count_ref, lhs_ref, spare_ref, diag_ref, norm_ref, field_ref, resid_ref, dirn_ref = refs[:9]
    pieces = refs[9 : 9 + sz.plane]
    tile_refs = refs[9 + sz.plane : 9 + sz.plane + ARRAYS]
    rest = refs[9 + sz.plane + ARRAYS :]
    mapped_ref, next_norm_ref, next_field_ref, next_resid_ref, next_dirn_ref = rest[:5]
    if last:
        dot_ref, dirn = rest[5:7]
    else:
        dirn = next_dirn_ref
    mapped, acc, features, others, done = rest[-5:]
    me = sz.me()
    assemble(sz, pieces, sz.own, mapped)
    norm = norm_ref[0:1, 0:1]
    step = norm / total_of(dirn_ref[...] * mapped[...])
    resid = resid_ref[...] - step * mapped[...]
    next_norm = total_of(resid * resid)
    dirn[...] = resid + (next_norm / norm) * dirn_ref[...]
    next_norm_ref[...] = jnp.broadcast_to(next_norm, (8, BS))
    home = pl.ds(pl.multiple_of(lax.axis_index("blk") * sz.local_blocks, 8), sz.local_blocks)
    own = pl.ds(pl.multiple_of(me * sz.own, 8), sz.own)
    field = step * dirn_ref[home, :]
    if last:
        next_field_ref[...] = field_ref[...] + field
        next_resid_ref[...] = resid_ref[home, :] - step * mapped[home, :]
        next_dirn_ref[...] = dirn[home, :]
    else:
        next_field_ref[...] = field
        next_resid_ref[...] = resid

    def remake(i, j):
        for source, start, size, target in ((lhs_ref, i, BS, features), (spare_ref, j, DEPTH, others)):
            copy = pltpu.make_async_copy(source.at[pl.ds(pl.multiple_of(start * size, size), size), :], target, done)
            copy.start()
            copy.wait()
        return features[:, :DEPTH], others[...]

    sweep(sz, list_ref, count_ref[0], tile_refs, dirn, acc)
    extras(sz, list_ref, count_ref[0], dirn, acc, None, remake)
    finish(sz, acc, mapped_ref)
    ours = mapped_ref[...] + diag_ref[...] * dirn[own, :]
    mapped_ref[...] = ours
    if last:
        dot_ref[...] = jnp.broadcast_to(total_of(ours * dirn[own, :]), dot_ref.shape)


def last_kernel(sz, *refs):
    norm_ref, field_ref, resid_ref, dirn_ref = refs[:4]
    pieces = refs[4 : 4 + sz.plane]
    out_field_ref, out_resid_ref = refs[4 + sz.plane :]
    product = jnp.zeros((8, BS), F32)
    for ref in pieces:
        for z in range(sz.blks):
            product = product + ref[sz.own + 8 * z : sz.own + 8 * (z + 1), :]
    step = norm_ref[0:1, :] / product[0:1, :]
    out_field_ref[...] = field_ref[...] + step * dirn_ref[...]
    quarter = lax.axis_index("col") * sz.reps + lax.axis_index("rep")
    for k, ref in enumerate(pieces):
        rows = pl.ds(pl.multiple_of(jnp.bitwise_xor(quarter, k) * sz.own, 8), sz.own)
        out_resid_ref[rows, :] = resid_ref[rows, :] - step * ref[: sz.own, :]


def call(kernel, mib, in_specs, shapes, out_specs, scratch, flops, *args):
    return pl.pallas_call(
        kernel,
        in_specs=in_specs,
        out_shape=shapes,
        out_specs=out_specs,
        scratch_shapes=scratch,
        compiler_params=pltpu.CompilerParams(vmem_limit_bytes=mib * MIB),
        cost_estimate=pl.CostEstimate(flops=flops, bytes_accessed=1 << 20, transcendentals=0),
    )(*args)


def array(*shape, dtype=F32):
    return jax.ShapeDtypeStruct(shape, dtype)


def local(coords, observations, nugget, tile_pairs, tile_live):
    sz = Sizes(observations.shape[0], tile_pairs.shape[1])
    own, blocks, home = sz.own, sz.blocks, sz.local_blocks
    alive = jnp.arange(sz.slots, dtype=jnp.int32) < tile_live[0]
    pairs = jnp.where(alive, tile_pairs, -1).reshape(2 * sz.slots // BS, BS)
    rep = lax.axis_index("rep")
    part = home // sz.reps
    obs_rows = observations.reshape(home, BS)
    rows = coords.reshape(3, home, BS)
    half = lax.dynamic_slice_in_dim(jnp.concatenate([rows, obs_rows[None]], axis=0), rep * part, part, axis=1)
    half = half.reshape(4 * part, BS)
    nears = [swap(half, "blk", z) for z in range(1, sz.blks)]
    pair_arrays = over_plane(along_blk(pairs))

    lhs = call(
        functools.partial(lhs_kernel, sz),
        12,
        [VMEM],
        array((own + 1) * BS, BS, dtype=BF16),
        VMEM,
        [],
        10_000_000,
        rows,
    )
    lines = 2 * sz.slots // BS * sz.devs
    table, count = call(
        functools.partial(list_kernel, sz),
        12,
        [VMEM] * sz.plane,
        (array(sz.capacity // BS, BS, dtype=jnp.int32), array(1, dtype=jnp.int32)),
        (VMEM, SMEM),
        [pltpu.VMEM((lines, BS), jnp.int32)] * 2
        + [pltpu.VMEM((lines, BS), F32)] * 2
        + [pltpu.VMEM((sz.capacity, BS), F32)]
        + [pltpu.VMEM((sz.capacity // BS, BS), F32)] * 2,
        10_000_000,
        *pair_arrays,
    )
    table, lhs, *nears = lax.optimization_barrier((table.reshape(sz.capacity), lhs, *nears))
    coord_arrays = []
    for near in nears:
        coord_arrays += [near] + [swap(near, "rep", r) for r in range(1, sz.reps)]
    tall = pltpu.VMEM(((own + 1) * BS, BS), F32)
    kept = [pltpu.VMEM((sz.kept * BS, BS), F32)] * ARRAYS
    *tiles, spare, obs, diag, mapped, norm = call(
        functools.partial(first_kernel, sz),
        sz.first_mib,
        [SMEM, SMEM, VMEM, ANY, ANY] + [VMEM] * (1 + len(coord_arrays)),
        kept
        + [
            pltpu.HBM(((blocks + 1) * DEPTH, BS), BF16),
            array(blocks, BS),
            array(own, BS),
            array(own, BS),
            array(8, BS),
        ],
        [VMEM] * ARRAYS + [ANY] + [VMEM] * 4,
        [
            pltpu.VMEM(((blocks + 1) * DEPTH, BS), BF16),
            tall,
            tall,
            pltpu.VMEM((own, BS), F32),
            pltpu.VMEM((UNROLL // 2 * BS, 2 * BS), F32),
            pltpu.VMEM((home, BS), F32),
            pltpu.SemaphoreType.DMA,
            pltpu.SemaphoreType.DMA((2,)),
        ],
        100_000_000,
        table,
        count,
        lhs,
        pltpu.with_memory_space_constraint(nugget.reshape(home, BS), pltpu.HBM),
        pltpu.with_memory_space_constraint(obs_rows, pltpu.HBM),
        rows,
        *coord_arrays,
    )
    tiles = [pltpu.with_memory_space_constraint(tile, pltpu.VMEM) for tile in tiles]
    spare = pltpu.with_memory_space_constraint(spare, pltpu.HBM)
    field, resid, dirn = norm, obs, obs
    for sweep_index in range(1, ITERS):
        last = sweep_index + 1 == ITERS
        span = home if last else blocks
        outs = [array(own, BS), array(8, BS), array(home, BS), array(span, BS), array(span, BS)]
        mapped, norm, field, resid, dirn, *dot = call(
            functools.partial(step_kernel, sz, last),
            8,
            [SMEM, SMEM, ANY, ANY] + [VMEM] * (5 + sz.plane + ARRAYS),
            outs + [array(8, BS)] * last,
            [VMEM] * (len(outs) + last),
            [pltpu.VMEM((blocks, BS), F32)] * (1 + last)
            + [tall, pltpu.VMEM((BS, BS), BF16), pltpu.VMEM((DEPTH, BS), BF16), pltpu.SemaphoreType.DMA],
            100_000_000,
            table,
            count,
            lhs,
            spare,
            diag,
            norm,
            field,
            resid,
            dirn,
            *over_plane(along_blk(mapped)),
            *tiles,
        )
    ends = over_plane(jnp.concatenate([mapped, along_blk(dot[0])], axis=0))
    field, resid = call(
        functools.partial(last_kernel, sz),
        4,
        [VMEM] * (4 + sz.plane),
        (array(home, BS), array(home, BS)),
        (VMEM, VMEM),
        [],
        100_000,
        norm,
        field,
        resid,
        dirn,
        *ends,
    )
    return field.reshape(sz.points), resid.reshape(sz.points)


def solution(mesh):
    in_specs = (
        P(None, ("grp", "blk")),
        P(("grp", "blk")),
        P(("grp", "blk")),
        P(None, ("grp", "blk", "col", "rep")),
        P(("grp", "blk", "col", "rep")),
    )
    out_specs = (P(("grp", "blk")), P(("grp", "blk")))
    return jax.shard_map(local, mesh=mesh, in_specs=in_specs, out_specs=out_specs, check_vma=False)
```
